256 devices in a mesh: gx: 4 (over x_lo, core), gy: 8 (over z), gz: 8 (over x_hi, y).
Axes of the slice: x: 4 (x_hi: 2, x_lo: 2; x = x_hi * 2 + x_lo), y: 4, z: 8, core: 2. Of those that a mesh axis runs over, the one named last changes fastest.
Arguments:
- features: bfloat16 [96, 96, 6144], P('gx', 'gy', 'gz'), may hold values from -6 to 6
- fine_weight: bfloat16 [27, 4096], replicated, may hold values from -0.15625 to 0.15625
- coarse_weight: bfloat16 [27, 8192], replicated, may hold values from -0.15625 to 0.15625
- cotangent: bfloat16 [48, 48, 6144], P('gx', 'gy', 'gz'), may hold values from -24 to 24
Outputs:
- grad_features: bfloat16 [96, 96, 6144], P('gx', 'gy', 'gz')
- grad_fine: float32 [27, 4096], replicated
- grad_coarse: float32 [27, 8192], replicated
The draws below stay inside these ranges and needn't reach their ends.
All inputs are finite; a program needn't handle non-finite values.
Results may differ from the reference program's by a relative error of at most 0.015.
Values may be sent and summed in bfloat16 or wider, within the bound.
No kernel may reach another device: no remote copies, remote signals or barrier semaphores. Data moves between devices by JAX's collectives and lax.ppermute only.
A program may use at most 64 MiB of HBM per device.

```python
import math
import jax
import jax.numpy as jnp
from jax import lax

CH_FINE = 64
CH_COARSE = 128
NX = 96
NY = 96
NZ = 96


def level_of(rng, extent, cuts, least, largest):
    level = 1.0
    for dim, parts in cuts:
        draws = jax.random.uniform(jax.random.fold_in(jax.random.fold_in(rng, 6), dim), (parts,), jnp.float32, least / len(cuts), largest / len(cuts))
        level = level * jnp.repeat(jnp.exp(draws), extent[dim] // parts).reshape((-1,) + (1,) * (len(extent) - 1 - dim))
    return level


def centred(own_key, shape, spread, most, cuts=(), held_as=jnp.bfloat16):
    entries = spread * jax.random.normal(own_key, shape, jnp.float32)
    if cuts:
        entries = entries * level_of(own_key, shape, cuts, -0.22, 0.18)
    return jnp.clip(entries, -most, most).astype(held_as)


def setup_inputs(seed: int = 0) -> dict:
    arg_keys = jax.random.split(jax.random.key(seed), 5)
    features = centred(arg_keys[0], (NX, NY, NZ * CH_FINE), 1.0, 6.0, ((0, 4), (1, 8), (2, 8)))
    fine_weight = centred(arg_keys[1], (27, CH_FINE * CH_FINE), (27 * CH_FINE) ** -0.5, 0.15625)
    coarse_weight = centred(arg_keys[2], (27, CH_FINE * CH_COARSE), (27 * CH_FINE) ** -0.5, 0.15625)
    cotangent = centred(arg_keys[3], (NX // 2, NY // 2, (NZ // 2) * CH_COARSE), 4.0, 24.0, ((0, 4), (1, 8), (2, 8)))
    return dict(features=features, fine_weight=fine_weight, coarse_weight=coarse_weight, cotangent=cotangent)


def local_conv(volume, kernel):
    return lax.conv_general_dilated(volume[None], kernel, (1, 1, 1), 'VALID', dimension_numbers=('NDHWC', 'DHWIO', 'NDHWC'), preferred_element_type=jnp.float32)[0]

def kernel_cells(flat, inputs):
    return flat.reshape(3, 3, 3, inputs, flat.shape[1] // inputs)

def flipped_kernel(kernel):
    return jnp.transpose(kernel[::-1, ::-1, ::-1], (0, 1, 2, 4, 3))

def silu_slope(value):
    sigma = jax.nn.sigmoid(value)
    return sigma * (1.0 + value * (1.0 - sigma))

def pool_mean(volume):
    sx, sy, sz, chans = volume.shape
    blocks = volume.astype(jnp.float32).reshape(sx // 2, 2, sy // 2, 2, sz // 2, 2, chans)
    return blocks.mean(axis=(1, 3, 5))

def spread_up(volume):
    sx, sy, sz, chans = volume.shape
    values = volume.astype(jnp.float32)[:, None, :, None, :, None, :]
    return jnp.broadcast_to(values, (sx, 2, sy, 2, sz, 2, chans)).reshape(2 * sx, 2 * sy, 2 * sz, chans)

def weight_grad(gradient, padded):
    sx, sy, sz, outs = gradient.shape
    chans = padded.shape[3]
    rows = gradient.reshape(-1, outs)
    pieces = []
    for shift_a in range(3):
        for shift_b in range(3):
            for shift_c in range(3):
                shifted = padded[shift_a:shift_a + sx, shift_b:shift_b + sy, shift_c:shift_c + sz, :].reshape(-1, chans)
                pieces.append(lax.dot_general(shifted, rows, (((0,), (0,)), ((), ())), preferred_element_type=jnp.float32))
    return jnp.stack(pieces, axis=0)

def wrap_pad(volume):
    return jnp.pad(volume, ((1, 1), (1, 1), (1, 1), (0, 0)), mode='wrap')

def reference(features, fine_weight, coarse_weight, cotangent):
    fine_k = kernel_cells(fine_weight, CH_FINE)
    coarse_k = kernel_cells(coarse_weight, CH_FINE)
    cells_in = features.reshape(NX, NY, NZ, CH_FINE)
    cot = cotangent.reshape(NX // 2, NY // 2, NZ // 2, CH_COARSE)
    padded = wrap_pad(cells_in)
    activation = local_conv(padded, fine_k)
    hidden = jax.nn.silu(activation).astype(jnp.bfloat16)
    pooled = pool_mean(hidden).astype(jnp.bfloat16)
    pooled_pad = wrap_pad(pooled)
    coarse_pre = local_conv(pooled_pad, coarse_k)
    grad_pre = (cot.astype(jnp.float32) * silu_slope(coarse_pre)).astype(jnp.bfloat16)
    coarse_raw = weight_grad(grad_pre, pooled_pad)
    grad_pooled = local_conv(wrap_pad(grad_pre), flipped_kernel(coarse_k)).astype(jnp.bfloat16)
    grad_act = (spread_up(grad_pooled) * 0.125 * silu_slope(activation)).astype(jnp.bfloat16)
    fine_raw = weight_grad(grad_act, padded)
    grad_features = local_conv(wrap_pad(grad_act), flipped_kernel(fine_k)).astype(jnp.bfloat16)
    cells = NX * NY * NZ
    return (grad_features.reshape(NX, NY, NZ * CH_FINE), fine_raw.reshape(27, -1) / math.sqrt(cells), coarse_raw.reshape(27, -1) / math.sqrt(cells // 8))
```

```python
import functools
import math

import jax
import jax.numpy as jnp
from jax import lax
from jax.experimental import pallas as pl
from jax.experimental.pallas import tpu as pltpu
from jax.sharding import PartitionSpec as P

F32 = jnp.float32
BF16 = jnp.bfloat16
VMEM = pl.BlockSpec(memory_space=pltpu.VMEM)
SMEM = pl.BlockSpec(memory_space=pltpu.SMEM)
ANY = pl.BlockSpec(memory_space=pl.ANY)
CONV = 2 * 384 * 6 * 2304 * 256


def shift(value, axis, step):
    count = lax.axis_size(axis)
    return lax.ppermute(value, axis, [(i, (i + step) % count) for i in range(count)])


def call(kernel, outs, operands, scratch=(), flops=0, place=None, after=()):
    moved = sum(math.prod(v.shape) * v.dtype.itemsize for v in operands)
    moved += sum(math.prod(s) * jnp.dtype(d).itemsize for s, d in outs)
    extra = () if place is None else (place,)
    first, last = len(extra) + len(operands), len(extra) + len(operands) + len(after)

    def run(*refs):
        kernel(*refs[:first], *refs[last:])

    return pl.pallas_call(
        run,
        out_shape=[jax.ShapeDtypeStruct(s, d) for s, d in outs],
        in_specs=[SMEM] * len(extra) + [VMEM] * len(operands) + [ANY] * len(after),
        out_specs=[VMEM] * len(outs),
        scratch_shapes=list(scratch),
        compiler_params=pltpu.CompilerParams(vmem_limit_bytes=48 * 1024 * 1024),
        cost_estimate=pl.CostEstimate(flops=flops, bytes_accessed=moved, transcendentals=0),
    )(*extra, *operands, *after)


def low_half(shape):
    return lax.broadcasted_iota(jnp.int32, shape, len(shape) - 1) < 64


def swap(value):
    return pltpu.roll(value, 64, value.ndim - 1)


def rolled_rows(value, step):
    return pltpu.roll(value, step % value.shape[-2], value.ndim - 2)


def pack_faces(low, high):
    mask = low_half((6, 24, 128))
    to_high = jnp.where(mask, swap(high[:6]), high[6:])
    to_low = jnp.where(mask, low[:6], swap(low[6:]))
    return to_high, to_low


def with_faces(own, lo, hi):
    mask = low_half((6, 24, 128))
    first = jnp.where(mask, hi, swap(lo))
    second = jnp.where(mask, swap(hi), lo)
    full = jnp.concatenate([own, jnp.concatenate([first, second], axis=0)], axis=2)
    return pltpu.roll(full, 64, 2)


def weights_kernel(fine, coarse, wf, wc, wfb, wcb, flat_f, flat_c):
    mask = low_half((27, 128))
    for k in range(32):
        value = fine[:, 128 * k : 128 * k + 128].astype(F32)
        turned = swap(value)
        flat_f[pl.ds(2 * k, 27, stride=64), :] = jnp.where(mask, value, turned)
        flat_f[pl.ds(2 * k + 1, 27, stride=64), :] = jnp.where(mask, turned, value)
    for c in range(64):
        flat_c[pl.ds(c, 27, stride=64), :] = coarse[:, 128 * c : 128 * c + 128].astype(F32)
    flat_f[1728:1792, :] = jnp.zeros((64, 128), F32)
    flat_c[1728:1792, :] = jnp.zeros((64, 128), F32)
    mask = low_half((64, 128))
    wide = low_half((128, 128))
    none = jnp.zeros((64, 128), F32)
    f_turned = []
    c_turned = []
    for m in range(14):
        value = flat_f[128 * m : 128 * m + 128, :].T[0:64]
        f_turned += [jnp.where(mask, value, swap(value)), jnp.where(mask, swap(value), value)]
        value = flat_c[128 * m : 128 * m + 128, :].T
        c_turned += [jnp.where(wide, value, swap(value)), jnp.where(wide, swap(value), value)]
    for ab in range(9):
        for j in range(4):
            row = (4 * ab + j) * 64
            at = (3 * ab + j) * 64
            left = flat_f[at : at + 64, :] if j < 3 else none
            right = flat_f[at - 64 : at, :] if j > 0 else none
            wf[row : row + 64, :] = jnp.where(mask, left, right).astype(BF16)
            left = flat_c[at : at + 64, :] if j < 3 else none
            right = flat_c[at - 64 : at, :] if j > 0 else none
            wc[row : row + 64, 0:128] = left.astype(BF16)
            wc[row : row + 64, 128:256] = right.astype(BF16)
            slot = 26 - 3 * ab - j
            left = f_turned[slot] if j < 3 else none
            right = f_turned[slot + 1] if j > 0 else none
            wfb[row : row + 64, :] = jnp.where(mask, left, right).astype(BF16)
            row = 2 * row
            zero = jnp.zeros((128, 128), F32)
            left = c_turned[slot] if j < 3 else zero
            right = c_turned[slot + 1] if j > 0 else zero
            wcb[row : row + 128, 0:128] = left.astype(BF16)
            wcb[row : row + 128, 128:256] = right.astype(BF16)


def z_faces_kernel(own, cot, zl, zh, edge):
    low = own[:, :, 0:128].astype(F32)
    high = own[:, :, 640:768].astype(F32)
    to_high, to_low = pack_faces(low, high)
    for out, face, lane in ((zl, to_high, 640), (zh, to_low, 0)):
        edge[:, 0:6, :] = cot[:, :, lane : lane + 128].astype(F32)
        turned = [edge[:, y : y + 1, :].reshape(12, 128)[None] for y in range(6)]
        turned = jnp.concatenate(turned, axis=0)
        pad = jnp.zeros((6, 4, 128), F32)
        out[...] = jnp.concatenate([face, turned, pad], axis=1).astype(BF16)


def x_faces_kernel(own, cot, zlo, zhi, rows_out, cot_out, xl, xh, rows, crows, message):
    lo = zlo[...].astype(F32)
    hi = zhi[...].astype(F32)
    rows[:, 0:24, :] = with_faces(own[...].astype(F32), lo[:, 0:24], hi[:, 0:24])
    rows[:, 24:32, :] = jnp.zeros((12, 8, 896), F32)
    crows[:, 8:16, :] = jnp.zeros((6, 8, 1024), F32)
    crows[:, 0:12, 0:128] = lo[:, 24:36]
    crows[:, 0:12, 128:896] = cot[...].astype(F32)
    crows[:, 0:12, 896:1024] = hi[:, 24:36]
    rows_out[...] = rows[...].astype(BF16)
    cot_out[...] = crows[...].astype(BF16)
    message[...] = jnp.zeros(message.shape, F32)
    for out, x, cx in ((xl, 23, 11), (xh, 0, 0)):
        for y in range(12):
            message[y : y + 1, 0:896] = rows[y, x : x + 1, :]
        for y in range(6):
            message[12 + y : 13 + y, :] = crows[y, cx : cx + 1, :]
        out[...] = message[...].astype(BF16)


def y_faces_kernel(rows_in, cot_in, xlo, xhi, rows_out, cot_out, yl, yh, rows, crows, lo, hi):
    lo[...] = xlo[...].astype(F32)
    hi[...] = xhi[...].astype(F32)
    rows[...] = rows_in[...].astype(F32)
    crows[...] = cot_in[...].astype(F32)
    for y in range(12):
        rows[y, 24:25, :] = hi[y : y + 1, 0:896]
        rows[y, 31:32, :] = lo[y : y + 1, 0:896]
    for y in range(6):
        crows[y, 12:13, :] = hi[12 + y : 13 + y, :]
        crows[y, 15:16, :] = lo[12 + y : 13 + y, :]
    rows_out[...] = rows[...].astype(BF16)
    cot_out[...] = crows[...].astype(BF16)
    for out, y, cy in ((yl, 11, 5), (yh, 0, 0)):
        out[0:32, 0:896] = rows[y].astype(BF16)
        out[0:32, 896:1024] = jnp.zeros((32, 128), BF16)
        out[32:48, :] = crows[cy].astype(BF16)


def act_x_faces_kernel(own, zlo, zhi, rows_out, xl, xh, rows, message):
    rows[:, 0:24, :] = with_faces(
        own[...].astype(F32)[:, 0:24], zlo[...].astype(F32), zhi[...].astype(F32)
    )
    rows[:, 24:32, :] = jnp.zeros((12, 8, 896), F32)
    rows_out[...] = rows[...].astype(BF16)
    message[...] = jnp.zeros(message.shape, F32)
    for out, x in ((xl, 23), (xh, 0)):
        for y in range(12):
            message[y : y + 1, :] = rows[y, x : x + 1, :]
        out[...] = message[...].astype(BF16)


def act_y_faces_kernel(rows_in, xlo, xhi, rows_out, yl, yh, rows, lo, hi):
    lo[...] = xlo[...].astype(F32)
    hi[...] = xhi[...].astype(F32)
    rows[...] = rows_in[...].astype(F32)
    for y in range(12):
        rows[y, 24:25, :] = hi[y : y + 1, :]
        rows[y, 31:32, :] = lo[y : y + 1, :]
    value = rows[...].astype(BF16)
    rows_out[...] = value
    yl[...] = value[11]
    yh[...] = value[0]


def sigmoid(value):
    return 0.5 + 0.5 * jnp.tanh(0.5 * value)


def silu_parts(act):
    sigma = sigmoid(act)
    return (act * sigma).astype(BF16), (sigma * (1.0 + act * (1.0 - sigma))).astype(BF16)


def pool_matrix(shape, rule):
    r = lax.broadcasted_iota(jnp.int32, shape, 0)
    q = lax.broadcasted_iota(jnp.int32, shape, 1)
    return jnp.where(rule(r, q), 0.125, 0.0).astype(BF16)


def fold_pairs(part):
    return part + swap(part)


def interior_kernel(rows, weight, shifted, slope, edges, pooled):
    full = rows[...].astype(F32)
    for a in range(3):
        shifted[a] = rolled_rows(full, 1 - a).astype(BF16).reshape(384, 896)
    pool = pool_matrix(
        (64, 320),
        lambda r, q: ((((q >> 5) + 1) >> 1) == (r >> 4) + 1) & (((q & 31) >> 1) == (r & 15)),
    )
    mask = low_half((64, 128))
    pieces = []
    for p in range(6):
        lanes = slice(128 * p, 128 * p + 256)
        left = jnp.concatenate(
            [shifted[a, 32 * b : 32 * b + 320, lanes] for a in range(3) for b in range(3)], axis=1
        )
        act = jnp.dot(left, weight[...], preferred_element_type=F32)
        hidden, tilt = silu_parts(act)
        own = slice(128 * p, 128 * p + 128)
        slope[:, own] = tilt
        edges[0:32, own] = hidden[0:32]
        edges[32:64, own] = hidden[288:320]
        pieces.append(fold_pairs(jnp.dot(pool, hidden, preferred_element_type=F32)))
    for j in range(3):
        both = jnp.where(mask, pieces[2 * j], pieces[2 * j + 1])
        pooled[:, :, 128 * j : 128 * j + 128] = both.astype(BF16).reshape(4, 16, 128)


def border_kernel(shifted, ylo, yhi, weight, edges, inner, outer, slope, pooled, zl, zh):
    both = jnp.concatenate(
        [ylo[0:32, 0:896][None], yhi[0:32, 0:896][None]], axis=0
    ).astype(F32)
    for a in range(3):
        outer[a] = rolled_rows(both, 1 - a).astype(BF16).reshape(64, 896)
    blocks = []
    for p in range(6):
        lanes = slice(128 * p, 128 * p + 256)
        first = []
        last = []
        for a in range(3):
            first += [outer[a, 0:32, lanes], shifted[a, 0:32, lanes], shifted[a, 32:64, lanes]]
            last += [
                shifted[a, 320:352, lanes], shifted[a, 352:384, lanes], outer[a, 32:64, lanes]
            ]
        blocks.append(jnp.concatenate(first, axis=1))
        blocks.append(jnp.concatenate(last, axis=1))
    act = jnp.dot(jnp.concatenate(blocks, axis=0), weight[...], preferred_element_type=F32)
    hidden, tilt = silu_parts(act)
    pool = pool_matrix(
        (32, 128),
        lambda r, q: (((q >> 5) & 1) == (r >> 4)) & (((q & 31) >> 1) == (r & 15)),
    )
    mask = low_half((32, 128))
    pieces = []
    for p in range(6):
        own = slice(128 * p, 128 * p + 128)
        slope[:, own] = tilt[64 * p : 64 * p + 64]
        column = jnp.concatenate([hidden[64 * p : 64 * p + 64], edges[:, own]], axis=0)
        pieces.append(fold_pairs(jnp.dot(pool, column, preferred_element_type=F32)))
    for j in range(3):
        own = slice(128 * j, 128 * j + 128)
        both = jnp.where(mask, pieces[2 * j], pieces[2 * j + 1]).astype(BF16)
        pooled[0:1, :, own] = both[0:16][None]
        pooled[5:6, :, own] = both[16:32][None]
    pooled[1:5] = inner[...]
    zl[...] = pooled[:, :, 256:384]
    zh[...] = pooled[:, :, 0:128]


def pooled_x_kernel(own, zlo, zhi, rows_out, xl, xh, rows, message):
    rows[...] = jnp.concatenate([zlo[...], own[...], zhi[...]], axis=2).astype(F32)
    rows_out[...] = rows[...].astype(BF16)
    message[...] = jnp.zeros(message.shape, F32)
    for out, x in ((xl, 10), (xh, 0)):
        for y in range(6):
            message[2 * y : 2 * y + 2, :] = rows[y, x : x + 2, :]
        out[...] = message[...].astype(BF16)


def pooled_y_kernel(rows_in, xlo, xhi, rows_out, yl, yh, rows, lo, hi):
    lo[...] = xlo[...].astype(F32)
    hi[...] = xhi[...].astype(F32)
    rows[...] = rows_in[...].astype(F32)
    for y in range(6):
        rows[y, 12:14, :] = hi[2 * y : 2 * y + 2, :]
        rows[y, 14:16, :] = lo[2 * y : 2 * y + 2, :]
    value = rows[...].astype(BF16)
    rows_out[...] = value
    yl[...] = value[4:6]
    yh[...] = value[0:2]


def backward_kernel(
    core, prow, pylo, pyhi, crow, ylo, yhi, slope_in, slope_out, shifted, outer, wc, wb,
    act_out, zl, zh, keep, send, pshift, gshift, ftrans, ctrans, pairs, sums,
):
    full = jnp.concatenate([pylo[...], prow[...], pyhi[...]], axis=0).astype(F32)
    for a in range(3):
        pshift[a] = rolled_rows(full, 1 - a).astype(BF16).reshape(160, 640)
    blocks = []
    for p in range(4):
        lanes = slice(128 * p, 128 * p + 256)
        blocks.append(
            jnp.concatenate(
                [pshift[a, 16 * b : 16 * b + 128, lanes] for a in range(3) for b in range(3)], axis=1
            )
        )
    pre = jnp.dot(jnp.concatenate(blocks, axis=0), wc[...], preferred_element_type=F32)
    sigma = sigmoid(pre)
    tilt = sigma * (1.0 + pre * (1.0 - sigma))
    cot = jnp.concatenate([ylo[32:48][None], crow[...], yhi[32:48][None]], axis=0).astype(F32)
    row = lax.broadcasted_iota(jnp.int32, (128, 256), 0)
    lane = lax.broadcasted_iota(jnp.int32, (128, 256), 1)
    own_rows = (row >= 16) & (row < 112) & ((row & 15) < 12)
    parts = []
    owned = []
    for p in range(4):
        grad = cot[:, :, 256 * p : 256 * p + 256].reshape(128, 256) * tilt[128 * p : 128 * p + 128]
        grad = grad.astype(BF16).astype(F32)
        parts.append(grad)
        valid = own_rows
        if p == 0:
            valid = valid & (lane >= 128)
        if p == 3:
            valid = valid & (lane < 128)
        owned.append(jnp.where(valid, grad, 0.0).T.astype(BF16))
    both = jnp.concatenate(parts, axis=1).reshape(8, 16, 1024)
    for a in range(3):
        gshift[a] = rolled_rows(both, 1 - a).astype(BF16).reshape(128, 1024)
    blocks = []
    for p in range(3):
        lanes = slice(256 * p, 256 * p + 512)
        blocks.append(
            jnp.concatenate(
                [gshift[a, 16 * b : 16 * b + 96, lanes] for a in range(3) for b in range(3)], axis=1
            )
        )
    small = jnp.dot(jnp.concatenate(blocks, axis=0), wb[...], preferred_element_type=F32)
    small = small.astype(BF16)
    q = lax.broadcasted_iota(jnp.int32, (384, 96), 0)
    r = lax.broadcasted_iota(jnp.int32, (384, 96), 1)
    inside = ((q >> 6) == (r >> 4)) & (((q & 31) >> 1) == (r & 15)) & ((q & 31) < 24)
    spread = jnp.where(inside, 1.0, 0.0).astype(BF16)
    turned = []
    for p in range(3):
        lanes = slice(256 * p, 256 * p + 256)
        up = jnp.dot(spread, small[96 * p : 96 * p + 96], preferred_element_type=F32)
        slope = jnp.concatenate(
            [slope_out[0:32, lanes], slope_in[:, lanes], slope_out[32:64, lanes]], axis=0
        )
        part = (up * 0.125 * slope.astype(F32)).astype(BF16)
        act_out[:, :, lanes] = part.reshape(12, 32, 256)
        wide = part.astype(F32)
        turned.append(wide[:, 0:128].T.astype(BF16))
        turned.append(wide[:, 128:256].T.astype(BF16))
        if p == 0:
            low = wide[:, 0:128].reshape(12, 32, 128)[:, 0:24]
        if p == 2:
            high = wide[:, 128:256].reshape(12, 32, 128)[:, 0:24]
    to_high, to_low = pack_faces(low, high)
    zl[...] = to_high.astype(BF16)
    zh[...] = to_low.astype(BF16)
    fine_left = jnp.concatenate(turned, axis=1)
    coarse_left = jnp.concatenate(owned, axis=1)
    mask = low_half((32, 128))
    sums[...] = jnp.zeros(sums.shape, F32)
    for a in range(3):
        for b in range(3):
            rights = []
            for p in range(6):
                lanes = slice(128 * p, 128 * p + 256)
                if b == 0:
                    rights += [outer[a, 0:32, lanes], shifted[a, 0:352, lanes]]
                elif b == 1:
                    rights += [shifted[a, :, lanes]]
                else:
                    rights += [shifted[a, 32:384, lanes], outer[a, 32:64, lanes]]
            right = jnp.concatenate(rights, axis=0)
            ftrans[...] = jnp.dot(fine_left, right, preferred_element_type=F32).T
            right = jnp.concatenate(
                [pshift[a, 16 * b : 16 * b + 128, 128 * p : 128 * p + 256] for p in range(4)], axis=0
            )
            ctrans[...] = jnp.dot(coarse_left, right, preferred_element_type=F32).T
            for e in range(3):
                slot = 9 * a + 3 * b + e
                near = slice(64 * e, 64 * e + 64)
                far = slice(64 * e + 64, 64 * e + 128)
                pairs[...] = ftrans[near] + swap(ftrans[far])
                even = pairs[pl.ds(0, 32, stride=2), :]
                odd = pairs[pl.ds(1, 32, stride=2), :]
                sums[pl.ds(slot, 32, stride=32), :] = jnp.where(mask, even, swap(odd))
                wide = ctrans[near, 0:128] + ctrans[far, 128:256]
                sums[pl.ds(1024 + slot, 64, stride=32), :] = wide
    mine = pl.multiple_of(core[0] * 1536, 1536)
    other = pl.multiple_of((1 - core[0]) * 1536, 1536)
    keep[...] = sums[pl.ds(mine, 1536), :].astype(BF16).reshape(48, 32, 128)
    send[...] = sums[pl.ds(other, 1536), :].astype(BF16).reshape(48, 32, 128)


def features_kernel(rows, ylo, yhi, weight, out, done, shifted):
    done[...] = jnp.zeros(done.shape, F32)
    full = jnp.concatenate([ylo[...][None], rows[...], yhi[...][None]], axis=0).astype(F32)
    for a in range(3):
        shifted[a] = rolled_rows(full, 1 - a).astype(BF16).reshape(448, 896)
    for p in range(6):
        lanes = slice(128 * p, 128 * p + 256)
        left = jnp.concatenate(
            [shifted[a, 32 * b : 32 * b + 384, lanes] for a in range(3) for b in range(3)], axis=1
        )
        grad = jnp.dot(left, weight[...], preferred_element_type=F32)
        grad = grad.reshape(12, 32, 128)[:, 0:24, :]
        out[:, :, 128 * p : 128 * p + 128] = grad.astype(BF16)


def combine_kernel(count, parts, *refs):
    at, ins, outs = refs[0], refs[1 : 1 + parts], refs[1 + parts :]
    size = outs[0].shape[0]
    for k in range(count):
        start = lax.rem(at[0] + k, count) * size
        total = ins[0][pl.ds(start, size)].astype(F32)
        for ref in ins[1:]:
            total = total + ref[pl.ds(start, size)].astype(F32)
        outs[k][...] = total.astype(outs[k].dtype)


def combine(values, place, count, dtype=BF16, after=()):
    size = values[0].shape[0] // count
    return call(
        functools.partial(combine_kernel, count, len(values)),
        [((size, 32, 128), dtype)] * count, values, place=place, after=after,
    )


def place_kernel(count, *refs):
    at, ins, out = refs[0], refs[1 : 1 + count], refs[-1]
    size = ins[0].shape[0]
    for k in range(count):
        out[pl.ds(lax.rem(at[0] + count - k, count) * size, size)] = ins[k][...]


def placed(values, place):
    count = len(values)
    size = values[0].shape[0]
    return call(
        functools.partial(place_kernel, count),
        [((count * size, 32, 128), BF16)], values, place=place,
    )[0]


def last_kernel(core, own, other, fine, coarse, whole):
    whole[pl.ds(core[0] * 48, 48)] = own[...]
    whole[pl.ds((1 - core[0]) * 48, 48)] = other[...]
    cells = 96 * 96 * 96
    for r in range(96):
        value = whole[r].astype(F32)[0:27]
        if r < 32:
            fine[:, 128 * r : 128 * r + 128] = value * (1.0 / math.sqrt(cells))
        else:
            at = 128 * (r - 32)
            coarse[:, at : at + 128] = value * (1.0 / math.sqrt(cells // 8))


def core_partner(value):
    return lax.ppermute(value, "gx", [(i, i ^ 1) for i in range(4)])


def z_partner(value, far):
    return lax.ppermute(value, "gy", [(i, i ^ far) for i in range(8)])


def y_turn(value, step):
    pairs = [(i, i // 4 * 4 + (i + step) % 4) for i in range(8)]
    return lax.ppermute(value, "gz", pairs)


def x_turn(value, step):
    pairs = []
    for gx in range(4):
        for gz in range(8):
            x = (gz // 4 * 2 + gx // 2 + step) % 4
            pairs.append((gx * 8 + gz, (x % 2 * 2 + gx % 2) * 8 + x // 2 * 4 + gz % 4))
    return lax.ppermute(value, ("gx", "gz"), pairs)


def body(features, fine_weight, coarse_weight, cotangent):
    gx = lax.axis_index("gx").astype(jnp.int32)
    gz = lax.axis_index("gz").astype(jnp.int32)
    core = (gx % 2).reshape(1)
    y_at = (gz % 4).reshape(1)
    x_at = (gz // 4 * 2 + gx // 2).reshape(1)
    z_at = jnp.zeros((1,), jnp.int32)

    own = jnp.transpose(features, (1, 0, 2))
    zl, zh = call(
        z_faces_kernel, [((6, 40, 128), BF16)] * 2, (own, cotangent),
        [pltpu.VMEM((12, 8, 128), F32)],
    )
    zlo = shift(zl, "gz", 1)
    zhi = shift(zh, "gz", -1)
    w_fine, w_coarse, w_fine_back, w_coarse_back = call(
        weights_kernel,
        [((2304, 128), BF16), ((2304, 256), BF16), ((2304, 128), BF16), ((4608, 256), BF16)],
        (fine_weight, coarse_weight),
        [pltpu.VMEM((1792, 128), F32), pltpu.VMEM((1792, 128), F32)],
        flops=CONV // 4, after=(zl,),
    )
    frows, crows, xl, xh = call(
        x_faces_kernel,
        [((12, 32, 896), BF16), ((6, 16, 1024), BF16), ((24, 1024), BF16), ((24, 1024), BF16)],
        (own, jnp.transpose(cotangent, (1, 0, 2)), zlo, zhi),
        [pltpu.VMEM((12, 32, 896), F32), pltpu.VMEM((6, 16, 1024), F32), pltpu.VMEM((24, 1024), F32)],
        after=(w_fine,),
    )
    xlo = shift(xl, "gx", 1)
    xhi = shift(xh, "gx", -1)
    frows, crows, yl, yh = call(
        y_faces_kernel,
        [((12, 32, 896), BF16), ((6, 16, 1024), BF16), ((48, 1024), BF16), ((48, 1024), BF16)],
        (frows, crows, xlo, xhi),
        [
            pltpu.VMEM((12, 32, 896), F32), pltpu.VMEM((6, 16, 1024), F32),
            pltpu.VMEM((24, 1024), F32), pltpu.VMEM((24, 1024), F32),
        ],
    )
    ylo = shift(yl, "gy", 1)
    yhi = shift(yh, "gy", -1)
    shifted, slope_in, edges, inner = call(
        interior_kernel,
        [((3, 384, 896), BF16), ((320, 768), BF16), ((64, 768), BF16), ((4, 16, 384), BF16)],
        (frows, w_fine),
        flops=CONV,
    )
    outer, slope_out, pooled, pzl, pzh = call(
        border_kernel,
        [
            ((3, 64, 896), BF16), ((64, 768), BF16), ((6, 16, 384), BF16),
            ((6, 16, 128), BF16), ((6, 16, 128), BF16),
        ],
        (shifted, ylo, yhi, w_fine, edges, inner),
        flops=CONV // 6,
    )
    pzlo = shift(pzl, "gz", 1)
    pzhi = shift(pzh, "gz", -1)
    prows, pxl, pxh = call(
        pooled_x_kernel,
        [((6, 16, 640), BF16), ((16, 640), BF16), ((16, 640), BF16)],
        (pooled, pzlo, pzhi),
        [pltpu.VMEM((6, 16, 640), F32), pltpu.VMEM((16, 640), F32)],
    )
    pxlo = shift(pxl, "gx", 1)
    pxhi = shift(pxh, "gx", -1)
    prows, pyl, pyh = call(
        pooled_y_kernel,
        [((6, 16, 640), BF16), ((2, 16, 640), BF16), ((2, 16, 640), BF16)],
        (prows, pxlo, pxhi),
        [pltpu.VMEM((6, 16, 640), F32), pltpu.VMEM((16, 640), F32), pltpu.VMEM((16, 640), F32)],
    )
    pylo = shift(pyl, "gy", 1)
    pyhi = shift(pyh, "gy", -1)
    act, azl, azh, keep, send = call(
        backward_kernel,
        [
            ((12, 32, 768), BF16), ((6, 24, 128), BF16), ((6, 24, 128), BF16),
            ((48, 32, 128), BF16), ((48, 32, 128), BF16),
        ],
        (
            prows, pylo, pyhi, crows, ylo, yhi, slope_in, slope_out, shifted, outer,
            w_coarse, w_coarse_back,
        ),
        [
            pltpu.VMEM((3, 160, 640), BF16), pltpu.VMEM((3, 128, 1024), BF16),
            pltpu.VMEM((256, 128), F32), pltpu.VMEM((256, 256), F32),
            pltpu.VMEM((64, 128), F32), pltpu.VMEM((3072, 128), F32),
        ],
        flops=CONV * 3, place=core,
    )

    azlo = shift(azl, "gz", 1)
    azhi = shift(azh, "gz", -1)
    got = core_partner(send)
    arows, axl, axh = call(
        act_x_faces_kernel,
        [((12, 32, 896), BF16), ((16, 896), BF16), ((16, 896), BF16)],
        (act, azlo, azhi),
        [pltpu.VMEM((12, 32, 896), F32), pltpu.VMEM((16, 896), F32)],
        after=(got,),
    )
    parts = combine((keep, got), y_at, 4, after=(axl,))
    axlo = shift(axl, "gx", 1)
    axhi = shift(axh, "gx", -1)
    got = tuple(y_turn(parts[k], k) for k in (1, 2, 3))
    arows, ayl, ayh = call(
        act_y_faces_kernel,
        [((12, 32, 896), BF16), ((32, 896), BF16), ((32, 896), BF16)],
        (arows, axlo, axhi),
        [pltpu.VMEM((12, 32, 896), F32), pltpu.VMEM((16, 896), F32), pltpu.VMEM((16, 896), F32)],
        after=got,
    )
    parts = combine((parts[0],) + got, x_at, 4, after=(ayl,))
    aylo = shift(ayl, "gy", 1)
    ayhi = shift(ayh, "gy", -1)
    got = tuple(x_turn(parts[k], k) for k in (1, 2, 3))
    (part,) = combine((parts[0],) + got, z_at, 1, F32, after=(aylo, ayhi))
    (part,) = combine((part, z_partner(part, 1)), z_at, 1, F32)
    (part,) = combine((part, z_partner(part, 2)), z_at, 1, F32)
    got = z_partner(part, 4)
    grad_features, done = call(
        features_kernel,
        [((12, 24, 768), BF16), ((8, 128), F32)],
        (arows, aylo, ayhi, w_fine_back),
        [pltpu.VMEM((3, 448, 896), BF16)],
        flops=CONV, after=(part,),
    )
    (part,) = combine((part, got), z_at, 1, after=(done,))
    part = placed((part,) + tuple(x_turn(part, k) for k in (1, 2, 3)), x_at)
    part = placed((part,) + tuple(y_turn(part, k) for k in (1, 2, 3)), y_at)
    fine, coarse = call(
        last_kernel,
        [((27, 4096), F32), ((27, 8192), F32)],
        (part, core_partner(part)),
        [pltpu.VMEM((96, 32, 128), BF16)],
        place=core,
    )
    return jnp.transpose(grad_features, (1, 0, 2)), fine, coarse


def solution(mesh):
    in_specs = (P("gx", "gy", "gz"), P(), P(), P("gx", "gy", "gz"))
    out_specs = (P("gx", "gy", "gz"), P(), P())
    return jax.shard_map(body, mesh=mesh, in_specs=in_specs, out_specs=out_specs, check_vma=False)
```

```python
import functools
import math

import jax
import jax.numpy as jnp
from jax import lax
from jax.experimental import pallas as pl
from jax.experimental.pallas import tpu as pltpu
from jax.sharding import PartitionSpec as P

F32 = jnp.float32
BF16 = jnp.bfloat16
VMEM = pl.BlockSpec(memory_space=pltpu.VMEM)
SMEM = pl.BlockSpec(memory_space=pltpu.SMEM)
ANY = pl.BlockSpec(memory_space=pl.ANY)
HBM = pl.BlockSpec(memory_space=pltpu.HBM)
CONV = 2 * 384 * 6 * 2304 * 256


def shift(value, axis, step):
    count = lax.axis_size(axis)
    return lax.ppermute(value, axis, [(i, (i + step) % count) for i in range(count)])


def call(kernel, outs, operands, scratch=(), flops=0, place=None, after=(), space=VMEM):
    moved = sum(math.prod(v.shape) * v.dtype.itemsize for v in operands)
    moved += sum(math.prod(s) * jnp.dtype(d).itemsize for s, d in outs)
    extra = () if place is None else (place,)
    first, last = len(extra) + len(operands), len(extra) + len(operands) + len(after)

    def run(*refs):
        kernel(*refs[:first], *refs[last:])

    return pl.pallas_call(
        run,
        out_shape=[jax.ShapeDtypeStruct(s, d) for s, d in outs],
        in_specs=[SMEM] * len(extra) + [space] * len(operands) + [ANY] * len(after),
        out_specs=[VMEM] * len(outs),
        scratch_shapes=list(scratch),
        compiler_params=pltpu.CompilerParams(vmem_limit_bytes=16 * 1024 * 1024),
        cost_estimate=pl.CostEstimate(flops=flops, bytes_accessed=moved, transcendentals=0),
    )(*extra, *operands, *after)


def low_half(shape):
    return lax.broadcasted_iota(jnp.int32, shape, len(shape) - 1) < 64


def swap(value):
    return pltpu.roll(value, 64, value.ndim - 1)


def rolled_rows(value, step):
    return pltpu.roll(value, step % value.shape[-2], value.ndim - 2)


def pack_faces(low, high):
    mask = low_half((6, 24, 128))
    to_high = jnp.where(mask, swap(high[:6]), high[6:])
    to_low = jnp.where(mask, low[:6], swap(low[6:]))
    return to_high, to_low


def with_faces(own, lo, hi):
    mask = low_half((6, 24, 128))
    first = jnp.where(mask, hi, swap(lo))
    second = jnp.where(mask, swap(hi), lo)
    full = jnp.concatenate([own, jnp.concatenate([first, second], axis=0)], axis=2)
    return pltpu.roll(full, 64, 2)


def weights_kernel(fine, coarse, wf, wc, wfb, wcb, flat_f, flat_c):
    mask = low_half((27, 128))
    for k in range(32):
        value = fine[:, 128 * k : 128 * k + 128].astype(F32)
        turned = swap(value)
        flat_f[pl.ds(2 * k, 27, stride=64), :] = jnp.where(mask, value, turned)
        flat_f[pl.ds(2 * k + 1, 27, stride=64), :] = jnp.where(mask, turned, value)
    for c in range(64):
        flat_c[pl.ds(c, 27, stride=64), :] = coarse[:, 128 * c : 128 * c + 128].astype(F32)
    flat_f[1728:1792, :] = jnp.zeros((64, 128), F32)
    flat_c[1728:1792, :] = jnp.zeros((64, 128), F32)
    mask = low_half((64, 128))
    wide = low_half((128, 128))
    none = jnp.zeros((64, 128), F32)
    f_turned = []
    c_turned = []
    for m in range(14):
        value = flat_f[128 * m : 128 * m + 128, :].T[0:64]
        f_turned += [jnp.where(mask, value, swap(value)), jnp.where(mask, swap(value), value)]
        value = flat_c[128 * m : 128 * m + 128, :].T
        c_turned += [jnp.where(wide, value, swap(value)), jnp.where(wide, swap(value), value)]
    for ab in range(9):
        for j in range(4):
            row = (4 * ab + j) * 64
            at = (3 * ab + j) * 64
            left = flat_f[at : at + 64, :] if j < 3 else none
            right = flat_f[at - 64 : at, :] if j > 0 else none
            wf[row : row + 64, :] = jnp.where(mask, left, right).astype(BF16)
            left = flat_c[at : at + 64, :] if j < 3 else none
            right = flat_c[at - 64 : at, :] if j > 0 else none
            wc[row : row + 64, 0:128] = left.astype(BF16)
            wc[row : row + 64, 128:256] = right.astype(BF16)
            slot = 26 - 3 * ab - j
            left = f_turned[slot] if j < 3 else none
            right = f_turned[slot + 1] if j > 0 else none
            wfb[row : row + 64, :] = jnp.where(mask, left, right).astype(BF16)
            row = 2 * row
            zero = jnp.zeros((128, 128), F32)
            left = c_turned[slot] if j < 3 else zero
            right = c_turned[slot + 1] if j > 0 else zero
            wcb[row : row + 128, 0:128] = left.astype(BF16)
            wcb[row : row + 128, 128:256] = right.astype(BF16)


def z_faces_kernel(own, cot, zl, zh, faces, cfaces, edge, sems):
    copies = []
    for k, lane in enumerate((0, 640)):
        lanes = pl.ds(lane, 128)
        copies.append(pltpu.make_async_copy(own.at[:, :, lanes], faces.at[k], sems.at[2 * k]))
        copies.append(pltpu.make_async_copy(cot.at[:, :, lanes], cfaces.at[k], sems.at[2 * k + 1]))
    for copy in copies:
        copy.start()
    for copy in copies:
        copy.wait()
    to_high, to_low = pack_faces(faces[0].astype(F32), faces[1].astype(F32))
    for out, face, k in ((zl, to_high, 1), (zh, to_low, 0)):
        edge[:, 0:6, :] = cfaces[k].astype(F32)
        turned = [edge[:, y : y + 1, :].reshape(12, 128)[None] for y in range(6)]
        turned = jnp.concatenate(turned, axis=0)
        pad = jnp.zeros((6, 4, 128), F32)
        out[...] = jnp.concatenate([face, turned, pad], axis=1).astype(BF16)


def x_faces_kernel(own, cot, zlo, zhi, rows_out, cot_out, xl, xh, rows, crows, message):
    lo = zlo[...].astype(F32)
    hi = zhi[...].astype(F32)
    rows[:, 0:24, :] = with_faces(own[...].astype(F32), lo[:, 0:24], hi[:, 0:24])
    rows[:, 24:32, :] = jnp.zeros((12, 8, 896), F32)
    crows[:, 8:16, :] = jnp.zeros((6, 8, 1024), F32)
    crows[:, 0:12, 0:128] = lo[:, 24:36]
    crows[:, 0:12, 128:896] = cot[...].astype(F32)
    crows[:, 0:12, 896:1024] = hi[:, 24:36]
    rows_out[...] = rows[...].astype(BF16)
    cot_out[...] = crows[...].astype(BF16)
    message[...] = jnp.zeros(message.shape, F32)
    for out, x, cx in ((xl, 23, 11), (xh, 0, 0)):
        for y in range(12):
            message[y : y + 1, 0:896] = rows[y, x : x + 1, :]
        for y in range(6):
            message[12 + y : 13 + y, :] = crows[y, cx : cx + 1, :]
        out[...] = message[...].astype(BF16)


def y_faces_kernel(rows_in, cot_in, xlo, xhi, rows_out, cot_out, yl, yh, rows, crows, lo, hi):
    lo[...] = xlo[...].astype(F32)
    hi[...] = xhi[...].astype(F32)
    rows[...] = rows_in[...].astype(F32)
    crows[...] = cot_in[...].astype(F32)
    for y in range(12):
        rows[y, 24:25, :] = hi[y : y + 1, 0:896]
        rows[y, 31:32, :] = lo[y : y + 1, 0:896]
    for y in range(6):
        crows[y, 12:13, :] = hi[12 + y : 13 + y, :]
        crows[y, 15:16, :] = lo[12 + y : 13 + y, :]
    rows_out[...] = rows[...].astype(BF16)
    cot_out[...] = crows[...].astype(BF16)
    for out, y, cy in ((yl, 11, 5), (yh, 0, 0)):
        out[0:32, 0:896] = rows[y].astype(BF16)
        out[0:32, 896:1024] = jnp.zeros((32, 128), BF16)
        out[32:48, :] = crows[cy].astype(BF16)


def act_x_faces_kernel(own, zlo, zhi, rows_out, xl, xh, rows, message):
    rows[:, 0:24, :] = with_faces(
        own[...].astype(F32)[:, 0:24], zlo[...].astype(F32), zhi[...].astype(F32)
    )
    rows[:, 24:32, :] = jnp.zeros((12, 8, 896), F32)
    rows_out[...] = rows[...].astype(BF16)
    message[...] = jnp.zeros(message.shape, F32)
    for out, x in ((xl, 23), (xh, 0)):
        for y in range(12):
            message[y : y + 1, :] = rows[y, x : x + 1, :]
        out[...] = message[...].astype(BF16)


def act_y_faces_kernel(rows_in, xlo, xhi, rows_out, yl, yh, rows, lo, hi):
    lo[...] = xlo[...].astype(F32)
    hi[...] = xhi[...].astype(F32)
    rows[...] = rows_in[...].astype(F32)
    for y in range(12):
        rows[y, 24:25, :] = hi[y : y + 1, :]
        rows[y, 31:32, :] = lo[y : y + 1, :]
    value = rows[...].astype(BF16)
    rows_out[...] = value
    yl[...] = value[11]
    yh[...] = value[0]


def sigmoid(value):
    return 0.5 + 0.5 * jnp.tanh(0.5 * value)


def silu(act):
    return (act * sigmoid(act)).astype(BF16)


def silu_slope(act):
    sigma = sigmoid(act)
    return sigma * (1.0 + act * (1.0 - sigma))


def slope_kernel(inner, outer, slope, done):
    slope[0:32, :] = silu_slope(outer[0:32, :]).astype(BF16)
    slope[32:352, :] = silu_slope(inner[...]).astype(BF16)
    slope[352:384, :] = silu_slope(outer[32:64, :]).astype(BF16)
    done[...] = jnp.zeros(done.shape, F32)


def pool_matrix(shape, rule):
    r = lax.broadcasted_iota(jnp.int32, shape, 0)
    q = lax.broadcasted_iota(jnp.int32, shape, 1)
    return jnp.where(rule(r, q), 0.125, 0.0).astype(BF16)


def fold_pairs(part):
    return part + swap(part)


def interior_kernel(rows, weight, shifted, kept, edges, pooled):
    full = rows[...].astype(F32)
    for a in range(3):
        shifted[a] = rolled_rows(full, 1 - a).astype(BF16).reshape(384, 896)
    pool = pool_matrix(
        (64, 320),
        lambda r, q: ((((q >> 5) + 1) >> 1) == (r >> 4) + 1) & (((q & 31) >> 1) == (r & 15)),
    )
    mask = low_half((64, 128))
    pieces = []
    for p in range(6):
        lanes = slice(128 * p, 128 * p + 256)
        left = jnp.concatenate(
            [shifted[a, 32 * b : 32 * b + 320, lanes] for a in range(3) for b in range(3)], axis=1
        )
        act = jnp.dot(left, weight[...], preferred_element_type=F32)
        hidden = silu(act)
        own = slice(128 * p, 128 * p + 128)
        kept[:, own] = act
        edges[0:32, own] = hidden[0:32]
        edges[32:64, own] = hidden[288:320]
        pieces.append(fold_pairs(jnp.dot(pool, hidden, preferred_element_type=F32)))
    for j in range(3):
        both = jnp.where(mask, pieces[2 * j], pieces[2 * j + 1])
        pooled[:, :, 128 * j : 128 * j + 128] = both.astype(BF16).reshape(4, 16, 128)


def border_kernel(shifted, ylo, yhi, weight, edges, inner, outer, kept, pooled, zl, zh):
    both = jnp.concatenate(
        [ylo[0:32, 0:896][None], yhi[0:32, 0:896][None]], axis=0
    ).astype(F32)
    for a in range(3):
        outer[a] = rolled_rows(both, 1 - a).astype(BF16).reshape(64, 896)
    blocks = []
    for p in range(6):
        lanes = slice(128 * p, 128 * p + 256)
        first = []
        last = []
        for a in range(3):
            first += [outer[a, 0:32, lanes], shifted[a, 0:32, lanes], shifted[a, 32:64, lanes]]
            last += [
                shifted[a, 320:352, lanes], shifted[a, 352:384, lanes], outer[a, 32:64, lanes]
            ]
        blocks.append(jnp.concatenate(first, axis=1))
        blocks.append(jnp.concatenate(last, axis=1))
    act = jnp.dot(jnp.concatenate(blocks, axis=0), weight[...], preferred_element_type=F32)
    hidden = silu(act)
    pool = pool_matrix(
        (32, 128),
        lambda r, q: (((q >> 5) & 1) == (r >> 4)) & (((q & 31) >> 1) == (r & 15)),
    )
    mask = low_half((32, 128))
    pieces = []
    for p in range(6):
        own = slice(128 * p, 128 * p + 128)
        kept[:, own] = act[64 * p : 64 * p + 64]
        column = jnp.concatenate([hidden[64 * p : 64 * p + 64], edges[:, own]], axis=0)
        pieces.append(fold_pairs(jnp.dot(pool, column, preferred_element_type=F32)))
    for j in range(3):
        own = slice(128 * j, 128 * j + 128)
        both = jnp.where(mask, pieces[2 * j], pieces[2 * j + 1]).astype(BF16)
        pooled[0:1, :, own] = both[0:16][None]
        pooled[5:6, :, own] = both[16:32][None]
    pooled[1:5] = inner[...]
    zl[...] = pooled[:, :, 256:384]
    zh[...] = pooled[:, :, 0:128]


def pooled_x_kernel(own, zlo, zhi, rows_out, xl, xh, rows, message):
    rows[...] = jnp.concatenate([zlo[...], own[...], zhi[...]], axis=2).astype(F32)
    rows_out[...] = rows[...].astype(BF16)
    message[...] = jnp.zeros(message.shape, F32)
    for out, x in ((xl, 10), (xh, 0)):
        for y in range(6):
            message[2 * y : 2 * y + 2, :] = rows[y, x : x + 2, :]
        out[...] = message[...].astype(BF16)


def pooled_y_kernel(rows_in, xlo, xhi, rows_out, yl, yh, rows, lo, hi):
    lo[...] = xlo[...].astype(F32)
    hi[...] = xhi[...].astype(F32)
    rows[...] = rows_in[...].astype(F32)
    for y in range(6):
        rows[y, 12:14, :] = hi[2 * y : 2 * y + 2, :]
        rows[y, 14:16, :] = lo[2 * y : 2 * y + 2, :]
    value = rows[...].astype(BF16)
    rows_out[...] = value
    yl[...] = value[4:6]
    yh[...] = value[0:2]


def backward_kernel(
    prow, pylo, pyhi, crow, ylo, yhi, slope, wc, wb,
    act_out, zl, zh, fine_left, coarse_left, pshift, gshift,
):
    full = jnp.concatenate([pylo[...], prow[...], pyhi[...]], axis=0).astype(F32)
    for a in range(3):
        pshift[a] = rolled_rows(full, 1 - a).astype(BF16).reshape(160, 640)
    blocks = []
    for p in range(4):
        lanes = slice(128 * p, 128 * p + 256)
        blocks.append(
            jnp.concatenate(
                [pshift[a, 16 * b : 16 * b + 128, lanes] for a in range(3) for b in range(3)], axis=1
            )
        )
    pre = jnp.dot(jnp.concatenate(blocks, axis=0), wc[...], preferred_element_type=F32)
    tilt = silu_slope(pre)
    cot = jnp.concatenate([ylo[32:48][None], crow[...], yhi[32:48][None]], axis=0).astype(F32)
    row = lax.broadcasted_iota(jnp.int32, (128, 256), 0)
    lane = lax.broadcasted_iota(jnp.int32, (128, 256), 1)
    own_rows = (row >= 16) & (row < 112) & ((row & 15) < 12)
    parts = []
    for p in range(4):
        grad = cot[:, :, 256 * p : 256 * p + 256].reshape(128, 256) * tilt[128 * p : 128 * p + 128]
        grad = grad.astype(BF16).astype(F32)
        parts.append(grad)
        valid = own_rows
        if p == 0:
            valid = valid & (lane >= 128)
        if p == 3:
            valid = valid & (lane < 128)
        coarse_left[:, 128 * p : 128 * p + 128] = jnp.where(valid, grad, 0.0).T.astype(BF16)
    both = jnp.concatenate(parts, axis=1).reshape(8, 16, 1024)
    for a in range(3):
        gshift[a] = rolled_rows(both, 1 - a).astype(BF16).reshape(128, 1024)
    blocks = []
    for p in range(3):
        lanes = slice(256 * p, 256 * p + 512)
        blocks.append(
            jnp.concatenate(
                [gshift[a, 16 * b : 16 * b + 96, lanes] for a in range(3) for b in range(3)], axis=1
            )
        )
    small = jnp.dot(jnp.concatenate(blocks, axis=0), wb[...], preferred_element_type=F32)
    small = small.astype(BF16)
    q = lax.broadcasted_iota(jnp.int32, (384, 96), 0)
    r = lax.broadcasted_iota(jnp.int32, (384, 96), 1)
    inside = ((q >> 6) == (r >> 4)) & (((q & 31) >> 1) == (r & 15)) & ((q & 31) < 24)
    spread = jnp.where(inside, 1.0, 0.0).astype(BF16)
    for p in range(3):
        lanes = slice(256 * p, 256 * p + 256)
        up = jnp.dot(spread, small[96 * p : 96 * p + 96], preferred_element_type=F32)
        part = (up * 0.125 * slope[:, lanes].astype(F32)).astype(BF16)
        act_out[:, :, lanes] = part.reshape(12, 32, 256)
        wide = part.astype(F32)
        fine_left[:, 768 * p : 768 * p + 384] = wide[:, 0:128].T.astype(BF16)
        fine_left[:, 768 * p + 384 : 768 * p + 768] = wide[:, 128:256].T.astype(BF16)
        if p == 0:
            low = wide[:, 0:128].reshape(12, 32, 128)[:, 0:24]
        if p == 2:
            high = wide[:, 128:256].reshape(12, 32, 128)[:, 0:24]
    to_high, to_low = pack_faces(low, high)
    zl[...] = to_high.astype(BF16)
    zh[...] = to_low.astype(BF16)


def coarse_grads_kernel(left, pshift, out, turned, sums):
    sums[...] = jnp.zeros(sums.shape, F32)
    for a in range(3):
        for b in range(3):
            right = jnp.concatenate(
                [pshift[a, 16 * b : 16 * b + 128, 128 * p : 128 * p + 256] for p in range(4)], axis=0
            )
            turned[...] = jnp.dot(left[...], right, preferred_element_type=F32).T
            for e in range(3):
                near = turned[64 * e : 64 * e + 64, 0:128]
                far = turned[64 * e + 64 : 64 * e + 128, 128:256]
                sums[pl.ds(9 * a + 3 * b + e, 64, stride=32), :] = near + far
    out[...] = sums[...].astype(BF16).reshape(64, 32, 128)


def fine_grads_kernel(
    core, left, shifted, outer, coarse, keep, send, turned, pairs, sums, whole
):
    mask = low_half((32, 128))
    sums[...] = jnp.zeros(sums.shape, F32)
    for a in range(3):
        for b in range(3):
            rights = []
            for p in range(6):
                lanes = slice(128 * p, 128 * p + 256)
                if b == 0:
                    rights += [outer[a, 0:32, lanes], shifted[a, 0:352, lanes]]
                elif b == 1:
                    rights += [shifted[a, :, lanes]]
                else:
                    rights += [shifted[a, 32:384, lanes], outer[a, 32:64, lanes]]
            right = jnp.concatenate(rights, axis=0)
            turned[...] = jnp.dot(left[...], right, preferred_element_type=F32).T
            for e in range(3):
                near = turned[64 * e : 64 * e + 64]
                pairs[...] = near + swap(turned[64 * e + 64 : 64 * e + 128])
                even = pairs[pl.ds(0, 32, stride=2), :]
                odd = pairs[pl.ds(1, 32, stride=2), :]
                slot = 9 * a + 3 * b + e
                sums[pl.ds(slot, 32, stride=32), :] = jnp.where(mask, even, swap(odd))
    whole[0:32] = sums[...].astype(BF16).reshape(32, 32, 128)
    whole[32:96] = coarse[...]
    keep[...] = whole[pl.ds(core[0] * 48, 48)]
    send[...] = whole[pl.ds((1 - core[0]) * 48, 48)]


def features_kernel(rows, ylo, yhi, weight, out, done, shifted):
    done[...] = jnp.zeros(done.shape, F32)
    full = jnp.concatenate([ylo[...][None], rows[...], yhi[...][None]], axis=0).astype(F32)
    for a in range(3):
        shifted[a] = rolled_rows(full, 1 - a).astype(BF16).reshape(448, 896)
    for p in range(6):
        lanes = slice(128 * p, 128 * p + 256)
        left = jnp.concatenate(
            [shifted[a, 32 * b : 32 * b + 384, lanes] for a in range(3) for b in range(3)], axis=1
        )
        grad = jnp.dot(left, weight[...], preferred_element_type=F32)
        grad = grad.reshape(12, 32, 128)[:, 0:24, :]
        out[:, :, 128 * p : 128 * p + 128] = grad.astype(BF16)


def combine_kernel(count, parts, *refs):
    at, ins, outs = refs[0], refs[1 : 1 + parts], refs[1 + parts :]
    size = outs[0].shape[0]
    for k in range(count):
        start = lax.rem(at[0] + k, count) * size
        total = ins[0][pl.ds(start, size)].astype(F32)
        for ref in ins[1:]:
            total = total + ref[pl.ds(start, size)].astype(F32)
        outs[k][...] = total.astype(outs[k].dtype)


def combine(values, place, count, dtype=BF16, after=()):
    size = values[0].shape[0] // count
    return call(
        functools.partial(combine_kernel, count, len(values)),
        [((size, 32, 128), dtype)] * count, values, place=place, after=after,
    )


def place_kernel(count, *refs):
    at, ins, out = refs[0], refs[1 : 1 + count], refs[-1]
    size = ins[0].shape[0]
    for k in range(count):
        out[pl.ds(lax.rem(at[0] + count - k, count) * size, size)] = ins[k][...]


def placed(values, place):
    count = len(values)
    size = values[0].shape[0]
    return call(
        functools.partial(place_kernel, count),
        [((count * size, 32, 128), BF16)], values, place=place,
    )[0]


def last_kernel(core, own, other, fine, coarse, whole):
    whole[pl.ds(core[0] * 48, 48)] = own[...]
    whole[pl.ds((1 - core[0]) * 48, 48)] = other[...]
    cells = 96 * 96 * 96
    for r in range(96):
        value = whole[r].astype(F32)[0:27]
        if r < 32:
            fine[:, 128 * r : 128 * r + 128] = value * (1.0 / math.sqrt(cells))
        else:
            at = 128 * (r - 32)
            coarse[:, at : at + 128] = value * (1.0 / math.sqrt(cells // 8))


def core_partner(value):
    return lax.ppermute(value, "gx", [(i, i ^ 1) for i in range(4)])


def z_partner(value, far):
    return lax.ppermute(value, "gy", [(i, i ^ far) for i in range(8)])


def y_turn(value, step):
    pairs = [(i, i // 4 * 4 + (i + step) % 4) for i in range(8)]
    return lax.ppermute(value, "gz", pairs)


def x_turn(value, step):
    pairs = []
    for gx in range(4):
        for gz in range(8):
            x = (gz // 4 * 2 + gx // 2 + step) % 4
            pairs.append((gx * 8 + gz, (x % 2 * 2 + gx % 2) * 8 + x // 2 * 4 + gz % 4))
    return lax.ppermute(value, ("gx", "gz"), pairs)


def body(features, fine_weight, coarse_weight, cotangent):
    gx = lax.axis_index("gx").astype(jnp.int32)
    gz = lax.axis_index("gz").astype(jnp.int32)
    core = (gx % 2).reshape(1)
    y_at = (gz % 4).reshape(1)
    x_at = (gz // 4 * 2 + gx // 2).reshape(1)
    z_at = jnp.zeros((1,), jnp.int32)

    own = jnp.transpose(features, (1, 0, 2))
    zl, zh = call(
        z_faces_kernel, [((6, 40, 128), BF16)] * 2, (own, cotangent),
        [
            pltpu.VMEM((2, 12, 24, 128), BF16), pltpu.VMEM((2, 12, 6, 128), BF16),
            pltpu.VMEM((12, 8, 128), F32), pltpu.SemaphoreType.DMA((4,)),
        ],
        space=HBM,
    )
    zlo = shift(zl, "gz", 1)
    zhi = shift(zh, "gz", -1)
    w_fine, w_coarse, w_fine_back, w_coarse_back = call(
        weights_kernel,
        [((2304, 128), BF16), ((2304, 256), BF16), ((2304, 128), BF16), ((4608, 256), BF16)],
        (fine_weight, coarse_weight),
        [pltpu.VMEM((1792, 128), F32), pltpu.VMEM((1792, 128), F32)],
        flops=CONV // 4, after=(zl,),
    )
    frows, crows, xl, xh = call(
        x_faces_kernel,
        [((12, 32, 896), BF16), ((6, 16, 1024), BF16), ((24, 1024), BF16), ((24, 1024), BF16)],
        (own, jnp.transpose(cotangent, (1, 0, 2)), zlo, zhi),
        [pltpu.VMEM((12, 32, 896), F32), pltpu.VMEM((6, 16, 1024), F32), pltpu.VMEM((24, 1024), F32)],
        after=(w_fine,),
    )
    xlo = shift(xl, "gx", 1)
    xhi = shift(xh, "gx", -1)
    frows, crows, yl, yh = call(
        y_faces_kernel,
        [((12, 32, 896), BF16), ((6, 16, 1024), BF16), ((48, 1024), BF16), ((48, 1024), BF16)],
        (frows, crows, xlo, xhi),
        [
            pltpu.VMEM((12, 32, 896), F32), pltpu.VMEM((6, 16, 1024), F32),
            pltpu.VMEM((24, 1024), F32), pltpu.VMEM((24, 1024), F32),
        ],
    )
    ylo = shift(yl, "gy", 1)
    yhi = shift(yh, "gy", -1)
    shifted, act_in, edges, inner = call(
        interior_kernel,
        [((3, 384, 896), BF16), ((320, 768), F32), ((64, 768), BF16), ((4, 16, 384), BF16)],
        (frows, w_fine),
        flops=CONV,
    )
    outer, act_out, pooled, pzl, pzh = call(
        border_kernel,
        [
            ((3, 64, 896), BF16), ((64, 768), F32), ((6, 16, 384), BF16),
            ((6, 16, 128), BF16), ((6, 16, 128), BF16),
        ],
        (shifted, ylo, yhi, w_fine, edges, inner),
        flops=CONV // 6,
    )
    pzlo = shift(pzl, "gz", 1)
    pzhi = shift(pzh, "gz", -1)
    slope, done = call(
        slope_kernel, [((384, 768), BF16), ((8, 128), F32)], (act_in, act_out), after=(pzl,)
    )
    prows, pxl, pxh = call(
        pooled_x_kernel,
        [((6, 16, 640), BF16), ((16, 640), BF16), ((16, 640), BF16)],
        (pooled, pzlo, pzhi),
        [pltpu.VMEM((6, 16, 640), F32), pltpu.VMEM((16, 640), F32)],
        after=(done,),
    )
    pxlo = shift(pxl, "gx", 1)
    pxhi = shift(pxh, "gx", -1)
    prows, pyl, pyh = call(
        pooled_y_kernel,
        [((6, 16, 640), BF16), ((2, 16, 640), BF16), ((2, 16, 640), BF16)],
        (prows, pxlo, pxhi),
        [pltpu.VMEM((6, 16, 640), F32), pltpu.VMEM((16, 640), F32), pltpu.VMEM((16, 640), F32)],
    )
    pylo = shift(pyl, "gy", 1)
    pyhi = shift(pyh, "gy", -1)
    act, azl, azh, fine_left, coarse_left, pshift = call(
        backward_kernel,
        [
            ((12, 32, 768), BF16), ((6, 24, 128), BF16), ((6, 24, 128), BF16),
            ((128, 2304), BF16), ((256, 512), BF16), ((3, 160, 640), BF16),
        ],
        (prows, pylo, pyhi, crows, ylo, yhi, slope, w_coarse, w_coarse_back),
        [pltpu.VMEM((3, 128, 1024), BF16)],
        flops=CONV,
    )
    azlo = shift(azl, "gz", 1)
    azhi = shift(azh, "gz", -1)
    (coarse_part,) = call(
        coarse_grads_kernel, [((64, 32, 128), BF16)], (coarse_left, pshift),
        [pltpu.VMEM((256, 256), F32), pltpu.VMEM((2048, 128), F32)],
        flops=CONV // 3,
    )
    keep, send = call(
        fine_grads_kernel,
        [((48, 32, 128), BF16), ((48, 32, 128), BF16)],
        (fine_left, shifted, outer, coarse_part),
        [
            pltpu.VMEM((256, 128), F32), pltpu.VMEM((64, 128), F32),
            pltpu.VMEM((1024, 128), F32), pltpu.VMEM((96, 32, 128), BF16),
        ],
        flops=CONV, place=core, after=(azlo, azhi),
    )

    got = core_partner(send)
    arows, axl, axh = call(
        act_x_faces_kernel,
        [((12, 32, 896), BF16), ((16, 896), BF16), ((16, 896), BF16)],
        (act, azlo, azhi),
        [pltpu.VMEM((12, 32, 896), F32), pltpu.VMEM((16, 896), F32)],
        after=(send,),
    )
    axlo = shift(axl, "gx", 1)
    axhi = shift(axh, "gx", -1)
    arows, ayl, ayh = call(
        act_y_faces_kernel,
        [((12, 32, 896), BF16), ((32, 896), BF16), ((32, 896), BF16)],
        (arows, axlo, axhi),
        [pltpu.VMEM((12, 32, 896), F32), pltpu.VMEM((16, 896), F32), pltpu.VMEM((16, 896), F32)],
        after=(got,),
    )
    parts = combine((keep, got), y_at, 4, after=(ayl,))
    aylo = shift(ayl, "gy", 1)
    ayhi = shift(ayh, "gy", -1)
    got = tuple(y_turn(parts[k], k) for k in (1, 2, 3))
    parts = combine((parts[0],) + got, x_at, 4, after=(aylo, ayhi))
    got = tuple(x_turn(parts[k], k) for k in (1, 2, 3))
    grad_features, done = call(
        features_kernel,
        [((12, 24, 768), BF16), ((8, 128), F32)],
        (arows, aylo, ayhi, w_fine_back),
        [pltpu.VMEM((3, 448, 896), BF16)],
        flops=CONV, after=(parts[0],),
    )
    (part,) = combine((parts[0],) + got, z_at, 1, F32, after=(done,))
    (part,) = combine((part, z_partner(part, 1)), z_at, 1, F32)
    (part,) = combine((part, z_partner(part, 2)), z_at, 1, F32)
    (part,) = combine((part, z_partner(part, 4)), z_at, 1)
    part = placed((part,) + tuple(x_turn(part, k) for k in (1, 2, 3)), x_at)
    part = placed((part,) + tuple(y_turn(part, k) for k in (1, 2, 3)), y_at)
    fine, coarse = call(
        last_kernel,
        [((27, 4096), F32), ((27, 8192), F32)],
        (part, core_partner(part)),
        [pltpu.VMEM((96, 32, 128), BF16)],
        place=core,
    )
    return jnp.transpose(grad_features, (1, 0, 2)), fine, coarse


def solution(mesh):
    in_specs = (P("gx", "gy", "gz"), P(), P(), P("gx", "gy", "gz"))
    out_specs = (P("gx", "gy", "gz"), P(), P())
    return jax.shard_map(body, mesh=mesh, in_specs=in_specs, out_specs=out_specs, check_vma=False)
```

```python
import functools
import math

import jax
import jax.numpy as jnp
from jax import lax
from jax.experimental import pallas as pl
from jax.experimental.pallas import tpu as pltpu
from jax.sharding import PartitionSpec as P

F32 = jnp.float32
BF16 = jnp.bfloat16
VMEM = pl.BlockSpec(memory_space=pltpu.VMEM)
SMEM = pl.BlockSpec(memory_space=pltpu.SMEM)
ANY = pl.BlockSpec(memory_space=pl.ANY)
HBM = pl.BlockSpec(memory_space=pltpu.HBM)
CONV = 2 * 384 * 6 * 2304 * 256


def shift(value, axis, step):
    count = lax.axis_size(axis)
    return lax.ppermute(value, axis, [(i, (i + step) % count) for i in range(count)])


def call(kernel, outs, operands, scratch=(), flops=0, place=None, after=(), space=VMEM):
    moved = sum(math.prod(v.shape) * v.dtype.itemsize for v in operands)
    moved += sum(math.prod(s) * jnp.dtype(d).itemsize for s, d in outs)
    extra = () if place is None else (place,)
    first, last = len(extra) + len(operands), len(extra) + len(operands) + len(after)

    def run(*refs):
        kernel(*refs[:first], *refs[last:])

    return pl.pallas_call(
        run,
        out_shape=[jax.ShapeDtypeStruct(s, d) for s, d in outs],
        in_specs=[SMEM] * len(extra) + [space] * len(operands) + [ANY] * len(after),
        out_specs=[VMEM] * len(outs),
        scratch_shapes=list(scratch),
        compiler_params=pltpu.CompilerParams(vmem_limit_bytes=16 * 1024 * 1024),
        cost_estimate=pl.CostEstimate(flops=flops, bytes_accessed=moved, transcendentals=0),
    )(*extra, *operands, *after)


def low_half(shape):
    return lax.broadcasted_iota(jnp.int32, shape, len(shape) - 1) < 64


def swap(value):
    return pltpu.roll(value, 64, value.ndim - 1)


def rolled_rows(value, step):
    return pltpu.roll(value, step % value.shape[-2], value.ndim - 2)


def pack_faces(low, high):
    mask = low_half((6, 24, 128))
    to_high = jnp.where(mask, swap(high[:6]), high[6:])
    to_low = jnp.where(mask, low[:6], swap(low[6:]))
    return to_high, to_low


def with_faces(own, lo, hi):
    mask = low_half((6, 24, 128))
    first = jnp.where(mask, hi, swap(lo))
    second = jnp.where(mask, swap(hi), lo)
    full = jnp.concatenate([own, jnp.concatenate([first, second], axis=0)], axis=2)
    return pltpu.roll(full, 64, 2)


def flat_fine(fine, flat):
    mask = low_half((27, 128))
    for k in range(32):
        value = fine[:, 128 * k : 128 * k + 128].astype(F32)
        turned = swap(value)
        flat[pl.ds(2 * k, 27, stride=64), :] = jnp.where(mask, value, turned)
        flat[pl.ds(2 * k + 1, 27, stride=64), :] = jnp.where(mask, turned, value)


def forward_weights_kernel(fine, wf, done, flat):
    done[...] = jnp.zeros(done.shape, F32)
    flat_fine(fine, flat)
    mask = low_half((64, 128))
    none = jnp.zeros((64, 128), F32)
    for ab in range(9):
        for j in range(4):
            row = (4 * ab + j) * 64
            at = (3 * ab + j) * 64
            left = flat[at : at + 64, :] if j < 3 else none
            right = flat[at - 64 : at, :] if j > 0 else none
            wf[row : row + 64, :] = jnp.where(mask, left, right).astype(BF16)


def weights_kernel(fine, coarse, wc, wfb, wcb, done, flat_f, flat_c):
    done[...] = jnp.zeros(done.shape, F32)
    flat_fine(fine, flat_f)
    for c in range(64):
        flat_c[pl.ds(c, 27, stride=64), :] = coarse[:, 128 * c : 128 * c + 128].astype(F32)
    flat_f[1728:1792, :] = jnp.zeros((64, 128), F32)
    flat_c[1728:1792, :] = jnp.zeros((64, 128), F32)
    mask = low_half((64, 128))
    wide = low_half((128, 128))
    none = jnp.zeros((64, 128), F32)
    f_turned = []
    c_turned = []
    for m in range(14):
        value = flat_f[128 * m : 128 * m + 128, :].T[0:64]
        f_turned += [jnp.where(mask, value, swap(value)), jnp.where(mask, swap(value), value)]
        value = flat_c[128 * m : 128 * m + 128, :].T
        c_turned += [jnp.where(wide, value, swap(value)), jnp.where(wide, swap(value), value)]
    for ab in range(9):
        for j in range(4):
            row = (4 * ab + j) * 64
            at = (3 * ab + j) * 64
            left = flat_c[at : at + 64, :] if j < 3 else none
            right = flat_c[at - 64 : at, :] if j > 0 else none
            wc[row : row + 64, 0:128] = left.astype(BF16)
            wc[row : row + 64, 128:256] = right.astype(BF16)
            slot = 26 - 3 * ab - j
            left = f_turned[slot] if j < 3 else none
            right = f_turned[slot + 1] if j > 0 else none
            wfb[row : row + 64, :] = jnp.where(mask, left, right).astype(BF16)
            row = 2 * row
            zero = jnp.zeros((128, 128), F32)
            left = c_turned[slot] if j < 3 else zero
            right = c_turned[slot + 1] if j > 0 else zero
            wcb[row : row + 128, 0:128] = left.astype(BF16)
            wcb[row : row + 128, 128:256] = right.astype(BF16)


def z_faces_kernel(own, cot, zl, zh, faces, cfaces, edge, sems):
    copies = []
    for k, lane in enumerate((0, 640)):
        lanes = pl.ds(lane, 128)
        copies.append(pltpu.make_async_copy(own.at[:, :, lanes], faces.at[k], sems.at[2 * k]))
        copies.append(pltpu.make_async_copy(cot.at[:, :, lanes], cfaces.at[k], sems.at[2 * k + 1]))
    for copy in copies:
        copy.start()
    for copy in copies:
        copy.wait()
    to_high, to_low = pack_faces(faces[0].astype(F32), faces[1].astype(F32))
    for out, face, k in ((zl, to_high, 1), (zh, to_low, 0)):
        edge[:, 0:6, :] = cfaces[k].astype(F32)
        turned = [edge[:, y : y + 1, :].reshape(12, 128)[None] for y in range(6)]
        turned = jnp.concatenate(turned, axis=0)
        pad = jnp.zeros((6, 4, 128), F32)
        out[...] = jnp.concatenate([face, turned, pad], axis=1).astype(BF16)


def x_faces_kernel(own, cot, zlo, zhi, rows_out, cot_out, xl, xh, rows, crows, message):
    lo = zlo[...].astype(F32)
    hi = zhi[...].astype(F32)
    rows[:, 0:24, :] = with_faces(own[...].astype(F32), lo[:, 0:24], hi[:, 0:24])
    rows[:, 24:32, :] = jnp.zeros((12, 8, 896), F32)
    crows[:, 8:16, :] = jnp.zeros((6, 8, 1024), F32)
    crows[:, 0:12, 0:128] = lo[:, 24:36]
    crows[:, 0:12, 128:896] = cot[...].astype(F32)
    crows[:, 0:12, 896:1024] = hi[:, 24:36]
    rows_out[...] = rows[...].astype(BF16)
    cot_out[...] = crows[...].astype(BF16)
    message[...] = jnp.zeros(message.shape, F32)
    for out, x, cx in ((xl, 23, 11), (xh, 0, 0)):
        for y in range(12):
            message[y : y + 1, 0:896] = rows[y, x : x + 1, :]
        for y in range(6):
            message[12 + y : 13 + y, :] = crows[y, cx : cx + 1, :]
        out[...] = message[...].astype(BF16)


def y_faces_kernel(rows_in, cot_in, xlo, xhi, rows_out, cot_out, yl, yh, rows, crows, lo, hi):
    lo[...] = xlo[...].astype(F32)
    hi[...] = xhi[...].astype(F32)
    rows[...] = rows_in[...].astype(F32)
    crows[...] = cot_in[...].astype(F32)
    for y in range(12):
        rows[y, 24:25, :] = hi[y : y + 1, 0:896]
        rows[y, 31:32, :] = lo[y : y + 1, 0:896]
    for y in range(6):
        crows[y, 12:13, :] = hi[12 + y : 13 + y, :]
        crows[y, 15:16, :] = lo[12 + y : 13 + y, :]
    rows_out[...] = rows[...].astype(BF16)
    cot_out[...] = crows[...].astype(BF16)
    for out, y, cy in ((yl, 11, 5), (yh, 0, 0)):
        out[0:32, 0:896] = rows[y].astype(BF16)
        out[0:32, 896:1024] = jnp.zeros((32, 128), BF16)
        out[32:48, :] = crows[cy].astype(BF16)


def act_x_faces_kernel(own, zlo, zhi, rows_out, xl, xh, rows, message):
    rows[:, 0:24, :] = with_faces(
        own[...].astype(F32)[:, 0:24], zlo[...].astype(F32), zhi[...].astype(F32)
    )
    rows[:, 24:32, :] = jnp.zeros((12, 8, 896), F32)
    rows_out[...] = rows[...].astype(BF16)
    message[...] = jnp.zeros(message.shape, F32)
    for out, x in ((xl, 23), (xh, 0)):
        for y in range(12):
            message[y : y + 1, :] = rows[y, x : x + 1, :]
        out[...] = message[...].astype(BF16)


def act_y_faces_kernel(rows_in, xlo, xhi, rows_out, yl, yh, rows, lo, hi):
    lo[...] = xlo[...].astype(F32)
    hi[...] = xhi[...].astype(F32)
    rows[...] = rows_in[...].astype(F32)
    for y in range(12):
        rows[y, 24:25, :] = hi[y : y + 1, :]
        rows[y, 31:32, :] = lo[y : y + 1, :]
    value = rows[...].astype(BF16)
    rows_out[...] = value
    yl[...] = value[11]
    yh[...] = value[0]


def sigmoid(value):
    return 0.5 + 0.5 * jnp.tanh(0.5 * value)


def silu(act):
    return (act * sigmoid(act)).astype(BF16)


def silu_slope(act):
    sigma = sigmoid(act)
    return sigma * (1.0 + act * (1.0 - sigma))


def slope_kernel(inner, outer, slope, done):
    slope[0:32, :] = silu_slope(outer[0:32, :]).astype(BF16)
    slope[32:352, :] = silu_slope(inner[...]).astype(BF16)
    slope[352:384, :] = silu_slope(outer[32:64, :]).astype(BF16)
    done[...] = jnp.zeros(done.shape, F32)


def pool_matrix(shape, rule):
    r = lax.broadcasted_iota(jnp.int32, shape, 0)
    q = lax.broadcasted_iota(jnp.int32, shape, 1)
    return jnp.where(rule(r, q), 0.125, 0.0).astype(BF16)


def fold_pairs(part):
    return part + swap(part)


def interior_kernel(rows, weight, shifted, kept, edges, pooled):
    full = rows[...].astype(F32)
    for a in range(3):
        shifted[a] = rolled_rows(full, 1 - a).astype(BF16).reshape(384, 896)
    pool = pool_matrix(
        (64, 320),
        lambda r, q: ((((q >> 5) + 1) >> 1) == (r >> 4) + 1) & (((q & 31) >> 1) == (r & 15)),
    )
    mask = low_half((64, 128))
    for p in range(6):
        lanes = slice(128 * p, 128 * p + 256)
        left = jnp.concatenate(
            [shifted[a, 32 * b : 32 * b + 320, lanes] for a in range(3) for b in range(3)], axis=1
        )
        kept[:, 128 * p : 128 * p + 128] = jnp.dot(
            left, weight[...], preferred_element_type=F32
        )
    hidden = silu(kept[...])
    edges[0:32, :] = hidden[0:32]
    edges[32:64, :] = hidden[288:320]
    sums = jnp.dot(pool, hidden, preferred_element_type=F32)
    pieces = [fold_pairs(sums[:, 128 * p : 128 * p + 128]) for p in range(6)]
    for j in range(3):
        both = jnp.where(mask, pieces[2 * j], pieces[2 * j + 1])
        pooled[:, :, 128 * j : 128 * j + 128] = both.astype(BF16).reshape(4, 16, 128)


def border_kernel(shifted, ylo, yhi, weight, edges, inner, outer, kept, pooled, zl, zh):
    both = jnp.concatenate(
        [ylo[0:32, 0:896][None], yhi[0:32, 0:896][None]], axis=0
    ).astype(F32)
    for a in range(3):
        outer[a] = rolled_rows(both, 1 - a).astype(BF16).reshape(64, 896)
    blocks = []
    for p in range(6):
        lanes = slice(128 * p, 128 * p + 256)
        first = []
        last = []
        for a in range(3):
            first += [outer[a, 0:32, lanes], shifted[a, 0:32, lanes], shifted[a, 32:64, lanes]]
            last += [
                shifted[a, 320:352, lanes], shifted[a, 352:384, lanes], outer[a, 32:64, lanes]
            ]
        blocks.append(jnp.concatenate(first, axis=1))
        blocks.append(jnp.concatenate(last, axis=1))
    act = jnp.dot(jnp.concatenate(blocks, axis=0), weight[...], preferred_element_type=F32)
    hidden = silu(act)
    pool = pool_matrix(
        (32, 128),
        lambda r, q: (((q >> 5) & 1) == (r >> 4)) & (((q & 31) >> 1) == (r & 15)),
    )
    mask = low_half((32, 128))
    pieces = []
    for p in range(6):
        own = slice(128 * p, 128 * p + 128)
        kept[:, own] = act[64 * p : 64 * p + 64]
        column = jnp.concatenate([hidden[64 * p : 64 * p + 64], edges[:, own]], axis=0)
        pieces.append(fold_pairs(jnp.dot(pool, column, preferred_element_type=F32)))
    for j in range(3):
        own = slice(128 * j, 128 * j + 128)
        both = jnp.where(mask, pieces[2 * j], pieces[2 * j + 1]).astype(BF16)
        pooled[0:1, :, own] = both[0:16][None]
        pooled[5:6, :, own] = both[16:32][None]
    pooled[1:5] = inner[...]
    zl[...] = pooled[:, :, 256:384]
    zh[...] = pooled[:, :, 0:128]


def pooled_x_kernel(own, zlo, zhi, rows_out, xl, xh, rows, message):
    rows[...] = jnp.concatenate([zlo[...], own[...], zhi[...]], axis=2).astype(F32)
    rows_out[...] = rows[...].astype(BF16)
    message[...] = jnp.zeros(message.shape, F32)
    for out, x in ((xl, 10), (xh, 0)):
        for y in range(6):
            message[2 * y : 2 * y + 2, :] = rows[y, x : x + 2, :]
        out[...] = message[...].astype(BF16)


def pooled_y_kernel(rows_in, xlo, xhi, rows_out, yl, yh, rows, lo, hi):
    lo[...] = xlo[...].astype(F32)
    hi[...] = xhi[...].astype(F32)
    rows[...] = rows_in[...].astype(F32)
    for y in range(6):
        rows[y, 12:14, :] = hi[2 * y : 2 * y + 2, :]
        rows[y, 14:16, :] = lo[2 * y : 2 * y + 2, :]
    value = rows[...].astype(BF16)
    rows_out[...] = value
    yl[...] = value[4:6]
    yh[...] = value[0:2]


def backward_kernel(
    prow, pylo, pyhi, crow, ylo, yhi, slope, wc, wb,
    act_out, zl, zh, fine_left, coarse_left, pshift, gshift,
):
    full = jnp.concatenate([pylo[...], prow[...], pyhi[...]], axis=0).astype(F32)
    for a in range(3):
        pshift[a] = rolled_rows(full, 1 - a).astype(BF16).reshape(160, 640)
    blocks = []
    for p in range(4):
        lanes = slice(128 * p, 128 * p + 256)
        blocks.append(
            jnp.concatenate(
                [pshift[a, 16 * b : 16 * b + 128, lanes] for a in range(3) for b in range(3)], axis=1
            )
        )
    pre = jnp.dot(jnp.concatenate(blocks, axis=0), wc[...], preferred_element_type=F32)
    tilt = silu_slope(pre)
    cot = jnp.concatenate([ylo[32:48][None], crow[...], yhi[32:48][None]], axis=0).astype(F32)
    row = lax.broadcasted_iota(jnp.int32, (128, 256), 0)
    lane = lax.broadcasted_iota(jnp.int32, (128, 256), 1)
    own_rows = (row >= 16) & (row < 112) & ((row & 15) < 12)
    parts = []
    for p in range(4):
        grad = cot[:, :, 256 * p : 256 * p + 256].reshape(128, 256) * tilt[128 * p : 128 * p + 128]
        grad = grad.astype(BF16).astype(F32)
        parts.append(grad)
        valid = own_rows
        if p == 0:
            valid = valid & (lane >= 128)
        if p == 3:
            valid = valid & (lane < 128)
        coarse_left[:, 128 * p : 128 * p + 128] = jnp.where(valid, grad, 0.0).T.astype(BF16)
    both = jnp.concatenate(parts, axis=1).reshape(8, 16, 1024)
    for a in range(3):
        gshift[a] = rolled_rows(both, 1 - a).astype(BF16).reshape(128, 1024)
    blocks = []
    for p in range(3):
        lanes = slice(256 * p, 256 * p + 512)
        blocks.append(
            jnp.concatenate(
                [gshift[a, 16 * b : 16 * b + 96, lanes] for a in range(3) for b in range(3)], axis=1
            )
        )
    small = jnp.dot(jnp.concatenate(blocks, axis=0), wb[...], preferred_element_type=F32)
    small = small.astype(BF16)
    q = lax.broadcasted_iota(jnp.int32, (384, 96), 0)
    r = lax.broadcasted_iota(jnp.int32, (384, 96), 1)
    inside = ((q >> 6) == (r >> 4)) & (((q & 31) >> 1) == (r & 15)) & ((q & 31) < 24)
    spread = jnp.where(inside, 1.0, 0.0).astype(BF16)
    for p in range(3):
        lanes = slice(256 * p, 256 * p + 256)
        up = jnp.dot(spread, small[96 * p : 96 * p + 96], preferred_element_type=F32)
        part = (up * 0.125 * slope[:, lanes].astype(F32)).astype(BF16)
        act_out[:, :, lanes] = part.reshape(12, 32, 256)
        wide = part.astype(F32)
        fine_left[:, 768 * p : 768 * p + 384] = wide[:, 0:128].T.astype(BF16)
        fine_left[:, 768 * p + 384 : 768 * p + 768] = wide[:, 128:256].T.astype(BF16)
        if p == 0:
            low = wide[:, 0:128].reshape(12, 32, 128)[:, 0:24]
        if p == 2:
            high = wide[:, 128:256].reshape(12, 32, 128)[:, 0:24]
    to_high, to_low = pack_faces(low, high)
    zl[...] = to_high.astype(BF16)
    zh[...] = to_low.astype(BF16)


def fine_grads(left, shifted, outer, turned, pairs, sums, offsets):
    mask = low_half((32, 128))
    for a, b in offsets:
        rights = []
        for p in range(6):
            lanes = slice(128 * p, 128 * p + 256)
            if b == 0:
                rights += [outer[a, 0:32, lanes], shifted[a, 0:352, lanes]]
            elif b == 1:
                rights += [shifted[a, :, lanes]]
            else:
                rights += [shifted[a, 32:384, lanes], outer[a, 32:64, lanes]]
        right = jnp.concatenate(rights, axis=0)
        turned[...] = jnp.dot(left[...], right, preferred_element_type=F32).T
        for e in range(3):
            near = turned[64 * e : 64 * e + 64]
            pairs[...] = near + swap(turned[64 * e + 64 : 64 * e + 128])
            even = pairs[pl.ds(0, 32, stride=2), :]
            odd = pairs[pl.ds(1, 32, stride=2), :]
            slot = 9 * a + 3 * b + e
            sums[pl.ds(slot, 32, stride=32), :] = jnp.where(mask, even, swap(odd))


EARLY = [(0, 0), (0, 1), (0, 2), (1, 0), (1, 1)]
LATE = [(1, 2), (2, 0), (2, 1), (2, 2)]


def early_grads_kernel(
    coarse_left, pshift, left, shifted, outer, out, turned, pairs, sums, cturned
):
    sums[...] = jnp.zeros(sums.shape, F32)
    for a in range(3):
        for b in range(3):
            right = jnp.concatenate(
                [pshift[a, 16 * b : 16 * b + 128, 128 * p : 128 * p + 256] for p in range(4)], axis=0
            )
            cturned[...] = jnp.dot(coarse_left[...], right, preferred_element_type=F32).T
            for e in range(3):
                near = cturned[64 * e : 64 * e + 64, 0:128]
                far = cturned[64 * e + 64 : 64 * e + 128, 128:256]
                sums[pl.ds(1024 + 9 * a + 3 * b + e, 64, stride=32), :] = near + far
    fine_grads(left, shifted, outer, turned, pairs, sums, EARLY)
    out[...] = sums[...].astype(BF16).reshape(96, 32, 128)


def late_grads_kernel(
    core, left, shifted, outer, early, keep, send, turned, pairs, sums, whole
):
    sums[...] = early[0:32].astype(F32).reshape(1024, 128)
    fine_grads(left, shifted, outer, turned, pairs, sums, LATE)
    whole[0:32] = sums[...].astype(BF16).reshape(32, 32, 128)
    whole[32:96] = early[32:96]
    keep[...] = whole[pl.ds(core[0] * 48, 48)]
    send[...] = whole[pl.ds((1 - core[0]) * 48, 48)]


def features_kernel(rows, ylo, yhi, weight, out, done, shifted):
    done[...] = jnp.zeros(done.shape, F32)
    full = jnp.concatenate([ylo[...][None], rows[...], yhi[...][None]], axis=0).astype(F32)
    for a in range(3):
        shifted[a] = rolled_rows(full, 1 - a).astype(BF16).reshape(448, 896)
    for p in range(6):
        lanes = slice(128 * p, 128 * p + 256)
        left = jnp.concatenate(
            [shifted[a, 32 * b : 32 * b + 384, lanes] for a in range(3) for b in range(3)], axis=1
        )
        grad = jnp.dot(left, weight[...], preferred_element_type=F32)
        grad = grad.reshape(12, 32, 128)[:, 0:24, :]
        out[:, :, 128 * p : 128 * p + 128] = grad.astype(BF16)


def combine_kernel(count, parts, *refs):
    at, ins, outs = refs[0], refs[1 : 1 + parts], refs[1 + parts :]
    size = outs[0].shape[0]
    for k in range(count):
        start = lax.rem(at[0] + k, count) * size
        total = ins[0][pl.ds(start, size)].astype(F32)
        for ref in ins[1:]:
            total = total + ref[pl.ds(start, size)].astype(F32)
        outs[k][...] = total.astype(outs[k].dtype)


def combine(values, place, count, after=()):
    size = values[0].shape[0] // count
    return call(
        functools.partial(combine_kernel, count, len(values)),
        [((size, 32, 128), BF16)] * count, values, place=place, after=after,
    )


def place_kernel(count, *refs):
    at, ins, out = refs[0], refs[1 : 1 + count], refs[-1]
    size = ins[0].shape[0]
    for k in range(count):
        out[pl.ds(lax.rem(at[0] + count - k, count) * size, size)] = ins[k][...]


def placed(values, place):
    count = len(values)
    size = values[0].shape[0]
    return call(
        functools.partial(place_kernel, count),
        [((count * size, 32, 128), BF16)], values, place=place,
    )[0]


def last_kernel(core, own, other, fine, coarse, whole):
    whole[pl.ds(core[0] * 48, 48)] = own[...]
    whole[pl.ds((1 - core[0]) * 48, 48)] = other[...]
    cells = 96 * 96 * 96
    for r in range(96):
        value = whole[r].astype(F32)[0:27]
        if r < 32:
            fine[:, 128 * r : 128 * r + 128] = value * (1.0 / math.sqrt(cells))
        else:
            at = 128 * (r - 32)
            coarse[:, at : at + 128] = value * (1.0 / math.sqrt(cells // 8))


def core_partner(value):
    return lax.ppermute(value, "gx", [(i, i ^ 1) for i in range(4)])


def z_partner(value, far):
    return lax.ppermute(value, "gy", [(i, i ^ far) for i in range(8)])


def y_turn(value, step):
    pairs = [(i, i // 4 * 4 + (i + step) % 4) for i in range(8)]
    return lax.ppermute(value, "gz", pairs)


def x_turn(value, step):
    pairs = []
    for gx in range(4):
        for gz in range(8):
            x = (gz // 4 * 2 + gx // 2 + step) % 4
            pairs.append((gx * 8 + gz, (x % 2 * 2 + gx % 2) * 8 + x // 2 * 4 + gz % 4))
    return lax.ppermute(value, ("gx", "gz"), pairs)


def body(features, fine_weight, coarse_weight, cotangent):
    gx = lax.axis_index("gx").astype(jnp.int32)
    gz = lax.axis_index("gz").astype(jnp.int32)
    core = (gx % 2).reshape(1)
    y_at = (gz % 4).reshape(1)
    x_at = (gz // 4 * 2 + gx // 2).reshape(1)
    z_at = jnp.zeros((1,), jnp.int32)

    own = jnp.transpose(features, (1, 0, 2))
    zl, zh = call(
        z_faces_kernel, [((6, 40, 128), BF16)] * 2, (own, cotangent),
        [
            pltpu.VMEM((2, 12, 24, 128), BF16), pltpu.VMEM((2, 12, 6, 128), BF16),
            pltpu.VMEM((12, 8, 128), F32), pltpu.SemaphoreType.DMA((4,)),
        ],
        space=HBM,
    )
    zlo = shift(zl, "gz", 1)
    zhi = shift(zh, "gz", -1)
    w_fine, done = call(
        forward_weights_kernel, [((2304, 128), BF16), ((8, 128), F32)], (fine_weight,),
        [pltpu.VMEM((1728, 128), F32)], after=(zl,),
    )
    frows, crows, xl, xh = call(
        x_faces_kernel,
        [((12, 32, 896), BF16), ((6, 16, 1024), BF16), ((24, 1024), BF16), ((24, 1024), BF16)],
        (own, jnp.transpose(cotangent, (1, 0, 2)), zlo, zhi),
        [pltpu.VMEM((12, 32, 896), F32), pltpu.VMEM((6, 16, 1024), F32), pltpu.VMEM((24, 1024), F32)],
        after=(done,),
    )
    xlo = shift(xl, "gx", 1)
    xhi = shift(xh, "gx", -1)
    frows, crows, yl, yh = call(
        y_faces_kernel,
        [((12, 32, 896), BF16), ((6, 16, 1024), BF16), ((48, 1024), BF16), ((48, 1024), BF16)],
        (frows, crows, xlo, xhi),
        [
            pltpu.VMEM((12, 32, 896), F32), pltpu.VMEM((6, 16, 1024), F32),
            pltpu.VMEM((24, 1024), F32), pltpu.VMEM((24, 1024), F32),
        ],
    )
    ylo = shift(yl, "gy", 1)
    yhi = shift(yh, "gy", -1)
    shifted, act_in, edges, inner = call(
        interior_kernel,
        [((3, 384, 896), BF16), ((320, 768), F32), ((64, 768), BF16), ((4, 16, 384), BF16)],
        (frows, w_fine),
        flops=CONV,
    )
    outer, act_out, pooled, pzl, pzh = call(
        border_kernel,
        [
            ((3, 64, 896), BF16), ((64, 768), F32), ((6, 16, 384), BF16),
            ((6, 16, 128), BF16), ((6, 16, 128), BF16),
        ],
        (shifted, ylo, yhi, w_fine, edges, inner),
        flops=CONV // 6,
    )
    pzlo = shift(pzl, "gz", 1)
    pzhi = shift(pzh, "gz", -1)
    w_coarse, w_fine_back, w_coarse_back, done = call(
        weights_kernel,
        [((2304, 256), BF16), ((2304, 128), BF16), ((4608, 256), BF16), ((8, 128), F32)],
        (fine_weight, coarse_weight),
        [pltpu.VMEM((1792, 128), F32), pltpu.VMEM((1792, 128), F32)],
        after=(pzl,),
    )
    prows, pxl, pxh = call(
        pooled_x_kernel,
        [((6, 16, 640), BF16), ((16, 640), BF16), ((16, 640), BF16)],
        (pooled, pzlo, pzhi),
        [pltpu.VMEM((6, 16, 640), F32), pltpu.VMEM((16, 640), F32)],
        after=(done,),
    )
    pxlo = shift(pxl, "gx", 1)
    pxhi = shift(pxh, "gx", -1)
    slope, done = call(
        slope_kernel, [((384, 768), BF16), ((8, 128), F32)], (act_in, act_out), after=(pxl,)
    )
    prows, pyl, pyh = call(
        pooled_y_kernel,
        [((6, 16, 640), BF16), ((2, 16, 640), BF16), ((2, 16, 640), BF16)],
        (prows, pxlo, pxhi),
        [pltpu.VMEM((6, 16, 640), F32), pltpu.VMEM((16, 640), F32), pltpu.VMEM((16, 640), F32)],
        after=(done,),
    )
    pylo = shift(pyl, "gy", 1)
    pyhi = shift(pyh, "gy", -1)
    act, azl, azh, fine_left, coarse_left, pshift = call(
        backward_kernel,
        [
            ((12, 32, 768), BF16), ((6, 24, 128), BF16), ((6, 24, 128), BF16),
            ((128, 2304), BF16), ((256, 512), BF16), ((3, 160, 640), BF16),
        ],
        (prows, pylo, pyhi, crows, ylo, yhi, slope, w_coarse, w_coarse_back),
        [pltpu.VMEM((3, 128, 1024), BF16)],
        flops=CONV,
    )
    azlo = shift(azl, "gz", 1)
    azhi = shift(azh, "gz", -1)
    (early,) = call(
        early_grads_kernel, [((96, 32, 128), BF16)],
        (coarse_left, pshift, fine_left, shifted, outer),
        [
            pltpu.VMEM((256, 128), F32), pltpu.VMEM((64, 128), F32),
            pltpu.VMEM((3072, 128), F32), pltpu.VMEM((256, 256), F32),
        ],
        flops=CONV,
    )
    keep, send = call(
        late_grads_kernel,
        [((48, 32, 128), BF16), ((48, 32, 128), BF16)],
        (fine_left, shifted, outer, early),
        [
            pltpu.VMEM((256, 128), F32), pltpu.VMEM((64, 128), F32),
            pltpu.VMEM((1024, 128), F32), pltpu.VMEM((96, 32, 128), BF16),
        ],
        flops=CONV // 2, place=core, after=(azlo, azhi),
    )

    got = core_partner(send)
    arows, axl, axh = call(
        act_x_faces_kernel,
        [((12, 32, 896), BF16), ((16, 896), BF16), ((16, 896), BF16)],
        (act, azlo, azhi),
        [pltpu.VMEM((12, 32, 896), F32), pltpu.VMEM((16, 896), F32)],
        after=(send,),
    )
    axlo = shift(axl, "gx", 1)
    axhi = shift(axh, "gx", -1)
    arows, ayl, ayh = call(
        act_y_faces_kernel,
        [((12, 32, 896), BF16), ((32, 896), BF16), ((32, 896), BF16)],
        (arows, axlo, axhi),
        [pltpu.VMEM((12, 32, 896), F32), pltpu.VMEM((16, 896), F32), pltpu.VMEM((16, 896), F32)],
        after=(got,),
    )
    parts = combine((keep, got), y_at, 4, after=(ayl,))
    aylo = shift(ayl, "gy", 1)
    ayhi = shift(ayh, "gy", -1)
    got = tuple(y_turn(parts[k], k) for k in (1, 2, 3))
    parts = combine((parts[0],) + got, x_at, 4, after=(aylo, ayhi))
    got = tuple(x_turn(parts[k], k) for k in (1, 2, 3))
    grad_features, done = call(
        features_kernel,
        [((12, 24, 768), BF16), ((8, 128), F32)],
        (arows, aylo, ayhi, w_fine_back),
        [pltpu.VMEM((3, 448, 896), BF16)],
        flops=CONV, after=(parts[0],),
    )
    (part,) = combine((parts[0],) + got, z_at, 1, after=(done,))
    for far in (1, 2, 7):
        (part,) = combine((part, z_partner(part, far)), z_at, 1)
    part = placed((part,) + tuple(x_turn(part, k) for k in (1, 2, 3)), x_at)
    part = placed((part,) + tuple(y_turn(part, k) for k in (1, 2, 3)), y_at)
    fine, coarse = call(
        last_kernel,
        [((27, 4096), F32), ((27, 8192), F32)],
        (part, core_partner(part)),
        [pltpu.VMEM((96, 32, 128), BF16)],
        place=core,
    )
    return jnp.transpose(grad_features, (1, 0, 2)), fine, coarse


def solution(mesh):
    in_specs = (P("gx", "gy", "gz"), P(), P(), P("gx", "gy", "gz"))
    out_specs = (P("gx", "gy", "gz"), P(), P())
    return jax.shard_map(body, mesh=mesh, in_specs=in_specs, out_specs=out_specs, check_vma=False)
```

```python
import functools
import math

import jax
import jax.numpy as jnp
from jax import lax
from jax.experimental import pallas as pl
from jax.experimental.pallas import tpu as pltpu
from jax.sharding import PartitionSpec as P

F32 = jnp.float32
BF16 = jnp.bfloat16
VMEM = pl.BlockSpec(memory_space=pltpu.VMEM)
SMEM = pl.BlockSpec(memory_space=pltpu.SMEM)
ANY = pl.BlockSpec(memory_space=pl.ANY)
HBM = pl.BlockSpec(memory_space=pltpu.HBM)
CONV = 2 * 384 * 6 * 2304 * 256


def shift(value, axis, step):
    count = lax.axis_size(axis)
    return lax.ppermute(value, axis, [(i, (i + step) % count) for i in range(count)])


def call(kernel, outs, operands, scratch=(), flops=0, place=None, after=(), space=VMEM):
    moved = sum(math.prod(v.shape) * v.dtype.itemsize for v in operands)
    moved += sum(math.prod(s) * jnp.dtype(d).itemsize for s, d in outs)
    extra = () if place is None else (place,)
    first, last = len(extra) + len(operands), len(extra) + len(operands) + len(after)

    def run(*refs):
        kernel(*refs[:first], *refs[last:])

    return pl.pallas_call(
        run,
        out_shape=[jax.ShapeDtypeStruct(s, d) for s, d in outs],
        in_specs=[SMEM] * len(extra) + [space] * len(operands) + [ANY] * len(after),
        out_specs=[VMEM] * len(outs),
        scratch_shapes=list(scratch),
        compiler_params=pltpu.CompilerParams(vmem_limit_bytes=16 * 1024 * 1024),
        cost_estimate=pl.CostEstimate(flops=flops // 8, bytes_accessed=moved // 8, transcendentals=0),
    )(*extra, *operands, *after)


def low_half(shape):
    return lax.broadcasted_iota(jnp.int32, shape, len(shape) - 1) < 64


def swap(value):
    return pltpu.roll(value, 64, value.ndim - 1)


def rolled_rows(value, step):
    return pltpu.roll(value, step % value.shape[-2], value.ndim - 2)


def pack_faces(low, high):
    mask = low_half((6, 24, 128))
    to_high = jnp.where(mask, swap(high[:6]), high[6:])
    to_low = jnp.where(mask, low[:6], swap(low[6:]))
    return to_high, to_low


def with_faces(own, lo, hi):
    mask = low_half((6, 24, 128))
    first = jnp.where(mask, hi, swap(lo))
    second = jnp.where(mask, swap(hi), lo)
    full = jnp.concatenate([own, jnp.concatenate([first, second], axis=0)], axis=2)
    return pltpu.roll(full, 64, 2)


def flat_fine(fine, flat):
    mask = low_half((27, 128))
    for k in range(32):
        value = fine[:, 128 * k : 128 * k + 128].astype(F32)
        turned = swap(value)
        flat[pl.ds(2 * k, 27, stride=64), :] = jnp.where(mask, value, turned)
        flat[pl.ds(2 * k + 1, 27, stride=64), :] = jnp.where(mask, turned, value)


def forward_weights_kernel(fine, wf, done, flat):
    done[...] = jnp.zeros(done.shape, F32)
    flat_fine(fine, flat)
    mask = low_half((64, 128))
    none = jnp.zeros((64, 128), F32)
    for ab in range(9):
        for j in range(4):
            row = (4 * ab + j) * 64
            at = (3 * ab + j) * 64
            left = flat[at : at + 64, :] if j < 3 else none
            right = flat[at - 64 : at, :] if j > 0 else none
            wf[row : row + 64, :] = jnp.where(mask, left, right).astype(BF16)


def weights_kernel(fine, coarse, wc, wfb, wcb, done, flat_f, flat_c):
    done[...] = jnp.zeros(done.shape, F32)
    flat_fine(fine, flat_f)
    for c in range(64):
        flat_c[pl.ds(c, 27, stride=64), :] = coarse[:, 128 * c : 128 * c + 128].astype(F32)
    flat_f[1728:1792, :] = jnp.zeros((64, 128), F32)
    flat_c[1728:1792, :] = jnp.zeros((64, 128), F32)
    mask = low_half((64, 128))
    wide = low_half((128, 128))
    none = jnp.zeros((64, 128), F32)
    f_turned = []
    c_turned = []
    for m in range(14):
        value = flat_f[128 * m : 128 * m + 128, :].T[0:64]
        f_turned += [jnp.where(mask, value, swap(value)), jnp.where(mask, swap(value), value)]
        value = flat_c[128 * m : 128 * m + 128, :].T
        c_turned += [jnp.where(wide, value, swap(value)), jnp.where(wide, swap(value), value)]
    for ab in range(9):
        for j in range(4):
            row = (4 * ab + j) * 64
            at = (3 * ab + j) * 64
            left = flat_c[at : at + 64, :] if j < 3 else none
            right = flat_c[at - 64 : at, :] if j > 0 else none
            wc[row : row + 64, 0:128] = left.astype(BF16)
            wc[row : row + 64, 128:256] = right.astype(BF16)
            slot = 26 - 3 * ab - j
            left = f_turned[slot] if j < 3 else none
            right = f_turned[slot + 1] if j > 0 else none
            wfb[row : row + 64, :] = jnp.where(mask, left, right).astype(BF16)
            row = 2 * row
            zero = jnp.zeros((128, 128), F32)
            left = c_turned[slot] if j < 3 else zero
            right = c_turned[slot + 1] if j > 0 else zero
            wcb[row : row + 128, 0:128] = left.astype(BF16)
            wcb[row : row + 128, 128:256] = right.astype(BF16)


def z_faces_kernel(own, cot, zl, zh, faces, cfaces, edge, sems):
    copies = []
    for k, lane in enumerate((0, 640)):
        lanes = pl.ds(lane, 128)
        copies.append(pltpu.make_async_copy(own.at[:, :, lanes], faces.at[k], sems.at[2 * k]))
        copies.append(pltpu.make_async_copy(cot.at[:, :, lanes], cfaces.at[k], sems.at[2 * k + 1]))
    for copy in copies:
        copy.start()
    for copy in copies:
        copy.wait()
    to_high, to_low = pack_faces(faces[0].astype(F32), faces[1].astype(F32))
    for out, face, k in ((zl, to_high, 1), (zh, to_low, 0)):
        edge[:, 0:6, :] = cfaces[k].astype(F32)
        turned = [edge[:, y : y + 1, :].reshape(12, 128)[None] for y in range(6)]
        turned = jnp.concatenate(turned, axis=0)
        pad = jnp.zeros((6, 4, 128), F32)
        out[...] = jnp.concatenate([face, turned, pad], axis=1).astype(BF16)


def x_faces_kernel(own, cot, zlo, zhi, rows_out, cot_out, xl, xh, rows, crows, message):
    lo = zlo[...].astype(F32)
    hi = zhi[...].astype(F32)
    rows[:, 0:24, :] = with_faces(own[...].astype(F32), lo[:, 0:24], hi[:, 0:24])
    rows[:, 24:32, :] = jnp.zeros((12, 8, 896), F32)
    crows[:, 8:16, :] = jnp.zeros((6, 8, 1024), F32)
    crows[:, 0:12, 0:128] = lo[:, 24:36]
    crows[:, 0:12, 128:896] = cot[...].astype(F32)
    crows[:, 0:12, 896:1024] = hi[:, 24:36]
    rows_out[...] = rows[...].astype(BF16)
    cot_out[...] = crows[...].astype(BF16)
    message[...] = jnp.zeros(message.shape, F32)
    for out, x, cx in ((xl, 23, 11), (xh, 0, 0)):
        for y in range(12):
            message[y : y + 1, 0:896] = rows[y, x : x + 1, :]
        for y in range(6):
            message[12 + y : 13 + y, :] = crows[y, cx : cx + 1, :]
        out[...] = message[...].astype(BF16)


def y_faces_kernel(rows_in, cot_in, xlo, xhi, rows_out, cot_out, yl, yh, rows, crows, lo, hi):
    lo[...] = xlo[...].astype(F32)
    hi[...] = xhi[...].astype(F32)
    rows[...] = rows_in[...].astype(F32)
    crows[...] = cot_in[...].astype(F32)
    for y in range(12):
        rows[y, 24:25, :] = hi[y : y + 1, 0:896]
        rows[y, 31:32, :] = lo[y : y + 1, 0:896]
    for y in range(6):
        crows[y, 12:13, :] = hi[12 + y : 13 + y, :]
        crows[y, 15:16, :] = lo[12 + y : 13 + y, :]
    rows_out[...] = rows[...].astype(BF16)
    cot_out[...] = crows[...].astype(BF16)
    for out, y, cy in ((yl, 11, 5), (yh, 0, 0)):
        out[0:32, 0:896] = rows[y].astype(BF16)
        out[0:32, 896:1024] = jnp.zeros((32, 128), BF16)
        out[32:48, :] = crows[cy].astype(BF16)


def act_x_faces_kernel(own, zlo, zhi, rows_out, xl, xh, rows, message):
    rows[:, 0:24, :] = with_faces(
        own[...].astype(F32)[:, 0:24], zlo[...].astype(F32), zhi[...].astype(F32)
    )
    rows[:, 24:32, :] = jnp.zeros((12, 8, 896), F32)
    rows_out[...] = rows[...].astype(BF16)
    message[...] = jnp.zeros(message.shape, F32)
    for out, x in ((xl, 23), (xh, 0)):
        for y in range(12):
            message[y : y + 1, :] = rows[y, x : x + 1, :]
        out[...] = message[...].astype(BF16)


def act_y_faces_kernel(rows_in, xlo, xhi, rows_out, yl, yh, rows, lo, hi):
    lo[...] = xlo[...].astype(F32)
    hi[...] = xhi[...].astype(F32)
    rows[...] = rows_in[...].astype(F32)
    for y in range(12):
        rows[y, 24:25, :] = hi[y : y + 1, :]
        rows[y, 31:32, :] = lo[y : y + 1, :]
    value = rows[...].astype(BF16)
    rows_out[...] = value
    yl[...] = value[11]
    yh[...] = value[0]


def sigmoid(value):
    return 0.5 + 0.5 * jnp.tanh(0.5 * value)


def silu(act):
    return (act * sigmoid(act)).astype(BF16)


def silu_slope(act):
    sigma = sigmoid(act)
    return sigma * (1.0 + act * (1.0 - sigma))


def slope_kernel(inner, outer, slope, done):
    slope[0:32, :] = silu_slope(outer[0:32, :]).astype(BF16)
    slope[32:352, :] = silu_slope(inner[...]).astype(BF16)
    slope[352:384, :] = silu_slope(outer[32:64, :]).astype(BF16)
    done[...] = jnp.zeros(done.shape, F32)


def pool_matrix(shape, rule):
    r = lax.broadcasted_iota(jnp.int32, shape, 0)
    q = lax.broadcasted_iota(jnp.int32, shape, 1)
    return jnp.where(rule(r, q), 0.125, 0.0).astype(BF16)


def fold_pairs(part):
    return part + swap(part)


def interior_kernel(rows, weight, shifted, kept, edges, pooled):
    full = rows[...].astype(F32)
    for a in range(3):
        shifted[a] = rolled_rows(full, 1 - a).astype(BF16).reshape(384, 896)
    pool = pool_matrix(
        (64, 320),
        lambda r, q: ((((q >> 5) + 1) >> 1) == (r >> 4) + 1) & (((q & 31) >> 1) == (r & 15)),
    )
    mask = low_half((64, 128))
    for p in range(6):
        lanes = slice(128 * p, 128 * p + 256)
        left = jnp.concatenate(
            [shifted[a, 32 * b : 32 * b + 320, lanes] for a in range(3) for b in range(3)], axis=1
        )
        kept[:, 128 * p : 128 * p + 128] = jnp.dot(
            left, weight[...], preferred_element_type=F32
        )
    hidden = silu(kept[...])
    edges[0:32, :] = hidden[0:32]
    edges[32:64, :] = hidden[288:320]
    sums = jnp.dot(pool, hidden, preferred_element_type=F32)
    pieces = [fold_pairs(sums[:, 128 * p : 128 * p + 128]) for p in range(6)]
    for j in range(3):
        both = jnp.where(mask, pieces[2 * j], pieces[2 * j + 1])
        pooled[:, :, 128 * j : 128 * j + 128] = both.astype(BF16).reshape(4, 16, 128)


def border_kernel(shifted, ylo, yhi, weight, edges, inner, kept, pooled, zl, zh, outer):
    both = jnp.concatenate(
        [ylo[0:32, 0:896][None], yhi[0:32, 0:896][None]], axis=0
    ).astype(F32)
    for a in range(3):
        outer[a] = rolled_rows(both, 1 - a).astype(BF16).reshape(64, 896)
    blocks = []
    for p in range(6):
        lanes = slice(128 * p, 128 * p + 256)
        first = []
        last = []
        for a in range(3):
            first += [outer[a, 0:32, lanes], shifted[a, 0:32, lanes], shifted[a, 32:64, lanes]]
            last += [
                shifted[a, 320:352, lanes], shifted[a, 352:384, lanes], outer[a, 32:64, lanes]
            ]
        blocks.append(jnp.concatenate(first, axis=1))
        blocks.append(jnp.concatenate(last, axis=1))
    act = jnp.dot(jnp.concatenate(blocks, axis=0), weight[...], preferred_element_type=F32)
    hidden = silu(act)
    pool = pool_matrix(
        (32, 128),
        lambda r, q: (((q >> 5) & 1) == (r >> 4)) & (((q & 31) >> 1) == (r & 15)),
    )
    mask = low_half((32, 128))
    pieces = []
    for p in range(6):
        own = slice(128 * p, 128 * p + 128)
        kept[:, own] = act[64 * p : 64 * p + 64]
        column = jnp.concatenate([hidden[64 * p : 64 * p + 64], edges[:, own]], axis=0)
        pieces.append(fold_pairs(jnp.dot(pool, column, preferred_element_type=F32)))
    for j in range(3):
        own = slice(128 * j, 128 * j + 128)
        both = jnp.where(mask, pieces[2 * j], pieces[2 * j + 1]).astype(BF16)
        pooled[0:1, :, own] = both[0:16][None]
        pooled[5:6, :, own] = both[16:32][None]
    pooled[1:5] = inner[...]
    zl[...] = pooled[:, :, 256:384]
    zh[...] = pooled[:, :, 0:128]


def pooled_x_kernel(own, zlo, zhi, rows_out, xl, xh, rows, message):
    rows[...] = jnp.concatenate([zlo[...], own[...], zhi[...]], axis=2).astype(F32)
    rows_out[...] = rows[...].astype(BF16)
    message[...] = jnp.zeros(message.shape, F32)
    for out, x in ((xl, 10), (xh, 0)):
        for y in range(6):
            message[2 * y : 2 * y + 2, :] = rows[y, x : x + 2, :]
        out[...] = message[...].astype(BF16)


def pooled_y_kernel(rows_in, xlo, xhi, rows_out, yl, yh, rows, lo, hi):
    lo[...] = xlo[...].astype(F32)
    hi[...] = xhi[...].astype(F32)
    rows[...] = rows_in[...].astype(F32)
    for y in range(6):
        rows[y, 12:14, :] = hi[2 * y : 2 * y + 2, :]
        rows[y, 14:16, :] = lo[2 * y : 2 * y + 2, :]
    value = rows[...].astype(BF16)
    rows_out[...] = value
    yl[...] = value[4:6]
    yh[...] = value[0:2]


def backward_kernel(
    prow, pylo, pyhi, crow, ylo, yhi, slope, wc, wb,
    act_out, zl, zh, fine_left, coarse_left, pshift, gshift,
):
    full = jnp.concatenate([pylo[...], prow[...], pyhi[...]], axis=0).astype(F32)
    for a in range(3):
        pshift[a] = rolled_rows(full, 1 - a).astype(BF16).reshape(160, 640)
    blocks = []
    for p in range(4):
        lanes = slice(128 * p, 128 * p + 256)
        blocks.append(
            jnp.concatenate(
                [pshift[a, 16 * b : 16 * b + 128, lanes] for a in range(3) for b in range(3)], axis=1
            )
        )
    pre = jnp.dot(jnp.concatenate(blocks, axis=0), wc[...], preferred_element_type=F32)
    tilt = silu_slope(pre)
    cot = jnp.concatenate([ylo[32:48][None], crow[...], yhi[32:48][None]], axis=0).astype(F32)
    row = lax.broadcasted_iota(jnp.int32, (128, 256), 0)
    lane = lax.broadcasted_iota(jnp.int32, (128, 256), 1)
    own_rows = (row >= 16) & (row < 112) & ((row & 15) < 12)
    parts = []
    for p in range(4):
        grad = cot[:, :, 256 * p : 256 * p + 256].reshape(128, 256) * tilt[128 * p : 128 * p + 128]
        grad = grad.astype(BF16).astype(F32)
        parts.append(grad)
        valid = own_rows
        if p == 0:
            valid = valid & (lane >= 128)
        if p == 3:
            valid = valid & (lane < 128)
        coarse_left[:, 128 * p : 128 * p + 128] = jnp.where(valid, grad, 0.0).T.astype(BF16)
    both = jnp.concatenate(parts, axis=1).reshape(8, 16, 1024)
    for a in range(3):
        gshift[a] = rolled_rows(both, 1 - a).astype(BF16).reshape(128, 1024)
    blocks = []
    for p in range(3):
        lanes = slice(256 * p, 256 * p + 512)
        blocks.append(
            jnp.concatenate(
                [gshift[a, 16 * b : 16 * b + 96, lanes] for a in range(3) for b in range(3)], axis=1
            )
        )
    small = jnp.dot(jnp.concatenate(blocks, axis=0), wb[...], preferred_element_type=F32)
    small = small.astype(BF16)
    q = lax.broadcasted_iota(jnp.int32, (384, 96), 0)
    r = lax.broadcasted_iota(jnp.int32, (384, 96), 1)
    inside = ((q >> 6) == (r >> 4)) & (((q & 31) >> 1) == (r & 15)) & ((q & 31) < 24)
    spread = jnp.where(inside, 1.0, 0.0).astype(BF16)
    for p in range(3):
        lanes = slice(256 * p, 256 * p + 256)
        up = jnp.dot(spread, small[96 * p : 96 * p + 96], preferred_element_type=F32)
        part = (up * 0.125 * slope[:, lanes].astype(F32)).astype(BF16)
        act_out[:, :, lanes] = part.reshape(12, 32, 256)
        wide = part.astype(F32)
        fine_left[:, 768 * p : 768 * p + 384] = wide[:, 0:128].T.astype(BF16)
        fine_left[:, 768 * p + 384 : 768 * p + 768] = wide[:, 128:256].T.astype(BF16)
        if p == 0:
            low = wide[:, 0:128].reshape(12, 32, 128)[:, 0:24]
        if p == 2:
            high = wide[:, 128:256].reshape(12, 32, 128)[:, 0:24]
    to_high, to_low = pack_faces(low, high)
    zl[...] = to_high.astype(BF16)
    zh[...] = to_low.astype(BF16)


def all_rows(rows, ylo, yhi, shifted, used):
    lo = ylo[0:32, 0:896][None]
    hi = yhi[0:32, 0:896][None]
    full = jnp.concatenate([lo, rows[...], hi], axis=0).astype(F32)
    for a in used:
        shifted[a] = rolled_rows(full, 1 - a).astype(BF16).reshape(448, 896)


def fine_grads(left, shifted, turned, pairs, sums, offsets):
    mask = low_half((32, 128))
    for a, b in offsets:
        right = jnp.concatenate(
            [shifted[a, 32 * b : 32 * b + 384, 128 * p : 128 * p + 256] for p in range(6)], axis=0
        )
        turned[...] = jnp.dot(left[...], right, preferred_element_type=F32).T
        for e in range(3):
            near = turned[64 * e : 64 * e + 64]
            pairs[...] = near + swap(turned[64 * e + 64 : 64 * e + 128])
            even = pairs[pl.ds(0, 32, stride=2), :]
            odd = pairs[pl.ds(1, 32, stride=2), :]
            slot = 9 * a + 3 * b + e
            sums[pl.ds(slot, 32, stride=32), :] = jnp.where(mask, even, swap(odd))


EARLY = [(0, 0), (0, 1), (0, 2), (1, 0), (1, 1)]
LATE = [(1, 2), (2, 0), (2, 1), (2, 2)]


def early_grads_kernel(
    coarse_left, pshift, left, rows, ylo, yhi, out, turned, pairs, sums, cturned, shifted
):
    all_rows(rows, ylo, yhi, shifted, (0, 1))
    sums[...] = jnp.zeros(sums.shape, F32)
    for a in range(3):
        for b in range(3):
            right = jnp.concatenate(
                [pshift[a, 16 * b : 16 * b + 128, 128 * p : 128 * p + 256] for p in range(4)], axis=0
            )
            cturned[...] = jnp.dot(coarse_left[...], right, preferred_element_type=F32).T
            for e in range(3):
                near = cturned[64 * e : 64 * e + 64, 0:128]
                far = cturned[64 * e + 64 : 64 * e + 128, 128:256]
                sums[pl.ds(1024 + 9 * a + 3 * b + e, 64, stride=32), :] = near + far
    fine_grads(left, shifted, turned, pairs, sums, EARLY)
    out[...] = sums[...].astype(BF16).reshape(96, 32, 128)


def late_grads_kernel(
    core, left, rows, ylo, yhi, early, keep, send, turned, pairs, sums, whole, shifted
):
    all_rows(rows, ylo, yhi, shifted, (1, 2))
    sums[...] = early[0:32].astype(F32).reshape(1024, 128)
    fine_grads(left, shifted, turned, pairs, sums, LATE)
    whole[0:32] = sums[...].astype(BF16).reshape(32, 32, 128)
    whole[32:96] = early[32:96]
    keep[...] = whole[pl.ds(core[0] * 48, 48)]
    send[...] = whole[pl.ds((1 - core[0]) * 48, 48)]


def features_kernel(rows, ylo, yhi, weight, out, done, shifted):
    done[...] = jnp.zeros(done.shape, F32)
    full = jnp.concatenate([ylo[...][None], rows[...], yhi[...][None]], axis=0).astype(F32)
    for a in range(3):
        shifted[a] = rolled_rows(full, 1 - a).astype(BF16).reshape(448, 896)
    for p in range(6):
        lanes = slice(128 * p, 128 * p + 256)
        left = jnp.concatenate(
            [shifted[a, 32 * b : 32 * b + 384, lanes] for a in range(3) for b in range(3)], axis=1
        )
        grad = jnp.dot(left, weight[...], preferred_element_type=F32)
        grad = grad.reshape(12, 32, 128)[:, 0:24, :]
        out[:, :, 128 * p : 128 * p + 128] = grad.astype(BF16)


def combine_kernel(count, parts, *refs):
    at, ins, outs = refs[0], refs[1 : 1 + parts], refs[1 + parts :]
    size = outs[0].shape[0]
    for k in range(count):
        start = lax.rem(at[0] + k, count) * size
        total = ins[0][pl.ds(start, size)].astype(F32)
        for ref in ins[1:]:
            total = total + ref[pl.ds(start, size)].astype(F32)
        outs[k][...] = total.astype(outs[k].dtype)


def combine(values, place, count, after=()):
    size = values[0].shape[0] // count
    return call(
        functools.partial(combine_kernel, count, len(values)),
        [((size, 32, 128), BF16)] * count, values, place=place, after=after,
    )


def place_kernel(count, *refs):
    at, ins, out = refs[0], refs[1 : 1 + count], refs[-1]
    size = ins[0].shape[0]
    for k in range(count):
        out[pl.ds(lax.rem(at[0] + count - k, count) * size, size)] = ins[k][...]


def placed(values, place):
    count = len(values)
    size = values[0].shape[0]
    return call(
        functools.partial(place_kernel, count),
        [((count * size, 32, 128), BF16)], values, place=place,
    )[0]


def last_kernel(core, own, other, fine, coarse, whole):
    whole[pl.ds(core[0] * 48, 48)] = own[...]
    whole[pl.ds((1 - core[0]) * 48, 48)] = other[...]
    cells = 96 * 96 * 96
    for r in range(96):
        value = whole[r].astype(F32)[0:27]
        if r < 32:
            fine[:, 128 * r : 128 * r + 128] = value * (1.0 / math.sqrt(cells))
        else:
            at = 128 * (r - 32)
            coarse[:, at : at + 128] = value * (1.0 / math.sqrt(cells // 8))


def core_partner(value):
    return lax.ppermute(value, "gx", [(i, i ^ 1) for i in range(4)])


def z_partner(value, far):
    return lax.ppermute(value, "gy", [(i, i ^ far) for i in range(8)])


def y_turn(value, step):
    pairs = [(i, i // 4 * 4 + (i + step) % 4) for i in range(8)]
    return lax.ppermute(value, "gz", pairs)


def x_turn(value, step):
    pairs = []
    for gx in range(4):
        for gz in range(8):
            x = (gz // 4 * 2 + gx // 2 + step) % 4
            pairs.append((gx * 8 + gz, (x % 2 * 2 + gx % 2) * 8 + x // 2 * 4 + gz % 4))
    return lax.ppermute(value, ("gx", "gz"), pairs)


def body(features, fine_weight, coarse_weight, cotangent):
    gx = lax.axis_index("gx").astype(jnp.int32)
    gz = lax.axis_index("gz").astype(jnp.int32)
    core = (gx % 2).reshape(1)
    y_at = (gz % 4).reshape(1)
    x_at = (gz // 4 * 2 + gx // 2).reshape(1)
    z_at = jnp.zeros((1,), jnp.int32)

    own = jnp.transpose(features, (1, 0, 2))
    zl, zh = call(
        z_faces_kernel, [((6, 40, 128), BF16)] * 2, (own, cotangent),
        [
            pltpu.VMEM((2, 12, 24, 128), BF16), pltpu.VMEM((2, 12, 6, 128), BF16),
            pltpu.VMEM((12, 8, 128), F32), pltpu.SemaphoreType.DMA((4,)),
        ],
        space=HBM,
    )
    zlo = shift(zl, "gz", 1)
    zhi = shift(zh, "gz", -1)
    w_fine, done = call(
        forward_weights_kernel, [((2304, 128), BF16), ((8, 128), F32)], (fine_weight,),
        [pltpu.VMEM((1728, 128), F32)], after=(zl,),
    )
    frows, crows, xl, xh = call(
        x_faces_kernel,
        [((12, 32, 896), BF16), ((6, 16, 1024), BF16), ((24, 1024), BF16), ((24, 1024), BF16)],
        (own, jnp.transpose(cotangent, (1, 0, 2)), zlo, zhi),
        [pltpu.VMEM((12, 32, 896), F32), pltpu.VMEM((6, 16, 1024), F32), pltpu.VMEM((24, 1024), F32)],
        after=(done,),
    )
    xlo = shift(xl, "gx", 1)
    xhi = shift(xh, "gx", -1)
    frows, crows, yl, yh = call(
        y_faces_kernel,
        [((12, 32, 896), BF16), ((6, 16, 1024), BF16), ((48, 1024), BF16), ((48, 1024), BF16)],
        (frows, crows, xlo, xhi),
        [
            pltpu.VMEM((12, 32, 896), F32), pltpu.VMEM((6, 16, 1024), F32),
            pltpu.VMEM((24, 1024), F32), pltpu.VMEM((24, 1024), F32),
        ],
    )
    ylo = shift(yl, "gy", 1)
    yhi = shift(yh, "gy", -1)
    shifted, act_in, edges, inner = call(
        interior_kernel,
        [((3, 384, 896), BF16), ((320, 768), F32), ((64, 768), BF16), ((4, 16, 384), BF16)],
        (frows, w_fine),
        flops=CONV,
    )
    act_out, pooled, pzl, pzh = call(
        border_kernel,
        [
            ((64, 768), F32), ((6, 16, 384), BF16),
            ((6, 16, 128), BF16), ((6, 16, 128), BF16),
        ],
        (shifted, ylo, yhi, w_fine, edges, inner),
        [pltpu.VMEM((3, 64, 896), BF16)],
        flops=CONV // 6,
    )
    pzlo = shift(pzl, "gz", 1)
    pzhi = shift(pzh, "gz", -1)
    w_coarse, w_fine_back, w_coarse_back, done = call(
        weights_kernel,
        [((2304, 256), BF16), ((2304, 128), BF16), ((4608, 256), BF16), ((8, 128), F32)],
        (fine_weight, coarse_weight),
        [pltpu.VMEM((1792, 128), F32), pltpu.VMEM((1792, 128), F32)],
        after=(pzl,),
    )
    prows, pxl, pxh = call(
        pooled_x_kernel,
        [((6, 16, 640), BF16), ((16, 640), BF16), ((16, 640), BF16)],
        (pooled, pzlo, pzhi),
        [pltpu.VMEM((6, 16, 640), F32), pltpu.VMEM((16, 640), F32)],
        after=(done,),
    )
    pxlo = shift(pxl, "gx", 1)
    pxhi = shift(pxh, "gx", -1)
    slope, done = call(
        slope_kernel, [((384, 768), BF16), ((8, 128), F32)], (act_in, act_out), after=(pxl,)
    )
    prows, pyl, pyh = call(
        pooled_y_kernel,
        [((6, 16, 640), BF16), ((2, 16, 640), BF16), ((2, 16, 640), BF16)],
        (prows, pxlo, pxhi),
        [pltpu.VMEM((6, 16, 640), F32), pltpu.VMEM((16, 640), F32), pltpu.VMEM((16, 640), F32)],
        after=(done,),
    )
    pylo = shift(pyl, "gy", 1)
    pyhi = shift(pyh, "gy", -1)
    act, azl, azh, fine_left, coarse_left, pshift = call(
        backward_kernel,
        [
            ((12, 32, 768), BF16), ((6, 24, 128), BF16), ((6, 24, 128), BF16),
            ((128, 2304), BF16), ((256, 512), BF16), ((3, 160, 640), BF16),
        ],
        (prows, pylo, pyhi, crows, ylo, yhi, slope, w_coarse, w_coarse_back),
        [pltpu.VMEM((3, 128, 1024), BF16)],
        flops=CONV,
    )
    azlo = shift(azl, "gz", 1)
    azhi = shift(azh, "gz", -1)
    (early,) = call(
        early_grads_kernel, [((96, 32, 128), BF16)],
        (coarse_left, pshift, fine_left, frows, ylo, yhi),
        [
            pltpu.VMEM((256, 128), F32), pltpu.VMEM((64, 128), F32),
            pltpu.VMEM((3072, 128), F32), pltpu.VMEM((256, 256), F32),
            pltpu.VMEM((3, 448, 896), BF16),
        ],
        flops=CONV,
    )
    keep, send = call(
        late_grads_kernel,
        [((48, 32, 128), BF16), ((48, 32, 128), BF16)],
        (fine_left, frows, ylo, yhi, early),
        [
            pltpu.VMEM((256, 128), F32), pltpu.VMEM((64, 128), F32),
            pltpu.VMEM((1024, 128), F32), pltpu.VMEM((96, 32, 128), BF16),
            pltpu.VMEM((3, 448, 896), BF16),
        ],
        flops=CONV // 2, place=core, after=(azlo, azhi),
    )

    got = core_partner(send)
    arows, axl, axh = call(
        act_x_faces_kernel,
        [((12, 32, 896), BF16), ((16, 896), BF16), ((16, 896), BF16)],
        (act, azlo, azhi),
        [pltpu.VMEM((12, 32, 896), F32), pltpu.VMEM((16, 896), F32)],
        after=(send,),
    )
    axlo = shift(axl, "gx", 1)
    axhi = shift(axh, "gx", -1)
    arows, ayl, ayh = call(
        act_y_faces_kernel,
        [((12, 32, 896), BF16), ((32, 896), BF16), ((32, 896), BF16)],
        (arows, axlo, axhi),
        [pltpu.VMEM((12, 32, 896), F32), pltpu.VMEM((16, 896), F32), pltpu.VMEM((16, 896), F32)],
        after=(got,),
    )
    parts = combine((keep, got), y_at, 4, after=(ayl,))
    aylo = shift(ayl, "gy", 1)
    ayhi = shift(ayh, "gy", -1)
    got = tuple(y_turn(parts[k], k) for k in (1, 2, 3))
    parts = combine((parts[0],) + got, x_at, 4, after=(aylo, ayhi))
    got = tuple(x_turn(parts[k], k) for k in (1, 2, 3))
    grad_features, done = call(
        features_kernel,
        [((12, 24, 768), BF16), ((8, 128), F32)],
        (arows, aylo, ayhi, w_fine_back),
        [pltpu.VMEM((3, 448, 896), BF16)],
        flops=CONV, after=(parts[0],),
    )
    (part,) = combine((parts[0],) + got, z_at, 1, after=(done,))
    for far in (1, 2, 7):
        (part,) = combine((part, z_partner(part, far)), z_at, 1)
    part = placed((part,) + tuple(x_turn(part, k) for k in (1, 2, 3)), x_at)
    part = placed((part,) + tuple(y_turn(part, k) for k in (1, 2, 3)), y_at)
    fine, coarse = call(
        last_kernel,
        [((27, 4096), F32), ((27, 8192), F32)],
        (part, core_partner(part)),
        [pltpu.VMEM((96, 32, 128), BF16)],
        place=core,
    )
    return jnp.transpose(grad_features, (1, 0, 2)), fine, coarse


def solution(mesh):
    in_specs = (P("gx", "gy", "gz"), P(), P(), P("gx", "gy", "gz"))
    out_specs = (P("gx", "gy", "gz"), P(), P())
    return jax.shard_map(body, mesh=mesh, in_specs=in_specs, out_specs=out_specs, check_vma=False)
```

```python
import functools
import math

import jax
import jax.numpy as jnp
from jax import lax
from jax.experimental import pallas as pl
from jax.experimental.pallas import tpu as pltpu
from jax.sharding import PartitionSpec as P

F32 = jnp.float32
BF16 = jnp.bfloat16
VMEM = pl.BlockSpec(memory_space=pltpu.VMEM)
SMEM = pl.BlockSpec(memory_space=pltpu.SMEM)
ANY = pl.BlockSpec(memory_space=pl.ANY)
HBM = pl.BlockSpec(memory_space=pltpu.HBM)
CONV = 2 * 384 * 6 * 2304 * 256


def shift(value, axis, step):
    count = lax.axis_size(axis)
    return lax.ppermute(value, axis, [(i, (i + step) % count) for i in range(count)])


def call(kernel, outs, operands, scratch=(), flops=0, place=None, after=(), space=VMEM):
    moved = sum(math.prod(v.shape) * v.dtype.itemsize for v in operands)
    moved += sum(math.prod(s) * jnp.dtype(d).itemsize for s, d in outs)
    extra = () if place is None else (place,)
    first, last = len(extra) + len(operands), len(extra) + len(operands) + len(after)

    def run(*refs):
        kernel(*refs[:first], *refs[last:])

    return pl.pallas_call(
        run,
        out_shape=[jax.ShapeDtypeStruct(s, d) for s, d in outs],
        in_specs=[SMEM] * len(extra) + [space] * len(operands) + [ANY] * len(after),
        out_specs=[VMEM] * len(outs),
        scratch_shapes=list(scratch),
        compiler_params=pltpu.CompilerParams(vmem_limit_bytes=16 * 1024 * 1024),
        cost_estimate=pl.CostEstimate(flops=flops // 8, bytes_accessed=moved // 8, transcendentals=0),
    )(*extra, *operands, *after)


def low_half(shape):
    return lax.broadcasted_iota(jnp.int32, shape, len(shape) - 1) < 64


def swap(value):
    return pltpu.roll(value, 64, value.ndim - 1)


def rolled_rows(value, step):
    return pltpu.roll(value, step % value.shape[-2], value.ndim - 2)


def pack_faces(low, high):
    mask = low_half((6, 24, 128))
    to_high = jnp.where(mask, swap(high[:6]), high[6:])
    to_low = jnp.where(mask, low[:6], swap(low[6:]))
    return to_high, to_low


def with_faces(own, lo, hi):
    mask = low_half((6, 24, 128))
    first = jnp.where(mask, hi, swap(lo))
    second = jnp.where(mask, swap(hi), lo)
    full = jnp.concatenate([own, jnp.concatenate([first, second], axis=0)], axis=2)
    return pltpu.roll(full, 64, 2)


def flat_fine(fine, flat):
    mask = low_half((27, 128))
    for k in range(32):
        value = fine[:, 128 * k : 128 * k + 128].astype(F32)
        turned = swap(value)
        flat[pl.ds(2 * k, 27, stride=64), :] = jnp.where(mask, value, turned)
        flat[pl.ds(2 * k + 1, 27, stride=64), :] = jnp.where(mask, turned, value)


def forward_weights_kernel(fine, own, wf, rows_out, flat):
    wide = jnp.concatenate([own[...].astype(F32), jnp.zeros((12, 24, 128), F32)], axis=2)
    rows_out[:, 0:24, :] = pltpu.roll(wide, 64, 2).astype(BF16)
    rows_out[:, 24:32, :] = jnp.zeros((12, 8, 896), BF16)
    flat_fine(fine, flat)
    mask = low_half((64, 128))
    none = jnp.zeros((64, 128), F32)
    for ab in range(9):
        for j in range(4):
            row = (4 * ab + j) * 64
            at = (3 * ab + j) * 64
            left = flat[at : at + 64, :] if j < 3 else none
            right = flat[at - 64 : at, :] if j > 0 else none
            wf[row : row + 64, :] = jnp.where(mask, left, right).astype(BF16)


def coarse_weights_kernel(coarse, wc, wcb, done, flat):
    done[...] = jnp.zeros(done.shape, F32)
    for c in range(64):
        flat[pl.ds(c, 27, stride=64), :] = coarse[:, 128 * c : 128 * c + 128].astype(F32)
    flat[1728:1792, :] = jnp.zeros((64, 128), F32)
    wide = low_half((128, 128))
    none = jnp.zeros((64, 128), F32)
    zero = jnp.zeros((128, 128), F32)
    turned = []
    for m in range(14):
        value = flat[128 * m : 128 * m + 128, :].T
        turned += [jnp.where(wide, value, swap(value)), jnp.where(wide, swap(value), value)]
    for ab in range(9):
        for j in range(4):
            row = (4 * ab + j) * 64
            at = (3 * ab + j) * 64
            left = flat[at : at + 64, :] if j < 3 else none
            right = flat[at - 64 : at, :] if j > 0 else none
            wc[row : row + 64, 0:128] = left.astype(BF16)
            wc[row : row + 64, 128:256] = right.astype(BF16)
            slot = 26 - 3 * ab - j
            row = 2 * row
            left = turned[slot] if j < 3 else zero
            right = turned[slot + 1] if j > 0 else zero
            wcb[row : row + 128, 0:128] = left.astype(BF16)
            wcb[row : row + 128, 128:256] = right.astype(BF16)


def backward_weights_kernel(fine, wfb, done, flat):
    done[...] = jnp.zeros(done.shape, F32)
    flat_fine(fine, flat)
    flat[1728:1792, :] = jnp.zeros((64, 128), F32)
    mask = low_half((64, 128))
    none = jnp.zeros((64, 128), F32)
    turned = []
    for m in range(14):
        value = flat[128 * m : 128 * m + 128, :].T[0:64]
        turned += [jnp.where(mask, value, swap(value)), jnp.where(mask, swap(value), value)]
    for ab in range(9):
        for j in range(4):
            row = (4 * ab + j) * 64
            slot = 26 - 3 * ab - j
            left = turned[slot] if j < 3 else none
            right = turned[slot + 1] if j > 0 else none
            wfb[row : row + 64, :] = jnp.where(mask, left, right).astype(BF16)


def z_faces_kernel(own, cot, zl, zh, faces, cfaces, edge, sems):
    copies = []
    for k, lane in enumerate((0, 640)):
        lanes = pl.ds(lane, 128)
        copies.append(pltpu.make_async_copy(own.at[:, :, lanes], faces.at[k], sems.at[2 * k]))
        copies.append(pltpu.make_async_copy(cot.at[:, :, lanes], cfaces.at[k], sems.at[2 * k + 1]))
    for copy in copies:
        copy.start()
    for copy in copies:
        copy.wait()
    to_high, to_low = pack_faces(faces[0].astype(F32), faces[1].astype(F32))
    for out, face, k in ((zl, to_high, 1), (zh, to_low, 0)):
        edge[:, 0:6, :] = cfaces[k].astype(F32)
        turned = [edge[:, y : y + 1, :].reshape(12, 128)[None] for y in range(6)]
        turned = jnp.concatenate(turned, axis=0)
        pad = jnp.zeros((6, 4, 128), F32)
        out[...] = jnp.concatenate([face, turned, pad], axis=1).astype(BF16)


def edge_lanes(lo, hi):
    low = jnp.concatenate([lo, swap(lo)], axis=0)
    high = jnp.concatenate([swap(hi), hi], axis=0)
    return low, high


def x_faces_kernel(own, cot, zlo, zhi, rows_out, cot_out, xl, xh, ends, crows, message):
    lo = zlo[...].astype(F32)
    hi = zhi[...].astype(F32)
    low, high = edge_lanes(lo[:, 0:24], hi[:, 0:24])
    mask = low_half((12, 24, 128))
    rows_out[...] = own[...]
    for at, part in ((0, jnp.where(mask, low, 0.0)), (768, jnp.where(mask, 0.0, high))):
        lanes = slice(at, at + 128)
        rows_out[:, 0:24, lanes] = (own[:, 0:24, lanes].astype(F32) + part).astype(BF16)
    crows[:, 8:16, :] = jnp.zeros((6, 8, 1024), F32)
    crows[:, 0:12, 0:128] = lo[:, 24:36]
    crows[:, 0:12, 128:896] = cot[...].astype(F32)
    crows[:, 0:12, 896:1024] = hi[:, 24:36]
    cot_out[...] = crows[...].astype(BF16)
    ends[0] = rows_out[:, 0:8, :].astype(F32)
    ends[1] = rows_out[:, 16:24, :].astype(F32)
    message[...] = jnp.zeros(message.shape, F32)
    for out, k, x, cx in ((xl, 1, 7, 11), (xh, 0, 0, 0)):
        for y in range(12):
            message[y : y + 1, 0:896] = ends[k, y, x : x + 1, :]
        for y in range(6):
            message[12 + y : 13 + y, :] = crows[y, cx : cx + 1, :]
        out[...] = message[...].astype(BF16)


def y_faces_kernel(rows_in, cot_in, xlo, xhi, rows_out, cot_out, yl, yh, rows, crows, lo, hi):
    lo[...] = xlo[...].astype(F32)
    hi[...] = xhi[...].astype(F32)
    rows[...] = rows_in[...].astype(F32)
    crows[...] = cot_in[...].astype(F32)
    for y in range(12):
        rows[y, 24:25, :] = hi[y : y + 1, 0:896]
        rows[y, 31:32, :] = lo[y : y + 1, 0:896]
    for y in range(6):
        crows[y, 12:13, :] = hi[12 + y : 13 + y, :]
        crows[y, 15:16, :] = lo[12 + y : 13 + y, :]
    rows_out[...] = rows[...].astype(BF16)
    cot_out[...] = crows[...].astype(BF16)
    for out, y, cy in ((yl, 11, 5), (yh, 0, 0)):
        out[0:32, 0:896] = rows[y].astype(BF16)
        out[0:32, 896:1024] = jnp.zeros((32, 128), BF16)
        out[32:48, :] = crows[cy].astype(BF16)


def act_x_faces_kernel(own, zlo, zhi, rows_out, xl, xh, rows, message):
    rows[:, 0:24, :] = with_faces(
        own[...].astype(F32)[:, 0:24], zlo[...].astype(F32), zhi[...].astype(F32)
    )
    rows[:, 24:32, :] = jnp.zeros((12, 8, 896), F32)
    rows_out[...] = rows[...].astype(BF16)
    message[...] = jnp.zeros(message.shape, F32)
    for out, x in ((xl, 23), (xh, 0)):
        for y in range(12):
            message[y : y + 1, :] = rows[y, x : x + 1, :]
        out[...] = message[...].astype(BF16)


def act_y_faces_kernel(rows_in, xlo, xhi, rows_out, yl, yh, rows, lo, hi):
    lo[...] = xlo[...].astype(F32)
    hi[...] = xhi[...].astype(F32)
    rows[...] = rows_in[...].astype(F32)
    for y in range(12):
        rows[y, 24:25, :] = hi[y : y + 1, :]
        rows[y, 31:32, :] = lo[y : y + 1, :]
    value = rows[...].astype(BF16)
    rows_out[...] = value
    yl[...] = value[11]
    yh[...] = value[0]


def sigmoid(value):
    return 0.5 + 0.5 * jnp.tanh(0.5 * value)


def silu(act):
    return (act * sigmoid(act)).astype(BF16)


def silu_slope(act):
    sigma = sigmoid(act)
    return sigma * (1.0 + act * (1.0 - sigma))


def slope_kernel(inner, outer, slope, done):
    slope[0:32, :] = silu_slope(outer[0:32, :]).astype(BF16)
    slope[32:352, :] = silu_slope(inner[...]).astype(BF16)
    slope[352:384, :] = silu_slope(outer[32:64, :]).astype(BF16)
    done[...] = jnp.zeros(done.shape, F32)


def pool_matrix(shape, rule):
    r = lax.broadcasted_iota(jnp.int32, shape, 0)
    q = lax.broadcasted_iota(jnp.int32, shape, 1)
    return jnp.where(rule(r, q), 0.125, 0.0).astype(BF16)


def fold_pairs(part):
    return part + swap(part)


def interior_kernel(rows, weight, shifted, kept, edges, pooled):
    full = rows[...].astype(F32)
    for a in range(3):
        shifted[a] = rolled_rows(full, 1 - a).astype(BF16).reshape(384, 896)
    pool = pool_matrix(
        (64, 320),
        lambda r, q: ((((q >> 5) + 1) >> 1) == (r >> 4) + 1) & (((q & 31) >> 1) == (r & 15)),
    )
    mask = low_half((64, 128))
    for p in range(6):
        lanes = slice(128 * p, 128 * p + 256)
        left = jnp.concatenate(
            [shifted[a, 32 * b : 32 * b + 320, lanes] for a in range(3) for b in range(3)], axis=1
        )
        kept[:, 128 * p : 128 * p + 128] = jnp.dot(
            left, weight[...], preferred_element_type=F32
        )
    hidden = silu(kept[...])
    edges[0:32, :] = hidden[0:32]
    edges[32:64, :] = hidden[288:320]
    sums = jnp.dot(pool, hidden, preferred_element_type=F32)
    pieces = [fold_pairs(sums[:, 128 * p : 128 * p + 128]) for p in range(6)]
    for j in range(3):
        both = jnp.where(mask, pieces[2 * j], pieces[2 * j + 1])
        pooled[:, :, 128 * j : 128 * j + 128] = both.astype(BF16).reshape(4, 16, 128)


def border_kernel(shifted, ylo, yhi, weight, edges, inner, kept, pooled, zl, zh, outer):
    both = jnp.concatenate(
        [ylo[0:32, 0:896][None], yhi[0:32, 0:896][None]], axis=0
    ).astype(F32)
    for a in range(3):
        outer[a] = rolled_rows(both, 1 - a).astype(BF16).reshape(64, 896)
    blocks = []
    for p in range(6):
        lanes = slice(128 * p, 128 * p + 256)
        first = []
        last = []
        for a in range(3):
            first += [outer[a, 0:32, lanes], shifted[a, 0:32, lanes], shifted[a, 32:64, lanes]]
            last += [
                shifted[a, 320:352, lanes], shifted[a, 352:384, lanes], outer[a, 32:64, lanes]
            ]
        blocks.append(jnp.concatenate(first, axis=1))
        blocks.append(jnp.concatenate(last, axis=1))
    act = jnp.dot(jnp.concatenate(blocks, axis=0), weight[...], preferred_element_type=F32)
    hidden = silu(act)
    pool = pool_matrix(
        (32, 128),
        lambda r, q: (((q >> 5) & 1) == (r >> 4)) & (((q & 31) >> 1) == (r & 15)),
    )
    mask = low_half((32, 128))
    pieces = []
    for p in range(6):
        own = slice(128 * p, 128 * p + 128)
        kept[:, own] = act[64 * p : 64 * p + 64]
        column = jnp.concatenate([hidden[64 * p : 64 * p + 64], edges[:, own]], axis=0)
        pieces.append(fold_pairs(jnp.dot(pool, column, preferred_element_type=F32)))
    for j in range(3):
        own = slice(128 * j, 128 * j + 128)
        both = jnp.where(mask, pieces[2 * j], pieces[2 * j + 1]).astype(BF16)
        pooled[0:1, :, own] = both[0:16][None]
        pooled[5:6, :, own] = both[16:32][None]
    pooled[1:5] = inner[...]
    zl[...] = pooled[:, :, 256:384]
    zh[...] = pooled[:, :, 0:128]


def pooled_x_kernel(own, zlo, zhi, rows_out, xl, xh, rows, message):
    rows[...] = jnp.concatenate([zlo[...], own[...], zhi[...]], axis=2).astype(F32)
    rows_out[...] = rows[...].astype(BF16)
    message[...] = jnp.zeros(message.shape, F32)
    for out, x in ((xl, 10), (xh, 0)):
        for y in range(6):
            message[2 * y : 2 * y + 2, :] = rows[y, x : x + 2, :]
        out[...] = message[...].astype(BF16)


def pooled_y_kernel(rows_in, xlo, xhi, rows_out, yl, yh, rows, lo, hi):
    lo[...] = xlo[...].astype(F32)
    hi[...] = xhi[...].astype(F32)
    rows[...] = rows_in[...].astype(F32)
    for y in range(6):
        rows[y, 12:14, :] = hi[2 * y : 2 * y + 2, :]
        rows[y, 14:16, :] = lo[2 * y : 2 * y + 2, :]
    value = rows[...].astype(BF16)
    rows_out[...] = value
    yl[...] = value[4:6]
    yh[...] = value[0:2]


def backward_kernel(
    prow, pylo, pyhi, crow, ylo, yhi, slope, wc, wb,
    act_out, zl, zh, fine_left, coarse_left, pshift, gshift,
):
    full = jnp.concatenate([pylo[...], prow[...], pyhi[...]], axis=0).astype(F32)
    for a in range(3):
        pshift[a] = rolled_rows(full, 1 - a).astype(BF16).reshape(160, 640)
    blocks = []
    for p in range(4):
        lanes = slice(128 * p, 128 * p + 256)
        blocks.append(
            jnp.concatenate(
                [pshift[a, 16 * b : 16 * b + 128, lanes] for a in range(3) for b in range(3)], axis=1
            )
        )
    pre = jnp.dot(jnp.concatenate(blocks, axis=0), wc[...], preferred_element_type=F32)
    tilt = silu_slope(pre)
    cot = jnp.concatenate([ylo[32:48][None], crow[...], yhi[32:48][None]], axis=0).astype(F32)
    row = lax.broadcasted_iota(jnp.int32, (128, 256), 0)
    lane = lax.broadcasted_iota(jnp.int32, (128, 256), 1)
    own_rows = (row >= 16) & (row < 112) & ((row & 15) < 12)
    parts = []
    for p in range(4):
        grad = cot[:, :, 256 * p : 256 * p + 256].reshape(128, 256) * tilt[128 * p : 128 * p + 128]
        grad = grad.astype(BF16).astype(F32)
        parts.append(grad)
        valid = own_rows
        if p == 0:
            valid = valid & (lane >= 128)
        if p == 3:
            valid = valid & (lane < 128)
        coarse_left[:, 128 * p : 128 * p + 128] = jnp.where(valid, grad, 0.0).T.astype(BF16)
    both = jnp.concatenate(parts, axis=1).reshape(8, 16, 1024)
    for a in range(3):
        gshift[a] = rolled_rows(both, 1 - a).astype(BF16).reshape(128, 1024)
    blocks = []
    for p in range(3):
        lanes = slice(256 * p, 256 * p + 512)
        blocks.append(
            jnp.concatenate(
                [gshift[a, 16 * b : 16 * b + 96, lanes] for a in range(3) for b in range(3)], axis=1
            )
        )
    small = jnp.dot(jnp.concatenate(blocks, axis=0), wb[...], preferred_element_type=F32)
    small = small.astype(BF16)
    q = lax.broadcasted_iota(jnp.int32, (384, 96), 0)
    r = lax.broadcasted_iota(jnp.int32, (384, 96), 1)
    inside = ((q >> 6) == (r >> 4)) & (((q & 31) >> 1) == (r & 15)) & ((q & 31) < 24)
    spread = jnp.where(inside, 1.0, 0.0).astype(BF16)
    for p in range(3):
        lanes = slice(256 * p, 256 * p + 256)
        up = jnp.dot(spread, small[96 * p : 96 * p + 96], preferred_element_type=F32)
        part = (up * 0.125 * slope[:, lanes].astype(F32)).astype(BF16)
        act_out[:, :, lanes] = part.reshape(12, 32, 256)
        wide = part.astype(F32)
        fine_left[:, 768 * p : 768 * p + 384] = wide[:, 0:128].T.astype(BF16)
        fine_left[:, 768 * p + 384 : 768 * p + 768] = wide[:, 128:256].T.astype(BF16)
        if p == 0:
            low = wide[:, 0:128].reshape(12, 32, 128)[:, 0:24]
        if p == 2:
            high = wide[:, 128:256].reshape(12, 32, 128)[:, 0:24]
    to_high, to_low = pack_faces(low, high)
    zl[...] = to_high.astype(BF16)
    zh[...] = to_low.astype(BF16)


def all_rows(rows, ylo, yhi, shifted, used):
    lo = ylo[0:32, 0:896][None]
    hi = yhi[0:32, 0:896][None]
    full = jnp.concatenate([lo, rows[...], hi], axis=0).astype(F32)
    for a in used:
        shifted[a] = rolled_rows(full, 1 - a).astype(BF16).reshape(448, 896)


def fine_grads(left, shifted, turned, pairs, sums, offsets):
    mask = low_half((32, 128))
    for a, b in offsets:
        right = jnp.concatenate(
            [shifted[a, 32 * b : 32 * b + 384, 128 * p : 128 * p + 256] for p in range(6)], axis=0
        )
        turned[...] = jnp.dot(left[...], right, preferred_element_type=F32).T
        for e in range(3):
            near = turned[64 * e : 64 * e + 64]
            pairs[...] = near + swap(turned[64 * e + 64 : 64 * e + 128])
            even = pairs[pl.ds(0, 32, stride=2), :]
            odd = pairs[pl.ds(1, 32, stride=2), :]
            slot = 9 * a + 3 * b + e
            sums[pl.ds(slot, 32, stride=32), :] = jnp.where(mask, even, swap(odd))


EARLY = [(0, 0), (0, 1), (0, 2), (1, 0), (1, 1), (1, 2)]
LATE = [(2, 0), (2, 1), (2, 2)]


def early_grads_kernel(
    coarse_left, pshift, left, rows, ylo, yhi, out, turned, pairs, sums, cturned, shifted
):
    all_rows(rows, ylo, yhi, shifted, (0, 1))
    sums[...] = jnp.zeros(sums.shape, F32)
    for a in range(3):
        for b in range(3):
            right = jnp.concatenate(
                [pshift[a, 16 * b : 16 * b + 128, 128 * p : 128 * p + 256] for p in range(4)], axis=0
            )
            cturned[...] = jnp.dot(coarse_left[...], right, preferred_element_type=F32).T
            for e in range(3):
                near = cturned[64 * e : 64 * e + 64, 0:128]
                far = cturned[64 * e + 64 : 64 * e + 128, 128:256]
                sums[pl.ds(1024 + 9 * a + 3 * b + e, 64, stride=32), :] = near + far
    fine_grads(left, shifted, turned, pairs, sums, EARLY)
    out[...] = sums[...].astype(BF16).reshape(96, 32, 128)


def late_grads_kernel(
    core, left, rows, ylo, yhi, early, keep, send, turned, pairs, sums, whole, shifted
):
    all_rows(rows, ylo, yhi, shifted, (2,))
    sums[...] = early[0:32].astype(F32).reshape(1024, 128)
    fine_grads(left, shifted, turned, pairs, sums, LATE)
    whole[0:32] = sums[...].astype(BF16).reshape(32, 32, 128)
    whole[32:96] = early[32:96]
    keep[...] = whole[pl.ds(core[0] * 48, 48)]
    send[...] = whole[pl.ds((1 - core[0]) * 48, 48)]


def features_kernel(rows, ylo, yhi, weight, out, done, shifted):
    done[...] = jnp.zeros(done.shape, F32)
    full = jnp.concatenate([ylo[...][None], rows[...], yhi[...][None]], axis=0).astype(F32)
    for a in range(3):
        shifted[a] = rolled_rows(full, 1 - a).astype(BF16).reshape(448, 896)
    for p in range(6):
        lanes = slice(128 * p, 128 * p + 256)
        left = jnp.concatenate(
            [shifted[a, 32 * b : 32 * b + 384, lanes] for a in range(3) for b in range(3)], axis=1
        )
        grad = jnp.dot(left, weight[...], preferred_element_type=F32)
        grad = grad.reshape(12, 32, 128)[:, 0:24, :]
        out[:, :, 128 * p : 128 * p + 128] = grad.astype(BF16)


def combine_kernel(count, parts, *refs):
    at, ins, outs = refs[0], refs[1 : 1 + parts], refs[1 + parts :]
    size = outs[0].shape[0]
    for k in range(count):
        start = lax.rem(at[0] + k, count) * size
        terms = [ref[pl.ds(start, size)].astype(F32) for ref in ins]
        while len(terms) > 1:
            terms = [sum(terms[i : i + 2][1:], terms[i]) for i in range(0, len(terms), 2)]
        outs[k][...] = terms[0].astype(outs[k].dtype)


def combine(values, place, count, after=()):
    size = values[0].shape[0] // count
    return call(
        functools.partial(combine_kernel, count, len(values)),
        [((size, 32, 128), BF16)] * count, values, place=place, after=after,
    )


def place_kernel(count, *refs):
    at, ins, out = refs[0], refs[1 : 1 + count], refs[-1]
    size = ins[0].shape[0]
    for k in range(count):
        out[pl.ds(lax.rem(at[0] + count - k, count) * size, size)] = ins[k][...]


def placed(values, place):
    count = len(values)
    size = values[0].shape[0]
    return call(
        functools.partial(place_kernel, count),
        [((count * size, 32, 128), BF16)], values, place=place,
    )[0]


def last_kernel(core, own, other, fine, coarse, whole):
    whole[pl.ds(core[0] * 48, 48)] = own[...]
    whole[pl.ds((1 - core[0]) * 48, 48)] = other[...]
    cells = 96 * 96 * 96
    for r in range(96):
        value = whole[r].astype(F32)[0:27]
        if r < 32:
            fine[:, 128 * r : 128 * r + 128] = value * (1.0 / math.sqrt(cells))
        else:
            at = 128 * (r - 32)
            coarse[:, at : at + 128] = value * (1.0 / math.sqrt(cells // 8))


def core_partner(value):
    return lax.ppermute(value, "gx", [(i, i ^ 1) for i in range(4)])


def z_partner(value, far):
    return lax.ppermute(value, "gy", [(i, i ^ far) for i in range(8)])


def y_turn(value, step):
    pairs = [(i, i // 4 * 4 + (i + step) % 4) for i in range(8)]
    return lax.ppermute(value, "gz", pairs)


def x_turn(value, step):
    pairs = []
    for gx in range(4):
        for gz in range(8):
            x = (gz // 4 * 2 + gx // 2 + step) % 4
            pairs.append((gx * 8 + gz, (x % 2 * 2 + gx % 2) * 8 + x // 2 * 4 + gz % 4))
    return lax.ppermute(value, ("gx", "gz"), pairs)


def body(features, fine_weight, coarse_weight, cotangent):
    gx = lax.axis_index("gx").astype(jnp.int32)
    gz = lax.axis_index("gz").astype(jnp.int32)
    core = (gx % 2).reshape(1)
    y_at = (gz % 4).reshape(1)
    x_at = (gz // 4 * 2 + gx // 2).reshape(1)
    z_at = jnp.zeros((1,), jnp.int32)

    own = jnp.transpose(features, (1, 0, 2))
    zl, zh = call(
        z_faces_kernel, [((6, 40, 128), BF16)] * 2, (own, cotangent),
        [
            pltpu.VMEM((2, 12, 24, 128), BF16), pltpu.VMEM((2, 12, 6, 128), BF16),
            pltpu.VMEM((12, 8, 128), F32), pltpu.SemaphoreType.DMA((4,)),
        ],
        space=HBM,
    )
    zlo = shift(zl, "gz", 1)
    zhi = shift(zh, "gz", -1)
    w_fine, frows = call(
        forward_weights_kernel, [((2304, 128), BF16), ((12, 32, 896), BF16)], (fine_weight, own),
        [pltpu.VMEM((1728, 128), F32)], after=(zl,),
    )
    frows, crows, xl, xh = call(
        x_faces_kernel,
        [((12, 32, 896), BF16), ((6, 16, 1024), BF16), ((24, 1024), BF16), ((24, 1024), BF16)],
        (frows, jnp.transpose(cotangent, (1, 0, 2)), zlo, zhi),
        [
            pltpu.VMEM((2, 12, 8, 896), F32), pltpu.VMEM((6, 16, 1024), F32),
            pltpu.VMEM((24, 1024), F32),
        ],
    )
    xlo = shift(xl, "gx", 1)
    xhi = shift(xh, "gx", -1)
    frows, crows, yl, yh = call(
        y_faces_kernel,
        [((12, 32, 896), BF16), ((6, 16, 1024), BF16), ((48, 1024), BF16), ((48, 1024), BF16)],
        (frows, crows, xlo, xhi),
        [
            pltpu.VMEM((12, 32, 896), F32), pltpu.VMEM((6, 16, 1024), F32),
            pltpu.VMEM((24, 1024), F32), pltpu.VMEM((24, 1024), F32),
        ],
    )
    ylo = shift(yl, "gy", 1)
    yhi = shift(yh, "gy", -1)
    shifted, act_in, edges, inner = call(
        interior_kernel,
        [((3, 384, 896), BF16), ((320, 768), F32), ((64, 768), BF16), ((4, 16, 384), BF16)],
        (frows, w_fine),
        flops=CONV,
    )
    act_out, pooled, pzl, pzh = call(
        border_kernel,
        [
            ((64, 768), F32), ((6, 16, 384), BF16),
            ((6, 16, 128), BF16), ((6, 16, 128), BF16),
        ],
        (shifted, ylo, yhi, w_fine, edges, inner),
        [pltpu.VMEM((3, 64, 896), BF16)],
        flops=CONV // 6,
    )
    pzlo = shift(pzl, "gz", 1)
    pzhi = shift(pzh, "gz", -1)
    w_coarse, w_coarse_back, done = call(
        coarse_weights_kernel,
        [((2304, 256), BF16), ((4608, 256), BF16), ((8, 128), F32)],
        (coarse_weight,), [pltpu.VMEM((1792, 128), F32)], after=(pzl,),
    )
    prows, pxl, pxh = call(
        pooled_x_kernel,
        [((6, 16, 640), BF16), ((16, 640), BF16), ((16, 640), BF16)],
        (pooled, pzlo, pzhi),
        [pltpu.VMEM((6, 16, 640), F32), pltpu.VMEM((16, 640), F32)],
        after=(done,),
    )
    pxlo = shift(pxl, "gx", 1)
    pxhi = shift(pxh, "gx", -1)
    slope, done = call(
        slope_kernel, [((384, 768), BF16), ((8, 128), F32)], (act_in, act_out), after=(pxl,)
    )
    prows, pyl, pyh = call(
        pooled_y_kernel,
        [((6, 16, 640), BF16), ((2, 16, 640), BF16), ((2, 16, 640), BF16)],
        (prows, pxlo, pxhi),
        [pltpu.VMEM((6, 16, 640), F32), pltpu.VMEM((16, 640), F32), pltpu.VMEM((16, 640), F32)],
        after=(done,),
    )
    pylo = shift(pyl, "gy", 1)
    pyhi = shift(pyh, "gy", -1)
    act, azl, azh, fine_left, coarse_left, pshift = call(
        backward_kernel,
        [
            ((12, 32, 768), BF16), ((6, 24, 128), BF16), ((6, 24, 128), BF16),
            ((128, 2304), BF16), ((256, 512), BF16), ((3, 160, 640), BF16),
        ],
        (prows, pylo, pyhi, crows, ylo, yhi, slope, w_coarse, w_coarse_back),
        [pltpu.VMEM((3, 128, 1024), BF16)],
        flops=CONV,
    )
    azlo = shift(azl, "gz", 1)
    azhi = shift(azh, "gz", -1)
    (early,) = call(
        early_grads_kernel, [((96, 32, 128), BF16)],
        (coarse_left, pshift, fine_left, frows, ylo, yhi),
        [
            pltpu.VMEM((256, 128), F32), pltpu.VMEM((64, 128), F32),
            pltpu.VMEM((3072, 128), F32), pltpu.VMEM((256, 256), F32),
            pltpu.VMEM((3, 448, 896), BF16),
        ],
        flops=CONV,
    )
    keep, send = call(
        late_grads_kernel,
        [((48, 32, 128), BF16), ((48, 32, 128), BF16)],
        (fine_left, frows, ylo, yhi, early),
        [
            pltpu.VMEM((256, 128), F32), pltpu.VMEM((64, 128), F32),
            pltpu.VMEM((1024, 128), F32), pltpu.VMEM((96, 32, 128), BF16),
            pltpu.VMEM((3, 448, 896), BF16),
        ],
        flops=CONV // 2, place=core, after=(azlo, azhi),
    )

    got = core_partner(send)
    arows, axl, axh = call(
        act_x_faces_kernel,
        [((12, 32, 896), BF16), ((16, 896), BF16), ((16, 896), BF16)],
        (act, azlo, azhi),
        [pltpu.VMEM((12, 32, 896), F32), pltpu.VMEM((16, 896), F32)],
        after=(send,),
    )
    axlo = shift(axl, "gx", 1)
    axhi = shift(axh, "gx", -1)
    arows, ayl, ayh = call(
        act_y_faces_kernel,
        [((12, 32, 896), BF16), ((32, 896), BF16), ((32, 896), BF16)],
        (arows, axlo, axhi),
        [pltpu.VMEM((12, 32, 896), F32), pltpu.VMEM((16, 896), F32), pltpu.VMEM((16, 896), F32)],
        after=(got,),
    )
    parts = combine((keep, got), y_at, 4, after=(ayl,))
    aylo = shift(ayl, "gy", 1)
    ayhi = shift(ayh, "gy", -1)
    got = tuple(y_turn(parts[k], k) for k in (1, 2, 3))
    w_fine_back, done = call(
        backward_weights_kernel, [((2304, 128), BF16), ((8, 128), F32)],
        (fine_weight,), [pltpu.VMEM((1792, 128), F32)], after=(parts[0],),
    )
    parts = combine((parts[0],) + got, x_at, 4, after=(aylo, ayhi, done))
    got = tuple(x_turn(parts[k], k) for k in (1, 2, 3))
    grad_features, done = call(
        features_kernel,
        [((12, 24, 768), BF16), ((8, 128), F32)],
        (arows, aylo, ayhi, w_fine_back),
        [pltpu.VMEM((3, 448, 896), BF16)],
        flops=CONV, after=(parts[0],),
    )
    (part,) = combine((parts[0],) + got, z_at, 1, after=(done,))
    near, next_near, far = (z_partner(part, k) for k in (1, 2, 3))
    (part,) = combine((part, near, next_near, far), z_at, 1)
    (part,) = combine((part, z_partner(part, 7)), z_at, 1)
    part = placed((part,) + tuple(x_turn(part, k) for k in (1, 2, 3)), x_at)
    part = placed((part,) + tuple(y_turn(part, k) for k in (1, 2, 3)), y_at)
    fine, coarse = call(
        last_kernel,
        [((27, 4096), F32), ((27, 8192), F32)],
        (part, core_partner(part)),
        [pltpu.VMEM((96, 32, 128), BF16)],
        place=core,
    )
    return jnp.transpose(grad_features, (1, 0, 2)), fine, coarse


def solution(mesh):
    in_specs = (P("gx", "gy", "gz"), P(), P(), P("gx", "gy", "gz"))
    out_specs = (P("gx", "gy", "gz"), P(), P())
    return jax.shard_map(body, mesh=mesh, in_specs=in_specs, out_specs=out_specs, check_vma=False)
```

```python
import functools
import math

import jax
import jax.numpy as jnp
from jax import lax
from jax.experimental import pallas as pl
from jax.experimental.pallas import tpu as pltpu
from jax.sharding import PartitionSpec as P

F32 = jnp.float32
BF16 = jnp.bfloat16
VMEM = pl.BlockSpec(memory_space=pltpu.VMEM)
SMEM = pl.BlockSpec(memory_space=pltpu.SMEM)
ANY = pl.BlockSpec(memory_space=pl.ANY)
HBM = pl.BlockSpec(memory_space=pltpu.HBM)
CONV = 2 * 384 * 6 * 2304 * 256


def shift(value, axis, step):
    count = lax.axis_size(axis)
    return lax.ppermute(value, axis, [(i, (i + step) % count) for i in range(count)])


def call(kernel, outs, operands, scratch=(), flops=0, place=None, after=(), space=VMEM):
    moved = sum(math.prod(v.shape) * v.dtype.itemsize for v in operands)
    moved += sum(math.prod(s) * jnp.dtype(d).itemsize for s, d in outs)
    extra = () if place is None else (place,)
    first, last = len(extra) + len(operands), len(extra) + len(operands) + len(after)

    def run(*refs):
        kernel(*refs[:first], *refs[last:])

    return pl.pallas_call(
        run,
        out_shape=[jax.ShapeDtypeStruct(s, d) for s, d in outs],
        in_specs=[SMEM] * len(extra) + [space] * len(operands) + [ANY] * len(after),
        out_specs=[VMEM] * len(outs),
        scratch_shapes=list(scratch),
        compiler_params=pltpu.CompilerParams(vmem_limit_bytes=16 * 1024 * 1024),
        cost_estimate=pl.CostEstimate(flops=flops // 8, bytes_accessed=moved // 8, transcendentals=0),
    )(*extra, *operands, *after)


def low_half(shape):
    return lax.broadcasted_iota(jnp.int32, shape, len(shape) - 1) < 64


def swap(value):
    return pltpu.roll(value, 64, value.ndim - 1)


def rolled_rows(value, step):
    return pltpu.roll(value, step % value.shape[-2], value.ndim - 2)


def pack_faces(low, high):
    mask = low_half((6, 24, 128))
    to_high = jnp.where(mask, swap(high[:6]), high[6:])
    to_low = jnp.where(mask, low[:6], swap(low[6:]))
    return to_high, to_low


def with_faces(own, lo, hi):
    mask = low_half((6, 24, 128))
    first = jnp.where(mask, hi, swap(lo))
    second = jnp.where(mask, swap(hi), lo)
    full = jnp.concatenate([own, jnp.concatenate([first, second], axis=0)], axis=2)
    return pltpu.roll(full, 64, 2)


def flat_fine(fine, flat):
    mask = low_half((27, 128))
    for k in range(32):
        value = fine[:, 128 * k : 128 * k + 128].astype(F32)
        turned = swap(value)
        flat[pl.ds(2 * k, 27, stride=64), :] = jnp.where(mask, value, turned)
        flat[pl.ds(2 * k + 1, 27, stride=64), :] = jnp.where(mask, turned, value)


def forward_weights_kernel(fine, own, wf, rows_out, flat):
    wide = jnp.concatenate([own[...].astype(F32), jnp.zeros((12, 24, 128), F32)], axis=2)
    rows_out[:, 0:24, :] = pltpu.roll(wide, 64, 2).astype(BF16)
    rows_out[:, 24:32, :] = jnp.zeros((12, 8, 896), BF16)
    flat_fine(fine, flat)
    mask = low_half((64, 128))
    none = jnp.zeros((64, 128), F32)
    for ab in range(9):
        for j in range(4):
            row = (4 * ab + j) * 64
            at = (3 * ab + j) * 64
            left = flat[at : at + 64, :] if j < 3 else none
            right = flat[at - 64 : at, :] if j > 0 else none
            wf[row : row + 64, :] = jnp.where(mask, left, right).astype(BF16)


def coarse_weights_kernel(coarse, wc, wcb, done, flat):
    done[...] = jnp.zeros(done.shape, F32)
    for c in range(64):
        flat[pl.ds(c, 27, stride=64), :] = coarse[:, 128 * c : 128 * c + 128].astype(F32)
    flat[1728:1792, :] = jnp.zeros((64, 128), F32)
    wide = low_half((128, 128))
    none = jnp.zeros((64, 128), F32)
    zero = jnp.zeros((128, 128), F32)
    turned = []
    for m in range(14):
        value = flat[128 * m : 128 * m + 128, :].T
        turned += [jnp.where(wide, value, swap(value)), jnp.where(wide, swap(value), value)]
    for ab in range(9):
        for j in range(4):
            row = (4 * ab + j) * 64
            at = (3 * ab + j) * 64
            left = flat[at : at + 64, :] if j < 3 else none
            right = flat[at - 64 : at, :] if j > 0 else none
            wc[row : row + 64, 0:128] = left.astype(BF16)
            wc[row : row + 64, 128:256] = right.astype(BF16)
            slot = 26 - 3 * ab - j
            row = 2 * row
            left = turned[slot] if j < 3 else zero
            right = turned[slot + 1] if j > 0 else zero
            wcb[row : row + 128, 0:128] = left.astype(BF16)
            wcb[row : row + 128, 128:256] = right.astype(BF16)


def backward_weights_kernel(fine, wfb, done, flat):
    done[...] = jnp.zeros(done.shape, F32)
    flat_fine(fine, flat)
    flat[1728:1792, :] = jnp.zeros((64, 128), F32)
    mask = low_half((64, 128))
    none = jnp.zeros((64, 128), F32)
    turned = []
    for m in range(14):
        value = flat[128 * m : 128 * m + 128, :].T[0:64]
        turned += [jnp.where(mask, value, swap(value)), jnp.where(mask, swap(value), value)]
    for ab in range(9):
        for j in range(4):
            row = (4 * ab + j) * 64
            slot = 26 - 3 * ab - j
            left = turned[slot] if j < 3 else none
            right = turned[slot + 1] if j > 0 else none
            wfb[row : row + 64, :] = jnp.where(mask, left, right).astype(BF16)


def z_faces_kernel(own, cot, zl, zh, faces, cfaces, edge, sems):
    copies = []
    for k, lane in enumerate((0, 640)):
        lanes = pl.ds(lane, 128)
        copies.append(pltpu.make_async_copy(own.at[:, :, lanes], faces.at[k], sems.at[2 * k]))
        copies.append(pltpu.make_async_copy(cot.at[:, :, lanes], cfaces.at[k], sems.at[2 * k + 1]))
    for copy in copies:
        copy.start()
    for copy in copies:
        copy.wait()
    to_high, to_low = pack_faces(faces[0].astype(F32), faces[1].astype(F32))
    for out, face, k in ((zl, to_high, 1), (zh, to_low, 0)):
        edge[:, 0:6, :] = cfaces[k].astype(F32)
        turned = [edge[:, y : y + 1, :].reshape(12, 128)[None] for y in range(6)]
        turned = jnp.concatenate(turned, axis=0)
        pad = jnp.zeros((6, 4, 128), F32)
        out[...] = jnp.concatenate([face, turned, pad], axis=1).astype(BF16)


def edge_lanes(lo, hi):
    low = jnp.concatenate([lo, swap(lo)], axis=0)
    high = jnp.concatenate([swap(hi), hi], axis=0)
    return low, high


def x_faces_kernel(own, cot, zlo, zhi, rows_out, cot_out, xl, xh, ends, crows, message):
    lo = zlo[...].astype(F32)
    hi = zhi[...].astype(F32)
    low, high = edge_lanes(lo[:, 0:24], hi[:, 0:24])
    mask = low_half((12, 24, 128))
    rows_out[...] = own[...]
    for at, part in ((0, jnp.where(mask, low, 0.0)), (768, jnp.where(mask, 0.0, high))):
        lanes = slice(at, at + 128)
        rows_out[:, 0:24, lanes] = (own[:, 0:24, lanes].astype(F32) + part).astype(BF16)
    crows[:, 8:16, :] = jnp.zeros((6, 8, 1024), F32)
    crows[:, 0:12, 0:128] = lo[:, 24:36]
    crows[:, 0:12, 128:896] = cot[...].astype(F32)
    crows[:, 0:12, 896:1024] = hi[:, 24:36]
    cot_out[...] = crows[...].astype(BF16)
    ends[0] = rows_out[:, 0:8, :].astype(F32)
    ends[1] = rows_out[:, 16:24, :].astype(F32)
    message[...] = jnp.zeros(message.shape, F32)
    for out, k, x, cx in ((xl, 1, 7, 11), (xh, 0, 0, 0)):
        for y in range(12):
            message[y : y + 1, 0:896] = ends[k, y, x : x + 1, :]
        for y in range(6):
            message[12 + y : 13 + y, :] = crows[y, cx : cx + 1, :]
        out[...] = message[...].astype(BF16)


def y_faces_kernel(rows_in, cot_in, xlo, xhi, rows_out, cot_out, yl, yh, rows, crows, lo, hi):
    lo[...] = xlo[...].astype(F32)
    hi[...] = xhi[...].astype(F32)
    rows[...] = rows_in[...].astype(F32)
    crows[...] = cot_in[...].astype(F32)
    for y in range(12):
        rows[y, 24:25, :] = hi[y : y + 1, 0:896]
        rows[y, 31:32, :] = lo[y : y + 1, 0:896]
    for y in range(6):
        crows[y, 12:13, :] = hi[12 + y : 13 + y, :]
        crows[y, 15:16, :] = lo[12 + y : 13 + y, :]
    rows_out[...] = rows[...].astype(BF16)
    cot_out[...] = crows[...].astype(BF16)
    for out, y, cy in ((yl, 11, 5), (yh, 0, 0)):
        out[0:32, 0:896] = rows[y].astype(BF16)
        out[0:32, 896:1024] = jnp.zeros((32, 128), BF16)
        out[32:48, :] = crows[cy].astype(BF16)


def act_x_faces_kernel(own, zlo, zhi, rows_out, xl, xh, rows, message):
    rows[:, 0:24, :] = with_faces(
        own[...].astype(F32)[:, 0:24], zlo[...].astype(F32), zhi[...].astype(F32)
    )
    rows[:, 24:32, :] = jnp.zeros((12, 8, 896), F32)
    rows_out[...] = rows[...].astype(BF16)
    message[...] = jnp.zeros(message.shape, F32)
    for out, x in ((xl, 23), (xh, 0)):
        for y in range(12):
            message[y : y + 1, :] = rows[y, x : x + 1, :]
        out[...] = message[...].astype(BF16)


def act_y_faces_kernel(rows_in, xlo, xhi, rows_out, yl, yh, rows, lo, hi):
    lo[...] = xlo[...].astype(F32)
    hi[...] = xhi[...].astype(F32)
    rows[...] = rows_in[...].astype(F32)
    for y in range(12):
        rows[y, 24:25, :] = hi[y : y + 1, :]
        rows[y, 31:32, :] = lo[y : y + 1, :]
    value = rows[...].astype(BF16)
    rows_out[...] = value
    yl[...] = value[11]
    yh[...] = value[0]


def sigmoid(value):
    return 0.5 + 0.5 * jnp.tanh(0.5 * value)


def silu(act):
    return (act * sigmoid(act)).astype(BF16)


def silu_slope(act):
    sigma = sigmoid(act)
    return sigma * (1.0 + act * (1.0 - sigma))


def slope_kernel(inner, outer, slope, done):
    slope[0:32, :] = silu_slope(outer[0:32, :]).astype(BF16)
    slope[32:352, :] = silu_slope(inner[...]).astype(BF16)
    slope[352:384, :] = silu_slope(outer[32:64, :]).astype(BF16)
    done[...] = jnp.zeros(done.shape, F32)


def pool_matrix(shape, rule):
    r = lax.broadcasted_iota(jnp.int32, shape, 0)
    q = lax.broadcasted_iota(jnp.int32, shape, 1)
    return jnp.where(rule(r, q), 0.125, 0.0).astype(BF16)


def fold_pairs(part):
    return part + swap(part)


def interior_kernel(rows, weight, shifted, kept, edges, pooled):
    full = rows[...].astype(F32)
    for a in range(3):
        shifted[a] = rolled_rows(full, 1 - a).astype(BF16).reshape(384, 896)
    pool = pool_matrix(
        (64, 320),
        lambda r, q: ((((q >> 5) + 1) >> 1) == (r >> 4) + 1) & (((q & 31) >> 1) == (r & 15)),
    )
    mask = low_half((64, 128))
    for p in range(6):
        lanes = slice(128 * p, 128 * p + 256)
        left = jnp.concatenate(
            [shifted[a, 32 * b : 32 * b + 320, lanes] for a in range(3) for b in range(3)], axis=1
        )
        kept[:, 128 * p : 128 * p + 128] = jnp.dot(
            left, weight[...], preferred_element_type=F32
        )
    hidden = silu(kept[...])
    edges[0:32, :] = hidden[0:32]
    edges[32:64, :] = hidden[288:320]
    sums = jnp.dot(pool, hidden, preferred_element_type=F32)
    pieces = [fold_pairs(sums[:, 128 * p : 128 * p + 128]) for p in range(6)]
    for j in range(3):
        both = jnp.where(mask, pieces[2 * j], pieces[2 * j + 1])
        pooled[:, :, 128 * j : 128 * j + 128] = both.astype(BF16).reshape(4, 16, 128)


def border_kernel(shifted, ylo, yhi, weight, edges, inner, kept, pooled, zl, zh, outer):
    both = jnp.concatenate(
        [ylo[0:32, 0:896][None], yhi[0:32, 0:896][None]], axis=0
    ).astype(F32)
    for a in range(3):
        outer[a] = rolled_rows(both, 1 - a).astype(BF16).reshape(64, 896)
    blocks = []
    for p in range(6):
        lanes = slice(128 * p, 128 * p + 256)
        first = []
        last = []
        for a in range(3):
            first += [outer[a, 0:32, lanes], shifted[a, 0:32, lanes], shifted[a, 32:64, lanes]]
            last += [
                shifted[a, 320:352, lanes], shifted[a, 352:384, lanes], outer[a, 32:64, lanes]
            ]
        blocks.append(jnp.concatenate(first, axis=1))
        blocks.append(jnp.concatenate(last, axis=1))
    act = jnp.dot(jnp.concatenate(blocks, axis=0), weight[...], preferred_element_type=F32)
    hidden = silu(act)
    pool = pool_matrix(
        (32, 128),
        lambda r, q: (((q >> 5) & 1) == (r >> 4)) & (((q & 31) >> 1) == (r & 15)),
    )
    mask = low_half((32, 128))
    pieces = []
    for p in range(6):
        own = slice(128 * p, 128 * p + 128)
        kept[:, own] = act[64 * p : 64 * p + 64]
        column = jnp.concatenate([hidden[64 * p : 64 * p + 64], edges[:, own]], axis=0)
        pieces.append(fold_pairs(jnp.dot(pool, column, preferred_element_type=F32)))
    for j in range(3):
        own = slice(128 * j, 128 * j + 128)
        both = jnp.where(mask, pieces[2 * j], pieces[2 * j + 1]).astype(BF16)
        pooled[0:1, :, own] = both[0:16][None]
        pooled[5:6, :, own] = both[16:32][None]
    pooled[1:5] = inner[...]
    zl[...] = pooled[:, :, 256:384]
    zh[...] = pooled[:, :, 0:128]


def pooled_x_kernel(own, zlo, zhi, rows_out, xl, xh, rows, message):
    rows[...] = jnp.concatenate([zlo[...], own[...], zhi[...]], axis=2).astype(F32)
    rows_out[...] = rows[...].astype(BF16)
    message[...] = jnp.zeros(message.shape, F32)
    for out, x in ((xl, 10), (xh, 0)):
        for y in range(6):
            message[2 * y : 2 * y + 2, :] = rows[y, x : x + 2, :]
        out[...] = message[...].astype(BF16)


def pooled_y_kernel(rows_in, xlo, xhi, rows_out, yl, yh, rows, lo, hi):
    lo[...] = xlo[...].astype(F32)
    hi[...] = xhi[...].astype(F32)
    rows[...] = rows_in[...].astype(F32)
    for y in range(6):
        rows[y, 12:14, :] = hi[2 * y : 2 * y + 2, :]
        rows[y, 14:16, :] = lo[2 * y : 2 * y + 2, :]
    value = rows[...].astype(BF16)
    rows_out[...] = value
    yl[...] = value[4:6]
    yh[...] = value[0:2]


def backward_kernel(
    prow, pylo, pyhi, crow, ylo, yhi, slope, wc, wb,
    act_out, zl, zh, fine_left, coarse_left, pshift, gshift,
):
    full = jnp.concatenate([pylo[...], prow[...], pyhi[...]], axis=0).astype(F32)
    for a in range(3):
        pshift[a] = rolled_rows(full, 1 - a).astype(BF16).reshape(160, 640)
    blocks = []
    for p in range(4):
        lanes = slice(128 * p, 128 * p + 256)
        blocks.append(
            jnp.concatenate(
                [pshift[a, 16 * b : 16 * b + 128, lanes] for a in range(3) for b in range(3)], axis=1
            )
        )
    pre = jnp.dot(jnp.concatenate(blocks, axis=0), wc[...], preferred_element_type=F32)
    tilt = silu_slope(pre)
    cot = jnp.concatenate([ylo[32:48][None], crow[...], yhi[32:48][None]], axis=0).astype(F32)
    row = lax.broadcasted_iota(jnp.int32, (128, 256), 0)
    lane = lax.broadcasted_iota(jnp.int32, (128, 256), 1)
    own_rows = (row >= 16) & (row < 112) & ((row & 15) < 12)
    parts = []
    for p in range(4):
        grad = cot[:, :, 256 * p : 256 * p + 256].reshape(128, 256) * tilt[128 * p : 128 * p + 128]
        grad = grad.astype(BF16).astype(F32)
        parts.append(grad)
        valid = own_rows
        if p == 0:
            valid = valid & (lane >= 128)
        if p == 3:
            valid = valid & (lane < 128)
        coarse_left[:, 128 * p : 128 * p + 128] = jnp.where(valid, grad, 0.0).T.astype(BF16)
    both = jnp.concatenate(parts, axis=1).reshape(8, 16, 1024)
    for a in range(3):
        gshift[a] = rolled_rows(both, 1 - a).astype(BF16).reshape(128, 1024)
    blocks = []
    for p in range(3):
        lanes = slice(256 * p, 256 * p + 512)
        blocks.append(
            jnp.concatenate(
                [gshift[a, 16 * b : 16 * b + 96, lanes] for a in range(3) for b in range(3)], axis=1
            )
        )
    small = jnp.dot(jnp.concatenate(blocks, axis=0), wb[...], preferred_element_type=F32)
    small = small.astype(BF16)
    q = lax.broadcasted_iota(jnp.int32, (384, 96), 0)
    r = lax.broadcasted_iota(jnp.int32, (384, 96), 1)
    inside = ((q >> 6) == (r >> 4)) & (((q & 31) >> 1) == (r & 15)) & ((q & 31) < 24)
    spread = jnp.where(inside, 1.0, 0.0).astype(BF16)
    for p in range(3):
        lanes = slice(256 * p, 256 * p + 256)
        up = jnp.dot(spread, small[96 * p : 96 * p + 96], preferred_element_type=F32)
        part = (up * 0.125 * slope[:, lanes].astype(F32)).astype(BF16)
        act_out[:, :, lanes] = part.reshape(12, 32, 256)
        wide = part.astype(F32)
        fine_left[:, 768 * p : 768 * p + 384] = wide[:, 0:128].T.astype(BF16)
        fine_left[:, 768 * p + 384 : 768 * p + 768] = wide[:, 128:256].T.astype(BF16)
        if p == 0:
            low = wide[:, 0:128].reshape(12, 32, 128)[:, 0:24]
        if p == 2:
            high = wide[:, 128:256].reshape(12, 32, 128)[:, 0:24]
    to_high, to_low = pack_faces(low, high)
    zl[...] = to_high.astype(BF16)
    zh[...] = to_low.astype(BF16)


def all_rows(rows, ylo, yhi, shifted, used):
    lo = ylo[0:32, 0:896][None]
    hi = yhi[0:32, 0:896][None]
    full = jnp.concatenate([lo, rows[...], hi], axis=0).astype(F32)
    for a in used:
        shifted[a] = rolled_rows(full, 1 - a).astype(BF16).reshape(448, 896)


def fine_grads(left, shifted, turned, pairs, sums, offsets):
    mask = low_half((32, 128))
    for a, b in offsets:
        right = jnp.concatenate(
            [shifted[a, 32 * b : 32 * b + 384, 128 * p : 128 * p + 256] for p in range(6)], axis=0
        )
        turned[...] = jnp.dot(left[...], right, preferred_element_type=F32).T
        for e in range(3):
            near = turned[64 * e : 64 * e + 64]
            pairs[...] = near + swap(turned[64 * e + 64 : 64 * e + 128])
            even = pairs[pl.ds(0, 32, stride=2), :]
            odd = pairs[pl.ds(1, 32, stride=2), :]
            slot = 9 * a + 3 * b + e
            sums[pl.ds(slot, 32, stride=32), :] = jnp.where(mask, even, swap(odd))


EARLY = [(0, 0), (0, 1), (0, 2), (1, 0), (1, 1), (1, 2), (2, 0), (2, 1)]
LATE = [(2, 2)]


def early_grads_kernel(
    coarse_left, pshift, left, rows, ylo, yhi, out, turned, pairs, sums, cturned, shifted
):
    all_rows(rows, ylo, yhi, shifted, (0, 1, 2))
    sums[...] = jnp.zeros(sums.shape, F32)
    for a in range(3):
        for b in range(3):
            right = jnp.concatenate(
                [pshift[a, 16 * b : 16 * b + 128, 128 * p : 128 * p + 256] for p in range(4)], axis=0
            )
            cturned[...] = jnp.dot(coarse_left[...], right, preferred_element_type=F32).T
            for e in range(3):
                near = cturned[64 * e : 64 * e + 64, 0:128]
                far = cturned[64 * e + 64 : 64 * e + 128, 128:256]
                sums[pl.ds(1024 + 9 * a + 3 * b + e, 64, stride=32), :] = near + far
    fine_grads(left, shifted, turned, pairs, sums, EARLY)
    out[...] = sums[...].astype(BF16).reshape(96, 32, 128)


def late_grads_kernel(
    core, left, rows, ylo, yhi, early, keep, send, turned, pairs, sums, whole, shifted
):
    all_rows(rows, ylo, yhi, shifted, (2,))
    sums[...] = early[0:32].astype(F32).reshape(1024, 128)
    fine_grads(left, shifted, turned, pairs, sums, LATE)
    whole[0:32] = sums[...].astype(BF16).reshape(32, 32, 128)
    whole[32:96] = early[32:96]
    keep[...] = whole[pl.ds(core[0] * 48, 48)]
    send[...] = whole[pl.ds((1 - core[0]) * 48, 48)]


def features_kernel(rows, ylo, yhi, weight, out, done, shifted):
    done[...] = jnp.zeros(done.shape, F32)
    full = jnp.concatenate([ylo[...][None], rows[...], yhi[...][None]], axis=0).astype(F32)
    for a in range(3):
        shifted[a] = rolled_rows(full, 1 - a).astype(BF16).reshape(448, 896)
    for p in range(6):
        lanes = slice(128 * p, 128 * p + 256)
        left = jnp.concatenate(
            [shifted[a, 32 * b : 32 * b + 384, lanes] for a in range(3) for b in range(3)], axis=1
        )
        grad = jnp.dot(left, weight[...], preferred_element_type=F32)
        grad = grad.reshape(12, 32, 128)[:, 0:24, :]
        out[:, :, 128 * p : 128 * p + 128] = grad.astype(BF16)


def combine_kernel(count, parts, *refs):
    at, ins, outs = refs[0], refs[1 : 1 + parts], refs[1 + parts :]
    size = outs[0].shape[0]
    for k in range(count):
        start = lax.rem(at[0] + k, count) * size
        terms = [ref[pl.ds(start, size)].astype(F32) for ref in ins]
        while len(terms) > 1:
            terms = [sum(terms[i : i + 2][1:], terms[i]) for i in range(0, len(terms), 2)]
        outs[k][...] = terms[0].astype(outs[k].dtype)


def combine(values, place, count, after=()):
    size = values[0].shape[0] // count
    return call(
        functools.partial(combine_kernel, count, len(values)),
        [((size, 32, 128), BF16)] * count, values, place=place, after=after,
    )


def place_kernel(count, *refs):
    at, ins, out = refs[0], refs[1 : 1 + count], refs[-1]
    size = ins[0].shape[0]
    for k in range(count):
        out[pl.ds(lax.rem(at[0] + count - k, count) * size, size)] = ins[k][...]


def placed(values, place, after=()):
    count = len(values)
    size = values[0].shape[0]
    return call(
        functools.partial(place_kernel, count),
        [((count * size, 32, 128), BF16)], values, place=place, after=after,
    )[0]


def last_kernel(core, own, other, fine, coarse, whole):
    whole[pl.ds(core[0] * 48, 48)] = own[...]
    whole[pl.ds((1 - core[0]) * 48, 48)] = other[...]
    cells = 96 * 96 * 96
    for r in range(96):
        value = whole[r].astype(F32)[0:27]
        if r < 32:
            fine[:, 128 * r : 128 * r + 128] = value * (1.0 / math.sqrt(cells))
        else:
            at = 128 * (r - 32)
            coarse[:, at : at + 128] = value * (1.0 / math.sqrt(cells // 8))


def core_partner(value):
    return lax.ppermute(value, "gx", [(i, i ^ 1) for i in range(4)])


def z_partner(value, far):
    return lax.ppermute(value, "gy", [(i, i ^ far) for i in range(8)])


def y_turn(value, step):
    pairs = [(i, i // 4 * 4 + (i + step) % 4) for i in range(8)]
    return lax.ppermute(value, "gz", pairs)


def x_turn(value, step):
    pairs = []
    for gx in range(4):
        for gz in range(8):
            x = (gz // 4 * 2 + gx // 2 + step) % 4
            pairs.append((gx * 8 + gz, (x % 2 * 2 + gx % 2) * 8 + x // 2 * 4 + gz % 4))
    return lax.ppermute(value, ("gx", "gz"), pairs)


def body(features, fine_weight, coarse_weight, cotangent):
    gx = lax.axis_index("gx").astype(jnp.int32)
    gz = lax.axis_index("gz").astype(jnp.int32)
    core = (gx % 2).reshape(1)
    y_at = (gz % 4).reshape(1)
    x_at = (gz // 4 * 2 + gx // 2).reshape(1)
    z_at = jnp.zeros((1,), jnp.int32)

    own = jnp.transpose(features, (1, 0, 2))
    zl, zh = call(
        z_faces_kernel, [((6, 40, 128), BF16)] * 2, (own, cotangent),
        [
            pltpu.VMEM((2, 12, 24, 128), BF16), pltpu.VMEM((2, 12, 6, 128), BF16),
            pltpu.VMEM((12, 8, 128), F32), pltpu.SemaphoreType.DMA((4,)),
        ],
        space=HBM,
    )
    zlo = shift(zl, "gz", 1)
    zhi = shift(zh, "gz", -1)
    w_fine, frows = call(
        forward_weights_kernel, [((2304, 128), BF16), ((12, 32, 896), BF16)], (fine_weight, own),
        [pltpu.VMEM((1728, 128), F32)], after=(zl,),
    )
    frows, crows, xl, xh = call(
        x_faces_kernel,
        [((12, 32, 896), BF16), ((6, 16, 1024), BF16), ((24, 1024), BF16), ((24, 1024), BF16)],
        (frows, jnp.transpose(cotangent, (1, 0, 2)), zlo, zhi),
        [
            pltpu.VMEM((2, 12, 8, 896), F32), pltpu.VMEM((6, 16, 1024), F32),
            pltpu.VMEM((24, 1024), F32),
        ],
    )
    xlo = shift(xl, "gx", 1)
    xhi = shift(xh, "gx", -1)
    frows, crows, yl, yh = call(
        y_faces_kernel,
        [((12, 32, 896), BF16), ((6, 16, 1024), BF16), ((48, 1024), BF16), ((48, 1024), BF16)],
        (frows, crows, xlo, xhi),
        [
            pltpu.VMEM((12, 32, 896), F32), pltpu.VMEM((6, 16, 1024), F32),
            pltpu.VMEM((24, 1024), F32), pltpu.VMEM((24, 1024), F32),
        ],
    )
    ylo = shift(yl, "gy", 1)
    yhi = shift(yh, "gy", -1)
    shifted, act_in, edges, inner = call(
        interior_kernel,
        [((3, 384, 896), BF16), ((320, 768), F32), ((64, 768), BF16), ((4, 16, 384), BF16)],
        (frows, w_fine),
        flops=CONV,
    )
    act_out, pooled, pzl, pzh = call(
        border_kernel,
        [
            ((64, 768), F32), ((6, 16, 384), BF16),
            ((6, 16, 128), BF16), ((6, 16, 128), BF16),
        ],
        (shifted, ylo, yhi, w_fine, edges, inner),
        [pltpu.VMEM((3, 64, 896), BF16)],
        flops=CONV // 6,
    )
    pzlo = shift(pzl, "gz", 1)
    pzhi = shift(pzh, "gz", -1)
    w_coarse, w_coarse_back, done = call(
        coarse_weights_kernel,
        [((2304, 256), BF16), ((4608, 256), BF16), ((8, 128), F32)],
        (coarse_weight,), [pltpu.VMEM((1792, 128), F32)], after=(pzl,),
    )
    prows, pxl, pxh = call(
        pooled_x_kernel,
        [((6, 16, 640), BF16), ((16, 640), BF16), ((16, 640), BF16)],
        (pooled, pzlo, pzhi),
        [pltpu.VMEM((6, 16, 640), F32), pltpu.VMEM((16, 640), F32)],
        after=(done,),
    )
    pxlo = shift(pxl, "gx", 1)
    pxhi = shift(pxh, "gx", -1)
    slope, done = call(
        slope_kernel, [((384, 768), BF16), ((8, 128), F32)], (act_in, act_out), after=(pxl,)
    )
    prows, pyl, pyh = call(
        pooled_y_kernel,
        [((6, 16, 640), BF16), ((2, 16, 640), BF16), ((2, 16, 640), BF16)],
        (prows, pxlo, pxhi),
        [pltpu.VMEM((6, 16, 640), F32), pltpu.VMEM((16, 640), F32), pltpu.VMEM((16, 640), F32)],
        after=(done,),
    )
    pylo = shift(pyl, "gy", 1)
    pyhi = shift(pyh, "gy", -1)
    act, azl, azh, fine_left, coarse_left, pshift = call(
        backward_kernel,
        [
            ((12, 32, 768), BF16), ((6, 24, 128), BF16), ((6, 24, 128), BF16),
            ((128, 2304), BF16), ((256, 512), BF16), ((3, 160, 640), BF16),
        ],
        (prows, pylo, pyhi, crows, ylo, yhi, slope, w_coarse, w_coarse_back),
        [pltpu.VMEM((3, 128, 1024), BF16)],
        flops=CONV,
    )
    azlo = shift(azl, "gz", 1)
    azhi = shift(azh, "gz", -1)
    (early,) = call(
        early_grads_kernel, [((96, 32, 128), BF16)],
        (coarse_left, pshift, fine_left, frows, ylo, yhi),
        [
            pltpu.VMEM((256, 128), F32), pltpu.VMEM((64, 128), F32),
            pltpu.VMEM((3072, 128), F32), pltpu.VMEM((256, 256), F32),
            pltpu.VMEM((3, 448, 896), BF16),
        ],
        flops=CONV,
    )
    keep, send = call(
        late_grads_kernel,
        [((48, 32, 128), BF16), ((48, 32, 128), BF16)],
        (fine_left, frows, ylo, yhi, early),
        [
            pltpu.VMEM((256, 128), F32), pltpu.VMEM((64, 128), F32),
            pltpu.VMEM((1024, 128), F32), pltpu.VMEM((96, 32, 128), BF16),
            pltpu.VMEM((3, 448, 896), BF16),
        ],
        flops=CONV // 2, place=core, after=(azlo, azhi),
    )

    parts = combine((keep, core_partner(send)), y_at, 4)
    got = tuple(y_turn(parts[k], k) for k in (1, 2, 3))
    arows, axl, axh = call(
        act_x_faces_kernel,
        [((12, 32, 896), BF16), ((16, 896), BF16), ((16, 896), BF16)],
        (act, azlo, azhi),
        [pltpu.VMEM((12, 32, 896), F32), pltpu.VMEM((16, 896), F32)],
        after=(parts[0],),
    )
    axlo = shift(axl, "gx", 1)
    axhi = shift(axh, "gx", -1)
    parts = combine((parts[0],) + got, x_at, 4, after=(axlo, axhi))
    got = tuple(x_turn(parts[k], k) for k in (1, 2, 3))
    arows, ayl, ayh = call(
        act_y_faces_kernel,
        [((12, 32, 896), BF16), ((32, 896), BF16), ((32, 896), BF16)],
        (arows, axlo, axhi),
        [pltpu.VMEM((12, 32, 896), F32), pltpu.VMEM((16, 896), F32), pltpu.VMEM((16, 896), F32)],
        after=(parts[0],),
    )
    aylo = shift(ayl, "gy", 1)
    ayhi = shift(ayh, "gy", -1)
    (part,) = combine((parts[0],) + got, z_at, 1, after=(aylo, ayhi))
    near, next_near, far = (z_partner(part, k) for k in (1, 2, 3))
    w_fine_back, done = call(
        backward_weights_kernel, [((2304, 128), BF16), ((8, 128), F32)],
        (fine_weight,), [pltpu.VMEM((1792, 128), F32)], after=(part,),
    )
    (part,) = combine((part, near, next_near, far), z_at, 1, after=(done,))
    (part,) = combine((part, z_partner(part, 7)), z_at, 1)
    part = placed((part,) + tuple(x_turn(part, k) for k in (1, 2, 3)), x_at)
    got = tuple(y_turn(part, k) for k in (1, 2, 3))
    grad_features, done = call(
        features_kernel,
        [((12, 24, 768), BF16), ((8, 128), F32)],
        (arows, aylo, ayhi, w_fine_back),
        [pltpu.VMEM((3, 448, 896), BF16)],
        flops=CONV, after=(part,),
    )
    part = placed((part,) + got, y_at, after=(done,))
    fine, coarse = call(
        last_kernel,
        [((27, 4096), F32), ((27, 8192), F32)],
        (part, core_partner(part)),
        [pltpu.VMEM((96, 32, 128), BF16)],
        place=core,
    )
    return jnp.transpose(grad_features, (1, 0, 2)), fine, coarse


def solution(mesh):
    in_specs = (P("gx", "gy", "gz"), P(), P(), P("gx", "gy", "gz"))
    out_specs = (P("gx", "gy", "gz"), P(), P())
    return jax.shard_map(body, mesh=mesh, in_specs=in_specs, out_specs=out_specs, check_vma=False)
```

```python
import functools
import math

import jax
import jax.numpy as jnp
from jax import lax
from jax.experimental import pallas as pl
from jax.experimental.pallas import tpu as pltpu
from jax.sharding import PartitionSpec as P

F32 = jnp.float32
BF16 = jnp.bfloat16
VMEM = pl.BlockSpec(memory_space=pltpu.VMEM)
SMEM = pl.BlockSpec(memory_space=pltpu.SMEM)
ANY = pl.BlockSpec(memory_space=pl.ANY)
HBM = pl.BlockSpec(memory_space=pltpu.HBM)
CONV = 2 * 384 * 6 * 2304 * 256


def shift(value, axis, step):
    count = lax.axis_size(axis)
    return lax.ppermute(value, axis, [(i, (i + step) % count) for i in range(count)])


def call(kernel, outs, operands, scratch=(), flops=0, place=None, after=(), space=VMEM):
    moved = sum(math.prod(v.shape) * v.dtype.itemsize for v in operands)
    moved += sum(math.prod(s) * jnp.dtype(d).itemsize for s, d in outs)
    extra = () if place is None else (place,)
    first, last = len(extra) + len(operands), len(extra) + len(operands) + len(after)

    def run(*refs):
        kernel(*refs[:first], *refs[last:])

    return pl.pallas_call(
        run,
        out_shape=[jax.ShapeDtypeStruct(s, d) for s, d in outs],
        in_specs=[SMEM] * len(extra) + [space] * len(operands) + [ANY] * len(after),
        out_specs=[VMEM] * len(outs),
        scratch_shapes=list(scratch),
        compiler_params=pltpu.CompilerParams(vmem_limit_bytes=16 * 1024 * 1024),
        cost_estimate=pl.CostEstimate(flops=flops // 8, bytes_accessed=moved // 8, transcendentals=0),
    )(*extra, *operands, *after)


def low_half(shape):
    return lax.broadcasted_iota(jnp.int32, shape, len(shape) - 1) < 64


def swap(value):
    return pltpu.roll(value, 64, value.ndim - 1)


def rolled_rows(value, step):
    return pltpu.roll(value, step % value.shape[-2], value.ndim - 2)


def pack_faces(low, high):
    mask = low_half((6, 24, 128))
    to_high = jnp.where(mask, swap(high[:6]), high[6:])
    to_low = jnp.where(mask, low[:6], swap(low[6:]))
    return to_high, to_low


def with_faces(own, lo, hi):
    mask = low_half((6, 24, 128))
    first = jnp.where(mask, hi, swap(lo))
    second = jnp.where(mask, swap(hi), lo)
    full = jnp.concatenate([own, jnp.concatenate([first, second], axis=0)], axis=2)
    return pltpu.roll(full, 64, 2)


def flat_fine(fine, flat):
    mask = low_half((27, 128))
    for k in range(32):
        value = fine[:, 128 * k : 128 * k + 128].astype(F32)
        turned = swap(value)
        flat[pl.ds(2 * k, 27, stride=64), :] = jnp.where(mask, value, turned)
        flat[pl.ds(2 * k + 1, 27, stride=64), :] = jnp.where(mask, turned, value)


def forward_weights_kernel(fine, own, wf, rows_out, flat):
    wide = jnp.concatenate([own[...].astype(F32), jnp.zeros((12, 24, 128), F32)], axis=2)
    rows_out[:, 0:24, :] = pltpu.roll(wide, 64, 2).astype(BF16)
    rows_out[:, 24:32, :] = jnp.zeros((12, 8, 896), BF16)
    flat_fine(fine, flat)
    mask = low_half((64, 128))
    none = jnp.zeros((64, 128), F32)
    for ab in range(9):
        for j in range(4):
            row = (4 * ab + j) * 64
            at = (3 * ab + j) * 64
            left = flat[at : at + 64, :] if j < 3 else none
            right = flat[at - 64 : at, :] if j > 0 else none
            wf[row : row + 64, :] = jnp.where(mask, left, right).astype(BF16)


def coarse_weights_kernel(coarse, wc, wcb, done, flat):
    done[...] = jnp.zeros(done.shape, F32)
    for c in range(64):
        flat[pl.ds(c, 27, stride=64), :] = coarse[:, 128 * c : 128 * c + 128].astype(F32)
    flat[1728:1792, :] = jnp.zeros((64, 128), F32)
    wide = low_half((128, 128))
    none = jnp.zeros((64, 128), F32)
    zero = jnp.zeros((128, 128), F32)
    turned = []
    for m in range(14):
        value = flat[128 * m : 128 * m + 128, :].T
        turned += [jnp.where(wide, value, swap(value)), jnp.where(wide, swap(value), value)]
    for ab in range(9):
        for j in range(4):
            row = (4 * ab + j) * 64
            at = (3 * ab + j) * 64
            left = flat[at : at + 64, :] if j < 3 else none
            right = flat[at - 64 : at, :] if j > 0 else none
            wc[row : row + 64, 0:128] = left.astype(BF16)
            wc[row : row + 64, 128:256] = right.astype(BF16)
            slot = 26 - 3 * ab - j
            row = 2 * row
            left = turned[slot] if j < 3 else zero
            right = turned[slot + 1] if j > 0 else zero
            wcb[row : row + 128, 0:128] = left.astype(BF16)
            wcb[row : row + 128, 128:256] = right.astype(BF16)


def backward_weights_kernel(fine, wfb, done, flat):
    done[...] = jnp.zeros(done.shape, F32)
    flat_fine(fine, flat)
    flat[1728:1792, :] = jnp.zeros((64, 128), F32)
    mask = low_half((64, 128))
    none = jnp.zeros((64, 128), F32)
    turned = []
    for m in range(14):
        value = flat[128 * m : 128 * m + 128, :].T[0:64]
        turned += [jnp.where(mask, value, swap(value)), jnp.where(mask, swap(value), value)]
    for ab in range(9):
        for j in range(4):
            row = (4 * ab + j) * 64
            slot = 26 - 3 * ab - j
            left = turned[slot] if j < 3 else none
            right = turned[slot + 1] if j > 0 else none
            wfb[row : row + 64, :] = jnp.where(mask, left, right).astype(BF16)


def z_faces_kernel(own, cot, zl, zh, faces, cfaces, edge, sems):
    copies = []
    for k, lane in enumerate((0, 640)):
        lanes = pl.ds(lane, 128)
        copies.append(pltpu.make_async_copy(own.at[:, :, lanes], faces.at[k], sems.at[2 * k]))
        copies.append(pltpu.make_async_copy(cot.at[:, :, lanes], cfaces.at[k], sems.at[2 * k + 1]))
    for copy in copies:
        copy.start()
    for copy in copies:
        copy.wait()
    to_high, to_low = pack_faces(faces[0].astype(F32), faces[1].astype(F32))
    for out, face, k in ((zl, to_high, 1), (zh, to_low, 0)):
        edge[:, 0:6, :] = cfaces[k].astype(F32)
        turned = [edge[:, y : y + 1, :].reshape(12, 128)[None] for y in range(6)]
        turned = jnp.concatenate(turned, axis=0)
        pad = jnp.zeros((6, 4, 128), F32)
        out[...] = jnp.concatenate([face, turned, pad], axis=1).astype(BF16)


def edge_lanes(lo, hi):
    low = jnp.concatenate([lo, swap(lo)], axis=0)
    high = jnp.concatenate([swap(hi), hi], axis=0)
    return low, high


def x_faces_kernel(own, cot, zlo, zhi, rows_out, cot_out, xl, xh, ends, crows, message):
    lo = zlo[...].astype(F32)
    hi = zhi[...].astype(F32)
    low, high = edge_lanes(lo[:, 0:24], hi[:, 0:24])
    mask = low_half((12, 24, 128))
    rows_out[...] = own[...]
    for at, part in ((0, jnp.where(mask, low, 0.0)), (768, jnp.where(mask, 0.0, high))):
        lanes = slice(at, at + 128)
        rows_out[:, 0:24, lanes] = (own[:, 0:24, lanes].astype(F32) + part).astype(BF16)
    crows[:, 8:16, :] = jnp.zeros((6, 8, 1024), F32)
    crows[:, 0:12, 0:128] = lo[:, 24:36]
    crows[:, 0:12, 128:896] = cot[...].astype(F32)
    crows[:, 0:12, 896:1024] = hi[:, 24:36]
    cot_out[...] = crows[...].astype(BF16)
    ends[0] = rows_out[:, 0:8, :].astype(F32)
    ends[1] = rows_out[:, 16:24, :].astype(F32)
    message[...] = jnp.zeros(message.shape, F32)
    for out, k, x, cx in ((xl, 1, 7, 11), (xh, 0, 0, 0)):
        for y in range(12):
            message[y : y + 1, 0:896] = ends[k, y, x : x + 1, :]
        for y in range(6):
            message[12 + y : 13 + y, :] = crows[y, cx : cx + 1, :]
        out[...] = message[...].astype(BF16)


def y_faces_kernel(rows_in, cot_in, xlo, xhi, rows_out, cot_out, yl, yh, rows, crows, lo, hi):
    lo[...] = xlo[...].astype(F32)
    hi[...] = xhi[...].astype(F32)
    rows[...] = rows_in[...].astype(F32)
    crows[...] = cot_in[...].astype(F32)
    for y in range(12):
        rows[y, 24:25, :] = hi[y : y + 1, 0:896]
        rows[y, 31:32, :] = lo[y : y + 1, 0:896]
    for y in range(6):
        crows[y, 12:13, :] = hi[12 + y : 13 + y, :]
        crows[y, 15:16, :] = lo[12 + y : 13 + y, :]
    rows_out[...] = rows[...].astype(BF16)
    cot_out[...] = crows[...].astype(BF16)
    for out, y, cy in ((yl, 11, 5), (yh, 0, 0)):
        out[0:32, 0:896] = rows[y].astype(BF16)
        out[0:32, 896:1024] = jnp.zeros((32, 128), BF16)
        out[32:48, :] = crows[cy].astype(BF16)


def act_x_faces_kernel(own, zlo, zhi, rows_out, xl, xh, rows, message):
    rows[:, 0:24, :] = with_faces(
        own[...].astype(F32)[:, 0:24], zlo[...].astype(F32), zhi[...].astype(F32)
    )
    rows[:, 24:32, :] = jnp.zeros((12, 8, 896), F32)
    rows_out[...] = rows[...].astype(BF16)
    message[...] = jnp.zeros(message.shape, F32)
    for out, x in ((xl, 23), (xh, 0)):
        for y in range(12):
            message[y : y + 1, :] = rows[y, x : x + 1, :]
        out[...] = message[...].astype(BF16)


def act_y_faces_kernel(rows_in, xlo, xhi, rows_out, yl, yh, rows, lo, hi):
    lo[...] = xlo[...].astype(F32)
    hi[...] = xhi[...].astype(F32)
    rows[...] = rows_in[...].astype(F32)
    for y in range(12):
        rows[y, 24:25, :] = hi[y : y + 1, :]
        rows[y, 31:32, :] = lo[y : y + 1, :]
    value = rows[...].astype(BF16)
    rows_out[...] = value
    yl[...] = value[11]
    yh[...] = value[0]


def sigmoid(value):
    return 0.5 + 0.5 * jnp.tanh(0.5 * value)


def silu(act):
    return (act * sigmoid(act)).astype(BF16)


def silu_slope(act):
    sigma = sigmoid(act)
    return sigma * (1.0 + act * (1.0 - sigma))


def slope_kernel(inner, outer, slope, done):
    slope[0:32, :] = silu_slope(outer[0:32, :]).astype(BF16)
    slope[32:352, :] = silu_slope(inner[...]).astype(BF16)
    slope[352:384, :] = silu_slope(outer[32:64, :]).astype(BF16)
    done[...] = jnp.zeros(done.shape, F32)


def pool_matrix(shape, rule):
    r = lax.broadcasted_iota(jnp.int32, shape, 0)
    q = lax.broadcasted_iota(jnp.int32, shape, 1)
    return jnp.where(rule(r, q), 0.125, 0.0).astype(BF16)


def fold_pairs(part):
    return part + swap(part)


def interior_kernel(rows, weight, shifted, kept, edges, pooled):
    full = rows[...].astype(F32)
    for a in range(3):
        shifted[a] = rolled_rows(full, 1 - a).astype(BF16).reshape(384, 896)
    pool = pool_matrix(
        (64, 320),
        lambda r, q: ((((q >> 5) + 1) >> 1) == (r >> 4) + 1) & (((q & 31) >> 1) == (r & 15)),
    )
    mask = low_half((64, 128))
    for p in range(6):
        lanes = slice(128 * p, 128 * p + 256)
        left = jnp.concatenate(
            [shifted[a, 32 * b : 32 * b + 320, lanes] for a in range(3) for b in range(3)], axis=1
        )
        kept[:, 128 * p : 128 * p + 128] = jnp.dot(
            left, weight[...], preferred_element_type=F32
        )
    hidden = silu(kept[...])
    edges[0:32, :] = hidden[0:32]
    edges[32:64, :] = hidden[288:320]
    sums = jnp.dot(pool, hidden, preferred_element_type=F32)
    pieces = [fold_pairs(sums[:, 128 * p : 128 * p + 128]) for p in range(6)]
    for j in range(3):
        both = jnp.where(mask, pieces[2 * j], pieces[2 * j + 1])
        pooled[:, :, 128 * j : 128 * j + 128] = both.astype(BF16).reshape(4, 16, 128)


def border_kernel(shifted, ylo, yhi, weight, edges, inner, kept, pooled, zl, zh, outer):
    both = jnp.concatenate(
        [ylo[0:32, 0:896][None], yhi[0:32, 0:896][None]], axis=0
    ).astype(F32)
    for a in range(3):
        outer[a] = rolled_rows(both, 1 - a).astype(BF16).reshape(64, 896)
    blocks = []
    for p in range(6):
        lanes = slice(128 * p, 128 * p + 256)
        first = []
        last = []
        for a in range(3):
            first += [outer[a, 0:32, lanes], shifted[a, 0:32, lanes], shifted[a, 32:64, lanes]]
            last += [
                shifted[a, 320:352, lanes], shifted[a, 352:384, lanes], outer[a, 32:64, lanes]
            ]
        blocks.append(jnp.concatenate(first, axis=1))
        blocks.append(jnp.concatenate(last, axis=1))
    act = jnp.dot(jnp.concatenate(blocks, axis=0), weight[...], preferred_element_type=F32)
    hidden = silu(act)
    pool = pool_matrix(
        (32, 128),
        lambda r, q: (((q >> 5) & 1) == (r >> 4)) & (((q & 31) >> 1) == (r & 15)),
    )
    mask = low_half((32, 128))
    pieces = []
    for p in range(6):
        own = slice(128 * p, 128 * p + 128)
        kept[:, own] = act[64 * p : 64 * p + 64]
        column = jnp.concatenate([hidden[64 * p : 64 * p + 64], edges[:, own]], axis=0)
        pieces.append(fold_pairs(jnp.dot(pool, column, preferred_element_type=F32)))
    for j in range(3):
        own = slice(128 * j, 128 * j + 128)
        both = jnp.where(mask, pieces[2 * j], pieces[2 * j + 1]).astype(BF16)
        pooled[0:1, :, own] = both[0:16][None]
        pooled[5:6, :, own] = both[16:32][None]
    pooled[1:5] = inner[...]
    zl[...] = pooled[:, :, 256:384]
    zh[...] = pooled[:, :, 0:128]


def pooled_x_kernel(own, zlo, zhi, rows_out, xl, xh, rows, message):
    rows[...] = jnp.concatenate([zlo[...], own[...], zhi[...]], axis=2).astype(F32)
    rows_out[...] = rows[...].astype(BF16)
    message[...] = jnp.zeros(message.shape, F32)
    for out, x in ((xl, 10), (xh, 0)):
        for y in range(6):
            message[2 * y : 2 * y + 2, :] = rows[y, x : x + 2, :]
        out[...] = message[...].astype(BF16)


def pooled_y_kernel(rows_in, xlo, xhi, rows_out, yl, yh, rows, lo, hi):
    lo[...] = xlo[...].astype(F32)
    hi[...] = xhi[...].astype(F32)
    rows[...] = rows_in[...].astype(F32)
    for y in range(6):
        rows[y, 12:14, :] = hi[2 * y : 2 * y + 2, :]
        rows[y, 14:16, :] = lo[2 * y : 2 * y + 2, :]
    value = rows[...].astype(BF16)
    rows_out[...] = value
    yl[...] = value[4:6]
    yh[...] = value[0:2]


def backward_kernel(
    prow, pylo, pyhi, crow, ylo, yhi, slope, wc, wb,
    act_out, zl, zh, fine_left, coarse_left, pshift, gshift,
):
    full = jnp.concatenate([pylo[...], prow[...], pyhi[...]], axis=0).astype(F32)
    for a in range(3):
        pshift[a] = rolled_rows(full, 1 - a).astype(BF16).reshape(160, 640)
    blocks = []
    for p in range(4):
        lanes = slice(128 * p, 128 * p + 256)
        blocks.append(
            jnp.concatenate(
                [pshift[a, 16 * b : 16 * b + 128, lanes] for a in range(3) for b in range(3)], axis=1
            )
        )
    pre = jnp.dot(jnp.concatenate(blocks, axis=0), wc[...], preferred_element_type=F32)
    tilt = silu_slope(pre)
    cot = jnp.concatenate([ylo[32:48][None], crow[...], yhi[32:48][None]], axis=0).astype(F32)
    row = lax.broadcasted_iota(jnp.int32, (128, 256), 0)
    lane = lax.broadcasted_iota(jnp.int32, (128, 256), 1)
    own_rows = (row >= 16) & (row < 112) & ((row & 15) < 12)
    parts = []
    for p in range(4):
        grad = cot[:, :, 256 * p : 256 * p + 256].reshape(128, 256) * tilt[128 * p : 128 * p + 128]
        grad = grad.astype(BF16).astype(F32)
        parts.append(grad)
        valid = own_rows
        if p == 0:
            valid = valid & (lane >= 128)
        if p == 3:
            valid = valid & (lane < 128)
        coarse_left[:, 128 * p : 128 * p + 128] = jnp.where(valid, grad, 0.0).T.astype(BF16)
    both = jnp.concatenate(parts, axis=1).reshape(8, 16, 1024)
    for a in range(3):
        gshift[a] = rolled_rows(both, 1 - a).astype(BF16).reshape(128, 1024)
    blocks = []
    for p in range(3):
        lanes = slice(256 * p, 256 * p + 512)
        blocks.append(
            jnp.concatenate(
                [gshift[a, 16 * b : 16 * b + 96, lanes] for a in range(3) for b in range(3)], axis=1
            )
        )
    small = jnp.dot(jnp.concatenate(blocks, axis=0), wb[...], preferred_element_type=F32)
    small = small.astype(BF16)
    q = lax.broadcasted_iota(jnp.int32, (384, 96), 0)
    r = lax.broadcasted_iota(jnp.int32, (384, 96), 1)
    inside = ((q >> 6) == (r >> 4)) & (((q & 31) >> 1) == (r & 15)) & ((q & 31) < 24)
    spread = jnp.where(inside, 1.0, 0.0).astype(BF16)
    for p in range(3):
        lanes = slice(256 * p, 256 * p + 256)
        up = jnp.dot(spread, small[96 * p : 96 * p + 96], preferred_element_type=F32)
        part = (up * 0.125 * slope[:, lanes].astype(F32)).astype(BF16)
        act_out[:, :, lanes] = part.reshape(12, 32, 256)
        wide = part.astype(F32)
        fine_left[:, 768 * p : 768 * p + 384] = wide[:, 0:128].T.astype(BF16)
        fine_left[:, 768 * p + 384 : 768 * p + 768] = wide[:, 128:256].T.astype(BF16)
        if p == 0:
            low = wide[:, 0:128].reshape(12, 32, 128)[:, 0:24]
        if p == 2:
            high = wide[:, 128:256].reshape(12, 32, 128)[:, 0:24]
    to_high, to_low = pack_faces(low, high)
    zl[...] = to_high.astype(BF16)
    zh[...] = to_low.astype(BF16)


def all_rows(rows, ylo, yhi, shifted, used):
    lo = ylo[0:32, 0:896][None]
    hi = yhi[0:32, 0:896][None]
    full = jnp.concatenate([lo, rows[...], hi], axis=0).astype(F32)
    for a in used:
        shifted[a] = rolled_rows(full, 1 - a).astype(BF16).reshape(448, 896)


def fine_grads(left, shifted, turned, pairs, sums, offsets):
    mask = low_half((32, 128))
    for a, b in offsets:
        right = jnp.concatenate(
            [shifted[a, 32 * b : 32 * b + 384, 128 * p : 128 * p + 256] for p in range(6)], axis=0
        )
        turned[...] = jnp.dot(left[...], right, preferred_element_type=F32).T
        for e in range(3):
            near = turned[64 * e : 64 * e + 64]
            pairs[...] = near + swap(turned[64 * e + 64 : 64 * e + 128])
            even = pairs[pl.ds(0, 32, stride=2), :]
            odd = pairs[pl.ds(1, 32, stride=2), :]
            slot = 9 * a + 3 * b + e
            sums[pl.ds(slot, 32, stride=32), :] = jnp.where(mask, even, swap(odd))


EARLY = [(0, 0), (0, 1), (0, 2), (1, 0), (1, 1), (1, 2), (2, 0), (2, 1)]
LATE = [(2, 2)]


def early_grads_kernel(
    coarse_left, pshift, left, rows, ylo, yhi, out, turned, pairs, sums, cturned, shifted
):
    all_rows(rows, ylo, yhi, shifted, (0, 1, 2))
    sums[...] = jnp.zeros(sums.shape, F32)
    for a in range(3):
        for b in range(3):
            right = jnp.concatenate(
                [pshift[a, 16 * b : 16 * b + 128, 128 * p : 128 * p + 256] for p in range(4)], axis=0
            )
            cturned[...] = jnp.dot(coarse_left[...], right, preferred_element_type=F32).T
            for e in range(3):
                near = cturned[64 * e : 64 * e + 64, 0:128]
                far = cturned[64 * e + 64 : 64 * e + 128, 128:256]
                sums[pl.ds(1024 + 9 * a + 3 * b + e, 64, stride=32), :] = near + far
    fine_grads(left, shifted, turned, pairs, sums, EARLY)
    out[...] = sums[...].astype(BF16).reshape(96, 32, 128)


def late_grads_kernel(
    core, left, rows, ylo, yhi, early, keep, send, turned, pairs, sums, whole, shifted
):
    all_rows(rows, ylo, yhi, shifted, (2,))
    sums[...] = early[0:32].astype(F32).reshape(1024, 128)
    fine_grads(left, shifted, turned, pairs, sums, LATE)
    whole[0:32] = sums[...].astype(BF16).reshape(32, 32, 128)
    whole[32:96] = early[32:96]
    keep[...] = whole[pl.ds(core[0] * 48, 48)]
    send[...] = whole[pl.ds((1 - core[0]) * 48, 48)]


def features_kernel(rows, ylo, yhi, weight, out, done, shifted):
    done[...] = jnp.zeros(done.shape, F32)
    full = jnp.concatenate([ylo[...][None], rows[...], yhi[...][None]], axis=0).astype(F32)
    for a in range(3):
        shifted[a] = rolled_rows(full, 1 - a).astype(BF16).reshape(448, 896)
    for p in range(6):
        lanes = slice(128 * p, 128 * p + 256)
        left = jnp.concatenate(
            [shifted[a, 32 * b : 32 * b + 384, lanes] for a in range(3) for b in range(3)], axis=1
        )
        grad = jnp.dot(left, weight[...], preferred_element_type=F32)
        grad = grad.reshape(12, 32, 128)[:, 0:24, :]
        out[:, :, 128 * p : 128 * p + 128] = grad.astype(BF16)


def combine_kernel(count, parts, *refs):
    at, ins, outs = refs[0], refs[1 : 1 + parts], refs[1 + parts :]
    size = outs[0].shape[0]
    for k in range(count):
        start = lax.rem(at[0] + k, count) * size
        terms = [ref[pl.ds(start, size)].astype(F32) for ref in ins]
        while len(terms) > 1:
            terms = [sum(terms[i : i + 2][1:], terms[i]) for i in range(0, len(terms), 2)]
        outs[k][...] = terms[0].astype(outs[k].dtype)


def combine(values, place, count, after=()):
    size = values[0].shape[0] // count
    return call(
        functools.partial(combine_kernel, count, len(values)),
        [((size, 32, 128), BF16)] * count, values, place=place, after=after,
    )


def place_kernel(count, *refs):
    at, ins, out = refs[0], refs[1 : 1 + count], refs[-1]
    size = ins[0].shape[0]
    for k in range(count):
        out[pl.ds(lax.rem(at[0] + count - k, count) * size, size)] = ins[k][...]


def placed(values, place, after=()):
    count = len(values)
    size = values[0].shape[0]
    return call(
        functools.partial(place_kernel, count),
        [((count * size, 32, 128), BF16)], values, place=place, after=after,
    )[0]


def last_kernel(core, own, other, fine, coarse, whole):
    whole[pl.ds(core[0] * 48, 48)] = own[...]
    whole[pl.ds((1 - core[0]) * 48, 48)] = other[...]
    for r in range(96):
        value = whole[r].astype(F32)[0:27]
        if r < 32:
            fine[:, 128 * r : 128 * r + 128] = value
        else:
            at = 128 * (r - 32)
            coarse[:, at : at + 128] = value


def core_partner(value):
    return lax.ppermute(value, "gx", [(i, i ^ 1) for i in range(4)])


def z_partner(value, far):
    return lax.ppermute(value, "gy", [(i, i ^ far) for i in range(8)])


def y_turn(value, step):
    pairs = [(i, i // 4 * 4 + (i + step) % 4) for i in range(8)]
    return lax.ppermute(value, "gz", pairs)


def x_turn(value, step):
    pairs = []
    for gx in range(4):
        for gz in range(8):
            x = (gz // 4 * 2 + gx // 2 + step) % 4
            pairs.append((gx * 8 + gz, (x % 2 * 2 + gx % 2) * 8 + x // 2 * 4 + gz % 4))
    return lax.ppermute(value, ("gx", "gz"), pairs)


def body(features, fine_weight, coarse_weight, cotangent):
    gx = lax.axis_index("gx").astype(jnp.int32)
    gz = lax.axis_index("gz").astype(jnp.int32)
    core = (gx % 2).reshape(1)
    y_at = (gz % 4).reshape(1)
    x_at = (gz // 4 * 2 + gx // 2).reshape(1)
    z_at = jnp.zeros((1,), jnp.int32)

    own = jnp.transpose(features, (1, 0, 2))
    zl, zh = call(
        z_faces_kernel, [((6, 40, 128), BF16)] * 2, (own, cotangent),
        [
            pltpu.VMEM((2, 12, 24, 128), BF16), pltpu.VMEM((2, 12, 6, 128), BF16),
            pltpu.VMEM((12, 8, 128), F32), pltpu.SemaphoreType.DMA((4,)),
        ],
        space=HBM,
    )
    zlo = shift(zl, "gz", 1)
    zhi = shift(zh, "gz", -1)
    w_fine, frows = call(
        forward_weights_kernel, [((2304, 128), BF16), ((12, 32, 896), BF16)], (fine_weight, own),
        [pltpu.VMEM((1728, 128), F32)], after=(zl,),
    )
    frows, crows, xl, xh = call(
        x_faces_kernel,
        [((12, 32, 896), BF16), ((6, 16, 1024), BF16), ((24, 1024), BF16), ((24, 1024), BF16)],
        (frows, jnp.transpose(cotangent, (1, 0, 2)), zlo, zhi),
        [
            pltpu.VMEM((2, 12, 8, 896), F32), pltpu.VMEM((6, 16, 1024), F32),
            pltpu.VMEM((24, 1024), F32),
        ],
    )
    xlo = shift(xl, "gx", 1)
    xhi = shift(xh, "gx", -1)
    frows, crows, yl, yh = call(
        y_faces_kernel,
        [((12, 32, 896), BF16), ((6, 16, 1024), BF16), ((48, 1024), BF16), ((48, 1024), BF16)],
        (frows, crows, xlo, xhi),
        [
            pltpu.VMEM((12, 32, 896), F32), pltpu.VMEM((6, 16, 1024), F32),
            pltpu.VMEM((24, 1024), F32), pltpu.VMEM((24, 1024), F32),
        ],
    )
    ylo = shift(yl, "gy", 1)
    yhi = shift(yh, "gy", -1)
    shifted, act_in, edges, inner = call(
        interior_kernel,
        [((3, 384, 896), BF16), ((320, 768), F32), ((64, 768), BF16), ((4, 16, 384), BF16)],
        (frows, w_fine),
        flops=CONV,
    )
    act_out, pooled, pzl, pzh = call(
        border_kernel,
        [
            ((64, 768), F32), ((6, 16, 384), BF16),
            ((6, 16, 128), BF16), ((6, 16, 128), BF16),
        ],
        (shifted, ylo, yhi, w_fine, edges, inner),
        [pltpu.VMEM((3, 64, 896), BF16)],
        flops=CONV // 6,
    )
    pzlo = shift(pzl, "gz", 1)
    pzhi = shift(pzh, "gz", -1)
    w_coarse, w_coarse_back, done = call(
        coarse_weights_kernel,
        [((2304, 256), BF16), ((4608, 256), BF16), ((8, 128), F32)],
        (coarse_weight,), [pltpu.VMEM((1792, 128), F32)], after=(pzl,),
    )
    prows, pxl, pxh = call(
        pooled_x_kernel,
        [((6, 16, 640), BF16), ((16, 640), BF16), ((16, 640), BF16)],
        (pooled, pzlo, pzhi),
        [pltpu.VMEM((6, 16, 640), F32), pltpu.VMEM((16, 640), F32)],
        after=(done,),
    )
    pxlo = shift(pxl, "gx", 1)
    pxhi = shift(pxh, "gx", -1)
    slope, done = call(
        slope_kernel, [((384, 768), BF16), ((8, 128), F32)], (act_in, act_out), after=(pxl,)
    )
    prows, pyl, pyh = call(
        pooled_y_kernel,
        [((6, 16, 640), BF16), ((2, 16, 640), BF16), ((2, 16, 640), BF16)],
        (prows, pxlo, pxhi),
        [pltpu.VMEM((6, 16, 640), F32), pltpu.VMEM((16, 640), F32), pltpu.VMEM((16, 640), F32)],
        after=(done,),
    )
    pylo = shift(pyl, "gy", 1)
    pyhi = shift(pyh, "gy", -1)
    act, azl, azh, fine_left, coarse_left, pshift = call(
        backward_kernel,
        [
            ((12, 32, 768), BF16), ((6, 24, 128), BF16), ((6, 24, 128), BF16),
            ((128, 2304), BF16), ((256, 512), BF16), ((3, 160, 640), BF16),
        ],
        (prows, pylo, pyhi, crows, ylo, yhi, slope, w_coarse, w_coarse_back),
        [pltpu.VMEM((3, 128, 1024), BF16)],
        flops=CONV,
    )
    azlo = shift(azl, "gz", 1)
    azhi = shift(azh, "gz", -1)
    (early,) = call(
        early_grads_kernel, [((96, 32, 128), BF16)],
        (coarse_left, pshift, fine_left, frows, ylo, yhi),
        [
            pltpu.VMEM((256, 128), F32), pltpu.VMEM((64, 128), F32),
            pltpu.VMEM((3072, 128), F32), pltpu.VMEM((256, 256), F32),
            pltpu.VMEM((3, 448, 896), BF16),
        ],
        flops=CONV,
    )
    keep, send = call(
        late_grads_kernel,
        [((48, 32, 128), BF16), ((48, 32, 128), BF16)],
        (fine_left, frows, ylo, yhi, early),
        [
            pltpu.VMEM((256, 128), F32), pltpu.VMEM((64, 128), F32),
            pltpu.VMEM((1024, 128), F32), pltpu.VMEM((96, 32, 128), BF16),
            pltpu.VMEM((3, 448, 896), BF16),
        ],
        flops=CONV // 2, place=core, after=(azlo, azhi),
    )

    parts = combine((keep, core_partner(send)), y_at, 4)
    got = tuple(y_turn(parts[k], k) for k in (1, 2, 3))
    arows, axl, axh = call(
        act_x_faces_kernel,
        [((12, 32, 896), BF16), ((16, 896), BF16), ((16, 896), BF16)],
        (act, azlo, azhi),
        [pltpu.VMEM((12, 32, 896), F32), pltpu.VMEM((16, 896), F32)],
        after=(parts[0],),
    )
    axlo = shift(axl, "gx", 1)
    axhi = shift(axh, "gx", -1)
    parts = combine((parts[0],) + got, x_at, 4, after=(axlo, axhi))
    got = tuple(x_turn(parts[k], k) for k in (1, 2, 3))
    arows, ayl, ayh = call(
        act_y_faces_kernel,
        [((12, 32, 896), BF16), ((32, 896), BF16), ((32, 896), BF16)],
        (arows, axlo, axhi),
        [pltpu.VMEM((12, 32, 896), F32), pltpu.VMEM((16, 896), F32), pltpu.VMEM((16, 896), F32)],
        after=(parts[0],),
    )
    aylo = shift(ayl, "gy", 1)
    ayhi = shift(ayh, "gy", -1)
    (part,) = combine((parts[0],) + got, z_at, 1, after=(aylo, ayhi))
    near, next_near, far = (z_partner(part, k) for k in (1, 2, 3))
    w_fine_back, done = call(
        backward_weights_kernel, [((2304, 128), BF16), ((8, 128), F32)],
        (fine_weight,), [pltpu.VMEM((1792, 128), F32)], after=(part,),
    )
    (part,) = combine((part, near, next_near, far), z_at, 1, after=(done,))
    (part,) = combine((part, z_partner(part, 7)), z_at, 1)
    part = placed((part,) + tuple(x_turn(part, k) for k in (1, 2, 3)), x_at)
    got = tuple(y_turn(part, k) for k in (1, 2, 3))
    grad_features, done = call(
        features_kernel,
        [((12, 24, 768), BF16), ((8, 128), F32)],
        (arows, aylo, ayhi, w_fine_back),
        [pltpu.VMEM((3, 448, 896), BF16)],
        flops=CONV, after=(part,),
    )
    part = placed((part,) + got, y_at, after=(done,))
    fine, coarse = call(
        last_kernel,
        [((27, 4096), F32), ((27, 8192), F32)],
        (part, core_partner(part)),
        [pltpu.VMEM((96, 32, 128), BF16)],
        place=core,
    )
    cells = 96 * 96 * 96
    fine = fine * (1.0 / math.sqrt(cells))
    coarse = coarse * (1.0 / math.sqrt(cells // 8))
    return jnp.transpose(grad_features, (1, 0, 2)), fine, coarse


def solution(mesh):
    in_specs = (P("gx", "gy", "gz"), P(), P(), P("gx", "gy", "gz"))
    out_specs = (P("gx", "gy", "gz"), P(), P())
    return jax.shard_map(body, mesh=mesh, in_specs=in_specs, out_specs=out_specs, check_vma=False)
```

```python
import functools
import math

import jax
import jax.numpy as jnp
from jax import lax
from jax.experimental import pallas as pl
from jax.experimental.pallas import tpu as pltpu
from jax.sharding import PartitionSpec as P

F32 = jnp.float32
BF16 = jnp.bfloat16
VMEM = pl.BlockSpec(memory_space=pltpu.VMEM)
ANY = pl.BlockSpec(memory_space=pl.ANY)
HBM = pl.BlockSpec(memory_space=pltpu.HBM)
CONV = 2 * 384 * 6 * 2304 * 256


def shift(value, axis, step):
    count = lax.axis_size(axis)
    return lax.ppermute(value, axis, [(i, (i + step) % count) for i in range(count)])


def call(kernel, outs, operands, scratch=(), flops=0, place=None, after=(), space=VMEM):
    moved = sum(math.prod(v.shape) * v.dtype.itemsize for v in operands)
    moved += sum(math.prod(s) * jnp.dtype(d).itemsize for s, d in outs)
    extra = () if place is None else (place,)
    first, last = len(extra) + len(operands), len(extra) + len(operands) + len(after)

    def run(*refs):
        kernel(*refs[:first], *refs[last:])

    return pl.pallas_call(
        run,
        out_shape=[jax.ShapeDtypeStruct(s, d) for s, d in outs],
        in_specs=[VMEM] * len(extra) + [space] * len(operands) + [ANY] * len(after),
        out_specs=[VMEM] * len(outs),
        scratch_shapes=list(scratch),
        compiler_params=pltpu.CompilerParams(vmem_limit_bytes=16 * 1024 * 1024),
        cost_estimate=pl.CostEstimate(flops=flops // 8, bytes_accessed=moved // 8, transcendentals=0),
    )(*extra, *operands, *after)


def place_of(ref):
    return jnp.max(ref[...])


def low_half(shape):
    return lax.broadcasted_iota(jnp.int32, shape, len(shape) - 1) < 64


def swap(value):
    return pltpu.roll(value, 64, value.ndim - 1)


def rolled_rows(value, step):
    return pltpu.roll(value, step % value.shape[-2], value.ndim - 2)


def pack_faces(low, high):
    mask = low_half((6, 24, 128))
    to_high = jnp.where(mask, swap(high[:6]), high[6:])
    to_low = jnp.where(mask, low[:6], swap(low[6:]))
    return to_high, to_low


def with_faces(own, lo, hi):
    mask = low_half((6, 24, 128))
    first = jnp.where(mask, hi, swap(lo))
    second = jnp.where(mask, swap(hi), lo)
    full = jnp.concatenate([own, jnp.concatenate([first, second], axis=0)], axis=2)
    return pltpu.roll(full, 64, 2)


def flat_fine(fine, flat):
    mask = low_half((27, 128))
    for k in range(32):
        value = fine[:, 128 * k : 128 * k + 128].astype(F32)
        turned = swap(value)
        flat[pl.ds(2 * k, 27, stride=64), :] = jnp.where(mask, value, turned)
        flat[pl.ds(2 * k + 1, 27, stride=64), :] = jnp.where(mask, turned, value)


def forward_weights_kernel(fine, own, wf, rows_out, one, flat):
    one[...] = jnp.ones(one.shape, F32)
    wide = jnp.concatenate([own[...].astype(F32), jnp.zeros((12, 24, 128), F32)], axis=2)
    rows_out[:, 0:24, :] = pltpu.roll(wide, 64, 2).astype(BF16)
    rows_out[:, 24:32, :] = jnp.zeros((12, 8, 896), BF16)
    flat_fine(fine, flat)
    mask = low_half((64, 128))
    none = jnp.zeros((64, 128), F32)
    for ab in range(9):
        for j in range(4):
            row = (4 * ab + j) * 64
            at = (3 * ab + j) * 64
            left = flat[at : at + 64, :] if j < 3 else none
            right = flat[at - 64 : at, :] if j > 0 else none
            wf[row : row + 64, :] = jnp.where(mask, left, right).astype(BF16)


def coarse_weights_kernel(coarse, wc, wcb, done, flat):
    done[...] = jnp.zeros(done.shape, F32)
    for c in range(64):
        flat[pl.ds(c, 27, stride=64), :] = coarse[:, 128 * c : 128 * c + 128].astype(F32)
    flat[1728:1792, :] = jnp.zeros((64, 128), F32)
    wide = low_half((128, 128))
    none = jnp.zeros((64, 128), F32)
    zero = jnp.zeros((128, 128), F32)
    turned = []
    for m in range(14):
        value = flat[128 * m : 128 * m + 128, :].T
        turned += [jnp.where(wide, value, swap(value)), jnp.where(wide, swap(value), value)]
    for ab in range(9):
        for j in range(4):
            row = (4 * ab + j) * 64
            at = (3 * ab + j) * 64
            left = flat[at : at + 64, :] if j < 3 else none
            right = flat[at - 64 : at, :] if j > 0 else none
            wc[row : row + 64, 0:128] = left.astype(BF16)
            wc[row : row + 64, 128:256] = right.astype(BF16)
            slot = 26 - 3 * ab - j
            row = 2 * row
            left = turned[slot] if j < 3 else zero
            right = turned[slot + 1] if j > 0 else zero
            wcb[row : row + 128, 0:128] = left.astype(BF16)
            wcb[row : row + 128, 128:256] = right.astype(BF16)


def backward_weights_kernel(fine, wfb, done, flat):
    done[...] = jnp.zeros(done.shape, F32)
    flat_fine(fine, flat)
    flat[1728:1792, :] = jnp.zeros((64, 128), F32)
    mask = low_half((64, 128))
    none = jnp.zeros((64, 128), F32)
    turned = []
    for m in range(14):
        value = flat[128 * m : 128 * m + 128, :].T[0:64]
        turned += [jnp.where(mask, value, swap(value)), jnp.where(mask, swap(value), value)]
    for ab in range(9):
        for j in range(4):
            row = (4 * ab + j) * 64
            slot = 26 - 3 * ab - j
            left = turned[slot] if j < 3 else none
            right = turned[slot + 1] if j > 0 else none
            wfb[row : row + 64, :] = jnp.where(mask, left, right).astype(BF16)


def z_faces_kernel(own, cot, zl, zh, faces, cfaces, edge, sems):
    copies = []
    for k, lane in enumerate((0, 640)):
        lanes = pl.ds(lane, 128)
        copies.append(pltpu.make_async_copy(own.at[:, :, lanes], faces.at[k], sems.at[2 * k]))
        copies.append(pltpu.make_async_copy(cot.at[:, :, lanes], cfaces.at[k], sems.at[2 * k + 1]))
    for copy in copies:
        copy.start()
    for copy in copies:
        copy.wait()
    to_high, to_low = pack_faces(faces[0].astype(F32), faces[1].astype(F32))
    for out, face, k in ((zl, to_high, 1), (zh, to_low, 0)):
        edge[:, 0:6, :] = cfaces[k].astype(F32)
        turned = [edge[:, y : y + 1, :].reshape(12, 128)[None] for y in range(6)]
        turned = jnp.concatenate(turned, axis=0)
        pad = jnp.zeros((6, 4, 128), F32)
        out[...] = jnp.concatenate([face, turned, pad], axis=1).astype(BF16)


def edge_lanes(lo, hi):
    low = jnp.concatenate([lo, swap(lo)], axis=0)
    high = jnp.concatenate([swap(hi), hi], axis=0)
    return low, high


def x_faces_kernel(own, cot, zlo, zhi, rows_out, cot_out, xl, xh, ends, crows, message):
    lo = zlo[...].astype(F32)
    hi = zhi[...].astype(F32)
    low, high = edge_lanes(lo[:, 0:24], hi[:, 0:24])
    mask = low_half((12, 24, 128))
    rows_out[...] = own[...]
    for at, part in ((0, jnp.where(mask, low, 0.0)), (768, jnp.where(mask, 0.0, high))):
        lanes = slice(at, at + 128)
        rows_out[:, 0:24, lanes] = (own[:, 0:24, lanes].astype(F32) + part).astype(BF16)
    crows[:, 8:16, :] = jnp.zeros((6, 8, 1024), F32)
    crows[:, 0:12, 0:128] = lo[:, 24:36]
    crows[:, 0:12, 128:896] = cot[...].astype(F32)
    crows[:, 0:12, 896:1024] = hi[:, 24:36]
    cot_out[...] = crows[...].astype(BF16)
    ends[0] = rows_out[:, 0:8, :].astype(F32)
    ends[1] = rows_out[:, 16:24, :].astype(F32)
    message[...] = jnp.zeros(message.shape, F32)
    for out, k, x, cx in ((xl, 1, 7, 11), (xh, 0, 0, 0)):
        for y in range(12):
            message[y : y + 1, 0:896] = ends[k, y, x : x + 1, :]
        for y in range(6):
            message[12 + y : 13 + y, :] = crows[y, cx : cx + 1, :]
        out[...] = message[...].astype(BF16)


def y_faces_kernel(rows_in, cot_in, xlo, xhi, rows_out, cot_out, yl, yh, rows, crows, lo, hi):
    lo[...] = xlo[...].astype(F32)
    hi[...] = xhi[...].astype(F32)
    rows[...] = rows_in[...].astype(F32)
    crows[...] = cot_in[...].astype(F32)
    for y in range(12):
        rows[y, 24:25, :] = hi[y : y + 1, 0:896]
        rows[y, 31:32, :] = lo[y : y + 1, 0:896]
    for y in range(6):
        crows[y, 12:13, :] = hi[12 + y : 13 + y, :]
        crows[y, 15:16, :] = lo[12 + y : 13 + y, :]
    rows_out[...] = rows[...].astype(BF16)
    cot_out[...] = crows[...].astype(BF16)
    for out, y, cy in ((yl, 11, 5), (yh, 0, 0)):
        out[0:32, 0:896] = rows[y].astype(BF16)
        out[0:32, 896:1024] = jnp.zeros((32, 128), BF16)
        out[32:48, :] = crows[cy].astype(BF16)


def act_x_faces_kernel(own, zlo, zhi, rows_out, xl, xh, rows, message):
    rows[:, 0:24, :] = with_faces(
        own[...].astype(F32)[:, 0:24], zlo[...].astype(F32), zhi[...].astype(F32)
    )
    rows[:, 24:32, :] = jnp.zeros((12, 8, 896), F32)
    rows_out[...] = rows[...].astype(BF16)
    message[...] = jnp.zeros(message.shape, F32)
    for out, x in ((xl, 23), (xh, 0)):
        for y in range(12):
            message[y : y + 1, :] = rows[y, x : x + 1, :]
        out[...] = message[...].astype(BF16)


def act_y_faces_kernel(rows_in, xlo, xhi, rows_out, yl, yh, rows, lo, hi):
    lo[...] = xlo[...].astype(F32)
    hi[...] = xhi[...].astype(F32)
    rows[...] = rows_in[...].astype(F32)
    for y in range(12):
        rows[y, 24:25, :] = hi[y : y + 1, :]
        rows[y, 31:32, :] = lo[y : y + 1, :]
    value = rows[...].astype(BF16)
    rows_out[...] = value
    yl[...] = value[11]
    yh[...] = value[0]


def sigmoid(value):
    return 0.5 + 0.5 * jnp.tanh(0.5 * value)


def silu(act):
    return (act * sigmoid(act)).astype(BF16)


def silu_slope(act):
    sigma = sigmoid(act)
    return sigma * (1.0 + act * (1.0 - sigma))


def slope_kernel(inner, outer, slope, done):
    slope[0:32, :] = silu_slope(outer[0:32, :]).astype(BF16)
    slope[32:352, :] = silu_slope(inner[...]).astype(BF16)
    slope[352:384, :] = silu_slope(outer[32:64, :]).astype(BF16)
    done[...] = jnp.zeros(done.shape, F32)


def pool_matrix(shape, rule):
    r = lax.broadcasted_iota(jnp.int32, shape, 0)
    q = lax.broadcasted_iota(jnp.int32, shape, 1)
    return jnp.where(rule(r, q), 0.125, 0.0).astype(BF16)


def fold_pairs(part):
    return part + swap(part)


def interior_kernel(rows, weight, shifted, kept, edges, pooled):
    full = rows[...].astype(F32)
    for a in range(3):
        shifted[a] = rolled_rows(full, 1 - a).astype(BF16).reshape(384, 896)
    pool = pool_matrix(
        (64, 320),
        lambda r, q: ((((q >> 5) + 1) >> 1) == (r >> 4) + 1) & (((q & 31) >> 1) == (r & 15)),
    )
    mask = low_half((64, 128))
    for p in range(6):
        lanes = slice(128 * p, 128 * p + 256)
        left = jnp.concatenate(
            [shifted[a, 32 * b : 32 * b + 320, lanes] for a in range(3) for b in range(3)], axis=1
        )
        kept[:, 128 * p : 128 * p + 128] = jnp.dot(
            left, weight[...], preferred_element_type=F32
        )
    hidden = silu(kept[...])
    edges[0:32, :] = hidden[0:32]
    edges[32:64, :] = hidden[288:320]
    sums = jnp.dot(pool, hidden, preferred_element_type=F32)
    pieces = [fold_pairs(sums[:, 128 * p : 128 * p + 128]) for p in range(6)]
    for j in range(3):
        both = jnp.where(mask, pieces[2 * j], pieces[2 * j + 1])
        pooled[:, :, 128 * j : 128 * j + 128] = both.astype(BF16).reshape(4, 16, 128)


def border_kernel(shifted, ylo, yhi, weight, edges, inner, kept, pooled, zl, zh, outer):
    both = jnp.concatenate(
        [ylo[0:32, 0:896][None], yhi[0:32, 0:896][None]], axis=0
    ).astype(F32)
    for a in range(3):
        outer[a] = rolled_rows(both, 1 - a).astype(BF16).reshape(64, 896)
    blocks = []
    for p in range(6):
        lanes = slice(128 * p, 128 * p + 256)
        first = []
        last = []
        for a in range(3):
            first += [outer[a, 0:32, lanes], shifted[a, 0:32, lanes], shifted[a, 32:64, lanes]]
            last += [
                shifted[a, 320:352, lanes], shifted[a, 352:384, lanes], outer[a, 32:64, lanes]
            ]
        blocks.append(jnp.concatenate(first, axis=1))
        blocks.append(jnp.concatenate(last, axis=1))
    act = jnp.dot(jnp.concatenate(blocks, axis=0), weight[...], preferred_element_type=F32)
    hidden = silu(act)
    pool = pool_matrix(
        (32, 128),
        lambda r, q: (((q >> 5) & 1) == (r >> 4)) & (((q & 31) >> 1) == (r & 15)),
    )
    mask = low_half((32, 128))
    pieces = []
    for p in range(6):
        own = slice(128 * p, 128 * p + 128)
        kept[:, own] = act[64 * p : 64 * p + 64]
        column = jnp.concatenate([hidden[64 * p : 64 * p + 64], edges[:, own]], axis=0)
        pieces.append(fold_pairs(jnp.dot(pool, column, preferred_element_type=F32)))
    for j in range(3):
        own = slice(128 * j, 128 * j + 128)
        both = jnp.where(mask, pieces[2 * j], pieces[2 * j + 1]).astype(BF16)
        pooled[0:1, :, own] = both[0:16][None]
        pooled[5:6, :, own] = both[16:32][None]
    pooled[1:5] = inner[...]
    zl[...] = pooled[:, :, 256:384]
    zh[...] = pooled[:, :, 0:128]


def pooled_x_kernel(own, zlo, zhi, rows_out, xl, xh, rows, message):
    rows[...] = jnp.concatenate([zlo[...], own[...], zhi[...]], axis=2).astype(F32)
    rows_out[...] = rows[...].astype(BF16)
    message[...] = jnp.zeros(message.shape, F32)
    for out, x in ((xl, 10), (xh, 0)):
        for y in range(6):
            message[2 * y : 2 * y + 2, :] = rows[y, x : x + 2, :]
        out[...] = message[...].astype(BF16)


def pooled_y_kernel(rows_in, xlo, xhi, rows_out, yl, yh, rows, lo, hi):
    lo[...] = xlo[...].astype(F32)
    hi[...] = xhi[...].astype(F32)
    rows[...] = rows_in[...].astype(F32)
    for y in range(6):
        rows[y, 12:14, :] = hi[2 * y : 2 * y + 2, :]
        rows[y, 14:16, :] = lo[2 * y : 2 * y + 2, :]
    value = rows[...].astype(BF16)
    rows_out[...] = value
    yl[...] = value[4:6]
    yh[...] = value[0:2]


def backward_kernel(
    prow, pylo, pyhi, crow, ylo, yhi, slope, wc, wb,
    act_out, zl, zh, fine_left, coarse_left, pshift, gshift,
):
    full = jnp.concatenate([pylo[...], prow[...], pyhi[...]], axis=0).astype(F32)
    for a in range(3):
        pshift[a] = rolled_rows(full, 1 - a).astype(BF16).reshape(160, 640)
    blocks = []
    for p in range(4):
        lanes = slice(128 * p, 128 * p + 256)
        blocks.append(
            jnp.concatenate(
                [pshift[a, 16 * b : 16 * b + 128, lanes] for a in range(3) for b in range(3)], axis=1
            )
        )
    pre = jnp.dot(jnp.concatenate(blocks, axis=0), wc[...], preferred_element_type=F32)
    tilt = silu_slope(pre)
    cot = jnp.concatenate([ylo[32:48][None], crow[...], yhi[32:48][None]], axis=0).astype(F32)
    row = lax.broadcasted_iota(jnp.int32, (128, 256), 0)
    lane = lax.broadcasted_iota(jnp.int32, (128, 256), 1)
    own_rows = (row >= 16) & (row < 112) & ((row & 15) < 12)
    parts = []
    for p in range(4):
        grad = cot[:, :, 256 * p : 256 * p + 256].reshape(128, 256) * tilt[128 * p : 128 * p + 128]
        grad = grad.astype(BF16).astype(F32)
        parts.append(grad)
        valid = own_rows
        if p == 0:
            valid = valid & (lane >= 128)
        if p == 3:
            valid = valid & (lane < 128)
        coarse_left[:, 128 * p : 128 * p + 128] = jnp.where(valid, grad, 0.0).T.astype(BF16)
    both = jnp.concatenate(parts, axis=1).reshape(8, 16, 1024)
    for a in range(3):
        gshift[a] = rolled_rows(both, 1 - a).astype(BF16).reshape(128, 1024)
    blocks = []
    for p in range(3):
        lanes = slice(256 * p, 256 * p + 512)
        blocks.append(
            jnp.concatenate(
                [gshift[a, 16 * b : 16 * b + 96, lanes] for a in range(3) for b in range(3)], axis=1
            )
        )
    small = jnp.dot(jnp.concatenate(blocks, axis=0), wb[...], preferred_element_type=F32)
    small = small.astype(BF16)
    q = lax.broadcasted_iota(jnp.int32, (384, 96), 0)
    r = lax.broadcasted_iota(jnp.int32, (384, 96), 1)
    inside = ((q >> 6) == (r >> 4)) & (((q & 31) >> 1) == (r & 15)) & ((q & 31) < 24)
    spread = jnp.where(inside, 1.0, 0.0).astype(BF16)
    for p in range(3):
        lanes = slice(256 * p, 256 * p + 256)
        up = jnp.dot(spread, small[96 * p : 96 * p + 96], preferred_element_type=F32)
        part = (up * 0.125 * slope[:, lanes].astype(F32)).astype(BF16)
        act_out[:, :, lanes] = part.reshape(12, 32, 256)
        wide = part.astype(F32)
        fine_left[:, 768 * p : 768 * p + 384] = wide[:, 0:128].T.astype(BF16)
        fine_left[:, 768 * p + 384 : 768 * p + 768] = wide[:, 128:256].T.astype(BF16)
        if p == 0:
            low = wide[:, 0:128].reshape(12, 32, 128)[:, 0:24]
        if p == 2:
            high = wide[:, 128:256].reshape(12, 32, 128)[:, 0:24]
    to_high, to_low = pack_faces(low, high)
    zl[...] = to_high.astype(BF16)
    zh[...] = to_low.astype(BF16)


def all_rows(rows, ylo, yhi, shifted, used):
    lo = ylo[0:32, 0:896][None]
    hi = yhi[0:32, 0:896][None]
    full = jnp.concatenate([lo, rows[...], hi], axis=0).astype(F32)
    for a in used:
        shifted[a] = rolled_rows(full, 1 - a).astype(BF16).reshape(448, 896)


def fine_grads(left, shifted, turned, pairs, sums, offsets):
    mask = low_half((32, 128))
    for a, b in offsets:
        right = jnp.concatenate(
            [shifted[a, 32 * b : 32 * b + 384, 128 * p : 128 * p + 256] for p in range(6)], axis=0
        )
        turned[...] = jnp.dot(left[...], right, preferred_element_type=F32).T
        for e in range(3):
            near = turned[64 * e : 64 * e + 64]
            pairs[...] = near + swap(turned[64 * e + 64 : 64 * e + 128])
            even = pairs[pl.ds(0, 32, stride=2), :]
            odd = pairs[pl.ds(1, 32, stride=2), :]
            slot = 9 * a + 3 * b + e
            sums[pl.ds(slot, 32, stride=32), :] = jnp.where(mask, even, swap(odd))


EARLY = [(0, 0), (0, 1), (0, 2), (1, 0), (1, 1), (1, 2), (2, 0), (2, 1)]
LATE = [(2, 2)]


def early_grads_kernel(
    coarse_left, pshift, left, rows, ylo, yhi, out, turned, pairs, sums, cturned, shifted
):
    all_rows(rows, ylo, yhi, shifted, (0, 1, 2))
    sums[...] = jnp.zeros(sums.shape, F32)
    for a in range(3):
        for b in range(3):
            right = jnp.concatenate(
                [pshift[a, 16 * b : 16 * b + 128, 128 * p : 128 * p + 256] for p in range(4)], axis=0
            )
            cturned[...] = jnp.dot(coarse_left[...], right, preferred_element_type=F32).T
            for e in range(3):
                near = cturned[64 * e : 64 * e + 64, 0:128]
                far = cturned[64 * e + 64 : 64 * e + 128, 128:256]
                sums[pl.ds(1024 + 9 * a + 3 * b + e, 64, stride=32), :] = near + far
    fine_grads(left, shifted, turned, pairs, sums, EARLY)
    out[...] = sums[...].astype(BF16).reshape(96, 32, 128)


def late_grads_kernel(
    core, left, rows, ylo, yhi, early, keep, send, turned, pairs, sums, whole, shifted
):
    all_rows(rows, ylo, yhi, shifted, (2,))
    sums[...] = early[0:32].astype(F32).reshape(1024, 128)
    fine_grads(left, shifted, turned, pairs, sums, LATE)
    whole[0:32] = sums[...].astype(BF16).reshape(32, 32, 128)
    whole[32:96] = early[32:96]
    half = place_of(core)
    keep[...] = whole[pl.ds(half * 48, 48)]
    send[...] = whole[pl.ds((1 - half) * 48, 48)]


def features_kernel(rows, ylo, yhi, weight, out, done, shifted):
    done[...] = jnp.zeros(done.shape, F32)
    full = jnp.concatenate([ylo[...][None], rows[...], yhi[...][None]], axis=0).astype(F32)
    for a in range(3):
        shifted[a] = rolled_rows(full, 1 - a).astype(BF16).reshape(448, 896)
    for p in range(6):
        lanes = slice(128 * p, 128 * p + 256)
        left = jnp.concatenate(
            [shifted[a, 32 * b : 32 * b + 384, lanes] for a in range(3) for b in range(3)], axis=1
        )
        grad = jnp.dot(left, weight[...], preferred_element_type=F32)
        grad = grad.reshape(12, 32, 128)[:, 0:24, :]
        out[:, :, 128 * p : 128 * p + 128] = grad.astype(BF16)


def combine_kernel(count, parts, *refs):
    ins, outs = refs[-count - parts : -count], refs[-count:]
    size = outs[0].shape[0]
    at = place_of(refs[0]) if count > 1 else 0
    for k in range(count):
        start = lax.rem(at + k, count) * size if count > 1 else 0
        terms = [ref[pl.ds(start, size)].astype(F32) for ref in ins]
        while len(terms) > 1:
            terms = [sum(terms[i : i + 2][1:], terms[i]) for i in range(0, len(terms), 2)]
        outs[k][...] = terms[0].astype(outs[k].dtype)


def combine(values, place, count, after=()):
    size = values[0].shape[0] // count
    return call(
        functools.partial(combine_kernel, count, len(values)),
        [((size, 32, 128), BF16)] * count, values, place=place, after=after,
    )


def place_kernel(count, *refs):
    at, ins, out = place_of(refs[0]), refs[1 : 1 + count], refs[-1]
    size = ins[0].shape[0]
    for k in range(count):
        out[pl.ds(lax.rem(at + count - k, count) * size, size)] = ins[k][...]


def placed(values, place, after=()):
    count = len(values)
    size = values[0].shape[0]
    return call(
        functools.partial(place_kernel, count),
        [((count * size, 32, 128), BF16)], values, place=place, after=after,
    )[0]


def last_kernel(core, own, other, fine, coarse, whole):
    half = place_of(core)
    whole[pl.ds(half * 48, 48)] = own[...]
    whole[pl.ds((1 - half) * 48, 48)] = other[...]
    cells = 96 * 96 * 96
    for r in range(96):
        value = whole[r].astype(F32)[0:27]
        if r < 32:
            fine[:, 128 * r : 128 * r + 128] = value * (1.0 / math.sqrt(cells))
        else:
            at = 128 * (r - 32)
            coarse[:, at : at + 128] = value * (1.0 / math.sqrt(cells // 8))


def places_kernel(core_bit, x_low, y_low, y_high, x_high, core, y_at, x_at):
    core[...] = core_bit[...].astype(jnp.int32)
    y_at[...] = (y_low[...] + 2.0 * y_high[...]).astype(jnp.int32)
    x_at[...] = (x_low[...] + 2.0 * x_high[...]).astype(jnp.int32)


def bit_of(value, axis, chosen):
    return lax.ppermute(value, axis, [(i, i) for i in chosen])


def core_partner(value):
    return lax.ppermute(value, "gx", [(i, i ^ 1) for i in range(4)])


def z_partner(value, far):
    return lax.ppermute(value, "gy", [(i, i ^ far) for i in range(8)])


def y_turn(value, step):
    pairs = [(i, i // 4 * 4 + (i + step) % 4) for i in range(8)]
    return lax.ppermute(value, "gz", pairs)


def x_turn(value, step):
    pairs = []
    for gx in range(4):
        for gz in range(8):
            x = (gz // 4 * 2 + gx // 2 + step) % 4
            pairs.append((gx * 8 + gz, (x % 2 * 2 + gx % 2) * 8 + x // 2 * 4 + gz % 4))
    return lax.ppermute(value, ("gx", "gz"), pairs)


def body(features, fine_weight, coarse_weight, cotangent):
    own = jnp.transpose(features, (1, 0, 2))
    zl, zh = call(
        z_faces_kernel, [((6, 40, 128), BF16)] * 2, (own, cotangent),
        [
            pltpu.VMEM((2, 12, 24, 128), BF16), pltpu.VMEM((2, 12, 6, 128), BF16),
            pltpu.VMEM((12, 8, 128), F32), pltpu.SemaphoreType.DMA((4,)),
        ],
        space=HBM,
    )
    zlo = shift(zl, "gz", 1)
    zhi = shift(zh, "gz", -1)
    w_fine, frows, one = call(
        forward_weights_kernel,
        [((2304, 128), BF16), ((12, 32, 896), BF16), ((8, 128), F32)], (fine_weight, own),
        [pltpu.VMEM((1728, 128), F32)], after=(zl,),
    )
    frows, crows, xl, xh = call(
        x_faces_kernel,
        [((12, 32, 896), BF16), ((6, 16, 1024), BF16), ((24, 1024), BF16), ((24, 1024), BF16)],
        (frows, jnp.transpose(cotangent, (1, 0, 2)), zlo, zhi),
        [
            pltpu.VMEM((2, 12, 8, 896), F32), pltpu.VMEM((6, 16, 1024), F32),
            pltpu.VMEM((24, 1024), F32),
        ],
    )
    xlo = shift(xl, "gx", 1)
    xhi = shift(xh, "gx", -1)
    bits = (
        bit_of(one, "gx", (1, 3)), bit_of(one, "gx", (2, 3)), bit_of(one, "gz", (1, 3, 5, 7)),
        bit_of(one, "gz", (2, 3, 6, 7)), bit_of(one, "gz", (4, 5, 6, 7)),
    )
    core, y_at, x_at = call(places_kernel, [((8, 128), jnp.int32)] * 3, bits)
    frows, crows, yl, yh = call(
        y_faces_kernel,
        [((12, 32, 896), BF16), ((6, 16, 1024), BF16), ((48, 1024), BF16), ((48, 1024), BF16)],
        (frows, crows, xlo, xhi),
        [
            pltpu.VMEM((12, 32, 896), F32), pltpu.VMEM((6, 16, 1024), F32),
            pltpu.VMEM((24, 1024), F32), pltpu.VMEM((24, 1024), F32),
        ],
        after=(core,),
    )
    ylo = shift(yl, "gy", 1)
    yhi = shift(yh, "gy", -1)
    shifted, act_in, edges, inner = call(
        interior_kernel,
        [((3, 384, 896), BF16), ((320, 768), F32), ((64, 768), BF16), ((4, 16, 384), BF16)],
        (frows, w_fine),
        flops=CONV,
    )
    act_out, pooled, pzl, pzh = call(
        border_kernel,
        [
            ((64, 768), F32), ((6, 16, 384), BF16),
            ((6, 16, 128), BF16), ((6, 16, 128), BF16),
        ],
        (shifted, ylo, yhi, w_fine, edges, inner),
        [pltpu.VMEM((3, 64, 896), BF16)],
        flops=CONV // 6,
    )
    pzlo = shift(pzl, "gz", 1)
    pzhi = shift(pzh, "gz", -1)
    w_coarse, w_coarse_back, done = call(
        coarse_weights_kernel,
        [((2304, 256), BF16), ((4608, 256), BF16), ((8, 128), F32)],
        (coarse_weight,), [pltpu.VMEM((1792, 128), F32)], after=(pzl,),
    )
    prows, pxl, pxh = call(
        pooled_x_kernel,
        [((6, 16, 640), BF16), ((16, 640), BF16), ((16, 640), BF16)],
        (pooled, pzlo, pzhi),
        [pltpu.VMEM((6, 16, 640), F32), pltpu.VMEM((16, 640), F32)],
        after=(done,),
    )
    pxlo = shift(pxl, "gx", 1)
    pxhi = shift(pxh, "gx", -1)
    slope, done = call(
        slope_kernel, [((384, 768), BF16), ((8, 128), F32)], (act_in, act_out), after=(pxl,)
    )
    prows, pyl, pyh = call(
        pooled_y_kernel,
        [((6, 16, 640), BF16), ((2, 16, 640), BF16), ((2, 16, 640), BF16)],
        (prows, pxlo, pxhi),
        [pltpu.VMEM((6, 16, 640), F32), pltpu.VMEM((16, 640), F32), pltpu.VMEM((16, 640), F32)],
        after=(done,),
    )
    pylo = shift(pyl, "gy", 1)
    pyhi = shift(pyh, "gy", -1)
    act, azl, azh, fine_left, coarse_left, pshift = call(
        backward_kernel,
        [
            ((12, 32, 768), BF16), ((6, 24, 128), BF16), ((6, 24, 128), BF16),
            ((128, 2304), BF16), ((256, 512), BF16), ((3, 160, 640), BF16),
        ],
        (prows, pylo, pyhi, crows, ylo, yhi, slope, w_coarse, w_coarse_back),
        [pltpu.VMEM((3, 128, 1024), BF16)],
        flops=CONV,
    )
    azlo = shift(azl, "gz", 1)
    azhi = shift(azh, "gz", -1)
    (early,) = call(
        early_grads_kernel, [((96, 32, 128), BF16)],
        (coarse_left, pshift, fine_left, frows, ylo, yhi),
        [
            pltpu.VMEM((256, 128), F32), pltpu.VMEM((64, 128), F32),
            pltpu.VMEM((3072, 128), F32), pltpu.VMEM((256, 256), F32),
            pltpu.VMEM((3, 448, 896), BF16),
        ],
        flops=CONV,
    )
    keep, send = call(
        late_grads_kernel,
        [((48, 32, 128), BF16), ((48, 32, 128), BF16)],
        (fine_left, frows, ylo, yhi, early),
        [
            pltpu.VMEM((256, 128), F32), pltpu.VMEM((64, 128), F32),
            pltpu.VMEM((1024, 128), F32), pltpu.VMEM((96, 32, 128), BF16),
            pltpu.VMEM((3, 448, 896), BF16),
        ],
        flops=CONV // 2, place=core, after=(azlo, azhi),
    )

    parts = combine((keep, core_partner(send)), y_at, 4)
    got = tuple(y_turn(parts[k], k) for k in (1, 2, 3))
    arows, axl, axh = call(
        act_x_faces_kernel,
        [((12, 32, 896), BF16), ((16, 896), BF16), ((16, 896), BF16)],
        (act, azlo, azhi),
        [pltpu.VMEM((12, 32, 896), F32), pltpu.VMEM((16, 896), F32)],
        after=(parts[0],),
    )
    axlo = shift(axl, "gx", 1)
    axhi = shift(axh, "gx", -1)
    parts = combine((parts[0],) + got, x_at, 4, after=(axlo, axhi))
    got = tuple(x_turn(parts[k], k) for k in (1, 2, 3))
    arows, ayl, ayh = call(
        act_y_faces_kernel,
        [((12, 32, 896), BF16), ((32, 896), BF16), ((32, 896), BF16)],
        (arows, axlo, axhi),
        [pltpu.VMEM((12, 32, 896), F32), pltpu.VMEM((16, 896), F32), pltpu.VMEM((16, 896), F32)],
        after=(parts[0],),
    )
    aylo = shift(ayl, "gy", 1)
    ayhi = shift(ayh, "gy", -1)
    (part,) = combine((parts[0],) + got, None, 1, after=(aylo, ayhi))
    near, next_near, far = (z_partner(part, k) for k in (1, 2, 3))
    w_fine_back, done = call(
        backward_weights_kernel, [((2304, 128), BF16), ((8, 128), F32)],
        (fine_weight,), [pltpu.VMEM((1792, 128), F32)], after=(part,),
    )
    (part,) = combine((part, near, next_near, far), None, 1, after=(done,))
    (part,) = combine((part, z_partner(part, 7)), None, 1)
    part = placed((part,) + tuple(x_turn(part, k) for k in (1, 2, 3)), x_at)
    got = tuple(y_turn(part, k) for k in (1, 2, 3))
    grad_features, done = call(
        features_kernel,
        [((12, 24, 768), BF16), ((8, 128), F32)],
        (arows, aylo, ayhi, w_fine_back),
        [pltpu.VMEM((3, 448, 896), BF16)],
        flops=CONV, after=(part,),
    )
    part = placed((part,) + got, y_at, after=(done,))
    fine, coarse = call(
        last_kernel,
        [((27, 4096), F32), ((27, 8192), F32)],
        (part, core_partner(part)),
        [pltpu.VMEM((96, 32, 128), BF16)],
        place=core,
    )
    return jnp.transpose(grad_features, (1, 0, 2)), fine, coarse


def solution(mesh):
    in_specs = (P("gx", "gy", "gz"), P(), P(), P("gx", "gy", "gz"))
    out_specs = (P("gx", "gy", "gz"), P(), P())
    return jax.shard_map(body, mesh=mesh, in_specs=in_specs, out_specs=out_specs, check_vma=False)
```

```python
import functools
import math

import jax
import jax.numpy as jnp
from jax import lax
from jax.experimental import pallas as pl
from jax.experimental.pallas import tpu as pltpu
from jax.sharding import PartitionSpec as P

F32 = jnp.float32
BF16 = jnp.bfloat16
VMEM = pl.BlockSpec(memory_space=pltpu.VMEM)
SMEM = pl.BlockSpec(memory_space=pltpu.SMEM)
ANY = pl.BlockSpec(memory_space=pl.ANY)
HBM = pl.BlockSpec(memory_space=pltpu.HBM)
CONV = 2 * 384 * 6 * 2304 * 256


def shift(value, axis, step):
    count = lax.axis_size(axis)
    return lax.ppermute(value, axis, [(i, (i + step) % count) for i in range(count)])


def call(kernel, outs, operands, scratch=(), flops=0, place=None, after=(), space=VMEM):
    moved = sum(math.prod(v.shape) * v.dtype.itemsize for v in operands)
    moved += sum(math.prod(s) * jnp.dtype(d).itemsize for s, d in outs)
    extra = () if place is None else (place,)
    first, last = len(extra) + len(operands), len(extra) + len(operands) + len(after)

    def run(*refs):
        kernel(*refs[:first], *refs[last:])

    return pl.pallas_call(
        run,
        out_shape=[jax.ShapeDtypeStruct(s, d) for s, d in outs],
        in_specs=[SMEM] * len(extra) + [space] * len(operands) + [ANY] * len(after),
        out_specs=[VMEM] * len(outs),
        scratch_shapes=list(scratch),
        compiler_params=pltpu.CompilerParams(vmem_limit_bytes=16 * 1024 * 1024),
        cost_estimate=pl.CostEstimate(flops=flops // 8, bytes_accessed=moved // 8, transcendentals=0),
    )(*extra, *operands, *after)


def low_half(shape):
    return lax.broadcasted_iota(jnp.int32, shape, len(shape) - 1) < 64


def swap(value):
    return pltpu.roll(value, 64, value.ndim - 1)


def rolled_rows(value, step):
    return pltpu.roll(value, step % value.shape[-2], value.ndim - 2)


def wrap_face(at, to_high, to_low):
    return jnp.where(at[0] == 0, to_low, to_high)


def arrived(at, lo, hi, far):
    none = jnp.zeros_like(far)
    return lo + jnp.where(at[0] == 0, far, none), hi + jnp.where(at[0] == 3, far, none)


def pack_faces(low, high):
    mask = low_half((6, 24, 128))
    to_high = jnp.where(mask, swap(high[:6]), high[6:])
    to_low = jnp.where(mask, low[:6], swap(low[6:]))
    return to_high, to_low


def with_faces(own, lo, hi):
    mask = low_half((6, 24, 128))
    first = jnp.where(mask, hi, swap(lo))
    second = jnp.where(mask, swap(hi), lo)
    full = jnp.concatenate([own, jnp.concatenate([first, second], axis=0)], axis=2)
    return pltpu.roll(full, 64, 2)


def flat_fine(fine, flat):
    mask = low_half((27, 128))
    for k in range(32):
        value = fine[:, 128 * k : 128 * k + 128].astype(F32)
        turned = swap(value)
        flat[pl.ds(2 * k, 27, stride=64), :] = jnp.where(mask, value, turned)
        flat[pl.ds(2 * k + 1, 27, stride=64), :] = jnp.where(mask, turned, value)


def forward_weights_kernel(fine, own, wf, rows_out, flat):
    wide = jnp.concatenate([own[...].astype(F32), jnp.zeros((12, 24, 128), F32)], axis=2)
    rows_out[:, 0:24, :] = pltpu.roll(wide, 64, 2).astype(BF16)
    rows_out[:, 24:32, :] = jnp.zeros((12, 8, 896), BF16)
    flat_fine(fine, flat)
    mask = low_half((64, 128))
    none = jnp.zeros((64, 128), F32)
    for ab in range(9):
        for j in range(4):
            row = (4 * ab + j) * 64
            at = (3 * ab + j) * 64
            left = flat[at : at + 64, :] if j < 3 else none
            right = flat[at - 64 : at, :] if j > 0 else none
            wf[row : row + 64, :] = jnp.where(mask, left, right).astype(BF16)


def coarse_weights_kernel(coarse, wc, wcb, done, flat):
    done[...] = jnp.zeros(done.shape, F32)
    for c in range(64):
        flat[pl.ds(c, 27, stride=64), :] = coarse[:, 128 * c : 128 * c + 128].astype(F32)
    flat[1728:1792, :] = jnp.zeros((64, 128), F32)
    wide = low_half((128, 128))
    none = jnp.zeros((64, 128), F32)
    zero = jnp.zeros((128, 128), F32)
    turned = []
    for m in range(14):
        value = flat[128 * m : 128 * m + 128, :].T
        turned += [jnp.where(wide, value, swap(value)), jnp.where(wide, swap(value), value)]
    for ab in range(9):
        for j in range(4):
            row = (4 * ab + j) * 64
            at = (3 * ab + j) * 64
            left = flat[at : at + 64, :] if j < 3 else none
            right = flat[at - 64 : at, :] if j > 0 else none
            wc[row : row + 64, 0:128] = left.astype(BF16)
            wc[row : row + 64, 128:256] = right.astype(BF16)
            slot = 26 - 3 * ab - j
            row = 2 * row
            left = turned[slot] if j < 3 else zero
            right = turned[slot + 1] if j > 0 else zero
            wcb[row : row + 128, 0:128] = left.astype(BF16)
            wcb[row : row + 128, 128:256] = right.astype(BF16)


def backward_weights_kernel(fine, wfb, done, flat):
    done[...] = jnp.zeros(done.shape, F32)
    flat_fine(fine, flat)
    flat[1728:1792, :] = jnp.zeros((64, 128), F32)
    mask = low_half((64, 128))
    none = jnp.zeros((64, 128), F32)
    turned = []
    for m in range(14):
        value = flat[128 * m : 128 * m + 128, :].T[0:64]
        turned += [jnp.where(mask, value, swap(value)), jnp.where(mask, swap(value), value)]
    for ab in range(9):
        for j in range(4):
            row = (4 * ab + j) * 64
            slot = 26 - 3 * ab - j
            left = turned[slot] if j < 3 else none
            right = turned[slot + 1] if j > 0 else none
            wfb[row : row + 64, :] = jnp.where(mask, left, right).astype(BF16)


def z_faces_kernel(at, own, cot, zl, zh, zw, faces, cfaces, edge, sems):
    copies = []
    for k, lane in enumerate((0, 640)):
        lanes = pl.ds(lane, 128)
        copies.append(pltpu.make_async_copy(own.at[:, :, lanes], faces.at[k], sems.at[2 * k]))
        copies.append(pltpu.make_async_copy(cot.at[:, :, lanes], cfaces.at[k], sems.at[2 * k + 1]))
    for copy in copies:
        copy.start()
    for copy in copies:
        copy.wait()
    to_high, to_low = pack_faces(faces[0].astype(F32), faces[1].astype(F32))
    for out, face, k in ((zl, to_high, 1), (zh, to_low, 0)):
        edge[:, 0:6, :] = cfaces[k].astype(F32)
        turned = [edge[:, y : y + 1, :].reshape(12, 128)[None] for y in range(6)]
        turned = jnp.concatenate(turned, axis=0)
        pad = jnp.zeros((6, 4, 128), F32)
        out[...] = jnp.concatenate([face, turned, pad], axis=1).astype(BF16)
    zw[...] = wrap_face(at, zl[...].astype(F32), zh[...].astype(F32)).astype(BF16)


def edge_lanes(lo, hi):
    low = jnp.concatenate([lo, swap(lo)], axis=0)
    high = jnp.concatenate([swap(hi), hi], axis=0)
    return low, high


def x_faces_kernel(
    at, own, cot, zfar, zlo, zhi, rows_out, cot_out, xl, xh, ends, crows, message
):
    lo, hi = arrived(at, zlo[...].astype(F32), zhi[...].astype(F32), zfar[...].astype(F32))
    low, high = edge_lanes(lo[:, 0:24], hi[:, 0:24])
    mask = low_half((12, 24, 128))
    rows_out[...] = own[...]
    for lane, part in ((0, jnp.where(mask, low, 0.0)), (768, jnp.where(mask, 0.0, high))):
        lanes = slice(lane, lane + 128)
        rows_out[:, 0:24, lanes] = (own[:, 0:24, lanes].astype(F32) + part).astype(BF16)
    crows[:, 8:16, :] = jnp.zeros((6, 8, 1024), F32)
    crows[:, 0:12, 0:128] = lo[:, 24:36]
    crows[:, 0:12, 128:896] = cot[...].astype(F32)
    crows[:, 0:12, 896:1024] = hi[:, 24:36]
    cot_out[...] = crows[...].astype(BF16)
    ends[0] = rows_out[:, 0:8, :].astype(F32)
    ends[1] = rows_out[:, 16:24, :].astype(F32)
    message[...] = jnp.zeros(message.shape, F32)
    for out, k, x, cx in ((xl, 1, 7, 11), (xh, 0, 0, 0)):
        for y in range(12):
            message[y : y + 1, 0:896] = ends[k, y, x : x + 1, :]
        for y in range(6):
            message[12 + y : 13 + y, :] = crows[y, cx : cx + 1, :]
        out[...] = message[...].astype(BF16)


def y_faces_kernel(rows_in, cot_in, xlo, xhi, rows_out, cot_out, yl, yh, rows, crows, lo, hi):
    lo[...] = xlo[...].astype(F32)
    hi[...] = xhi[...].astype(F32)
    rows[...] = rows_in[...].astype(F32)
    crows[...] = cot_in[...].astype(F32)
    for y in range(12):
        rows[y, 24:25, :] = hi[y : y + 1, 0:896]
        rows[y, 31:32, :] = lo[y : y + 1, 0:896]
    for y in range(6):
        crows[y, 12:13, :] = hi[12 + y : 13 + y, :]
        crows[y, 15:16, :] = lo[12 + y : 13 + y, :]
    rows_out[...] = rows[...].astype(BF16)
    cot_out[...] = crows[...].astype(BF16)
    for out, y, cy in ((yl, 11, 5), (yh, 0, 0)):
        out[0:32, 0:896] = rows[y].astype(BF16)
        out[0:32, 896:1024] = jnp.zeros((32, 128), BF16)
        out[32:48, :] = crows[cy].astype(BF16)


def act_x_faces_kernel(at, own, zfar, zlo, zhi, rows_out, xl, xh, rows, message):
    lo, hi = arrived(at, zlo[...].astype(F32), zhi[...].astype(F32), zfar[...].astype(F32))
    rows[:, 0:24, :] = with_faces(own[...].astype(F32)[:, 0:24], lo, hi)
    rows[:, 24:32, :] = jnp.zeros((12, 8, 896), F32)
    rows_out[...] = rows[...].astype(BF16)
    message[...] = jnp.zeros(message.shape, F32)
    for out, x in ((xl, 23), (xh, 0)):
        for y in range(12):
            message[y : y + 1, :] = rows[y, x : x + 1, :]
        out[...] = message[...].astype(BF16)


def act_y_faces_kernel(rows_in, xlo, xhi, rows_out, yl, yh, rows, lo, hi):
    lo[...] = xlo[...].astype(F32)
    hi[...] = xhi[...].astype(F32)
    rows[...] = rows_in[...].astype(F32)
    for y in range(12):
        rows[y, 24:25, :] = hi[y : y + 1, :]
        rows[y, 31:32, :] = lo[y : y + 1, :]
    value = rows[...].astype(BF16)
    rows_out[...] = value
    yl[...] = value[11]
    yh[...] = value[0]


def sigmoid(value):
    return 0.5 + 0.5 * jnp.tanh(0.5 * value)


def silu(act):
    return (act * sigmoid(act)).astype(BF16)


def silu_slope(act):
    sigma = sigmoid(act)
    return sigma * (1.0 + act * (1.0 - sigma))


def slope_kernel(inner, outer, slope, done):
    slope[0:32, :] = silu_slope(outer[0:32, :]).astype(BF16)
    slope[32:352, :] = silu_slope(inner[...]).astype(BF16)
    slope[352:384, :] = silu_slope(outer[32:64, :]).astype(BF16)
    done[...] = jnp.zeros(done.shape, F32)


def pool_matrix(shape, rule):
    r = lax.broadcasted_iota(jnp.int32, shape, 0)
    q = lax.broadcasted_iota(jnp.int32, shape, 1)
    return jnp.where(rule(r, q), 0.125, 0.0).astype(BF16)


def fold_pairs(part):
    return part + swap(part)


def interior_kernel(rows, weight, shifted, kept, edges, pooled):
    full = rows[...].astype(F32)
    for a in range(3):
        shifted[a] = rolled_rows(full, 1 - a).astype(BF16).reshape(384, 896)
    pool = pool_matrix(
        (64, 320),
        lambda r, q: ((((q >> 5) + 1) >> 1) == (r >> 4) + 1) & (((q & 31) >> 1) == (r & 15)),
    )
    mask = low_half((64, 128))
    for p in range(6):
        lanes = slice(128 * p, 128 * p + 256)
        left = jnp.concatenate(
            [shifted[a, 32 * b : 32 * b + 320, lanes] for a in range(3) for b in range(3)], axis=1
        )
        kept[:, 128 * p : 128 * p + 128] = jnp.dot(
            left, weight[...], preferred_element_type=F32
        )
    hidden = silu(kept[...])
    edges[0:32, :] = hidden[0:32]
    edges[32:64, :] = hidden[288:320]
    sums = jnp.dot(pool, hidden, preferred_element_type=F32)
    pieces = [fold_pairs(sums[:, 128 * p : 128 * p + 128]) for p in range(6)]
    for j in range(3):
        both = jnp.where(mask, pieces[2 * j], pieces[2 * j + 1])
        pooled[:, :, 128 * j : 128 * j + 128] = both.astype(BF16).reshape(4, 16, 128)


def border_kernel(
    at, shifted, ylo, yhi, weight, edges, inner, kept, pooled, zl, zh, zw, outer
):
    both = jnp.concatenate(
        [ylo[0:32, 0:896][None], yhi[0:32, 0:896][None]], axis=0
    ).astype(F32)
    for a in range(3):
        outer[a] = rolled_rows(both, 1 - a).astype(BF16).reshape(64, 896)
    blocks = []
    for p in range(6):
        lanes = slice(128 * p, 128 * p + 256)
        first = []
        last = []
        for a in range(3):
            first += [outer[a, 0:32, lanes], shifted[a, 0:32, lanes], shifted[a, 32:64, lanes]]
            last += [
                shifted[a, 320:352, lanes], shifted[a, 352:384, lanes], outer[a, 32:64, lanes]
            ]
        blocks.append(jnp.concatenate(first, axis=1))
        blocks.append(jnp.concatenate(last, axis=1))
    act = jnp.dot(jnp.concatenate(blocks, axis=0), weight[...], preferred_element_type=F32)
    hidden = silu(act)
    pool = pool_matrix(
        (32, 128),
        lambda r, q: (((q >> 5) & 1) == (r >> 4)) & (((q & 31) >> 1) == (r & 15)),
    )
    mask = low_half((32, 128))
    pieces = []
    for p in range(6):
        own = slice(128 * p, 128 * p + 128)
        kept[:, own] = act[64 * p : 64 * p + 64]
        column = jnp.concatenate([hidden[64 * p : 64 * p + 64], edges[:, own]], axis=0)
        pieces.append(fold_pairs(jnp.dot(pool, column, preferred_element_type=F32)))
    for j in range(3):
        own = slice(128 * j, 128 * j + 128)
        both = jnp.where(mask, pieces[2 * j], pieces[2 * j + 1]).astype(BF16)
        pooled[0:1, :, own] = both[0:16][None]
        pooled[5:6, :, own] = both[16:32][None]
    pooled[1:5] = inner[...]
    zl[...] = pooled[:, :, 256:384]
    zh[...] = pooled[:, :, 0:128]
    zw[...] = wrap_face(at, zl[...].astype(F32), zh[...].astype(F32)).astype(BF16)


def pooled_x_kernel(at, own, zfar, zlo, zhi, rows_out, xl, xh, rows, message):
    lo, hi = arrived(at, zlo[...].astype(F32), zhi[...].astype(F32), zfar[...].astype(F32))
    rows[:, :, 0:128] = lo
    rows[:, :, 128:512] = own[...].astype(F32)
    rows[:, :, 512:640] = hi
    rows_out[...] = rows[...].astype(BF16)
    message[...] = jnp.zeros(message.shape, F32)
    for out, x in ((xl, 10), (xh, 0)):
        for y in range(6):
            message[2 * y : 2 * y + 2, :] = rows[y, x : x + 2, :]
        out[...] = message[...].astype(BF16)


def pooled_y_kernel(rows_in, xlo, xhi, rows_out, yl, yh, rows, lo, hi):
    lo[...] = xlo[...].astype(F32)
    hi[...] = xhi[...].astype(F32)
    rows[...] = rows_in[...].astype(F32)
    for y in range(6):
        rows[y, 12:14, :] = hi[2 * y : 2 * y + 2, :]
        rows[y, 14:16, :] = lo[2 * y : 2 * y + 2, :]
    value = rows[...].astype(BF16)
    rows_out[...] = value
    yl[...] = value[4:6]
    yh[...] = value[0:2]


def backward_kernel(
    at, prow, pylo, pyhi, crow, ylo, yhi, slope, wc, wb,
    act_out, zl, zh, zw, fine_left, coarse_left, pshift, gshift,
):
    full = jnp.concatenate([pylo[...], prow[...], pyhi[...]], axis=0).astype(F32)
    for a in range(3):
        pshift[a] = rolled_rows(full, 1 - a).astype(BF16).reshape(160, 640)
    blocks = []
    for p in range(4):
        lanes = slice(128 * p, 128 * p + 256)
        blocks.append(
            jnp.concatenate(
                [pshift[a, 16 * b : 16 * b + 128, lanes] for a in range(3) for b in range(3)], axis=1
            )
        )
    pre = jnp.dot(jnp.concatenate(blocks, axis=0), wc[...], preferred_element_type=F32)
    tilt = silu_slope(pre)
    cot = jnp.concatenate([ylo[32:48][None], crow[...], yhi[32:48][None]], axis=0).astype(F32)
    row = lax.broadcasted_iota(jnp.int32, (128, 256), 0)
    lane = lax.broadcasted_iota(jnp.int32, (128, 256), 1)
    own_rows = (row >= 16) & (row < 112) & ((row & 15) < 12)
    parts = []
    for p in range(4):
        grad = cot[:, :, 256 * p : 256 * p + 256].reshape(128, 256) * tilt[128 * p : 128 * p + 128]
        grad = grad.astype(BF16).astype(F32)
        parts.append(grad)
        valid = own_rows
        if p == 0:
            valid = valid & (lane >= 128)
        if p == 3:
            valid = valid & (lane < 128)
        coarse_left[:, 128 * p : 128 * p + 128] = jnp.where(valid, grad, 0.0).T.astype(BF16)
    both = jnp.concatenate(parts, axis=1).reshape(8, 16, 1024)
    for a in range(3):
        gshift[a] = rolled_rows(both, 1 - a).astype(BF16).reshape(128, 1024)
    blocks = []
    for p in range(3):
        lanes = slice(256 * p, 256 * p + 512)
        blocks.append(
            jnp.concatenate(
                [gshift[a, 16 * b : 16 * b + 96, lanes] for a in range(3) for b in range(3)], axis=1
            )
        )
    small = jnp.dot(jnp.concatenate(blocks, axis=0), wb[...], preferred_element_type=F32)
    small = small.astype(BF16)
    q = lax.broadcasted_iota(jnp.int32, (384, 96), 0)
    r = lax.broadcasted_iota(jnp.int32, (384, 96), 1)
    inside = ((q >> 6) == (r >> 4)) & (((q & 31) >> 1) == (r & 15)) & ((q & 31) < 24)
    spread = jnp.where(inside, 1.0, 0.0).astype(BF16)
    for p in range(3):
        lanes = slice(256 * p, 256 * p + 256)
        up = jnp.dot(spread, small[96 * p : 96 * p + 96], preferred_element_type=F32)
        part = (up * 0.125 * slope[:, lanes].astype(F32)).astype(BF16)
        act_out[:, :, lanes] = part.reshape(12, 32, 256)
        wide = part.astype(F32)
        fine_left[:, 768 * p : 768 * p + 384] = wide[:, 0:128].T.astype(BF16)
        fine_left[:, 768 * p + 384 : 768 * p + 768] = wide[:, 128:256].T.astype(BF16)
        if p == 0:
            low = wide[:, 0:128].reshape(12, 32, 128)[:, 0:24]
        if p == 2:
            high = wide[:, 128:256].reshape(12, 32, 128)[:, 0:24]
    to_high, to_low = pack_faces(low, high)
    zl[...] = to_high.astype(BF16)
    zh[...] = to_low.astype(BF16)
    zw[...] = wrap_face(at, to_high, to_low).astype(BF16)


def all_rows(rows, ylo, yhi, shifted, used):
    lo = ylo[0:32, 0:896][None]
    hi = yhi[0:32, 0:896][None]
    full = jnp.concatenate([lo, rows[...], hi], axis=0).astype(F32)
    for a in used:
        shifted[a] = rolled_rows(full, 1 - a).astype(BF16).reshape(448, 896)


def fine_grads(left, shifted, turned, pairs, sums, offsets):
    mask = low_half((32, 128))
    for a, b in offsets:
        right = jnp.concatenate(
            [shifted[a, 32 * b : 32 * b + 384, 128 * p : 128 * p + 256] for p in range(6)], axis=0
        )
        turned[...] = jnp.dot(left[...], right, preferred_element_type=F32).T
        for e in range(3):
            near = turned[64 * e : 64 * e + 64]
            pairs[...] = near + swap(turned[64 * e + 64 : 64 * e + 128])
            even = pairs[pl.ds(0, 32, stride=2), :]
            odd = pairs[pl.ds(1, 32, stride=2), :]
            slot = 9 * a + 3 * b + e
            sums[pl.ds(slot, 32, stride=32), :] = jnp.where(mask, even, swap(odd))


EARLY = [(0, 0), (0, 1), (0, 2), (1, 0), (1, 1), (1, 2), (2, 0), (2, 1)]
LATE = [(2, 2)]


def early_grads_kernel(
    coarse_left, pshift, left, rows, ylo, yhi, out, turned, pairs, sums, cturned, shifted
):
    all_rows(rows, ylo, yhi, shifted, (0, 1, 2))
    sums[...] = jnp.zeros(sums.shape, F32)
    for a in range(3):
        for b in range(3):
            right = jnp.concatenate(
                [pshift[a, 16 * b : 16 * b + 128, 128 * p : 128 * p + 256] for p in range(4)], axis=0
            )
            cturned[...] = jnp.dot(coarse_left[...], right, preferred_element_type=F32).T
            for e in range(3):
                near = cturned[64 * e : 64 * e + 64, 0:128]
                far = cturned[64 * e + 64 : 64 * e + 128, 128:256]
                sums[pl.ds(1024 + 9 * a + 3 * b + e, 64, stride=32), :] = near + far
    fine_grads(left, shifted, turned, pairs, sums, EARLY)
    out[...] = sums[...].astype(BF16).reshape(96, 32, 128)


def late_grads_kernel(
    core, left, rows, ylo, yhi, early, keep, send, turned, pairs, sums, whole, shifted
):
    all_rows(rows, ylo, yhi, shifted, (2,))
    sums[...] = early[0:32].astype(F32).reshape(1024, 128)
    fine_grads(left, shifted, turned, pairs, sums, LATE)
    whole[0:32] = sums[...].astype(BF16).reshape(32, 32, 128)
    whole[32:96] = early[32:96]
    keep[...] = whole[pl.ds(core[0] * 48, 48)]
    send[...] = whole[pl.ds((1 - core[0]) * 48, 48)]


def features_kernel(rows, ylo, yhi, weight, out, done, shifted):
    done[...] = jnp.zeros(done.shape, F32)
    full = jnp.concatenate([ylo[...][None], rows[...], yhi[...][None]], axis=0).astype(F32)
    for a in range(3):
        shifted[a] = rolled_rows(full, 1 - a).astype(BF16).reshape(448, 896)
    for p in range(6):
        lanes = slice(128 * p, 128 * p + 256)
        left = jnp.concatenate(
            [shifted[a, 32 * b : 32 * b + 384, lanes] for a in range(3) for b in range(3)], axis=1
        )
        grad = jnp.dot(left, weight[...], preferred_element_type=F32)
        grad = grad.reshape(12, 32, 128)[:, 0:24, :]
        out[:, :, 128 * p : 128 * p + 128] = grad.astype(BF16)


def combine_kernel(count, parts, *refs):
    at, ins, outs = refs[0], refs[1 : 1 + parts], refs[1 + parts :]
    size = outs[0].shape[0]
    for k in range(count):
        start = lax.rem(at[0] + k, count) * size
        terms = [ref[pl.ds(start, size)].astype(F32) for ref in ins]
        while len(terms) > 1:
            terms = [sum(terms[i : i + 2][1:], terms[i]) for i in range(0, len(terms), 2)]
        outs[k][...] = terms[0].astype(outs[k].dtype)


def combine(values, place, count, after=()):
    size = values[0].shape[0] // count
    return call(
        functools.partial(combine_kernel, count, len(values)),
        [((size, 32, 128), BF16)] * count, values, place=place, after=after,
    )


def place_kernel(count, *refs):
    at, ins, out = refs[0], refs[1 : 1 + count], refs[-1]
    size = ins[0].shape[0]
    for k in range(count):
        out[pl.ds(lax.rem(at[0] + count - k, count) * size, size)] = ins[k][...]


def placed(values, place, after=()):
    count = len(values)
    size = values[0].shape[0]
    return call(
        functools.partial(place_kernel, count),
        [((count * size, 32, 128), BF16)], values, place=place, after=after,
    )[0]


def last_kernel(core, own, other, fine, coarse, whole):
    whole[pl.ds(core[0] * 48, 48)] = own[...]
    whole[pl.ds((1 - core[0]) * 48, 48)] = other[...]
    cells = 96 * 96 * 96
    for r in range(96):
        value = whole[r].astype(F32)[0:27]
        if r < 32:
            fine[:, 128 * r : 128 * r + 128] = value * (1.0 / math.sqrt(cells))
        else:
            at = 128 * (r - 32)
            coarse[:, at : at + 128] = value * (1.0 / math.sqrt(cells // 8))


def core_partner(value):
    return lax.ppermute(value, "gx", [(i, i ^ 1) for i in range(4)])


def z_exchange(to_high, to_low, wrap):
    far = lax.ppermute(wrap, "gz", [(0, 7), (7, 0), (3, 4), (4, 3)])
    up = [(0, 1), (1, 2), (2, 3), (4, 5), (5, 6), (6, 7)]
    lo = lax.ppermute(to_high, "gz", up)
    hi = lax.ppermute(to_low, "gz", [(b, a) for a, b in up])
    return lo, hi, far


def z_partner(value, far):
    return lax.ppermute(value, "gy", [(i, i ^ far) for i in range(8)])


def y_turn(value, step):
    pairs = [(i, i // 4 * 4 + (i + step) % 4) for i in range(8)]
    return lax.ppermute(value, "gz", pairs)


def x_turn(value, step):
    pairs = []
    for gx in range(4):
        for gz in range(8):
            x = (gz // 4 * 2 + gx // 2 + step) % 4
            pairs.append((gx * 8 + gz, (x % 2 * 2 + gx % 2) * 8 + x // 2 * 4 + gz % 4))
    return lax.ppermute(value, ("gx", "gz"), pairs)


def body(features, fine_weight, coarse_weight, cotangent):
    gx = lax.axis_index("gx").astype(jnp.int32)
    gz = lax.axis_index("gz").astype(jnp.int32)
    core = (gx % 2).reshape(1)
    y_at = (gz % 4).reshape(1)
    x_at = (gz // 4 * 2 + gx // 2).reshape(1)
    z_at = jnp.zeros((1,), jnp.int32)

    own = jnp.transpose(features, (1, 0, 2))
    zl, zh, zw = call(
        z_faces_kernel, [((6, 40, 128), BF16)] * 3, (own, cotangent),
        [
            pltpu.VMEM((2, 12, 24, 128), BF16), pltpu.VMEM((2, 12, 6, 128), BF16),
            pltpu.VMEM((12, 8, 128), F32), pltpu.SemaphoreType.DMA((4,)),
        ],
        space=HBM, place=y_at,
    )
    zlo, zhi, zfar = z_exchange(zl, zh, zw)
    w_fine, frows = call(
        forward_weights_kernel, [((2304, 128), BF16), ((12, 32, 896), BF16)], (fine_weight, own),
        [pltpu.VMEM((1728, 128), F32)], after=(zl,),
    )
    frows, crows, xl, xh = call(
        x_faces_kernel,
        [((12, 32, 896), BF16), ((6, 16, 1024), BF16), ((24, 1024), BF16), ((24, 1024), BF16)],
        (frows, jnp.transpose(cotangent, (1, 0, 2)), zfar, zlo, zhi),
        [
            pltpu.VMEM((2, 12, 8, 896), F32), pltpu.VMEM((6, 16, 1024), F32),
            pltpu.VMEM((24, 1024), F32),
        ],
        place=y_at,
    )
    xlo = shift(xl, "gx", 1)
    xhi = shift(xh, "gx", -1)
    frows, crows, yl, yh = call(
        y_faces_kernel,
        [((12, 32, 896), BF16), ((6, 16, 1024), BF16), ((48, 1024), BF16), ((48, 1024), BF16)],
        (frows, crows, xlo, xhi),
        [
            pltpu.VMEM((12, 32, 896), F32), pltpu.VMEM((6, 16, 1024), F32),
            pltpu.VMEM((24, 1024), F32), pltpu.VMEM((24, 1024), F32),
        ],
    )
    ylo = shift(yl, "gy", 1)
    yhi = shift(yh, "gy", -1)
    shifted, act_in, edges, inner = call(
        interior_kernel,
        [((3, 384, 896), BF16), ((320, 768), F32), ((64, 768), BF16), ((4, 16, 384), BF16)],
        (frows, w_fine),
        flops=CONV,
    )
    act_out, pooled, pzl, pzh, pzw = call(
        border_kernel,
        [
            ((64, 768), F32), ((6, 16, 384), BF16),
            ((6, 16, 128), BF16), ((6, 16, 128), BF16), ((6, 16, 128), BF16),
        ],
        (shifted, ylo, yhi, w_fine, edges, inner),
        [pltpu.VMEM((3, 64, 896), BF16)],
        flops=CONV // 6, place=y_at,
    )
    pzlo, pzhi, pzfar = z_exchange(pzl, pzh, pzw)
    w_coarse, w_coarse_back, done = call(
        coarse_weights_kernel,
        [((2304, 256), BF16), ((4608, 256), BF16), ((8, 128), F32)],
        (coarse_weight,), [pltpu.VMEM((1792, 128), F32)], after=(pzl,),
    )
    prows, pxl, pxh = call(
        pooled_x_kernel,
        [((6, 16, 640), BF16), ((16, 640), BF16), ((16, 640), BF16)],
        (pooled, pzfar, pzlo, pzhi),
        [pltpu.VMEM((6, 16, 640), F32), pltpu.VMEM((16, 640), F32)],
        after=(done,), place=y_at,
    )
    pxlo = shift(pxl, "gx", 1)
    pxhi = shift(pxh, "gx", -1)
    slope, done = call(
        slope_kernel, [((384, 768), BF16), ((8, 128), F32)], (act_in, act_out), after=(pxl,)
    )
    prows, pyl, pyh = call(
        pooled_y_kernel,
        [((6, 16, 640), BF16), ((2, 16, 640), BF16), ((2, 16, 640), BF16)],
        (prows, pxlo, pxhi),
        [pltpu.VMEM((6, 16, 640), F32), pltpu.VMEM((16, 640), F32), pltpu.VMEM((16, 640), F32)],
        after=(done,),
    )
    pylo = shift(pyl, "gy", 1)
    pyhi = shift(pyh, "gy", -1)
    act, azl, azh, azw, fine_left, coarse_left, pshift = call(
        backward_kernel,
        [
            ((12, 32, 768), BF16), ((6, 24, 128), BF16), ((6, 24, 128), BF16),
            ((6, 24, 128), BF16), ((128, 2304), BF16), ((256, 512), BF16), ((3, 160, 640), BF16),
        ],
        (prows, pylo, pyhi, crows, ylo, yhi, slope, w_coarse, w_coarse_back),
        [pltpu.VMEM((3, 128, 1024), BF16)],
        flops=CONV, place=y_at,
    )
    azlo, azhi, azfar = z_exchange(azl, azh, azw)
    (early,) = call(
        early_grads_kernel, [((96, 32, 128), BF16)],
        (coarse_left, pshift, fine_left, frows, ylo, yhi),
        [
            pltpu.VMEM((256, 128), F32), pltpu.VMEM((64, 128), F32),
            pltpu.VMEM((3072, 128), F32), pltpu.VMEM((256, 256), F32),
            pltpu.VMEM((3, 448, 896), BF16),
        ],
        flops=CONV,
    )
    keep, send = call(
        late_grads_kernel,
        [((48, 32, 128), BF16), ((48, 32, 128), BF16)],
        (fine_left, frows, ylo, yhi, early),
        [
            pltpu.VMEM((256, 128), F32), pltpu.VMEM((64, 128), F32),
            pltpu.VMEM((1024, 128), F32), pltpu.VMEM((96, 32, 128), BF16),
            pltpu.VMEM((3, 448, 896), BF16),
        ],
        flops=CONV // 2, place=core, after=(azfar, azlo, azhi),
    )

    parts = combine((keep, core_partner(send)), y_at, 4)
    got = tuple(y_turn(parts[k], k) for k in (1, 2, 3))
    arows, axl, axh = call(
        act_x_faces_kernel,
        [((12, 32, 896), BF16), ((16, 896), BF16), ((16, 896), BF16)],
        (act, azfar, azlo, azhi),
        [pltpu.VMEM((12, 32, 896), F32), pltpu.VMEM((16, 896), F32)],
        after=(parts[0],), place=y_at,
    )
    axlo = shift(axl, "gx", 1)
    axhi = shift(axh, "gx", -1)
    parts = combine((parts[0],) + got, x_at, 4, after=(axlo, axhi))
    got = tuple(x_turn(parts[k], k) for k in (1, 2, 3))
    (part,) = combine((parts[0],) + got, z_at, 1)
    near, next_near, far = (z_partner(part, k) for k in (1, 2, 3))
    w_fine_back, done = call(
        backward_weights_kernel, [((2304, 128), BF16), ((8, 128), F32)],
        (fine_weight,), [pltpu.VMEM((1792, 128), F32)], after=(part,),
    )
    (part,) = combine((part, near, next_near, far), z_at, 1, after=(done,))
    got = z_partner(part, 7)
    arows, ayl, ayh = call(
        act_y_faces_kernel,
        [((12, 32, 896), BF16), ((32, 896), BF16), ((32, 896), BF16)],
        (arows, axlo, axhi),
        [pltpu.VMEM((12, 32, 896), F32), pltpu.VMEM((16, 896), F32), pltpu.VMEM((16, 896), F32)],
        after=(part,),
    )
    aylo = shift(ayl, "gy", 1)
    ayhi = shift(ayh, "gy", -1)
    (part,) = combine((part, got), z_at, 1, after=(ayl,))
    part = placed((part,) + tuple(x_turn(part, k) for k in (1, 2, 3)), x_at, after=(aylo, ayhi))
    got = tuple(y_turn(part, k) for k in (1, 2, 3))
    grad_features, done = call(
        features_kernel,
        [((12, 24, 768), BF16), ((8, 128), F32)],
        (arows, aylo, ayhi, w_fine_back),
        [pltpu.VMEM((3, 448, 896), BF16)],
        flops=CONV, after=(part,),
    )
    part = placed((part,) + got, y_at, after=(done,))
    fine, coarse = call(
        last_kernel,
        [((27, 4096), F32), ((27, 8192), F32)],
        (part, core_partner(part)),
        [pltpu.VMEM((96, 32, 128), BF16)],
        place=core,
    )
    return jnp.transpose(grad_features, (1, 0, 2)), fine, coarse


def solution(mesh):
    in_specs = (P("gx", "gy", "gz"), P(), P(), P("gx", "gy", "gz"))
    out_specs = (P("gx", "gy", "gz"), P(), P())
    return jax.shard_map(body, mesh=mesh, in_specs=in_specs, out_specs=out_specs, check_vma=False)
```

```python
import functools
import math

import jax
import jax.numpy as jnp
from jax import lax
from jax.experimental import pallas as pl
from jax.experimental.pallas import tpu as pltpu
from jax.sharding import PartitionSpec as P

F32 = jnp.float32
BF16 = jnp.bfloat16
VMEM = pl.BlockSpec(memory_space=pltpu.VMEM)
SMEM = pl.BlockSpec(memory_space=pltpu.SMEM)
ANY = pl.BlockSpec(memory_space=pl.ANY)
HBM = pl.BlockSpec(memory_space=pltpu.HBM)
CONV = 2 * 384 * 6 * 2304 * 256


def shift(value, axis, step):
    count = lax.axis_size(axis)
    return lax.ppermute(value, axis, [(i, (i + step) % count) for i in range(count)])


def call(kernel, outs, operands, scratch=(), flops=0, place=None, after=(), space=VMEM):
    moved = sum(math.prod(v.shape) * v.dtype.itemsize for v in operands)
    moved += sum(math.prod(s) * jnp.dtype(d).itemsize for s, d in outs)
    extra = () if place is None else (place,)
    first, last = len(extra) + len(operands), len(extra) + len(operands) + len(after)

    def run(*refs):
        kernel(*refs[:first], *refs[last:])

    return pl.pallas_call(
        run,
        out_shape=[jax.ShapeDtypeStruct(s, d) for s, d in outs],
        in_specs=[SMEM] * len(extra) + [space] * len(operands) + [ANY] * len(after),
        out_specs=[VMEM] * len(outs),
        scratch_shapes=list(scratch),
        compiler_params=pltpu.CompilerParams(vmem_limit_bytes=16 * 1024 * 1024),
        cost_estimate=pl.CostEstimate(flops=flops // 8, bytes_accessed=moved // 8, transcendentals=0),
    )(*extra, *operands, *after)


def low_half(shape):
    return lax.broadcasted_iota(jnp.int32, shape, len(shape) - 1) < 64


def swap(value):
    return pltpu.roll(value, 64, value.ndim - 1)


def rolled_rows(value, step):
    return pltpu.roll(value, step % value.shape[-2], value.ndim - 2)


def pair_up(odd, first, second):
    up = first[...].astype(F32)
    down = second[...].astype(F32)
    first[...] = jnp.where(odd, up, down).astype(BF16)
    second[...] = jnp.where(odd, down, up).astype(BF16)


def sides(odd, first, second):
    one = first[...].astype(F32)
    two = second[...].astype(F32)
    return jnp.where(odd, two, one), jnp.where(odd, one, two)


def pack_faces(low, high):
    mask = low_half((6, 24, 128))
    to_high = jnp.where(mask, swap(high[:6]), high[6:])
    to_low = jnp.where(mask, low[:6], swap(low[6:]))
    return to_high, to_low


def with_faces(own, lo, hi):
    mask = low_half((6, 24, 128))
    first = jnp.where(mask, hi, swap(lo))
    second = jnp.where(mask, swap(hi), lo)
    full = jnp.concatenate([own, jnp.concatenate([first, second], axis=0)], axis=2)
    return pltpu.roll(full, 64, 2)


def flat_fine(fine, flat):
    mask = low_half((27, 128))
    for k in range(32):
        value = fine[:, 128 * k : 128 * k + 128].astype(F32)
        turned = swap(value)
        flat[pl.ds(2 * k, 27, stride=64), :] = jnp.where(mask, value, turned)
        flat[pl.ds(2 * k + 1, 27, stride=64), :] = jnp.where(mask, turned, value)


def forward_weights_kernel(fine, own, wf, rows_out, flat):
    wide = jnp.concatenate([own[...].astype(F32), jnp.zeros((12, 24, 128), F32)], axis=2)
    rows_out[:, 0:24, :] = pltpu.roll(wide, 64, 2).astype(BF16)
    rows_out[:, 24:32, :] = jnp.zeros((12, 8, 896), BF16)
    flat_fine(fine, flat)
    mask = low_half((64, 128))
    none = jnp.zeros((64, 128), F32)
    for ab in range(9):
        for j in range(4):
            row = (4 * ab + j) * 64
            at = (3 * ab + j) * 64
            left = flat[at : at + 64, :] if j < 3 else none
            right = flat[at - 64 : at, :] if j > 0 else none
            wf[row : row + 64, :] = jnp.where(mask, left, right).astype(BF16)


def coarse_weights_kernel(coarse, wc, wcb, done, flat):
    done[...] = jnp.zeros(done.shape, F32)
    for c in range(64):
        flat[pl.ds(c, 27, stride=64), :] = coarse[:, 128 * c : 128 * c + 128].astype(F32)
    flat[1728:1792, :] = jnp.zeros((64, 128), F32)
    wide = low_half((128, 128))
    none = jnp.zeros((64, 128), F32)
    zero = jnp.zeros((128, 128), F32)
    turned = []
    for m in range(14):
        value = flat[128 * m : 128 * m + 128, :].T
        turned += [jnp.where(wide, value, swap(value)), jnp.where(wide, swap(value), value)]
    for ab in range(9):
        for j in range(4):
            row = (4 * ab + j) * 64
            at = (3 * ab + j) * 64
            left = flat[at : at + 64, :] if j < 3 else none
            right = flat[at - 64 : at, :] if j > 0 else none
            wc[row : row + 64, 0:128] = left.astype(BF16)
            wc[row : row + 64, 128:256] = right.astype(BF16)
            slot = 26 - 3 * ab - j
            row = 2 * row
            left = turned[slot] if j < 3 else zero
            right = turned[slot + 1] if j > 0 else zero
            wcb[row : row + 128, 0:128] = left.astype(BF16)
            wcb[row : row + 128, 128:256] = right.astype(BF16)


def backward_weights_kernel(fine, wfb, done, flat):
    done[...] = jnp.zeros(done.shape, F32)
    flat_fine(fine, flat)
    flat[1728:1792, :] = jnp.zeros((64, 128), F32)
    mask = low_half((64, 128))
    none = jnp.zeros((64, 128), F32)
    turned = []
    for m in range(14):
        value = flat[128 * m : 128 * m + 128, :].T[0:64]
        turned += [jnp.where(mask, value, swap(value)), jnp.where(mask, swap(value), value)]
    for ab in range(9):
        for j in range(4):
            row = (4 * ab + j) * 64
            slot = 26 - 3 * ab - j
            left = turned[slot] if j < 3 else none
            right = turned[slot + 1] if j > 0 else none
            wfb[row : row + 64, :] = jnp.where(mask, left, right).astype(BF16)


def z_faces_kernel(here, own, cot, zl, zh, faces, cfaces, edge, sems):
    copies = []
    for k, lane in enumerate((0, 640)):
        lanes = pl.ds(lane, 128)
        copies.append(pltpu.make_async_copy(own.at[:, :, lanes], faces.at[k], sems.at[2 * k]))
        copies.append(pltpu.make_async_copy(cot.at[:, :, lanes], cfaces.at[k], sems.at[2 * k + 1]))
    for copy in copies:
        copy.start()
    for copy in copies:
        copy.wait()
    to_high, to_low = pack_faces(faces[0].astype(F32), faces[1].astype(F32))
    for out, face, k in ((zl, to_high, 1), (zh, to_low, 0)):
        edge[:, 0:6, :] = cfaces[k].astype(F32)
        turned = [edge[:, y : y + 1, :].reshape(12, 128)[None] for y in range(6)]
        turned = jnp.concatenate(turned, axis=0)
        pad = jnp.zeros((6, 4, 128), F32)
        out[...] = jnp.concatenate([face, turned, pad], axis=1).astype(BF16)
    pair_up(here[1] == 1, zl, zh)


def edge_lanes(lo, hi):
    low = jnp.concatenate([lo, swap(lo)], axis=0)
    high = jnp.concatenate([swap(hi), hi], axis=0)
    return low, high


def x_faces_kernel(here, own, cot, zlo, zhi, rows_out, cot_out, xl, xh, ends, crows, message):
    lo, hi = sides(here[1] == 1, zlo, zhi)
    low, high = edge_lanes(lo[:, 0:24], hi[:, 0:24])
    mask = low_half((12, 24, 128))
    rows_out[...] = own[...]
    for at, part in ((0, jnp.where(mask, low, 0.0)), (768, jnp.where(mask, 0.0, high))):
        lanes = slice(at, at + 128)
        rows_out[:, 0:24, lanes] = (own[:, 0:24, lanes].astype(F32) + part).astype(BF16)
    crows[:, 8:16, :] = jnp.zeros((6, 8, 1024), F32)
    crows[:, 0:12, 0:128] = lo[:, 24:36]
    crows[:, 0:12, 128:896] = cot[...].astype(F32)
    crows[:, 0:12, 896:1024] = hi[:, 24:36]
    cot_out[...] = crows[...].astype(BF16)
    ends[0] = rows_out[:, 0:8, :].astype(F32)
    ends[1] = rows_out[:, 16:24, :].astype(F32)
    message[...] = jnp.zeros(message.shape, F32)
    for out, k, x, cx in ((xl, 1, 7, 11), (xh, 0, 0, 0)):
        for y in range(12):
            message[y : y + 1, 0:896] = ends[k, y, x : x + 1, :]
        for y in range(6):
            message[12 + y : 13 + y, :] = crows[y, cx : cx + 1, :]
        out[...] = message[...].astype(BF16)
    pair_up(here[0] == 1, xl, xh)


def y_faces_kernel(
    here, rows_in, cot_in, xlo, xhi, rows_out, cot_out, yl, yh, rows, crows, lo, hi
):
    lo[...], hi[...] = sides(here[0] == 1, xlo, xhi)
    rows[...] = rows_in[...].astype(F32)
    crows[...] = cot_in[...].astype(F32)
    for y in range(12):
        rows[y, 24:25, :] = hi[y : y + 1, 0:896]
        rows[y, 31:32, :] = lo[y : y + 1, 0:896]
    for y in range(6):
        crows[y, 12:13, :] = hi[12 + y : 13 + y, :]
        crows[y, 15:16, :] = lo[12 + y : 13 + y, :]
    rows_out[...] = rows[...].astype(BF16)
    cot_out[...] = crows[...].astype(BF16)
    for out, y, cy in ((yl, 11, 5), (yh, 0, 0)):
        out[0:32, 0:896] = rows[y].astype(BF16)
        out[0:32, 896:1024] = jnp.zeros((32, 128), BF16)
        out[32:48, :] = crows[cy].astype(BF16)


def act_x_faces_kernel(here, own, zlo, zhi, rows_out, xl, xh, rows, message):
    z_lo, z_hi = sides(here[1] == 1, zlo, zhi)
    rows[:, 0:24, :] = with_faces(own[...].astype(F32)[:, 0:24], z_lo, z_hi)
    rows[:, 24:32, :] = jnp.zeros((12, 8, 896), F32)
    rows_out[...] = rows[...].astype(BF16)
    message[...] = jnp.zeros(message.shape, F32)
    for out, x in ((xl, 23), (xh, 0)):
        for y in range(12):
            message[y : y + 1, :] = rows[y, x : x + 1, :]
        out[...] = message[...].astype(BF16)
    pair_up(here[0] == 1, xl, xh)


def act_y_faces_kernel(here, rows_in, xlo, xhi, rows_out, yl, yh, rows, lo, hi):
    lo[...], hi[...] = sides(here[0] == 1, xlo, xhi)
    rows[...] = rows_in[...].astype(F32)
    for y in range(12):
        rows[y, 24:25, :] = hi[y : y + 1, :]
        rows[y, 31:32, :] = lo[y : y + 1, :]
    value = rows[...].astype(BF16)
    rows_out[...] = value
    yl[...] = value[11]
    yh[...] = value[0]


def sigmoid(value):
    return 0.5 + 0.5 * jnp.tanh(0.5 * value)


def silu(act):
    return (act * sigmoid(act)).astype(BF16)


def silu_slope(act):
    sigma = sigmoid(act)
    return sigma * (1.0 + act * (1.0 - sigma))


def slope_kernel(inner, outer, slope, done):
    slope[0:32, :] = silu_slope(outer[0:32, :]).astype(BF16)
    slope[32:352, :] = silu_slope(inner[...]).astype(BF16)
    slope[352:384, :] = silu_slope(outer[32:64, :]).astype(BF16)
    done[...] = jnp.zeros(done.shape, F32)


def pool_matrix(shape, rule):
    r = lax.broadcasted_iota(jnp.int32, shape, 0)
    q = lax.broadcasted_iota(jnp.int32, shape, 1)
    return jnp.where(rule(r, q), 0.125, 0.0).astype(BF16)


def fold_pairs(part):
    return part + swap(part)


def interior_kernel(rows, weight, shifted, kept, edges, pooled):
    full = rows[...].astype(F32)
    for a in range(3):
        shifted[a] = rolled_rows(full, 1 - a).astype(BF16).reshape(384, 896)
    pool = pool_matrix(
        (64, 320),
        lambda r, q: ((((q >> 5) + 1) >> 1) == (r >> 4) + 1) & (((q & 31) >> 1) == (r & 15)),
    )
    mask = low_half((64, 128))
    for p in range(6):
        lanes = slice(128 * p, 128 * p + 256)
        left = jnp.concatenate(
            [shifted[a, 32 * b : 32 * b + 320, lanes] for a in range(3) for b in range(3)], axis=1
        )
        kept[:, 128 * p : 128 * p + 128] = jnp.dot(
            left, weight[...], preferred_element_type=F32
        )
    hidden = silu(kept[...])
    edges[0:32, :] = hidden[0:32]
    edges[32:64, :] = hidden[288:320]
    sums = jnp.dot(pool, hidden, preferred_element_type=F32)
    pieces = [fold_pairs(sums[:, 128 * p : 128 * p + 128]) for p in range(6)]
    for j in range(3):
        both = jnp.where(mask, pieces[2 * j], pieces[2 * j + 1])
        pooled[:, :, 128 * j : 128 * j + 128] = both.astype(BF16).reshape(4, 16, 128)


def border_kernel(
    here, shifted, ylo, yhi, weight, edges, inner, kept, pooled, zl, zh, outer
):
    both = jnp.concatenate(
        [ylo[0:32, 0:896][None], yhi[0:32, 0:896][None]], axis=0
    ).astype(F32)
    for a in range(3):
        outer[a] = rolled_rows(both, 1 - a).astype(BF16).reshape(64, 896)
    blocks = []
    for p in range(6):
        lanes = slice(128 * p, 128 * p + 256)
        first = []
        last = []
        for a in range(3):
            first += [outer[a, 0:32, lanes], shifted[a, 0:32, lanes], shifted[a, 32:64, lanes]]
            last += [
                shifted[a, 320:352, lanes], shifted[a, 352:384, lanes], outer[a, 32:64, lanes]
            ]
        blocks.append(jnp.concatenate(first, axis=1))
        blocks.append(jnp.concatenate(last, axis=1))
    act = jnp.dot(jnp.concatenate(blocks, axis=0), weight[...], preferred_element_type=F32)
    hidden = silu(act)
    pool = pool_matrix(
        (32, 128),
        lambda r, q: (((q >> 5) & 1) == (r >> 4)) & (((q & 31) >> 1) == (r & 15)),
    )
    mask = low_half((32, 128))
    pieces = []
    for p in range(6):
        own = slice(128 * p, 128 * p + 128)
        kept[:, own] = act[64 * p : 64 * p + 64]
        column = jnp.concatenate([hidden[64 * p : 64 * p + 64], edges[:, own]], axis=0)
        pieces.append(fold_pairs(jnp.dot(pool, column, preferred_element_type=F32)))
    for j in range(3):
        own = slice(128 * j, 128 * j + 128)
        both = jnp.where(mask, pieces[2 * j], pieces[2 * j + 1]).astype(BF16)
        pooled[0:1, :, own] = both[0:16][None]
        pooled[5:6, :, own] = both[16:32][None]
    pooled[1:5] = inner[...]
    zl[...] = pooled[:, :, 256:384]
    zh[...] = pooled[:, :, 0:128]
    pair_up(here[1] == 1, zl, zh)


def pooled_x_kernel(here, own, zlo, zhi, rows_out, xl, xh, rows, message):
    rows[:, :, 0:128], rows[:, :, 512:640] = sides(here[1] == 1, zlo, zhi)
    rows[:, :, 128:512] = own[...].astype(F32)
    rows_out[...] = rows[...].astype(BF16)
    message[...] = jnp.zeros(message.shape, F32)
    for out, x in ((xl, 10), (xh, 0)):
        for y in range(6):
            message[2 * y : 2 * y + 2, :] = rows[y, x : x + 2, :]
        out[...] = message[...].astype(BF16)
    pair_up(here[0] == 1, xl, xh)


def pooled_y_kernel(here, rows_in, xlo, xhi, rows_out, yl, yh, rows, lo, hi):
    lo[...], hi[...] = sides(here[0] == 1, xlo, xhi)
    rows[...] = rows_in[...].astype(F32)
    for y in range(6):
        rows[y, 12:14, :] = hi[2 * y : 2 * y + 2, :]
        rows[y, 14:16, :] = lo[2 * y : 2 * y + 2, :]
    value = rows[...].astype(BF16)
    rows_out[...] = value
    yl[...] = value[4:6]
    yh[...] = value[0:2]


def backward_kernel(
    here, prow, pylo, pyhi, crow, ylo, yhi, slope, wc, wb,
    act_out, zl, zh, fine_left, coarse_left, pshift, gshift,
):
    full = jnp.concatenate([pylo[...], prow[...], pyhi[...]], axis=0).astype(F32)
    for a in range(3):
        pshift[a] = rolled_rows(full, 1 - a).astype(BF16).reshape(160, 640)
    blocks = []
    for p in range(4):
        lanes = slice(128 * p, 128 * p + 256)
        blocks.append(
            jnp.concatenate(
                [pshift[a, 16 * b : 16 * b + 128, lanes] for a in range(3) for b in range(3)], axis=1
            )
        )
    pre = jnp.dot(jnp.concatenate(blocks, axis=0), wc[...], preferred_element_type=F32)
    tilt = silu_slope(pre)
    cot = jnp.concatenate([ylo[32:48][None], crow[...], yhi[32:48][None]], axis=0).astype(F32)
    row = lax.broadcasted_iota(jnp.int32, (128, 256), 0)
    lane = lax.broadcasted_iota(jnp.int32, (128, 256), 1)
    own_rows = (row >= 16) & (row < 112) & ((row & 15) < 12)
    parts = []
    for p in range(4):
        grad = cot[:, :, 256 * p : 256 * p + 256].reshape(128, 256) * tilt[128 * p : 128 * p + 128]
        grad = grad.astype(BF16).astype(F32)
        parts.append(grad)
        valid = own_rows
        if p == 0:
            valid = valid & (lane >= 128)
        if p == 3:
            valid = valid & (lane < 128)
        coarse_left[:, 128 * p : 128 * p + 128] = jnp.where(valid, grad, 0.0).T.astype(BF16)
    both = jnp.concatenate(parts, axis=1).reshape(8, 16, 1024)
    for a in range(3):
        gshift[a] = rolled_rows(both, 1 - a).astype(BF16).reshape(128, 1024)
    blocks = []
    for p in range(3):
        lanes = slice(256 * p, 256 * p + 512)
        blocks.append(
            jnp.concatenate(
                [gshift[a, 16 * b : 16 * b + 96, lanes] for a in range(3) for b in range(3)], axis=1
            )
        )
    small = jnp.dot(jnp.concatenate(blocks, axis=0), wb[...], preferred_element_type=F32)
    small = small.astype(BF16)
    q = lax.broadcasted_iota(jnp.int32, (384, 96), 0)
    r = lax.broadcasted_iota(jnp.int32, (384, 96), 1)
    inside = ((q >> 6) == (r >> 4)) & (((q & 31) >> 1) == (r & 15)) & ((q & 31) < 24)
    spread = jnp.where(inside, 1.0, 0.0).astype(BF16)
    for p in range(3):
        lanes = slice(256 * p, 256 * p + 256)
        up = jnp.dot(spread, small[96 * p : 96 * p + 96], preferred_element_type=F32)
        part = (up * 0.125 * slope[:, lanes].astype(F32)).astype(BF16)
        act_out[:, :, lanes] = part.reshape(12, 32, 256)
        wide = part.astype(F32)
        fine_left[:, 768 * p : 768 * p + 384] = wide[:, 0:128].T.astype(BF16)
        fine_left[:, 768 * p + 384 : 768 * p + 768] = wide[:, 128:256].T.astype(BF16)
        if p == 0:
            low = wide[:, 0:128].reshape(12, 32, 128)[:, 0:24]
        if p == 2:
            high = wide[:, 128:256].reshape(12, 32, 128)[:, 0:24]
    to_high, to_low = pack_faces(low, high)
    zl[...] = to_high.astype(BF16)
    zh[...] = to_low.astype(BF16)
    pair_up(here[1] == 1, zl, zh)


def all_rows(rows, ylo, yhi, shifted, used):
    lo = ylo[0:32, 0:896][None]
    hi = yhi[0:32, 0:896][None]
    full = jnp.concatenate([lo, rows[...], hi], axis=0).astype(F32)
    for a in used:
        shifted[a] = rolled_rows(full, 1 - a).astype(BF16).reshape(448, 896)


def fine_grads(left, shifted, turned, pairs, sums, offsets):
    mask = low_half((32, 128))
    for a, b in offsets:
        right = jnp.concatenate(
            [shifted[a, 32 * b : 32 * b + 384, 128 * p : 128 * p + 256] for p in range(6)], axis=0
        )
        turned[...] = jnp.dot(left[...], right, preferred_element_type=F32).T
        for e in range(3):
            near = turned[64 * e : 64 * e + 64]
            pairs[...] = near + swap(turned[64 * e + 64 : 64 * e + 128])
            even = pairs[pl.ds(0, 32, stride=2), :]
            odd = pairs[pl.ds(1, 32, stride=2), :]
            slot = 9 * a + 3 * b + e
            sums[pl.ds(slot, 32, stride=32), :] = jnp.where(mask, even, swap(odd))


EARLY = [(0, 0), (0, 1), (0, 2), (1, 0), (1, 1), (1, 2), (2, 0), (2, 1)]
LATE = [(2, 2)]


def early_grads_kernel(
    coarse_left, pshift, left, rows, ylo, yhi, out, turned, pairs, sums, cturned, shifted
):
    all_rows(rows, ylo, yhi, shifted, (0, 1, 2))
    sums[...] = jnp.zeros(sums.shape, F32)
    for a in range(3):
        for b in range(3):
            right = jnp.concatenate(
                [pshift[a, 16 * b : 16 * b + 128, 128 * p : 128 * p + 256] for p in range(4)], axis=0
            )
            cturned[...] = jnp.dot(coarse_left[...], right, preferred_element_type=F32).T
            for e in range(3):
                near = cturned[64 * e : 64 * e + 64, 0:128]
                far = cturned[64 * e + 64 : 64 * e + 128, 128:256]
                sums[pl.ds(1024 + 9 * a + 3 * b + e, 64, stride=32), :] = near + far
    fine_grads(left, shifted, turned, pairs, sums, EARLY)
    out[...] = sums[...].astype(BF16).reshape(96, 32, 128)


def late_grads_kernel(
    core, left, rows, ylo, yhi, early, keep, send, turned, pairs, sums, whole, shifted
):
    all_rows(rows, ylo, yhi, shifted, (2,))
    sums[...] = early[0:32].astype(F32).reshape(1024, 128)
    fine_grads(left, shifted, turned, pairs, sums, LATE)
    whole[0:32] = sums[...].astype(BF16).reshape(32, 32, 128)
    whole[32:96] = early[32:96]
    keep[...] = whole[pl.ds(core[0] * 48, 48)]
    send[...] = whole[pl.ds((1 - core[0]) * 48, 48)]


def features_kernel(rows, ylo, yhi, weight, out, done, shifted):
    done[...] = jnp.zeros(done.shape, F32)
    full = jnp.concatenate([ylo[...][None], rows[...], yhi[...][None]], axis=0).astype(F32)
    for a in range(3):
        shifted[a] = rolled_rows(full, 1 - a).astype(BF16).reshape(448, 896)
    for p in range(6):
        lanes = slice(128 * p, 128 * p + 256)
        left = jnp.concatenate(
            [shifted[a, 32 * b : 32 * b + 384, lanes] for a in range(3) for b in range(3)], axis=1
        )
        grad = jnp.dot(left, weight[...], preferred_element_type=F32)
        grad = grad.reshape(12, 32, 128)[:, 0:24, :]
        out[:, :, 128 * p : 128 * p + 128] = grad.astype(BF16)


def combine_kernel(count, parts, *refs):
    at, ins, outs = refs[0], refs[1 : 1 + parts], refs[1 + parts :]
    size = outs[0].shape[0]
    for k in range(count):
        start = lax.rem(at[0] + k, count) * size
        terms = [ref[pl.ds(start, size)].astype(F32) for ref in ins]
        while len(terms) > 1:
            terms = [sum(terms[i : i + 2][1:], terms[i]) for i in range(0, len(terms), 2)]
        outs[k][...] = terms[0].astype(outs[k].dtype)


def combine(values, place, count, after=()):
    size = values[0].shape[0] // count
    return call(
        functools.partial(combine_kernel, count, len(values)),
        [((size, 32, 128), BF16)] * count, values, place=place, after=after,
    )


def place_kernel(count, *refs):
    at, ins, out = refs[0], refs[1 : 1 + count], refs[-1]
    size = ins[0].shape[0]
    for k in range(count):
        out[pl.ds(lax.rem(at[0] + count - k, count) * size, size)] = ins[k][...]


def placed(values, place, after=()):
    count = len(values)
    size = values[0].shape[0]
    return call(
        functools.partial(place_kernel, count),
        [((count * size, 32, 128), BF16)], values, place=place, after=after,
    )[0]


def last_kernel(core, own, other, fine, coarse, whole):
    whole[pl.ds(core[0] * 48, 48)] = own[...]
    whole[pl.ds((1 - core[0]) * 48, 48)] = other[...]
    cells = 96 * 96 * 96
    for r in range(96):
        value = whole[r].astype(F32)[0:27]
        if r < 32:
            fine[:, 128 * r : 128 * r + 128] = value * (1.0 / math.sqrt(cells))
        else:
            at = 128 * (r - 32)
            coarse[:, at : at + 128] = value * (1.0 / math.sqrt(cells // 8))


def core_partner(value):
    return lax.ppermute(value, "gx", [(i, i ^ 1) for i in range(4)])


def matched(first, second, axis):
    count = lax.axis_size(axis)
    low = [(i, (i - 1 + 2 * (i % 2)) % count) for i in range(count)]
    high = [(i, (i + 1 - 2 * (i % 2)) % count) for i in range(count)]
    return lax.ppermute(first, axis, low), lax.ppermute(second, axis, high)


def z_partner(value, far):
    return lax.ppermute(value, "gy", [(i, i ^ far) for i in range(8)])


def y_turn(value, step):
    pairs = [(i, i // 4 * 4 + (i + step) % 4) for i in range(8)]
    return lax.ppermute(value, "gz", pairs)


def x_turn(value, step):
    pairs = []
    for gx in range(4):
        for gz in range(8):
            x = (gz // 4 * 2 + gx // 2 + step) % 4
            pairs.append((gx * 8 + gz, (x % 2 * 2 + gx % 2) * 8 + x // 2 * 4 + gz % 4))
    return lax.ppermute(value, ("gx", "gz"), pairs)


def body(features, fine_weight, coarse_weight, cotangent):
    gx = lax.axis_index("gx").astype(jnp.int32)
    gz = lax.axis_index("gz").astype(jnp.int32)
    core = (gx % 2).reshape(1)
    y_at = (gz % 4).reshape(1)
    x_at = (gz // 4 * 2 + gx // 2).reshape(1)
    z_at = jnp.zeros((1,), jnp.int32)
    here = jnp.stack([gx % 2, gz % 2])

    own = jnp.transpose(features, (1, 0, 2))
    zl, zh = call(
        z_faces_kernel, [((6, 40, 128), BF16)] * 2, (own, cotangent),
        [
            pltpu.VMEM((2, 12, 24, 128), BF16), pltpu.VMEM((2, 12, 6, 128), BF16),
            pltpu.VMEM((12, 8, 128), F32), pltpu.SemaphoreType.DMA((4,)),
        ],
        space=HBM, place=here,
    )
    zlo, zhi = matched(zl, zh, "gz")
    w_fine, frows = call(
        forward_weights_kernel, [((2304, 128), BF16), ((12, 32, 896), BF16)], (fine_weight, own),
        [pltpu.VMEM((1728, 128), F32)], after=(zh,),
    )
    frows, crows, xl, xh = call(
        x_faces_kernel,
        [((12, 32, 896), BF16), ((6, 16, 1024), BF16), ((24, 1024), BF16), ((24, 1024), BF16)],
        (frows, jnp.transpose(cotangent, (1, 0, 2)), zlo, zhi),
        [
            pltpu.VMEM((2, 12, 8, 896), F32), pltpu.VMEM((6, 16, 1024), F32),
            pltpu.VMEM((24, 1024), F32),
        ],
        place=here,
    )
    xlo, xhi = matched(xl, xh, "gx")
    frows, crows, yl, yh = call(
        y_faces_kernel,
        [((12, 32, 896), BF16), ((6, 16, 1024), BF16), ((48, 1024), BF16), ((48, 1024), BF16)],
        (frows, crows, xlo, xhi),
        [
            pltpu.VMEM((12, 32, 896), F32), pltpu.VMEM((6, 16, 1024), F32),
            pltpu.VMEM((24, 1024), F32), pltpu.VMEM((24, 1024), F32),
        ],
        place=here,
    )
    ylo = shift(yl, "gy", 1)
    yhi = shift(yh, "gy", -1)
    shifted, act_in, edges, inner = call(
        interior_kernel,
        [((3, 384, 896), BF16), ((320, 768), F32), ((64, 768), BF16), ((4, 16, 384), BF16)],
        (frows, w_fine),
        flops=CONV,
    )
    act_out, pooled, pzl, pzh = call(
        border_kernel,
        [
            ((64, 768), F32), ((6, 16, 384), BF16),
            ((6, 16, 128), BF16), ((6, 16, 128), BF16),
        ],
        (shifted, ylo, yhi, w_fine, edges, inner),
        [pltpu.VMEM((3, 64, 896), BF16)],
        flops=CONV // 6, place=here,
    )
    pzlo, pzhi = matched(pzl, pzh, "gz")
    w_coarse, w_coarse_back, done = call(
        coarse_weights_kernel,
        [((2304, 256), BF16), ((4608, 256), BF16), ((8, 128), F32)],
        (coarse_weight,), [pltpu.VMEM((1792, 128), F32)], after=(pzh,),
    )
    prows, pxl, pxh = call(
        pooled_x_kernel,
        [((6, 16, 640), BF16), ((16, 640), BF16), ((16, 640), BF16)],
        (pooled, pzlo, pzhi),
        [pltpu.VMEM((6, 16, 640), F32), pltpu.VMEM((16, 640), F32)],
        after=(done,), place=here,
    )
    pxlo, pxhi = matched(pxl, pxh, "gx")
    slope, done = call(
        slope_kernel, [((384, 768), BF16), ((8, 128), F32)], (act_in, act_out), after=(pxh,)
    )
    prows, pyl, pyh = call(
        pooled_y_kernel,
        [((6, 16, 640), BF16), ((2, 16, 640), BF16), ((2, 16, 640), BF16)],
        (prows, pxlo, pxhi),
        [pltpu.VMEM((6, 16, 640), F32), pltpu.VMEM((16, 640), F32), pltpu.VMEM((16, 640), F32)],
        after=(done,), place=here,
    )
    pylo = shift(pyl, "gy", 1)
    pyhi = shift(pyh, "gy", -1)
    act, azl, azh, fine_left, coarse_left, pshift = call(
        backward_kernel,
        [
            ((12, 32, 768), BF16), ((6, 24, 128), BF16), ((6, 24, 128), BF16),
            ((128, 2304), BF16), ((256, 512), BF16), ((3, 160, 640), BF16),
        ],
        (prows, pylo, pyhi, crows, ylo, yhi, slope, w_coarse, w_coarse_back),
        [pltpu.VMEM((3, 128, 1024), BF16)],
        flops=CONV, place=here,
    )
    azlo, azhi = matched(azl, azh, "gz")
    (early,) = call(
        early_grads_kernel, [((96, 32, 128), BF16)],
        (coarse_left, pshift, fine_left, frows, ylo, yhi),
        [
            pltpu.VMEM((256, 128), F32), pltpu.VMEM((64, 128), F32),
            pltpu.VMEM((3072, 128), F32), pltpu.VMEM((256, 256), F32),
            pltpu.VMEM((3, 448, 896), BF16),
        ],
        flops=CONV,
    )
    keep, send = call(
        late_grads_kernel,
        [((48, 32, 128), BF16), ((48, 32, 128), BF16)],
        (fine_left, frows, ylo, yhi, early),
        [
            pltpu.VMEM((256, 128), F32), pltpu.VMEM((64, 128), F32),
            pltpu.VMEM((1024, 128), F32), pltpu.VMEM((96, 32, 128), BF16),
            pltpu.VMEM((3, 448, 896), BF16),
        ],
        flops=CONV // 2, place=core, after=(azlo, azhi),
    )

    parts = combine((keep, core_partner(send)), y_at, 4)
    got = tuple(y_turn(parts[k], k) for k in (1, 2, 3))
    arows, axl, axh = call(
        act_x_faces_kernel,
        [((12, 32, 896), BF16), ((16, 896), BF16), ((16, 896), BF16)],
        (act, azlo, azhi),
        [pltpu.VMEM((12, 32, 896), F32), pltpu.VMEM((16, 896), F32)],
        after=(parts[0],), place=here,
    )
    axlo, axhi = matched(axl, axh, "gx")
    parts = combine((parts[0],) + got, x_at, 4, after=(axlo, axhi))
    got = tuple(x_turn(parts[k], k) for k in (1, 2, 3))
    arows, ayl, ayh = call(
        act_y_faces_kernel,
        [((12, 32, 896), BF16), ((32, 896), BF16), ((32, 896), BF16)],
        (arows, axlo, axhi),
        [pltpu.VMEM((12, 32, 896), F32), pltpu.VMEM((16, 896), F32), pltpu.VMEM((16, 896), F32)],
        after=(parts[0],), place=here,
    )
    aylo = shift(ayl, "gy", 1)
    ayhi = shift(ayh, "gy", -1)
    (part,) = combine((parts[0],) + got, z_at, 1, after=(aylo, ayhi))
    near, next_near, far = (z_partner(part, k) for k in (1, 2, 3))
    w_fine_back, done = call(
        backward_weights_kernel, [((2304, 128), BF16), ((8, 128), F32)],
        (fine_weight,), [pltpu.VMEM((1792, 128), F32)], after=(part,),
    )
    (part,) = combine((part, near, next_near, far), z_at, 1, after=(done,))
    (part,) = combine((part, z_partner(part, 7)), z_at, 1)
    part = placed((part,) + tuple(x_turn(part, k) for k in (1, 2, 3)), x_at)
    got = tuple(y_turn(part, k) for k in (1, 2, 3))
    grad_features, done = call(
        features_kernel,
        [((12, 24, 768), BF16), ((8, 128), F32)],
        (arows, aylo, ayhi, w_fine_back),
        [pltpu.VMEM((3, 448, 896), BF16)],
        flops=CONV, after=(part,),
    )
    part = placed((part,) + got, y_at, after=(done,))
    fine, coarse = call(
        last_kernel,
        [((27, 4096), F32), ((27, 8192), F32)],
        (part, core_partner(part)),
        [pltpu.VMEM((96, 32, 128), BF16)],
        place=core,
    )
    return jnp.transpose(grad_features, (1, 0, 2)), fine, coarse


def solution(mesh):
    in_specs = (P("gx", "gy", "gz"), P(), P(), P("gx", "gy", "gz"))
    out_specs = (P("gx", "gy", "gz"), P(), P())
    return jax.shard_map(body, mesh=mesh, in_specs=in_specs, out_specs=out_specs, check_vma=False)
```

```python
import functools
import math

import jax
import jax.numpy as jnp
from jax import lax
from jax.experimental import pallas as pl
from jax.experimental.pallas import tpu as pltpu
from jax.sharding import PartitionSpec as P

F32 = jnp.float32
BF16 = jnp.bfloat16
VMEM = pl.BlockSpec(memory_space=pltpu.VMEM)
SMEM = pl.BlockSpec(memory_space=pltpu.SMEM)
ANY = pl.BlockSpec(memory_space=pl.ANY)
HBM = pl.BlockSpec(memory_space=pltpu.HBM)
CONV = 2 * 384 * 6 * 2304 * 256


def shift(value, axis, step):
    count = lax.axis_size(axis)
    return lax.ppermute(value, axis, [(i, (i + step) % count) for i in range(count)])


def call(kernel, outs, operands, scratch=(), flops=0, place=None, after=(), space=VMEM):
    moved = sum(math.prod(v.shape) * v.dtype.itemsize for v in operands)
    moved += sum(math.prod(s) * jnp.dtype(d).itemsize for s, d in outs)
    extra = () if place is None else place if isinstance(place, tuple) else (place,)
    first, last = len(extra) + len(operands), len(extra) + len(operands) + len(after)

    def run(*refs):
        kernel(*refs[:first], *refs[last:])

    return pl.pallas_call(
        run,
        out_shape=[jax.ShapeDtypeStruct(s, d) for s, d in outs],
        in_specs=[SMEM] * len(extra) + [space] * len(operands) + [ANY] * len(after),
        out_specs=[VMEM] * len(outs),
        scratch_shapes=list(scratch),
        compiler_params=pltpu.CompilerParams(vmem_limit_bytes=16 * 1024 * 1024),
        cost_estimate=pl.CostEstimate(flops=flops // 8, bytes_accessed=moved // 8, transcendentals=0),
    )(*extra, *operands, *after)


def low_half(shape):
    return lax.broadcasted_iota(jnp.int32, shape, len(shape) - 1) < 64


def swap(value):
    return pltpu.roll(value, 64, value.ndim - 1)


def rolled_rows(value, step):
    return pltpu.roll(value, step % value.shape[-2], value.ndim - 2)


def pair_up(odd, first, second):
    up = first[...].astype(F32)
    down = second[...].astype(F32)
    first[...] = jnp.where(odd, up, down).astype(BF16)
    second[...] = jnp.where(odd, down, up).astype(BF16)


def sides(odd, first, second):
    one = first[...].astype(F32)
    two = second[...].astype(F32)
    return jnp.where(odd, two, one), jnp.where(odd, one, two)


def pack_faces(low, high):
    mask = low_half((6, 24, 128))
    to_high = jnp.where(mask, swap(high[:6]), high[6:])
    to_low = jnp.where(mask, low[:6], swap(low[6:]))
    return to_high, to_low


def with_faces(own, lo, hi):
    mask = low_half((6, 24, 128))
    first = jnp.where(mask, hi, swap(lo))
    second = jnp.where(mask, swap(hi), lo)
    full = jnp.concatenate([own, jnp.concatenate([first, second], axis=0)], axis=2)
    return pltpu.roll(full, 64, 2)


def flat_fine(fine, flat):
    mask = low_half((27, 128))
    for k in range(32):
        value = fine[:, 128 * k : 128 * k + 128].astype(F32)
        turned = swap(value)
        flat[pl.ds(2 * k, 27, stride=64), :] = jnp.where(mask, value, turned)
        flat[pl.ds(2 * k + 1, 27, stride=64), :] = jnp.where(mask, turned, value)


def forward_weights_kernel(fine, own, wf, rows_out, flat):
    wide = jnp.concatenate([own[...].astype(F32), jnp.zeros((12, 24, 128), F32)], axis=2)
    rows_out[:, 0:24, :] = pltpu.roll(wide, 64, 2).astype(BF16)
    rows_out[:, 24:32, :] = jnp.zeros((12, 8, 896), BF16)
    flat_fine(fine, flat)
    mask = low_half((64, 128))
    none = jnp.zeros((64, 128), F32)
    for ab in range(9):
        for j in range(4):
            row = (4 * ab + j) * 64
            at = (3 * ab + j) * 64
            left = flat[at : at + 64, :] if j < 3 else none
            right = flat[at - 64 : at, :] if j > 0 else none
            wf[row : row + 64, :] = jnp.where(mask, left, right).astype(BF16)


def coarse_weights_kernel(coarse, wc, wcb, done, flat):
    done[...] = jnp.zeros(done.shape, F32)
    for c in range(64):
        flat[pl.ds(c, 27, stride=64), :] = coarse[:, 128 * c : 128 * c + 128].astype(F32)
    flat[1728:1792, :] = jnp.zeros((64, 128), F32)
    wide = low_half((128, 128))
    none = jnp.zeros((64, 128), F32)
    zero = jnp.zeros((128, 128), F32)
    turned = []
    for m in range(14):
        value = flat[128 * m : 128 * m + 128, :].T
        turned += [jnp.where(wide, value, swap(value)), jnp.where(wide, swap(value), value)]
    for ab in range(9):
        for j in range(4):
            row = (4 * ab + j) * 64
            at = (3 * ab + j) * 64
            left = flat[at : at + 64, :] if j < 3 else none
            right = flat[at - 64 : at, :] if j > 0 else none
            wc[row : row + 64, 0:128] = left.astype(BF16)
            wc[row : row + 64, 128:256] = right.astype(BF16)
            slot = 26 - 3 * ab - j
            row = 2 * row
            left = turned[slot] if j < 3 else zero
            right = turned[slot + 1] if j > 0 else zero
            wcb[row : row + 128, 0:128] = left.astype(BF16)
            wcb[row : row + 128, 128:256] = right.astype(BF16)


def backward_weights_kernel(fine, wfb, done, flat):
    done[...] = jnp.zeros(done.shape, F32)
    flat_fine(fine, flat)
    flat[1728:1792, :] = jnp.zeros((64, 128), F32)
    mask = low_half((64, 128))
    none = jnp.zeros((64, 128), F32)
    turned = []
    for m in range(14):
        value = flat[128 * m : 128 * m + 128, :].T[0:64]
        turned += [jnp.where(mask, value, swap(value)), jnp.where(mask, swap(value), value)]
    for ab in range(9):
        for j in range(4):
            row = (4 * ab + j) * 64
            slot = 26 - 3 * ab - j
            left = turned[slot] if j < 3 else none
            right = turned[slot + 1] if j > 0 else none
            wfb[row : row + 64, :] = jnp.where(mask, left, right).astype(BF16)


def z_faces_kernel(z_odd, own, cot, zl, zh, faces, cfaces, edge, sems):
    copies = []
    for k, lane in enumerate((0, 640)):
        lanes = pl.ds(lane, 128)
        copies.append(pltpu.make_async_copy(own.at[:, :, lanes], faces.at[k], sems.at[2 * k]))
        copies.append(pltpu.make_async_copy(cot.at[:, :, lanes], cfaces.at[k], sems.at[2 * k + 1]))
    for copy in copies:
        copy.start()
    for copy in copies:
        copy.wait()
    to_high, to_low = pack_faces(faces[0].astype(F32), faces[1].astype(F32))
    for out, face, k in ((zl, to_high, 1), (zh, to_low, 0)):
        edge[:, 0:6, :] = cfaces[k].astype(F32)
        turned = [edge[:, y : y + 1, :].reshape(12, 128)[None] for y in range(6)]
        turned = jnp.concatenate(turned, axis=0)
        pad = jnp.zeros((6, 4, 128), F32)
        out[...] = jnp.concatenate([face, turned, pad], axis=1).astype(BF16)
    pair_up(z_odd[0] == 1, zl, zh)


def edge_lanes(lo, hi):
    low = jnp.concatenate([lo, swap(lo)], axis=0)
    high = jnp.concatenate([swap(hi), hi], axis=0)
    return low, high


def x_faces_kernel(core, z_odd, own, cot, zlo, zhi, rows_out, cot_out, xl, xh, ends, crows, message):
    lo, hi = sides(z_odd[0] == 1, zlo, zhi)
    low, high = edge_lanes(lo[:, 0:24], hi[:, 0:24])
    mask = low_half((12, 24, 128))
    rows_out[...] = own[...]
    for at, part in ((0, jnp.where(mask, low, 0.0)), (768, jnp.where(mask, 0.0, high))):
        lanes = slice(at, at + 128)
        rows_out[:, 0:24, lanes] = (own[:, 0:24, lanes].astype(F32) + part).astype(BF16)
    crows[:, 8:16, :] = jnp.zeros((6, 8, 1024), F32)
    crows[:, 0:12, 0:128] = lo[:, 24:36]
    crows[:, 0:12, 128:896] = cot[...].astype(F32)
    crows[:, 0:12, 896:1024] = hi[:, 24:36]
    cot_out[...] = crows[...].astype(BF16)
    ends[0] = rows_out[:, 0:8, :].astype(F32)
    ends[1] = rows_out[:, 16:24, :].astype(F32)
    message[...] = jnp.zeros(message.shape, F32)
    for out, k, x, cx in ((xl, 1, 7, 11), (xh, 0, 0, 0)):
        for y in range(12):
            message[y : y + 1, 0:896] = ends[k, y, x : x + 1, :]
        for y in range(6):
            message[12 + y : 13 + y, :] = crows[y, cx : cx + 1, :]
        out[...] = message[...].astype(BF16)
    pair_up(core[0] == 1, xl, xh)


def y_faces_kernel(
    core, rows_in, cot_in, xlo, xhi, rows_out, cot_out, yl, yh, rows, crows, lo, hi
):
    lo[...], hi[...] = sides(core[0] == 1, xlo, xhi)
    rows[...] = rows_in[...].astype(F32)
    crows[...] = cot_in[...].astype(F32)
    for y in range(12):
        rows[y, 24:25, :] = hi[y : y + 1, 0:896]
        rows[y, 31:32, :] = lo[y : y + 1, 0:896]
    for y in range(6):
        crows[y, 12:13, :] = hi[12 + y : 13 + y, :]
        crows[y, 15:16, :] = lo[12 + y : 13 + y, :]
    rows_out[...] = rows[...].astype(BF16)
    cot_out[...] = crows[...].astype(BF16)
    for out, y, cy in ((yl, 11, 5), (yh, 0, 0)):
        out[0:32, 0:896] = rows[y].astype(BF16)
        out[0:32, 896:1024] = jnp.zeros((32, 128), BF16)
        out[32:48, :] = crows[cy].astype(BF16)


def act_x_faces_kernel(core, z_odd, own, zlo, zhi, rows_out, xl, xh, rows, message):
    z_lo, z_hi = sides(z_odd[0] == 1, zlo, zhi)
    rows[:, 0:24, :] = with_faces(own[...].astype(F32)[:, 0:24], z_lo, z_hi)
    rows[:, 24:32, :] = jnp.zeros((12, 8, 896), F32)
    rows_out[...] = rows[...].astype(BF16)
    message[...] = jnp.zeros(message.shape, F32)
    for out, x in ((xl, 23), (xh, 0)):
        for y in range(12):
            message[y : y + 1, :] = rows[y, x : x + 1, :]
        out[...] = message[...].astype(BF16)
    pair_up(core[0] == 1, xl, xh)


def act_y_faces_kernel(core, rows_in, xlo, xhi, rows_out, yl, yh, rows, lo, hi):
    lo[...], hi[...] = sides(core[0] == 1, xlo, xhi)
    rows[...] = rows_in[...].astype(F32)
    for y in range(12):
        rows[y, 24:25, :] = hi[y : y + 1, :]
        rows[y, 31:32, :] = lo[y : y + 1, :]
    value = rows[...].astype(BF16)
    rows_out[...] = value
    yl[...] = value[11]
    yh[...] = value[0]


def sigmoid(value):
    return 0.5 + 0.5 * jnp.tanh(0.5 * value)


def silu(act):
    return (act * sigmoid(act)).astype(BF16)


def silu_slope(act):
    sigma = sigmoid(act)
    return sigma * (1.0 + act * (1.0 - sigma))


def slope_kernel(inner, outer, slope, done):
    slope[0:32, :] = silu_slope(outer[0:32, :]).astype(BF16)
    slope[32:352, :] = silu_slope(inner[...]).astype(BF16)
    slope[352:384, :] = silu_slope(outer[32:64, :]).astype(BF16)
    done[...] = jnp.zeros(done.shape, F32)


def pool_matrix(shape, rule):
    r = lax.broadcasted_iota(jnp.int32, shape, 0)
    q = lax.broadcasted_iota(jnp.int32, shape, 1)
    return jnp.where(rule(r, q), 0.125, 0.0).astype(BF16)


def fold_pairs(part):
    return part + swap(part)


def interior_kernel(rows, weight, shifted, kept, edges, pooled):
    full = rows[...].astype(F32)
    for a in range(3):
        shifted[a] = rolled_rows(full, 1 - a).astype(BF16).reshape(384, 896)
    pool = pool_matrix(
        (64, 320),
        lambda r, q: ((((q >> 5) + 1) >> 1) == (r >> 4) + 1) & (((q & 31) >> 1) == (r & 15)),
    )
    mask = low_half((64, 128))
    for p in range(6):
        lanes = slice(128 * p, 128 * p + 256)
        left = jnp.concatenate(
            [shifted[a, 32 * b : 32 * b + 320, lanes] for a in range(3) for b in range(3)], axis=1
        )
        kept[:, 128 * p : 128 * p + 128] = jnp.dot(
            left, weight[...], preferred_element_type=F32
        )
    hidden = silu(kept[...])
    edges[0:32, :] = hidden[0:32]
    edges[32:64, :] = hidden[288:320]
    sums = jnp.dot(pool, hidden, preferred_element_type=F32)
    pieces = [fold_pairs(sums[:, 128 * p : 128 * p + 128]) for p in range(6)]
    for j in range(3):
        both = jnp.where(mask, pieces[2 * j], pieces[2 * j + 1])
        pooled[:, :, 128 * j : 128 * j + 128] = both.astype(BF16).reshape(4, 16, 128)


def border_kernel(
    z_odd, shifted, ylo, yhi, weight, edges, inner, kept, pooled, zl, zh, outer
):
    both = jnp.concatenate(
        [ylo[0:32, 0:896][None], yhi[0:32, 0:896][None]], axis=0
    ).astype(F32)
    for a in range(3):
        outer[a] = rolled_rows(both, 1 - a).astype(BF16).reshape(64, 896)
    blocks = []
    for p in range(6):
        lanes = slice(128 * p, 128 * p + 256)
        first = []
        last = []
        for a in range(3):
            first += [outer[a, 0:32, lanes], shifted[a, 0:32, lanes], shifted[a, 32:64, lanes]]
            last += [
                shifted[a, 320:352, lanes], shifted[a, 352:384, lanes], outer[a, 32:64, lanes]
            ]
        blocks.append(jnp.concatenate(first, axis=1))
        blocks.append(jnp.concatenate(last, axis=1))
    act = jnp.dot(jnp.concatenate(blocks, axis=0), weight[...], preferred_element_type=F32)
    hidden = silu(act)
    pool = pool_matrix(
        (32, 128),
        lambda r, q: (((q >> 5) & 1) == (r >> 4)) & (((q & 31) >> 1) == (r & 15)),
    )
    mask = low_half((32, 128))
    pieces = []
    for p in range(6):
        own = slice(128 * p, 128 * p + 128)
        kept[:, own] = act[64 * p : 64 * p + 64]
        column = jnp.concatenate([hidden[64 * p : 64 * p + 64], edges[:, own]], axis=0)
        pieces.append(fold_pairs(jnp.dot(pool, column, preferred_element_type=F32)))
    for j in range(3):
        own = slice(128 * j, 128 * j + 128)
        both = jnp.where(mask, pieces[2 * j], pieces[2 * j + 1]).astype(BF16)
        pooled[0:1, :, own] = both[0:16][None]
        pooled[5:6, :, own] = both[16:32][None]
    pooled[1:5] = inner[...]
    zl[...] = pooled[:, :, 256:384]
    zh[...] = pooled[:, :, 0:128]
    pair_up(z_odd[0] == 1, zl, zh)


def pooled_x_kernel(core, z_odd, own, zlo, zhi, rows_out, xl, xh, rows, message):
    rows[:, :, 0:128], rows[:, :, 512:640] = sides(z_odd[0] == 1, zlo, zhi)
    rows[:, :, 128:512] = own[...].astype(F32)
    rows_out[...] = rows[...].astype(BF16)
    message[...] = jnp.zeros(message.shape, F32)
    for out, x in ((xl, 10), (xh, 0)):
        for y in range(6):
            message[2 * y : 2 * y + 2, :] = rows[y, x : x + 2, :]
        out[...] = message[...].astype(BF16)
    pair_up(core[0] == 1, xl, xh)


def pooled_y_kernel(core, rows_in, xlo, xhi, rows_out, yl, yh, rows, lo, hi):
    lo[...], hi[...] = sides(core[0] == 1, xlo, xhi)
    rows[...] = rows_in[...].astype(F32)
    for y in range(6):
        rows[y, 12:14, :] = hi[2 * y : 2 * y + 2, :]
        rows[y, 14:16, :] = lo[2 * y : 2 * y + 2, :]
    value = rows[...].astype(BF16)
    rows_out[...] = value
    yl[...] = value[4:6]
    yh[...] = value[0:2]


def backward_kernel(
    z_odd, prow, pylo, pyhi, crow, ylo, yhi, slope, wc, wb,
    act_out, zl, zh, fine_left, coarse_left, pshift, gshift,
):
    full = jnp.concatenate([pylo[...], prow[...], pyhi[...]], axis=0).astype(F32)
    for a in range(3):
        pshift[a] = rolled_rows(full, 1 - a).astype(BF16).reshape(160, 640)
    blocks = []
    for p in range(4):
        lanes = slice(128 * p, 128 * p + 256)
        blocks.append(
            jnp.concatenate(
                [pshift[a, 16 * b : 16 * b + 128, lanes] for a in range(3) for b in range(3)], axis=1
            )
        )
    pre = jnp.dot(jnp.concatenate(blocks, axis=0), wc[...], preferred_element_type=F32)
    tilt = silu_slope(pre)
    cot = jnp.concatenate([ylo[32:48][None], crow[...], yhi[32:48][None]], axis=0).astype(F32)
    row = lax.broadcasted_iota(jnp.int32, (128, 256), 0)
    lane = lax.broadcasted_iota(jnp.int32, (128, 256), 1)
    own_rows = (row >= 16) & (row < 112) & ((row & 15) < 12)
    parts = []
    for p in range(4):
        grad = cot[:, :, 256 * p : 256 * p + 256].reshape(128, 256) * tilt[128 * p : 128 * p + 128]
        grad = grad.astype(BF16).astype(F32)
        parts.append(grad)
        valid = own_rows
        if p == 0:
            valid = valid & (lane >= 128)
        if p == 3:
            valid = valid & (lane < 128)
        coarse_left[:, 128 * p : 128 * p + 128] = jnp.where(valid, grad, 0.0).T.astype(BF16)
    both = jnp.concatenate(parts, axis=1).reshape(8, 16, 1024)
    for a in range(3):
        gshift[a] = rolled_rows(both, 1 - a).astype(BF16).reshape(128, 1024)
    blocks = []
    for p in range(3):
        lanes = slice(256 * p, 256 * p + 512)
        blocks.append(
            jnp.concatenate(
                [gshift[a, 16 * b : 16 * b + 96, lanes] for a in range(3) for b in range(3)], axis=1
            )
        )
    small = jnp.dot(jnp.concatenate(blocks, axis=0), wb[...], preferred_element_type=F32)
    small = small.astype(BF16)
    q = lax.broadcasted_iota(jnp.int32, (384, 96), 0)
    r = lax.broadcasted_iota(jnp.int32, (384, 96), 1)
    inside = ((q >> 6) == (r >> 4)) & (((q & 31) >> 1) == (r & 15)) & ((q & 31) < 24)
    spread = jnp.where(inside, 1.0, 0.0).astype(BF16)
    for p in range(3):
        lanes = slice(256 * p, 256 * p + 256)
        up = jnp.dot(spread, small[96 * p : 96 * p + 96], preferred_element_type=F32)
        part = (up * 0.125 * slope[:, lanes].astype(F32)).astype(BF16)
        act_out[:, :, lanes] = part.reshape(12, 32, 256)
        wide = part.astype(F32)
        fine_left[:, 768 * p : 768 * p + 384] = wide[:, 0:128].T.astype(BF16)
        fine_left[:, 768 * p + 384 : 768 * p + 768] = wide[:, 128:256].T.astype(BF16)
        if p == 0:
            low = wide[:, 0:128].reshape(12, 32, 128)[:, 0:24]
        if p == 2:
            high = wide[:, 128:256].reshape(12, 32, 128)[:, 0:24]
    to_high, to_low = pack_faces(low, high)
    zl[...] = to_high.astype(BF16)
    zh[...] = to_low.astype(BF16)
    pair_up(z_odd[0] == 1, zl, zh)


def all_rows(rows, ylo, yhi, shifted, used):
    lo = ylo[0:32, 0:896][None]
    hi = yhi[0:32, 0:896][None]
    full = jnp.concatenate([lo, rows[...], hi], axis=0).astype(F32)
    for a in used:
        shifted[a] = rolled_rows(full, 1 - a).astype(BF16).reshape(448, 896)


def fine_grads(left, shifted, turned, pairs, sums, offsets):
    mask = low_half((32, 128))
    for a, b in offsets:
        right = jnp.concatenate(
            [shifted[a, 32 * b : 32 * b + 384, 128 * p : 128 * p + 256] for p in range(6)], axis=0
        )
        turned[...] = jnp.dot(left[...], right, preferred_element_type=F32).T
        for e in range(3):
            near = turned[64 * e : 64 * e + 64]
            pairs[...] = near + swap(turned[64 * e + 64 : 64 * e + 128])
            even = pairs[pl.ds(0, 32, stride=2), :]
            odd = pairs[pl.ds(1, 32, stride=2), :]
            slot = 9 * a + 3 * b + e
            sums[pl.ds(slot, 32, stride=32), :] = jnp.where(mask, even, swap(odd))


EARLY = [(0, 0), (0, 1), (0, 2), (1, 0), (1, 1), (1, 2), (2, 0), (2, 1)]
LATE = [(2, 2)]


def early_grads_kernel(
    coarse_left, pshift, left, rows, ylo, yhi, out, turned, pairs, sums, cturned, shifted
):
    all_rows(rows, ylo, yhi, shifted, (0, 1, 2))
    sums[...] = jnp.zeros(sums.shape, F32)
    for a in range(3):
        for b in range(3):
            right = jnp.concatenate(
                [pshift[a, 16 * b : 16 * b + 128, 128 * p : 128 * p + 256] for p in range(4)], axis=0
            )
            cturned[...] = jnp.dot(coarse_left[...], right, preferred_element_type=F32).T
            for e in range(3):
                near = cturned[64 * e : 64 * e + 64, 0:128]
                far = cturned[64 * e + 64 : 64 * e + 128, 128:256]
                sums[pl.ds(1024 + 9 * a + 3 * b + e, 64, stride=32), :] = near + far
    fine_grads(left, shifted, turned, pairs, sums, EARLY)
    out[...] = sums[...].astype(BF16).reshape(96, 32, 128)


def late_grads_kernel(
    core, left, rows, ylo, yhi, early, keep, send, turned, pairs, sums, whole, shifted
):
    all_rows(rows, ylo, yhi, shifted, (2,))
    sums[...] = early[0:32].astype(F32).reshape(1024, 128)
    fine_grads(left, shifted, turned, pairs, sums, LATE)
    whole[0:32] = sums[...].astype(BF16).reshape(32, 32, 128)
    whole[32:96] = early[32:96]
    keep[...] = whole[pl.ds(core[0] * 48, 48)]
    send[...] = whole[pl.ds((1 - core[0]) * 48, 48)]


def features_kernel(rows, ylo, yhi, weight, out, done, shifted):
    done[...] = jnp.zeros(done.shape, F32)
    full = jnp.concatenate([ylo[...][None], rows[...], yhi[...][None]], axis=0).astype(F32)
    for a in range(3):
        shifted[a] = rolled_rows(full, 1 - a).astype(BF16).reshape(448, 896)
    for p in range(6):
        lanes = slice(128 * p, 128 * p + 256)
        left = jnp.concatenate(
            [shifted[a, 32 * b : 32 * b + 384, lanes] for a in range(3) for b in range(3)], axis=1
        )
        grad = jnp.dot(left, weight[...], preferred_element_type=F32)
        grad = grad.reshape(12, 32, 128)[:, 0:24, :]
        out[:, :, 128 * p : 128 * p + 128] = grad.astype(BF16)


def combine_kernel(count, parts, *refs):
    at, ins, outs = refs[0], refs[1 : 1 + parts], refs[1 + parts :]
    size = outs[0].shape[0]
    for k in range(count):
        start = lax.rem(at[0] + k, count) * size
        terms = [ref[pl.ds(start, size)].astype(F32) for ref in ins]
        while len(terms) > 1:
            terms = [sum(terms[i : i + 2][1:], terms[i]) for i in range(0, len(terms), 2)]
        outs[k][...] = terms[0].astype(outs[k].dtype)


def combine(values, place, count, after=()):
    size = values[0].shape[0] // count
    return call(
        functools.partial(combine_kernel, count, len(values)),
        [((size, 32, 128), BF16)] * count, values, place=place, after=after,
    )


def place_kernel(count, *refs):
    at, ins, out = refs[0], refs[1 : 1 + count], refs[-1]
    size = ins[0].shape[0]
    for k in range(count):
        out[pl.ds(lax.rem(at[0] + count - k, count) * size, size)] = ins[k][...]


def placed(values, place, after=()):
    count = len(values)
    size = values[0].shape[0]
    return call(
        functools.partial(place_kernel, count),
        [((count * size, 32, 128), BF16)], values, place=place, after=after,
    )[0]


def last_kernel(core, own, other, fine, coarse, whole):
    whole[pl.ds(core[0] * 48, 48)] = own[...]
    whole[pl.ds((1 - core[0]) * 48, 48)] = other[...]
    cells = 96 * 96 * 96
    for r in range(96):
        value = whole[r].astype(F32)[0:27]
        if r < 32:
            fine[:, 128 * r : 128 * r + 128] = value * (1.0 / math.sqrt(cells))
        else:
            at = 128 * (r - 32)
            coarse[:, at : at + 128] = value * (1.0 / math.sqrt(cells // 8))


def core_partner(value):
    return lax.ppermute(value, "gx", [(i, i ^ 1) for i in range(4)])


def matched(first, second, axis):
    count = lax.axis_size(axis)
    low = [(i, (i - 1 + 2 * (i % 2)) % count) for i in range(count)]
    high = [(i, (i + 1 - 2 * (i % 2)) % count) for i in range(count)]
    return lax.ppermute(first, axis, low), lax.ppermute(second, axis, high)


def z_partner(value, far):
    return lax.ppermute(value, "gy", [(i, i ^ far) for i in range(8)])


def y_turn(value, step):
    pairs = [(i, i // 4 * 4 + (i + step) % 4) for i in range(8)]
    return lax.ppermute(value, "gz", pairs)


def x_turn(value, step):
    pairs = []
    for gx in range(4):
        for gz in range(8):
            x = (gz // 4 * 2 + gx // 2 + step) % 4
            pairs.append((gx * 8 + gz, (x % 2 * 2 + gx % 2) * 8 + x // 2 * 4 + gz % 4))
    return lax.ppermute(value, ("gx", "gz"), pairs)


def body(features, fine_weight, coarse_weight, cotangent):
    gx = lax.axis_index("gx").astype(jnp.int32)
    gz = lax.axis_index("gz").astype(jnp.int32)
    core = (gx % 2).reshape(1)
    y_at = (gz % 4).reshape(1)
    x_at = (gz // 4 * 2 + gx // 2).reshape(1)
    z_at = jnp.zeros((1,), jnp.int32)
    z_odd = (gz % 2).reshape(1)

    own = jnp.transpose(features, (1, 0, 2))
    zl, zh = call(
        z_faces_kernel, [((6, 40, 128), BF16)] * 2, (own, cotangent),
        [
            pltpu.VMEM((2, 12, 24, 128), BF16), pltpu.VMEM((2, 12, 6, 128), BF16),
            pltpu.VMEM((12, 8, 128), F32), pltpu.SemaphoreType.DMA((4,)),
        ],
        space=HBM, place=z_odd,
    )
    zlo, zhi = matched(zl, zh, "gz")
    w_fine, frows = call(
        forward_weights_kernel, [((2304, 128), BF16), ((12, 32, 896), BF16)], (fine_weight, own),
        [pltpu.VMEM((1728, 128), F32)], after=(zh,),
    )
    frows, crows, xl, xh = call(
        x_faces_kernel,
        [((12, 32, 896), BF16), ((6, 16, 1024), BF16), ((24, 1024), BF16), ((24, 1024), BF16)],
        (frows, jnp.transpose(cotangent, (1, 0, 2)), zlo, zhi),
        [
            pltpu.VMEM((2, 12, 8, 896), F32), pltpu.VMEM((6, 16, 1024), F32),
            pltpu.VMEM((24, 1024), F32),
        ],
        place=(core, z_odd),
    )
    xlo, xhi = matched(xl, xh, "gx")
    frows, crows, yl, yh = call(
        y_faces_kernel,
        [((12, 32, 896), BF16), ((6, 16, 1024), BF16), ((48, 1024), BF16), ((48, 1024), BF16)],
        (frows, crows, xlo, xhi),
        [
            pltpu.VMEM((12, 32, 896), F32), pltpu.VMEM((6, 16, 1024), F32),
            pltpu.VMEM((24, 1024), F32), pltpu.VMEM((24, 1024), F32),
        ],
        place=core,
    )
    ylo = shift(yl, "gy", 1)
    yhi = shift(yh, "gy", -1)
    shifted, act_in, edges, inner = call(
        interior_kernel,
        [((3, 384, 896), BF16), ((320, 768), F32), ((64, 768), BF16), ((4, 16, 384), BF16)],
        (frows, w_fine),
        flops=CONV,
    )
    act_out, pooled, pzl, pzh = call(
        border_kernel,
        [
            ((64, 768), F32), ((6, 16, 384), BF16),
            ((6, 16, 128), BF16), ((6, 16, 128), BF16),
        ],
        (shifted, ylo, yhi, w_fine, edges, inner),
        [pltpu.VMEM((3, 64, 896), BF16)],
        flops=CONV // 6, place=z_odd,
    )
    pzlo, pzhi = matched(pzl, pzh, "gz")
    w_coarse, w_coarse_back, done = call(
        coarse_weights_kernel,
        [((2304, 256), BF16), ((4608, 256), BF16), ((8, 128), F32)],
        (coarse_weight,), [pltpu.VMEM((1792, 128), F32)], after=(pzh,),
    )
    prows, pxl, pxh = call(
        pooled_x_kernel,
        [((6, 16, 640), BF16), ((16, 640), BF16), ((16, 640), BF16)],
        (pooled, pzlo, pzhi),
        [pltpu.VMEM((6, 16, 640), F32), pltpu.VMEM((16, 640), F32)],
        after=(done,), place=(core, z_odd),
    )
    pxlo, pxhi = matched(pxl, pxh, "gx")
    slope, done = call(
        slope_kernel, [((384, 768), BF16), ((8, 128), F32)], (act_in, act_out), after=(pxh,)
    )
    prows, pyl, pyh = call(
        pooled_y_kernel,
        [((6, 16, 640), BF16), ((2, 16, 640), BF16), ((2, 16, 640), BF16)],
        (prows, pxlo, pxhi),
        [pltpu.VMEM((6, 16, 640), F32), pltpu.VMEM((16, 640), F32), pltpu.VMEM((16, 640), F32)],
        after=(done,), place=core,
    )
    pylo = shift(pyl, "gy", 1)
    pyhi = shift(pyh, "gy", -1)
    act, azl, azh, fine_left, coarse_left, pshift = call(
        backward_kernel,
        [
            ((12, 32, 768), BF16), ((6, 24, 128), BF16), ((6, 24, 128), BF16),
            ((128, 2304), BF16), ((256, 512), BF16), ((3, 160, 640), BF16),
        ],
        (prows, pylo, pyhi, crows, ylo, yhi, slope, w_coarse, w_coarse_back),
        [pltpu.VMEM((3, 128, 1024), BF16)],
        flops=CONV, place=z_odd,
    )
    azlo, azhi = matched(azl, azh, "gz")
    (early,) = call(
        early_grads_kernel, [((96, 32, 128), BF16)],
        (coarse_left, pshift, fine_left, frows, ylo, yhi),
        [
            pltpu.VMEM((256, 128), F32), pltpu.VMEM((64, 128), F32),
            pltpu.VMEM((3072, 128), F32), pltpu.VMEM((256, 256), F32),
            pltpu.VMEM((3, 448, 896), BF16),
        ],
        flops=CONV,
    )
    keep, send = call(
        late_grads_kernel,
        [((48, 32, 128), BF16), ((48, 32, 128), BF16)],
        (fine_left, frows, ylo, yhi, early),
        [
            pltpu.VMEM((256, 128), F32), pltpu.VMEM((64, 128), F32),
            pltpu.VMEM((1024, 128), F32), pltpu.VMEM((96, 32, 128), BF16),
            pltpu.VMEM((3, 448, 896), BF16),
        ],
        flops=CONV // 2, place=core, after=(azlo, azhi),
    )

    parts = combine((keep, core_partner(send)), y_at, 4)
    got = tuple(y_turn(parts[k], k) for k in (1, 2, 3))
    arows, axl, axh = call(
        act_x_faces_kernel,
        [((12, 32, 896), BF16), ((16, 896), BF16), ((16, 896), BF16)],
        (act, azlo, azhi),
        [pltpu.VMEM((12, 32, 896), F32), pltpu.VMEM((16, 896), F32)],
        after=(parts[0],), place=(core, z_odd),
    )
    axlo, axhi = matched(axl, axh, "gx")
    parts = combine((parts[0],) + got, x_at, 4, after=(axlo, axhi))
    got = tuple(x_turn(parts[k], k) for k in (1, 2, 3))
    arows, ayl, ayh = call(
        act_y_faces_kernel,
        [((12, 32, 896), BF16), ((32, 896), BF16), ((32, 896), BF16)],
        (arows, axlo, axhi),
        [pltpu.VMEM((12, 32, 896), F32), pltpu.VMEM((16, 896), F32), pltpu.VMEM((16, 896), F32)],
        after=(parts[0],), place=core,
    )
    aylo = shift(ayl, "gy", 1)
    ayhi = shift(ayh, "gy", -1)
    (part,) = combine((parts[0],) + got, z_at, 1, after=(aylo, ayhi))
    near, next_near, far = (z_partner(part, k) for k in (1, 2, 3))
    w_fine_back, done = call(
        backward_weights_kernel, [((2304, 128), BF16), ((8, 128), F32)],
        (fine_weight,), [pltpu.VMEM((1792, 128), F32)], after=(part,),
    )
    (part,) = combine((part, near, next_near, far), z_at, 1, after=(done,))
    (part,) = combine((part, z_partner(part, 7)), z_at, 1)
    part = placed((part,) + tuple(x_turn(part, k) for k in (1, 2, 3)), x_at)
    got = tuple(y_turn(part, k) for k in (1, 2, 3))
    grad_features, done = call(
        features_kernel,
        [((12, 24, 768), BF16), ((8, 128), F32)],
        (arows, aylo, ayhi, w_fine_back),
        [pltpu.VMEM((3, 448, 896), BF16)],
        flops=CONV, after=(part,),
    )
    part = placed((part,) + got, y_at, after=(done,))
    fine, coarse = call(
        last_kernel,
        [((27, 4096), F32), ((27, 8192), F32)],
        (part, core_partner(part)),
        [pltpu.VMEM((96, 32, 128), BF16)],
        place=core,
    )
    return jnp.transpose(grad_features, (1, 0, 2)), fine, coarse


def solution(mesh):
    in_specs = (P("gx", "gy", "gz"), P(), P(), P("gx", "gy", "gz"))
    out_specs = (P("gx", "gy", "gz"), P(), P())
    return jax.shard_map(body, mesh=mesh, in_specs=in_specs, out_specs=out_specs, check_vma=False)
```

```python
import functools
import math

import jax
import jax.numpy as jnp
from jax import lax
from jax.experimental import pallas as pl
from jax.experimental.pallas import tpu as pltpu
from jax.sharding import PartitionSpec as P

F32 = jnp.float32
BF16 = jnp.bfloat16
VMEM = pl.BlockSpec(memory_space=pltpu.VMEM)
SMEM = pl.BlockSpec(memory_space=pltpu.SMEM)
ANY = pl.BlockSpec(memory_space=pl.ANY)
HBM = pl.BlockSpec(memory_space=pltpu.HBM)
CONV = 2 * 384 * 6 * 2304 * 256


def shift(value, axis, step):
    count = lax.axis_size(axis)
    return lax.ppermute(value, axis, [(i, (i + step) % count) for i in range(count)])


def call(kernel, outs, operands, scratch=(), flops=0, place=None, after=(), space=VMEM):
    moved = sum(math.prod(v.shape) * v.dtype.itemsize for v in operands)
    moved += sum(math.prod(s) * jnp.dtype(d).itemsize for s, d in outs)
    extra = () if place is None else place if isinstance(place, tuple) else (place,)
    first, last = len(extra) + len(operands), len(extra) + len(operands) + len(after)

    def run(*refs):
        kernel(*refs[:first], *refs[last:])

    return pl.pallas_call(
        run,
        out_shape=[jax.ShapeDtypeStruct(s, d) for s, d in outs],
        in_specs=[SMEM] * len(extra) + [space] * len(operands) + [ANY] * len(after),
        out_specs=[VMEM] * len(outs),
        scratch_shapes=list(scratch),
        compiler_params=pltpu.CompilerParams(vmem_limit_bytes=16 * 1024 * 1024),
        cost_estimate=pl.CostEstimate(flops=flops // 8, bytes_accessed=moved // 8, transcendentals=0),
    )(*extra, *operands, *after)


def low_half(shape):
    return lax.broadcasted_iota(jnp.int32, shape, len(shape) - 1) < 64


def swap(value):
    return pltpu.roll(value, 64, value.ndim - 1)


def rolled_rows(value, step):
    return pltpu.roll(value, step % value.shape[-2], value.ndim - 2)


def pair_up(odd, first, second):
    up = first[...].astype(F32)
    down = second[...].astype(F32)
    first[...] = jnp.where(odd, up, down).astype(BF16)
    second[...] = jnp.where(odd, down, up).astype(BF16)


def sides(odd, first, second):
    one = first[...].astype(F32)
    two = second[...].astype(F32)
    return jnp.where(odd, two, one), jnp.where(odd, one, two)


def pack_faces(low, high):
    mask = low_half((6, 24, 128))
    to_high = jnp.where(mask, swap(high[:6]), high[6:])
    to_low = jnp.where(mask, low[:6], swap(low[6:]))
    return to_high, to_low


def with_faces(own, lo, hi):
    mask = low_half((6, 24, 128))
    first = jnp.where(mask, hi, swap(lo))
    second = jnp.where(mask, swap(hi), lo)
    full = jnp.concatenate([own, jnp.concatenate([first, second], axis=0)], axis=2)
    return pltpu.roll(full, 64, 2)


def flat_fine(fine, flat):
    mask = low_half((27, 128))
    for k in range(32):
        value = fine[:, 128 * k : 128 * k + 128].astype(F32)
        turned = swap(value)
        flat[pl.ds(2 * k, 27, stride=64), :] = jnp.where(mask, value, turned)
        flat[pl.ds(2 * k + 1, 27, stride=64), :] = jnp.where(mask, turned, value)


def forward_weights_kernel(fine, own, wf, rows_out, flat):
    wide = jnp.concatenate([own[...].astype(F32), jnp.zeros((12, 24, 128), F32)], axis=2)
    rows_out[:, 0:24, :] = pltpu.roll(wide, 64, 2).astype(BF16)
    rows_out[:, 24:32, :] = jnp.zeros((12, 8, 896), BF16)
    flat_fine(fine, flat)
    mask = low_half((64, 128))
    none = jnp.zeros((64, 128), F32)
    for ab in range(9):
        for j in range(4):
            row = (4 * ab + j) * 64
            at = (3 * ab + j) * 64
            left = flat[at : at + 64, :] if j < 3 else none
            right = flat[at - 64 : at, :] if j > 0 else none
            wf[row : row + 64, :] = jnp.where(mask, left, right).astype(BF16)


def coarse_weights_kernel(coarse, wc, wcb, done, flat):
    done[...] = jnp.zeros(done.shape, F32)
    for c in range(64):
        flat[pl.ds(c, 27, stride=64), :] = coarse[:, 128 * c : 128 * c + 128].astype(F32)
    flat[1728:1792, :] = jnp.zeros((64, 128), F32)
    wide = low_half((128, 128))
    none = jnp.zeros((64, 128), F32)
    zero = jnp.zeros((128, 128), F32)
    turned = []
    for m in range(14):
        value = flat[128 * m : 128 * m + 128, :].T
        turned += [jnp.where(wide, value, swap(value)), jnp.where(wide, swap(value), value)]
    for ab in range(9):
        for j in range(4):
            row = (4 * ab + j) * 64
            at = (3 * ab + j) * 64
            left = flat[at : at + 64, :] if j < 3 else none
            right = flat[at - 64 : at, :] if j > 0 else none
            wc[row : row + 64, 0:128] = left.astype(BF16)
            wc[row : row + 64, 128:256] = right.astype(BF16)
            slot = 26 - 3 * ab - j
            row = 2 * row
            left = turned[slot] if j < 3 else zero
            right = turned[slot + 1] if j > 0 else zero
            wcb[row : row + 128, 0:128] = left.astype(BF16)
            wcb[row : row + 128, 128:256] = right.astype(BF16)


def backward_weights_kernel(fine, wfb, done, flat):
    done[...] = jnp.zeros(done.shape, F32)
    flat_fine(fine, flat)
    flat[1728:1792, :] = jnp.zeros((64, 128), F32)
    mask = low_half((64, 128))
    none = jnp.zeros((64, 128), F32)
    turned = []
    for m in range(14):
        value = flat[128 * m : 128 * m + 128, :].T[0:64]
        turned += [jnp.where(mask, value, swap(value)), jnp.where(mask, swap(value), value)]
    for ab in range(9):
        for j in range(4):
            row = (4 * ab + j) * 64
            slot = 26 - 3 * ab - j
            left = turned[slot] if j < 3 else none
            right = turned[slot + 1] if j > 0 else none
            wfb[row : row + 64, :] = jnp.where(mask, left, right).astype(BF16)


def z_faces_kernel(own, cot, zl, zh, faces, cfaces, edge, sems):
    copies = []
    for k, lane in enumerate((0, 640)):
        lanes = pl.ds(lane, 128)
        copies.append(pltpu.make_async_copy(own.at[:, :, lanes], faces.at[k], sems.at[2 * k]))
        copies.append(pltpu.make_async_copy(cot.at[:, :, lanes], cfaces.at[k], sems.at[2 * k + 1]))
    for copy in copies:
        copy.start()
    for copy in copies:
        copy.wait()
    to_high, to_low = pack_faces(faces[0].astype(F32), faces[1].astype(F32))
    for out, face, k in ((zl, to_high, 1), (zh, to_low, 0)):
        edge[:, 0:6, :] = cfaces[k].astype(F32)
        turned = [edge[:, y : y + 1, :].reshape(12, 128)[None] for y in range(6)]
        turned = jnp.concatenate(turned, axis=0)
        pad = jnp.zeros((6, 4, 128), F32)
        out[...] = jnp.concatenate([face, turned, pad], axis=1).astype(BF16)


def edge_lanes(lo, hi):
    low = jnp.concatenate([lo, swap(lo)], axis=0)
    high = jnp.concatenate([swap(hi), hi], axis=0)
    return low, high


def x_faces_kernel(own, cot, zlo, zhi, rows_out, cot_out, xl, xh, ends, crows, message):
    lo = zlo[...].astype(F32)
    hi = zhi[...].astype(F32)
    low, high = edge_lanes(lo[:, 0:24], hi[:, 0:24])
    mask = low_half((12, 24, 128))
    rows_out[...] = own[...]
    for at, part in ((0, jnp.where(mask, low, 0.0)), (768, jnp.where(mask, 0.0, high))):
        lanes = slice(at, at + 128)
        rows_out[:, 0:24, lanes] = (own[:, 0:24, lanes].astype(F32) + part).astype(BF16)
    crows[:, 8:16, :] = jnp.zeros((6, 8, 1024), F32)
    crows[:, 0:12, 0:128] = lo[:, 24:36]
    crows[:, 0:12, 128:896] = cot[...].astype(F32)
    crows[:, 0:12, 896:1024] = hi[:, 24:36]
    cot_out[...] = crows[...].astype(BF16)
    ends[0] = rows_out[:, 0:8, :].astype(F32)
    ends[1] = rows_out[:, 16:24, :].astype(F32)
    message[...] = jnp.zeros(message.shape, F32)
    for out, k, x, cx in ((xl, 1, 7, 11), (xh, 0, 0, 0)):
        for y in range(12):
            message[y : y + 1, 0:896] = ends[k, y, x : x + 1, :]
        for y in range(6):
            message[12 + y : 13 + y, :] = crows[y, cx : cx + 1, :]
        out[...] = message[...].astype(BF16)


def y_faces_kernel(
    rows_in, cot_in, xlo, xhi, rows_out, cot_out, yl, yh, rows, crows, lo, hi
):
    lo[...] = xlo[...].astype(F32)
    hi[...] = xhi[...].astype(F32)
    rows[...] = rows_in[...].astype(F32)
    crows[...] = cot_in[...].astype(F32)
    for y in range(12):
        rows[y, 24:25, :] = hi[y : y + 1, 0:896]
        rows[y, 31:32, :] = lo[y : y + 1, 0:896]
    for y in range(6):
        crows[y, 12:13, :] = hi[12 + y : 13 + y, :]
        crows[y, 15:16, :] = lo[12 + y : 13 + y, :]
    rows_out[...] = rows[...].astype(BF16)
    cot_out[...] = crows[...].astype(BF16)
    for out, y, cy in ((yl, 11, 5), (yh, 0, 0)):
        out[0:32, 0:896] = rows[y].astype(BF16)
        out[0:32, 896:1024] = jnp.zeros((32, 128), BF16)
        out[32:48, :] = crows[cy].astype(BF16)


def act_x_faces_kernel(core, z_odd, own, zlo, zhi, rows_out, xl, xh, rows, message):
    z_lo, z_hi = sides(z_odd[0] == 1, zlo, zhi)
    rows[:, 0:24, :] = with_faces(own[...].astype(F32)[:, 0:24], z_lo, z_hi)
    rows[:, 24:32, :] = jnp.zeros((12, 8, 896), F32)
    rows_out[...] = rows[...].astype(BF16)
    message[...] = jnp.zeros(message.shape, F32)
    for out, x in ((xl, 23), (xh, 0)):
        for y in range(12):
            message[y : y + 1, :] = rows[y, x : x + 1, :]
        out[...] = message[...].astype(BF16)
    pair_up(core[0] == 1, xl, xh)


def act_y_faces_kernel(core, rows_in, xlo, xhi, rows_out, yl, yh, rows, lo, hi):
    lo[...], hi[...] = sides(core[0] == 1, xlo, xhi)
    rows[...] = rows_in[...].astype(F32)
    for y in range(12):
        rows[y, 24:25, :] = hi[y : y + 1, :]
        rows[y, 31:32, :] = lo[y : y + 1, :]
    value = rows[...].astype(BF16)
    rows_out[...] = value
    yl[...] = value[11]
    yh[...] = value[0]


def sigmoid(value):
    return 0.5 + 0.5 * jnp.tanh(0.5 * value)


def silu(act):
    return (act * sigmoid(act)).astype(BF16)


def silu_slope(act):
    sigma = sigmoid(act)
    return sigma * (1.0 + act * (1.0 - sigma))


def slope_kernel(inner, outer, slope, done):
    slope[0:32, :] = silu_slope(outer[0:32, :]).astype(BF16)
    slope[32:352, :] = silu_slope(inner[...]).astype(BF16)
    slope[352:384, :] = silu_slope(outer[32:64, :]).astype(BF16)
    done[...] = jnp.zeros(done.shape, F32)


def pool_matrix(shape, rule):
    r = lax.broadcasted_iota(jnp.int32, shape, 0)
    q = lax.broadcasted_iota(jnp.int32, shape, 1)
    return jnp.where(rule(r, q), 0.125, 0.0).astype(BF16)


def fold_pairs(part):
    return part + swap(part)


def interior_kernel(rows, weight, shifted, kept, edges, pooled):
    full = rows[...].astype(F32)
    for a in range(3):
        shifted[a] = rolled_rows(full, 1 - a).astype(BF16).reshape(384, 896)
    pool = pool_matrix(
        (64, 320),
        lambda r, q: ((((q >> 5) + 1) >> 1) == (r >> 4) + 1) & (((q & 31) >> 1) == (r & 15)),
    )
    mask = low_half((64, 128))
    for p in range(6):
        lanes = slice(128 * p, 128 * p + 256)
        left = jnp.concatenate(
            [shifted[a, 32 * b : 32 * b + 320, lanes] for a in range(3) for b in range(3)], axis=1
        )
        kept[:, 128 * p : 128 * p + 128] = jnp.dot(
            left, weight[...], preferred_element_type=F32
        )
    hidden = silu(kept[...])
    edges[0:32, :] = hidden[0:32]
    edges[32:64, :] = hidden[288:320]
    sums = jnp.dot(pool, hidden, preferred_element_type=F32)
    pieces = [fold_pairs(sums[:, 128 * p : 128 * p + 128]) for p in range(6)]
    for j in range(3):
        both = jnp.where(mask, pieces[2 * j], pieces[2 * j + 1])
        pooled[:, :, 128 * j : 128 * j + 128] = both.astype(BF16).reshape(4, 16, 128)


def border_kernel(
    z_odd, shifted, ylo, yhi, weight, edges, inner, kept, pooled, zl, zh, outer
):
    both = jnp.concatenate(
        [ylo[0:32, 0:896][None], yhi[0:32, 0:896][None]], axis=0
    ).astype(F32)
    for a in range(3):
        outer[a] = rolled_rows(both, 1 - a).astype(BF16).reshape(64, 896)
    blocks = []
    for p in range(6):
        lanes = slice(128 * p, 128 * p + 256)
        first = []
        last = []
        for a in range(3):
            first += [outer[a, 0:32, lanes], shifted[a, 0:32, lanes], shifted[a, 32:64, lanes]]
            last += [
                shifted[a, 320:352, lanes], shifted[a, 352:384, lanes], outer[a, 32:64, lanes]
            ]
        blocks.append(jnp.concatenate(first, axis=1))
        blocks.append(jnp.concatenate(last, axis=1))
    act = jnp.dot(jnp.concatenate(blocks, axis=0), weight[...], preferred_element_type=F32)
    hidden = silu(act)
    pool = pool_matrix(
        (32, 128),
        lambda r, q: (((q >> 5) & 1) == (r >> 4)) & (((q & 31) >> 1) == (r & 15)),
    )
    mask = low_half((32, 128))
    pieces = []
    for p in range(6):
        own = slice(128 * p, 128 * p + 128)
        kept[:, own] = act[64 * p : 64 * p + 64]
        column = jnp.concatenate([hidden[64 * p : 64 * p + 64], edges[:, own]], axis=0)
        pieces.append(fold_pairs(jnp.dot(pool, column, preferred_element_type=F32)))
    for j in range(3):
        own = slice(128 * j, 128 * j + 128)
        both = jnp.where(mask, pieces[2 * j], pieces[2 * j + 1]).astype(BF16)
        pooled[0:1, :, own] = both[0:16][None]
        pooled[5:6, :, own] = both[16:32][None]
    pooled[1:5] = inner[...]
    zl[...] = pooled[:, :, 256:384]
    zh[...] = pooled[:, :, 0:128]
    pair_up(z_odd[0] == 1, zl, zh)


def pooled_x_kernel(core, z_odd, own, zlo, zhi, rows_out, xl, xh, rows, message):
    rows[:, :, 0:128], rows[:, :, 512:640] = sides(z_odd[0] == 1, zlo, zhi)
    rows[:, :, 128:512] = own[...].astype(F32)
    rows_out[...] = rows[...].astype(BF16)
    message[...] = jnp.zeros(message.shape, F32)
    for out, x in ((xl, 10), (xh, 0)):
        for y in range(6):
            message[2 * y : 2 * y + 2, :] = rows[y, x : x + 2, :]
        out[...] = message[...].astype(BF16)
    pair_up(core[0] == 1, xl, xh)


def pooled_y_kernel(core, rows_in, xlo, xhi, rows_out, yl, yh, rows, lo, hi):
    lo[...], hi[...] = sides(core[0] == 1, xlo, xhi)
    rows[...] = rows_in[...].astype(F32)
    for y in range(6):
        rows[y, 12:14, :] = hi[2 * y : 2 * y + 2, :]
        rows[y, 14:16, :] = lo[2 * y : 2 * y + 2, :]
    value = rows[...].astype(BF16)
    rows_out[...] = value
    yl[...] = value[4:6]
    yh[...] = value[0:2]


def backward_kernel(
    z_odd, prow, pylo, pyhi, crow, ylo, yhi, slope, wc, wb,
    act_out, zl, zh, fine_left, coarse_left, pshift, gshift,
):
    full = jnp.concatenate([pylo[...], prow[...], pyhi[...]], axis=0).astype(F32)
    for a in range(3):
        pshift[a] = rolled_rows(full, 1 - a).astype(BF16).reshape(160, 640)
    blocks = []
    for p in range(4):
        lanes = slice(128 * p, 128 * p + 256)
        blocks.append(
            jnp.concatenate(
                [pshift[a, 16 * b : 16 * b + 128, lanes] for a in range(3) for b in range(3)], axis=1
            )
        )
    pre = jnp.dot(jnp.concatenate(blocks, axis=0), wc[...], preferred_element_type=F32)
    tilt = silu_slope(pre)
    cot = jnp.concatenate([ylo[32:48][None], crow[...], yhi[32:48][None]], axis=0).astype(F32)
    row = lax.broadcasted_iota(jnp.int32, (128, 256), 0)
    lane = lax.broadcasted_iota(jnp.int32, (128, 256), 1)
    own_rows = (row >= 16) & (row < 112) & ((row & 15) < 12)
    parts = []
    for p in range(4):
        grad = cot[:, :, 256 * p : 256 * p + 256].reshape(128, 256) * tilt[128 * p : 128 * p + 128]
        grad = grad.astype(BF16).astype(F32)
        parts.append(grad)
        valid = own_rows
        if p == 0:
            valid = valid & (lane >= 128)
        if p == 3:
            valid = valid & (lane < 128)
        coarse_left[:, 128 * p : 128 * p + 128] = jnp.where(valid, grad, 0.0).T.astype(BF16)
    both = jnp.concatenate(parts, axis=1).reshape(8, 16, 1024)
    for a in range(3):
        gshift[a] = rolled_rows(both, 1 - a).astype(BF16).reshape(128, 1024)
    blocks = []
    for p in range(3):
        lanes = slice(256 * p, 256 * p + 512)
        blocks.append(
            jnp.concatenate(
                [gshift[a, 16 * b : 16 * b + 96, lanes] for a in range(3) for b in range(3)], axis=1
            )
        )
    small = jnp.dot(jnp.concatenate(blocks, axis=0), wb[...], preferred_element_type=F32)
    small = small.astype(BF16)
    q = lax.broadcasted_iota(jnp.int32, (384, 96), 0)
    r = lax.broadcasted_iota(jnp.int32, (384, 96), 1)
    inside = ((q >> 6) == (r >> 4)) & (((q & 31) >> 1) == (r & 15)) & ((q & 31) < 24)
    spread = jnp.where(inside, 1.0, 0.0).astype(BF16)
    for p in range(3):
        lanes = slice(256 * p, 256 * p + 256)
        up = jnp.dot(spread, small[96 * p : 96 * p + 96], preferred_element_type=F32)
        part = (up * 0.125 * slope[:, lanes].astype(F32)).astype(BF16)
        act_out[:, :, lanes] = part.reshape(12, 32, 256)
        wide = part.astype(F32)
        fine_left[:, 768 * p : 768 * p + 384] = wide[:, 0:128].T.astype(BF16)
        fine_left[:, 768 * p + 384 : 768 * p + 768] = wide[:, 128:256].T.astype(BF16)
        if p == 0:
            low = wide[:, 0:128].reshape(12, 32, 128)[:, 0:24]
        if p == 2:
            high = wide[:, 128:256].reshape(12, 32, 128)[:, 0:24]
    to_high, to_low = pack_faces(low, high)
    zl[...] = to_high.astype(BF16)
    zh[...] = to_low.astype(BF16)
    pair_up(z_odd[0] == 1, zl, zh)


def all_rows(rows, ylo, yhi, shifted, used):
    lo = ylo[0:32, 0:896][None]
    hi = yhi[0:32, 0:896][None]
    full = jnp.concatenate([lo, rows[...], hi], axis=0).astype(F32)
    for a in used:
        shifted[a] = rolled_rows(full, 1 - a).astype(BF16).reshape(448, 896)


def fine_grads(left, shifted, turned, pairs, sums, offsets):
    mask = low_half((32, 128))
    for a, b in offsets:
        right = jnp.concatenate(
            [shifted[a, 32 * b : 32 * b + 384, 128 * p : 128 * p + 256] for p in range(6)], axis=0
        )
        turned[...] = jnp.dot(left[...], right, preferred_element_type=F32).T
        for e in range(3):
            near = turned[64 * e : 64 * e + 64]
            pairs[...] = near + swap(turned[64 * e + 64 : 64 * e + 128])
            even = pairs[pl.ds(0, 32, stride=2), :]
            odd = pairs[pl.ds(1, 32, stride=2), :]
            slot = 9 * a + 3 * b + e
            sums[pl.ds(slot, 32, stride=32), :] = jnp.where(mask, even, swap(odd))


EARLY = [(0, 0), (0, 1), (0, 2), (1, 0), (1, 1), (1, 2), (2, 0), (2, 1)]
LATE = [(2, 2)]


def early_grads_kernel(
    coarse_left, pshift, left, rows, ylo, yhi, out, turned, pairs, sums, cturned, shifted
):
    all_rows(rows, ylo, yhi, shifted, (0, 1, 2))
    sums[...] = jnp.zeros(sums.shape, F32)
    for a in range(3):
        for b in range(3):
            right = jnp.concatenate(
                [pshift[a, 16 * b : 16 * b + 128, 128 * p : 128 * p + 256] for p in range(4)], axis=0
            )
            cturned[...] = jnp.dot(coarse_left[...], right, preferred_element_type=F32).T
            for e in range(3):
                near = cturned[64 * e : 64 * e + 64, 0:128]
                far = cturned[64 * e + 64 : 64 * e + 128, 128:256]
                sums[pl.ds(1024 + 9 * a + 3 * b + e, 64, stride=32), :] = near + far
    fine_grads(left, shifted, turned, pairs, sums, EARLY)
    out[...] = sums[...].astype(BF16).reshape(96, 32, 128)


def late_grads_kernel(
    core, left, rows, ylo, yhi, early, keep, send, turned, pairs, sums, whole, shifted
):
    all_rows(rows, ylo, yhi, shifted, (2,))
    sums[...] = early[0:32].astype(F32).reshape(1024, 128)
    fine_grads(left, shifted, turned, pairs, sums, LATE)
    whole[0:32] = sums[...].astype(BF16).reshape(32, 32, 128)
    whole[32:96] = early[32:96]
    keep[...] = whole[pl.ds(core[0] * 48, 48)]
    send[...] = whole[pl.ds((1 - core[0]) * 48, 48)]


def features_kernel(rows, ylo, yhi, weight, out, done, shifted):
    done[...] = jnp.zeros(done.shape, F32)
    full = jnp.concatenate([ylo[...][None], rows[...], yhi[...][None]], axis=0).astype(F32)
    for a in range(3):
        shifted[a] = rolled_rows(full, 1 - a).astype(BF16).reshape(448, 896)
    for p in range(6):
        lanes = slice(128 * p, 128 * p + 256)
        left = jnp.concatenate(
            [shifted[a, 32 * b : 32 * b + 384, lanes] for a in range(3) for b in range(3)], axis=1
        )
        grad = jnp.dot(left, weight[...], preferred_element_type=F32)
        grad = grad.reshape(12, 32, 128)[:, 0:24, :]
        out[:, :, 128 * p : 128 * p + 128] = grad.astype(BF16)


def combine_kernel(count, parts, *refs):
    at, ins, outs = refs[0], refs[1 : 1 + parts], refs[1 + parts :]
    size = outs[0].shape[0]
    for k in range(count):
        start = lax.rem(at[0] + k, count) * size
        terms = [ref[pl.ds(start, size)].astype(F32) for ref in ins]
        while len(terms) > 1:
            terms = [sum(terms[i : i + 2][1:], terms[i]) for i in range(0, len(terms), 2)]
        outs[k][...] = terms[0].astype(outs[k].dtype)


def combine(values, place, count, after=()):
    size = values[0].shape[0] // count
    return call(
        functools.partial(combine_kernel, count, len(values)),
        [((size, 32, 128), BF16)] * count, values, place=place, after=after,
    )


def place_kernel(count, *refs):
    at, ins, out = refs[0], refs[1 : 1 + count], refs[-1]
    size = ins[0].shape[0]
    for k in range(count):
        out[pl.ds(lax.rem(at[0] + count - k, count) * size, size)] = ins[k][...]


def placed(values, place, after=()):
    count = len(values)
    size = values[0].shape[0]
    return call(
        functools.partial(place_kernel, count),
        [((count * size, 32, 128), BF16)], values, place=place, after=after,
    )[0]


def last_kernel(core, own, other, fine, coarse, whole):
    whole[pl.ds(core[0] * 48, 48)] = own[...]
    whole[pl.ds((1 - core[0]) * 48, 48)] = other[...]
    cells = 96 * 96 * 96
    for r in range(96):
        value = whole[r].astype(F32)[0:27]
        if r < 32:
            fine[:, 128 * r : 128 * r + 128] = value * (1.0 / math.sqrt(cells))
        else:
            at = 128 * (r - 32)
            coarse[:, at : at + 128] = value * (1.0 / math.sqrt(cells // 8))


def core_partner(value):
    return lax.ppermute(value, "gx", [(i, i ^ 1) for i in range(4)])


def matched(first, second, axis):
    count = lax.axis_size(axis)
    low = [(i, (i - 1 + 2 * (i % 2)) % count) for i in range(count)]
    high = [(i, (i + 1 - 2 * (i % 2)) % count) for i in range(count)]
    return lax.ppermute(first, axis, low), lax.ppermute(second, axis, high)


def z_partner(value, far):
    return lax.ppermute(value, "gy", [(i, i ^ far) for i in range(8)])


def y_turn(value, step):
    pairs = [(i, i // 4 * 4 + (i + step) % 4) for i in range(8)]
    return lax.ppermute(value, "gz", pairs)


def x_turn(value, step):
    pairs = []
    for gx in range(4):
        for gz in range(8):
            x = (gz // 4 * 2 + gx // 2 + step) % 4
            pairs.append((gx * 8 + gz, (x % 2 * 2 + gx % 2) * 8 + x // 2 * 4 + gz % 4))
    return lax.ppermute(value, ("gx", "gz"), pairs)


def body(features, fine_weight, coarse_weight, cotangent):
    gx = lax.axis_index("gx").astype(jnp.int32)
    gz = lax.axis_index("gz").astype(jnp.int32)
    core = (gx % 2).reshape(1)
    y_at = (gz % 4).reshape(1)
    x_at = (gz // 4 * 2 + gx // 2).reshape(1)
    z_at = jnp.zeros((1,), jnp.int32)
    z_odd = (gz % 2).reshape(1)

    own = jnp.transpose(features, (1, 0, 2))
    zl, zh = call(
        z_faces_kernel, [((6, 40, 128), BF16)] * 2, (own, cotangent),
        [
            pltpu.VMEM((2, 12, 24, 128), BF16), pltpu.VMEM((2, 12, 6, 128), BF16),
            pltpu.VMEM((12, 8, 128), F32), pltpu.SemaphoreType.DMA((4,)),
        ],
        space=HBM,
    )
    zlo = shift(zl, "gz", 1)
    zhi = shift(zh, "gz", -1)
    w_fine, frows = call(
        forward_weights_kernel, [((2304, 128), BF16), ((12, 32, 896), BF16)], (fine_weight, own),
        [pltpu.VMEM((1728, 128), F32)], after=(zl,),
    )
    frows, crows, xl, xh = call(
        x_faces_kernel,
        [((12, 32, 896), BF16), ((6, 16, 1024), BF16), ((24, 1024), BF16), ((24, 1024), BF16)],
        (frows, jnp.transpose(cotangent, (1, 0, 2)), zlo, zhi),
        [
            pltpu.VMEM((2, 12, 8, 896), F32), pltpu.VMEM((6, 16, 1024), F32),
            pltpu.VMEM((24, 1024), F32),
        ],
    )
    xlo = shift(xl, "gx", 1)
    xhi = shift(xh, "gx", -1)
    frows, crows, yl, yh = call(
        y_faces_kernel,
        [((12, 32, 896), BF16), ((6, 16, 1024), BF16), ((48, 1024), BF16), ((48, 1024), BF16)],
        (frows, crows, xlo, xhi),
        [
            pltpu.VMEM((12, 32, 896), F32), pltpu.VMEM((6, 16, 1024), F32),
            pltpu.VMEM((24, 1024), F32), pltpu.VMEM((24, 1024), F32),
        ],
    )
    ylo = shift(yl, "gy", 1)
    yhi = shift(yh, "gy", -1)
    shifted, act_in, edges, inner = call(
        interior_kernel,
        [((3, 384, 896), BF16), ((320, 768), F32), ((64, 768), BF16), ((4, 16, 384), BF16)],
        (frows, w_fine),
        flops=CONV,
    )
    act_out, pooled, pzl, pzh = call(
        border_kernel,
        [
            ((64, 768), F32), ((6, 16, 384), BF16),
            ((6, 16, 128), BF16), ((6, 16, 128), BF16),
        ],
        (shifted, ylo, yhi, w_fine, edges, inner),
        [pltpu.VMEM((3, 64, 896), BF16)],
        flops=CONV // 6, place=z_odd,
    )
    pzlo, pzhi = matched(pzl, pzh, "gz")
    w_coarse, w_coarse_back, done = call(
        coarse_weights_kernel,
        [((2304, 256), BF16), ((4608, 256), BF16), ((8, 128), F32)],
        (coarse_weight,), [pltpu.VMEM((1792, 128), F32)], after=(pzh,),
    )
    prows, pxl, pxh = call(
        pooled_x_kernel,
        [((6, 16, 640), BF16), ((16, 640), BF16), ((16, 640), BF16)],
        (pooled, pzlo, pzhi),
        [pltpu.VMEM((6, 16, 640), F32), pltpu.VMEM((16, 640), F32)],
        after=(done,), place=(core, z_odd),
    )
    pxlo, pxhi = matched(pxl, pxh, "gx")
    slope, done = call(
        slope_kernel, [((384, 768), BF16), ((8, 128), F32)], (act_in, act_out), after=(pxh,)
    )
    prows, pyl, pyh = call(
        pooled_y_kernel,
        [((6, 16, 640), BF16), ((2, 16, 640), BF16), ((2, 16, 640), BF16)],
        (prows, pxlo, pxhi),
        [pltpu.VMEM((6, 16, 640), F32), pltpu.VMEM((16, 640), F32), pltpu.VMEM((16, 640), F32)],
        after=(done,), place=core,
    )
    pylo = shift(pyl, "gy", 1)
    pyhi = shift(pyh, "gy", -1)
    act, azl, azh, fine_left, coarse_left, pshift = call(
        backward_kernel,
        [
            ((12, 32, 768), BF16), ((6, 24, 128), BF16), ((6, 24, 128), BF16),
            ((128, 2304), BF16), ((256, 512), BF16), ((3, 160, 640), BF16),
        ],
        (prows, pylo, pyhi, crows, ylo, yhi, slope, w_coarse, w_coarse_back),
        [pltpu.VMEM((3, 128, 1024), BF16)],
        flops=CONV, place=z_odd,
    )
    azlo, azhi = matched(azl, azh, "gz")
    (early,) = call(
        early_grads_kernel, [((96, 32, 128), BF16)],
        (coarse_left, pshift, fine_left, frows, ylo, yhi),
        [
            pltpu.VMEM((256, 128), F32), pltpu.VMEM((64, 128), F32),
            pltpu.VMEM((3072, 128), F32), pltpu.VMEM((256, 256), F32),
            pltpu.VMEM((3, 448, 896), BF16),
        ],
        flops=CONV,
    )
    keep, send = call(
        late_grads_kernel,
        [((48, 32, 128), BF16), ((48, 32, 128), BF16)],
        (fine_left, frows, ylo, yhi, early),
        [
            pltpu.VMEM((256, 128), F32), pltpu.VMEM((64, 128), F32),
            pltpu.VMEM((1024, 128), F32), pltpu.VMEM((96, 32, 128), BF16),
            pltpu.VMEM((3, 448, 896), BF16),
        ],
        flops=CONV // 2, place=core, after=(azlo, azhi),
    )

    parts = combine((keep, core_partner(send)), y_at, 4)
    got = tuple(y_turn(parts[k], k) for k in (1, 2, 3))
    arows, axl, axh = call(
        act_x_faces_kernel,
        [((12, 32, 896), BF16), ((16, 896), BF16), ((16, 896), BF16)],
        (act, azlo, azhi),
        [pltpu.VMEM((12, 32, 896), F32), pltpu.VMEM((16, 896), F32)],
        after=(parts[0],), place=(core, z_odd),
    )
    axlo, axhi = matched(axl, axh, "gx")
    parts = combine((parts[0],) + got, x_at, 4, after=(axlo, axhi))
    got = tuple(x_turn(parts[k], k) for k in (1, 2, 3))
    arows, ayl, ayh = call(
        act_y_faces_kernel,
        [((12, 32, 896), BF16), ((32, 896), BF16), ((32, 896), BF16)],
        (arows, axlo, axhi),
        [pltpu.VMEM((12, 32, 896), F32), pltpu.VMEM((16, 896), F32), pltpu.VMEM((16, 896), F32)],
        after=(parts[0],), place=core,
    )
    aylo = shift(ayl, "gy", 1)
    ayhi = shift(ayh, "gy", -1)
    (part,) = combine((parts[0],) + got, z_at, 1, after=(aylo, ayhi))
    near, next_near, far = (z_partner(part, k) for k in (1, 2, 3))
    w_fine_back, done = call(
        backward_weights_kernel, [((2304, 128), BF16), ((8, 128), F32)],
        (fine_weight,), [pltpu.VMEM((1792, 128), F32)], after=(part,),
    )
    (part,) = combine((part, near, next_near, far), z_at, 1, after=(done,))
    (part,) = combine((part, z_partner(part, 7)), z_at, 1)
    part = placed((part,) + tuple(x_turn(part, k) for k in (1, 2, 3)), x_at)
    got = tuple(y_turn(part, k) for k in (1, 2, 3))
    grad_features, done = call(
        features_kernel,
        [((12, 24, 768), BF16), ((8, 128), F32)],
        (arows, aylo, ayhi, w_fine_back),
        [pltpu.VMEM((3, 448, 896), BF16)],
        flops=CONV, after=(part,),
    )
    part = placed((part,) + got, y_at, after=(done,))
    fine, coarse = call(
        last_kernel,
        [((27, 4096), F32), ((27, 8192), F32)],
        (part, core_partner(part)),
        [pltpu.VMEM((96, 32, 128), BF16)],
        place=core,
    )
    return jnp.transpose(grad_features, (1, 0, 2)), fine, coarse


def solution(mesh):
    in_specs = (P("gx", "gy", "gz"), P(), P(), P("gx", "gy", "gz"))
    out_specs = (P("gx", "gy", "gz"), P(), P())
    return jax.shard_map(body, mesh=mesh, in_specs=in_specs, out_specs=out_specs, check_vma=False)
```

```python
import functools
import math

import jax
import jax.numpy as jnp
from jax import lax
from jax.experimental import pallas as pl
from jax.experimental.pallas import tpu as pltpu
from jax.sharding import PartitionSpec as P

F32 = jnp.float32
BF16 = jnp.bfloat16
VMEM = pl.BlockSpec(memory_space=pltpu.VMEM)
SMEM = pl.BlockSpec(memory_space=pltpu.SMEM)
ANY = pl.BlockSpec(memory_space=pl.ANY)
HBM = pl.BlockSpec(memory_space=pltpu.HBM)
CONV = 2 * 384 * 6 * 2304 * 256


def shift(value, axis, step):
    count = lax.axis_size(axis)
    return lax.ppermute(value, axis, [(i, (i + step) % count) for i in range(count)])


def call(kernel, outs, operands, scratch=(), flops=0, place=None, after=(), space=VMEM):
    moved = sum(math.prod(v.shape) * v.dtype.itemsize for v in operands)
    moved += sum(math.prod(s) * jnp.dtype(d).itemsize for s, d in outs)
    extra = () if place is None else place if isinstance(place, tuple) else (place,)
    first, last = len(extra) + len(operands), len(extra) + len(operands) + len(after)

    def run(*refs):
        kernel(*refs[:first], *refs[last:])

    return pl.pallas_call(
        run,
        out_shape=[jax.ShapeDtypeStruct(s, d) for s, d in outs],
        in_specs=[SMEM] * len(extra) + [space] * len(operands) + [ANY] * len(after),
        out_specs=[VMEM] * len(outs),
        scratch_shapes=list(scratch),
        compiler_params=pltpu.CompilerParams(vmem_limit_bytes=16 * 1024 * 1024),
        cost_estimate=pl.CostEstimate(flops=flops // 8, bytes_accessed=moved // 8, transcendentals=0),
    )(*extra, *operands, *after)


def low_half(shape):
    return lax.broadcasted_iota(jnp.int32, shape, len(shape) - 1) < 64


def swap(value):
    return pltpu.roll(value, 64, value.ndim - 1)


def rolled_rows(value, step):
    return pltpu.roll(value, step % value.shape[-2], value.ndim - 2)


def pair_up(odd, first, second):
    up = first[...].astype(F32)
    down = second[...].astype(F32)
    first[...] = jnp.where(odd, up, down).astype(BF16)
    second[...] = jnp.where(odd, down, up).astype(BF16)


def sides(odd, first, second):
    one = first[...].astype(F32)
    two = second[...].astype(F32)
    return jnp.where(odd, two, one), jnp.where(odd, one, two)


def pack_faces(low, high):
    mask = low_half((6, 24, 128))
    to_high = jnp.where(mask, swap(high[:6]), high[6:])
    to_low = jnp.where(mask, low[:6], swap(low[6:]))
    return to_high, to_low


def with_faces(own, lo, hi):
    mask = low_half((6, 24, 128))
    first = jnp.where(mask, hi, swap(lo))
    second = jnp.where(mask, swap(hi), lo)
    full = jnp.concatenate([own, jnp.concatenate([first, second], axis=0)], axis=2)
    return pltpu.roll(full, 64, 2)


def flat_fine(fine, flat):
    mask = low_half((27, 128))
    for k in range(32):
        value = fine[:, 128 * k : 128 * k + 128].astype(F32)
        turned = swap(value)
        flat[pl.ds(2 * k, 27, stride=64), :] = jnp.where(mask, value, turned)
        flat[pl.ds(2 * k + 1, 27, stride=64), :] = jnp.where(mask, turned, value)


def forward_weights_kernel(fine, own, wf, rows_out, flat):
    wide = jnp.concatenate([own[...].astype(F32), jnp.zeros((12, 24, 128), F32)], axis=2)
    rows_out[:, 0:24, :] = pltpu.roll(wide, 64, 2).astype(BF16)
    rows_out[:, 24:32, :] = jnp.zeros((12, 8, 896), BF16)
    flat_fine(fine, flat)
    mask = low_half((64, 128))
    none = jnp.zeros((64, 128), F32)
    for ab in range(9):
        for j in range(4):
            row = (4 * ab + j) * 64
            at = (3 * ab + j) * 64
            left = flat[at : at + 64, :] if j < 3 else none
            right = flat[at - 64 : at, :] if j > 0 else none
            wf[row : row + 64, :] = jnp.where(mask, left, right).astype(BF16)


def coarse_weights_kernel(coarse, wc, wcb, done, flat):
    done[...] = jnp.zeros(done.shape, F32)
    for c in range(64):
        flat[pl.ds(c, 27, stride=64), :] = coarse[:, 128 * c : 128 * c + 128].astype(F32)
    flat[1728:1792, :] = jnp.zeros((64, 128), F32)
    wide = low_half((128, 128))
    none = jnp.zeros((64, 128), F32)
    zero = jnp.zeros((128, 128), F32)
    turned = []
    for m in range(14):
        value = flat[128 * m : 128 * m + 128, :].T
        turned += [jnp.where(wide, value, swap(value)), jnp.where(wide, swap(value), value)]
    for ab in range(9):
        for j in range(4):
            row = (4 * ab + j) * 64
            at = (3 * ab + j) * 64
            left = flat[at : at + 64, :] if j < 3 else none
            right = flat[at - 64 : at, :] if j > 0 else none
            wc[row : row + 64, 0:128] = left.astype(BF16)
            wc[row : row + 64, 128:256] = right.astype(BF16)
            slot = 26 - 3 * ab - j
            row = 2 * row
            left = turned[slot] if j < 3 else zero
            right = turned[slot + 1] if j > 0 else zero
            wcb[row : row + 128, 0:128] = left.astype(BF16)
            wcb[row : row + 128, 128:256] = right.astype(BF16)


def backward_weights_kernel(fine, wfb, done, flat):
    done[...] = jnp.zeros(done.shape, F32)
    flat_fine(fine, flat)
    flat[1728:1792, :] = jnp.zeros((64, 128), F32)
    mask = low_half((64, 128))
    none = jnp.zeros((64, 128), F32)
    turned = []
    for m in range(14):
        value = flat[128 * m : 128 * m + 128, :].T[0:64]
        turned += [jnp.where(mask, value, swap(value)), jnp.where(mask, swap(value), value)]
    for ab in range(9):
        for j in range(4):
            row = (4 * ab + j) * 64
            slot = 26 - 3 * ab - j
            left = turned[slot] if j < 3 else none
            right = turned[slot + 1] if j > 0 else none
            wfb[row : row + 64, :] = jnp.where(mask, left, right).astype(BF16)


def z_faces_kernel(z_odd, own, cot, zl, zh, faces, cfaces, edge, sems):
    copies = []
    for k, lane in enumerate((0, 640)):
        lanes = pl.ds(lane, 128)
        copies.append(pltpu.make_async_copy(own.at[:, :, lanes], faces.at[k], sems.at[2 * k]))
        copies.append(pltpu.make_async_copy(cot.at[:, :, lanes], cfaces.at[k], sems.at[2 * k + 1]))
    for copy in copies:
        copy.start()
    for copy in copies:
        copy.wait()
    to_high, to_low = pack_faces(faces[0].astype(F32), faces[1].astype(F32))
    for out, face, k in ((zl, to_high, 1), (zh, to_low, 0)):
        edge[:, 0:6, :] = cfaces[k].astype(F32)
        turned = [edge[:, y : y + 1, :].reshape(12, 128)[None] for y in range(6)]
        turned = jnp.concatenate(turned, axis=0)
        pad = jnp.zeros((6, 4, 128), F32)
        out[...] = jnp.concatenate([face, turned, pad], axis=1).astype(BF16)
    pair_up(z_odd[0] == 1, zl, zh)


def edge_lanes(lo, hi):
    low = jnp.concatenate([lo, swap(lo)], axis=0)
    high = jnp.concatenate([swap(hi), hi], axis=0)
    return low, high


def x_faces_kernel(z_odd, own, cot, zlo, zhi, rows_out, cot_out, xl, xh, ends, crows, message):
    lo, hi = sides(z_odd[0] == 1, zlo, zhi)
    low, high = edge_lanes(lo[:, 0:24], hi[:, 0:24])
    mask = low_half((12, 24, 128))
    rows_out[...] = own[...]
    for at, part in ((0, jnp.where(mask, low, 0.0)), (768, jnp.where(mask, 0.0, high))):
        lanes = slice(at, at + 128)
        rows_out[:, 0:24, lanes] = (own[:, 0:24, lanes].astype(F32) + part).astype(BF16)
    crows[:, 8:16, :] = jnp.zeros((6, 8, 1024), F32)
    crows[:, 0:12, 0:128] = lo[:, 24:36]
    crows[:, 0:12, 128:896] = cot[...].astype(F32)
    crows[:, 0:12, 896:1024] = hi[:, 24:36]
    cot_out[...] = crows[...].astype(BF16)
    ends[0] = rows_out[:, 0:8, :].astype(F32)
    ends[1] = rows_out[:, 16:24, :].astype(F32)
    message[...] = jnp.zeros(message.shape, F32)
    for out, k, x, cx in ((xl, 1, 7, 11), (xh, 0, 0, 0)):
        for y in range(12):
            message[y : y + 1, 0:896] = ends[k, y, x : x + 1, :]
        for y in range(6):
            message[12 + y : 13 + y, :] = crows[y, cx : cx + 1, :]
        out[...] = message[...].astype(BF16)


def y_faces_kernel(
    rows_in, cot_in, xlo, xhi, rows_out, cot_out, yl, yh, rows, crows, lo, hi
):
    lo[...] = xlo[...].astype(F32)
    hi[...] = xhi[...].astype(F32)
    rows[...] = rows_in[...].astype(F32)
    crows[...] = cot_in[...].astype(F32)
    for y in range(12):
        rows[y, 24:25, :] = hi[y : y + 1, 0:896]
        rows[y, 31:32, :] = lo[y : y + 1, 0:896]
    for y in range(6):
        crows[y, 12:13, :] = hi[12 + y : 13 + y, :]
        crows[y, 15:16, :] = lo[12 + y : 13 + y, :]
    rows_out[...] = rows[...].astype(BF16)
    cot_out[...] = crows[...].astype(BF16)
    for out, y, cy in ((yl, 11, 5), (yh, 0, 0)):
        out[0:32, 0:896] = rows[y].astype(BF16)
        out[0:32, 896:1024] = jnp.zeros((32, 128), BF16)
        out[32:48, :] = crows[cy].astype(BF16)


def act_x_faces_kernel(core, z_odd, own, zlo, zhi, rows_out, xl, xh, rows, message):
    z_lo, z_hi = sides(z_odd[0] == 1, zlo, zhi)
    rows[:, 0:24, :] = with_faces(own[...].astype(F32)[:, 0:24], z_lo, z_hi)
    rows[:, 24:32, :] = jnp.zeros((12, 8, 896), F32)
    rows_out[...] = rows[...].astype(BF16)
    message[...] = jnp.zeros(message.shape, F32)
    for out, x in ((xl, 23), (xh, 0)):
        for y in range(12):
            message[y : y + 1, :] = rows[y, x : x + 1, :]
        out[...] = message[...].astype(BF16)
    pair_up(core[0] == 1, xl, xh)


def act_y_faces_kernel(core, rows_in, xlo, xhi, rows_out, yl, yh, rows, lo, hi):
    lo[...], hi[...] = sides(core[0] == 1, xlo, xhi)
    rows[...] = rows_in[...].astype(F32)
    for y in range(12):
        rows[y, 24:25, :] = hi[y : y + 1, :]
        rows[y, 31:32, :] = lo[y : y + 1, :]
    value = rows[...].astype(BF16)
    rows_out[...] = value
    yl[...] = value[11]
    yh[...] = value[0]


def sigmoid(value):
    return 0.5 + 0.5 * jnp.tanh(0.5 * value)


def silu(act):
    return (act * sigmoid(act)).astype(BF16)


def silu_slope(act):
    sigma = sigmoid(act)
    return sigma * (1.0 + act * (1.0 - sigma))


def slope_kernel(inner, outer, slope, done):
    slope[0:32, :] = silu_slope(outer[0:32, :]).astype(BF16)
    slope[32:352, :] = silu_slope(inner[...]).astype(BF16)
    slope[352:384, :] = silu_slope(outer[32:64, :]).astype(BF16)
    done[...] = jnp.zeros(done.shape, F32)


def pool_matrix(shape, rule):
    r = lax.broadcasted_iota(jnp.int32, shape, 0)
    q = lax.broadcasted_iota(jnp.int32, shape, 1)
    return jnp.where(rule(r, q), 0.125, 0.0).astype(BF16)


def fold_pairs(part):
    return part + swap(part)


def interior_kernel(rows, weight, shifted, kept, edges, pooled):
    full = rows[...].astype(F32)
    for a in range(3):
        shifted[a] = rolled_rows(full, 1 - a).astype(BF16).reshape(384, 896)
    pool = pool_matrix(
        (64, 320),
        lambda r, q: ((((q >> 5) + 1) >> 1) == (r >> 4) + 1) & (((q & 31) >> 1) == (r & 15)),
    )
    mask = low_half((64, 128))
    for p in range(6):
        lanes = slice(128 * p, 128 * p + 256)
        left = jnp.concatenate(
            [shifted[a, 32 * b : 32 * b + 320, lanes] for a in range(3) for b in range(3)], axis=1
        )
        kept[:, 128 * p : 128 * p + 128] = jnp.dot(
            left, weight[...], preferred_element_type=F32
        )
    hidden = silu(kept[...])
    edges[0:32, :] = hidden[0:32]
    edges[32:64, :] = hidden[288:320]
    sums = jnp.dot(pool, hidden, preferred_element_type=F32)
    pieces = [fold_pairs(sums[:, 128 * p : 128 * p + 128]) for p in range(6)]
    for j in range(3):
        both = jnp.where(mask, pieces[2 * j], pieces[2 * j + 1])
        pooled[:, :, 128 * j : 128 * j + 128] = both.astype(BF16).reshape(4, 16, 128)


def border_kernel(
    z_odd, shifted, ylo, yhi, weight, edges, inner, kept, pooled, zl, zh, outer
):
    both = jnp.concatenate(
        [ylo[0:32, 0:896][None], yhi[0:32, 0:896][None]], axis=0
    ).astype(F32)
    for a in range(3):
        outer[a] = rolled_rows(both, 1 - a).astype(BF16).reshape(64, 896)
    blocks = []
    for p in range(6):
        lanes = slice(128 * p, 128 * p + 256)
        first = []
        last = []
        for a in range(3):
            first += [outer[a, 0:32, lanes], shifted[a, 0:32, lanes], shifted[a, 32:64, lanes]]
            last += [
                shifted[a, 320:352, lanes], shifted[a, 352:384, lanes], outer[a, 32:64, lanes]
            ]
        blocks.append(jnp.concatenate(first, axis=1))
        blocks.append(jnp.concatenate(last, axis=1))
    act = jnp.dot(jnp.concatenate(blocks, axis=0), weight[...], preferred_element_type=F32)
    hidden = silu(act)
    pool = pool_matrix(
        (32, 128),
        lambda r, q: (((q >> 5) & 1) == (r >> 4)) & (((q & 31) >> 1) == (r & 15)),
    )
    mask = low_half((32, 128))
    pieces = []
    for p in range(6):
        own = slice(128 * p, 128 * p + 128)
        kept[:, own] = act[64 * p : 64 * p + 64]
        column = jnp.concatenate([hidden[64 * p : 64 * p + 64], edges[:, own]], axis=0)
        pieces.append(fold_pairs(jnp.dot(pool, column, preferred_element_type=F32)))
    for j in range(3):
        own = slice(128 * j, 128 * j + 128)
        both = jnp.where(mask, pieces[2 * j], pieces[2 * j + 1]).astype(BF16)
        pooled[0:1, :, own] = both[0:16][None]
        pooled[5:6, :, own] = both[16:32][None]
    pooled[1:5] = inner[...]
    zl[...] = pooled[:, :, 256:384]
    zh[...] = pooled[:, :, 0:128]
    pair_up(z_odd[0] == 1, zl, zh)


def pooled_x_kernel(core, z_odd, own, zlo, zhi, rows_out, xl, xh, rows, message):
    rows[:, :, 0:128], rows[:, :, 512:640] = sides(z_odd[0] == 1, zlo, zhi)
    rows[:, :, 128:512] = own[...].astype(F32)
    rows_out[...] = rows[...].astype(BF16)
    message[...] = jnp.zeros(message.shape, F32)
    for out, x in ((xl, 10), (xh, 0)):
        for y in range(6):
            message[2 * y : 2 * y + 2, :] = rows[y, x : x + 2, :]
        out[...] = message[...].astype(BF16)
    pair_up(core[0] == 1, xl, xh)


def pooled_y_kernel(core, rows_in, xlo, xhi, rows_out, yl, yh, rows, lo, hi):
    lo[...], hi[...] = sides(core[0] == 1, xlo, xhi)
    rows[...] = rows_in[...].astype(F32)
    for y in range(6):
        rows[y, 12:14, :] = hi[2 * y : 2 * y + 2, :]
        rows[y, 14:16, :] = lo[2 * y : 2 * y + 2, :]
    value = rows[...].astype(BF16)
    rows_out[...] = value
    yl[...] = value[4:6]
    yh[...] = value[0:2]


def backward_kernel(
    z_odd, prow, pylo, pyhi, crow, ylo, yhi, slope, wc, wb,
    act_out, zl, zh, fine_left, coarse_left, pshift, gshift,
):
    full = jnp.concatenate([pylo[...], prow[...], pyhi[...]], axis=0).astype(F32)
    for a in range(3):
        pshift[a] = rolled_rows(full, 1 - a).astype(BF16).reshape(160, 640)
    blocks = []
    for p in range(4):
        lanes = slice(128 * p, 128 * p + 256)
        blocks.append(
            jnp.concatenate(
                [pshift[a, 16 * b : 16 * b + 128, lanes] for a in range(3) for b in range(3)], axis=1
            )
        )
    pre = jnp.dot(jnp.concatenate(blocks, axis=0), wc[...], preferred_element_type=F32)
    tilt = silu_slope(pre)
    cot = jnp.concatenate([ylo[32:48][None], crow[...], yhi[32:48][None]], axis=0).astype(F32)
    row = lax.broadcasted_iota(jnp.int32, (128, 256), 0)
    lane = lax.broadcasted_iota(jnp.int32, (128, 256), 1)
    own_rows = (row >= 16) & (row < 112) & ((row & 15) < 12)
    parts = []
    for p in range(4):
        grad = cot[:, :, 256 * p : 256 * p + 256].reshape(128, 256) * tilt[128 * p : 128 * p + 128]
        grad = grad.astype(BF16).astype(F32)
        parts.append(grad)
        valid = own_rows
        if p == 0:
            valid = valid & (lane >= 128)
        if p == 3:
            valid = valid & (lane < 128)
        coarse_left[:, 128 * p : 128 * p + 128] = jnp.where(valid, grad, 0.0).T.astype(BF16)
    both = jnp.concatenate(parts, axis=1).reshape(8, 16, 1024)
    for a in range(3):
        gshift[a] = rolled_rows(both, 1 - a).astype(BF16).reshape(128, 1024)
    blocks = []
    for p in range(3):
        lanes = slice(256 * p, 256 * p + 512)
        blocks.append(
            jnp.concatenate(
                [gshift[a, 16 * b : 16 * b + 96, lanes] for a in range(3) for b in range(3)], axis=1
            )
        )
    small = jnp.dot(jnp.concatenate(blocks, axis=0), wb[...], preferred_element_type=F32)
    small = small.astype(BF16)
    q = lax.broadcasted_iota(jnp.int32, (384, 96), 0)
    r = lax.broadcasted_iota(jnp.int32, (384, 96), 1)
    inside = ((q >> 6) == (r >> 4)) & (((q & 31) >> 1) == (r & 15)) & ((q & 31) < 24)
    spread = jnp.where(inside, 1.0, 0.0).astype(BF16)
    for p in range(3):
        lanes = slice(256 * p, 256 * p + 256)
        up = jnp.dot(spread, small[96 * p : 96 * p + 96], preferred_element_type=F32)
        part = (up * 0.125 * slope[:, lanes].astype(F32)).astype(BF16)
        act_out[:, :, lanes] = part.reshape(12, 32, 256)
        wide = part.astype(F32)
        fine_left[:, 768 * p : 768 * p + 384] = wide[:, 0:128].T.astype(BF16)
        fine_left[:, 768 * p + 384 : 768 * p + 768] = wide[:, 128:256].T.astype(BF16)
        if p == 0:
            low = wide[:, 0:128].reshape(12, 32, 128)[:, 0:24]
        if p == 2:
            high = wide[:, 128:256].reshape(12, 32, 128)[:, 0:24]
    to_high, to_low = pack_faces(low, high)
    zl[...] = to_high.astype(BF16)
    zh[...] = to_low.astype(BF16)
    pair_up(z_odd[0] == 1, zl, zh)


def all_rows(rows, ylo, yhi, shifted, used):
    lo = ylo[0:32, 0:896][None]
    hi = yhi[0:32, 0:896][None]
    full = jnp.concatenate([lo, rows[...], hi], axis=0).astype(F32)
    for a in used:
        shifted[a] = rolled_rows(full, 1 - a).astype(BF16).reshape(448, 896)


def fine_grads(left, shifted, turned, pairs, sums, offsets):
    mask = low_half((32, 128))
    for a, b in offsets:
        right = jnp.concatenate(
            [shifted[a, 32 * b : 32 * b + 384, 128 * p : 128 * p + 256] for p in range(6)], axis=0
        )
        turned[...] = jnp.dot(left[...], right, preferred_element_type=F32).T
        for e in range(3):
            near = turned[64 * e : 64 * e + 64]
            pairs[...] = near + swap(turned[64 * e + 64 : 64 * e + 128])
            even = pairs[pl.ds(0, 32, stride=2), :]
            odd = pairs[pl.ds(1, 32, stride=2), :]
            slot = 9 * a + 3 * b + e
            sums[pl.ds(slot, 32, stride=32), :] = jnp.where(mask, even, swap(odd))


EARLY = [(0, 0), (0, 1), (0, 2), (1, 0), (1, 1), (1, 2), (2, 0), (2, 1)]
LATE = [(2, 2)]


def early_grads_kernel(
    coarse_left, pshift, left, rows, ylo, yhi, out, turned, pairs, sums, cturned, shifted
):
    all_rows(rows, ylo, yhi, shifted, (0, 1, 2))
    sums[...] = jnp.zeros(sums.shape, F32)
    for a in range(3):
        for b in range(3):
            right = jnp.concatenate(
                [pshift[a, 16 * b : 16 * b + 128, 128 * p : 128 * p + 256] for p in range(4)], axis=0
            )
            cturned[...] = jnp.dot(coarse_left[...], right, preferred_element_type=F32).T
            for e in range(3):
                near = cturned[64 * e : 64 * e + 64, 0:128]
                far = cturned[64 * e + 64 : 64 * e + 128, 128:256]
                sums[pl.ds(1024 + 9 * a + 3 * b + e, 64, stride=32), :] = near + far
    fine_grads(left, shifted, turned, pairs, sums, EARLY)
    out[...] = sums[...].astype(BF16).reshape(96, 32, 128)


def late_grads_kernel(
    core, left, rows, ylo, yhi, early, keep, send, turned, pairs, sums, whole, shifted
):
    all_rows(rows, ylo, yhi, shifted, (2,))
    sums[...] = early[0:32].astype(F32).reshape(1024, 128)
    fine_grads(left, shifted, turned, pairs, sums, LATE)
    whole[0:32] = sums[...].astype(BF16).reshape(32, 32, 128)
    whole[32:96] = early[32:96]
    keep[...] = whole[pl.ds(core[0] * 48, 48)]
    send[...] = whole[pl.ds((1 - core[0]) * 48, 48)]


def features_kernel(rows, ylo, yhi, weight, out, done, shifted):
    done[...] = jnp.zeros(done.shape, F32)
    full = jnp.concatenate([ylo[...][None], rows[...], yhi[...][None]], axis=0).astype(F32)
    for a in range(3):
        shifted[a] = rolled_rows(full, 1 - a).astype(BF16).reshape(448, 896)
    for p in range(6):
        lanes = slice(128 * p, 128 * p + 256)
        left = jnp.concatenate(
            [shifted[a, 32 * b : 32 * b + 384, lanes] for a in range(3) for b in range(3)], axis=1
        )
        grad = jnp.dot(left, weight[...], preferred_element_type=F32)
        grad = grad.reshape(12, 32, 128)[:, 0:24, :]
        out[:, :, 128 * p : 128 * p + 128] = grad.astype(BF16)


def combine_kernel(count, parts, *refs):
    at, ins, outs = refs[0], refs[1 : 1 + parts], refs[1 + parts :]
    size = outs[0].shape[0]
    for k in range(count):
        start = lax.rem(at[0] + k, count) * size
        terms = [ref[pl.ds(start, size)].astype(F32) for ref in ins]
        while len(terms) > 1:
            terms = [sum(terms[i : i + 2][1:], terms[i]) for i in range(0, len(terms), 2)]
        outs[k][...] = terms[0].astype(outs[k].dtype)


def combine(values, place, count, after=()):
    size = values[0].shape[0] // count
    return call(
        functools.partial(combine_kernel, count, len(values)),
        [((size, 32, 128), BF16)] * count, values, place=place, after=after,
    )


def place_kernel(count, *refs):
    at, ins, out = refs[0], refs[1 : 1 + count], refs[-1]
    size = ins[0].shape[0]
    for k in range(count):
        out[pl.ds(lax.rem(at[0] + count - k, count) * size, size)] = ins[k][...]


def placed(values, place, after=()):
    count = len(values)
    size = values[0].shape[0]
    return call(
        functools.partial(place_kernel, count),
        [((count * size, 32, 128), BF16)], values, place=place, after=after,
    )[0]


def last_kernel(core, own, other, fine, coarse, whole):
    whole[pl.ds(core[0] * 48, 48)] = own[...]
    whole[pl.ds((1 - core[0]) * 48, 48)] = other[...]
    cells = 96 * 96 * 96
    for r in range(96):
        value = whole[r].astype(F32)[0:27]
        if r < 32:
            fine[:, 128 * r : 128 * r + 128] = value * (1.0 / math.sqrt(cells))
        else:
            at = 128 * (r - 32)
            coarse[:, at : at + 128] = value * (1.0 / math.sqrt(cells // 8))


def core_partner(value):
    return lax.ppermute(value, "gx", [(i, i ^ 1) for i in range(4)])


def matched(first, second, axis):
    count = lax.axis_size(axis)
    low = [(i, (i - 1 + 2 * (i % 2)) % count) for i in range(count)]
    high = [(i, (i + 1 - 2 * (i % 2)) % count) for i in range(count)]
    return lax.ppermute(first, axis, low), lax.ppermute(second, axis, high)


def z_partner(value, far):
    return lax.ppermute(value, "gy", [(i, i ^ far) for i in range(8)])


def y_turn(value, step):
    pairs = [(i, i // 4 * 4 + (i + step) % 4) for i in range(8)]
    return lax.ppermute(value, "gz", pairs)


def x_turn(value, step):
    pairs = []
    for gx in range(4):
        for gz in range(8):
            x = (gz // 4 * 2 + gx // 2 + step) % 4
            pairs.append((gx * 8 + gz, (x % 2 * 2 + gx % 2) * 8 + x // 2 * 4 + gz % 4))
    return lax.ppermute(value, ("gx", "gz"), pairs)


def body(features, fine_weight, coarse_weight, cotangent):
    gx = lax.axis_index("gx").astype(jnp.int32)
    gz = lax.axis_index("gz").astype(jnp.int32)
    core = (gx % 2).reshape(1)
    y_at = (gz % 4).reshape(1)
    x_at = (gz // 4 * 2 + gx // 2).reshape(1)
    z_at = jnp.zeros((1,), jnp.int32)
    z_odd = (gz % 2).reshape(1)

    own = jnp.transpose(features, (1, 0, 2))
    zl, zh = call(
        z_faces_kernel, [((6, 40, 128), BF16)] * 2, (own, cotangent),
        [
            pltpu.VMEM((2, 12, 24, 128), BF16), pltpu.VMEM((2, 12, 6, 128), BF16),
            pltpu.VMEM((12, 8, 128), F32), pltpu.SemaphoreType.DMA((4,)),
        ],
        space=HBM, place=z_odd,
    )
    zlo, zhi = matched(zl, zh, "gz")
    w_fine, frows = call(
        forward_weights_kernel, [((2304, 128), BF16), ((12, 32, 896), BF16)], (fine_weight, own),
        [pltpu.VMEM((1728, 128), F32)], after=(zh,),
    )
    frows, crows, xl, xh = call(
        x_faces_kernel,
        [((12, 32, 896), BF16), ((6, 16, 1024), BF16), ((24, 1024), BF16), ((24, 1024), BF16)],
        (frows, jnp.transpose(cotangent, (1, 0, 2)), zlo, zhi),
        [
            pltpu.VMEM((2, 12, 8, 896), F32), pltpu.VMEM((6, 16, 1024), F32),
            pltpu.VMEM((24, 1024), F32),
        ],
        place=z_odd,
    )
    xlo = shift(xl, "gx", 1)
    xhi = shift(xh, "gx", -1)
    frows, crows, yl, yh = call(
        y_faces_kernel,
        [((12, 32, 896), BF16), ((6, 16, 1024), BF16), ((48, 1024), BF16), ((48, 1024), BF16)],
        (frows, crows, xlo, xhi),
        [
            pltpu.VMEM((12, 32, 896), F32), pltpu.VMEM((6, 16, 1024), F32),
            pltpu.VMEM((24, 1024), F32), pltpu.VMEM((24, 1024), F32),
        ],
    )
    ylo = shift(yl, "gy", 1)
    yhi = shift(yh, "gy", -1)
    shifted, act_in, edges, inner = call(
        interior_kernel,
        [((3, 384, 896), BF16), ((320, 768), F32), ((64, 768), BF16), ((4, 16, 384), BF16)],
        (frows, w_fine),
        flops=CONV,
    )
    act_out, pooled, pzl, pzh = call(
        border_kernel,
        [
            ((64, 768), F32), ((6, 16, 384), BF16),
            ((6, 16, 128), BF16), ((6, 16, 128), BF16),
        ],
        (shifted, ylo, yhi, w_fine, edges, inner),
        [pltpu.VMEM((3, 64, 896), BF16)],
        flops=CONV // 6, place=z_odd,
    )
    pzlo, pzhi = matched(pzl, pzh, "gz")
    w_coarse, w_coarse_back, done = call(
        coarse_weights_kernel,
        [((2304, 256), BF16), ((4608, 256), BF16), ((8, 128), F32)],
        (coarse_weight,), [pltpu.VMEM((1792, 128), F32)], after=(pzh,),
    )
    prows, pxl, pxh = call(
        pooled_x_kernel,
        [((6, 16, 640), BF16), ((16, 640), BF16), ((16, 640), BF16)],
        (pooled, pzlo, pzhi),
        [pltpu.VMEM((6, 16, 640), F32), pltpu.VMEM((16, 640), F32)],
        after=(done,), place=(core, z_odd),
    )
    pxlo, pxhi = matched(pxl, pxh, "gx")
    slope, done = call(
        slope_kernel, [((384, 768), BF16), ((8, 128), F32)], (act_in, act_out), after=(pxh,)
    )
    prows, pyl, pyh = call(
        pooled_y_kernel,
        [((6, 16, 640), BF16), ((2, 16, 640), BF16), ((2, 16, 640), BF16)],
        (prows, pxlo, pxhi),
        [pltpu.VMEM((6, 16, 640), F32), pltpu.VMEM((16, 640), F32), pltpu.VMEM((16, 640), F32)],
        after=(done,), place=core,
    )
    pylo = shift(pyl, "gy", 1)
    pyhi = shift(pyh, "gy", -1)
    act, azl, azh, fine_left, coarse_left, pshift = call(
        backward_kernel,
        [
            ((12, 32, 768), BF16), ((6, 24, 128), BF16), ((6, 24, 128), BF16),
            ((128, 2304), BF16), ((256, 512), BF16), ((3, 160, 640), BF16),
        ],
        (prows, pylo, pyhi, crows, ylo, yhi, slope, w_coarse, w_coarse_back),
        [pltpu.VMEM((3, 128, 1024), BF16)],
        flops=CONV, place=z_odd,
    )
    azlo, azhi = matched(azl, azh, "gz")
    (early,) = call(
        early_grads_kernel, [((96, 32, 128), BF16)],
        (coarse_left, pshift, fine_left, frows, ylo, yhi),
        [
            pltpu.VMEM((256, 128), F32), pltpu.VMEM((64, 128), F32),
            pltpu.VMEM((3072, 128), F32), pltpu.VMEM((256, 256), F32),
            pltpu.VMEM((3, 448, 896), BF16),
        ],
        flops=CONV,
    )
    keep, send = call(
        late_grads_kernel,
        [((48, 32, 128), BF16), ((48, 32, 128), BF16)],
        (fine_left, frows, ylo, yhi, early),
        [
            pltpu.VMEM((256, 128), F32), pltpu.VMEM((64, 128), F32),
            pltpu.VMEM((1024, 128), F32), pltpu.VMEM((96, 32, 128), BF16),
            pltpu.VMEM((3, 448, 896), BF16),
        ],
        flops=CONV // 2, place=core, after=(azlo, azhi),
    )

    parts = combine((keep, core_partner(send)), y_at, 4)
    got = tuple(y_turn(parts[k], k) for k in (1, 2, 3))
    arows, axl, axh = call(
        act_x_faces_kernel,
        [((12, 32, 896), BF16), ((16, 896), BF16), ((16, 896), BF16)],
        (act, azlo, azhi),
        [pltpu.VMEM((12, 32, 896), F32), pltpu.VMEM((16, 896), F32)],
        after=(parts[0],), place=(core, z_odd),
    )
    axlo, axhi = matched(axl, axh, "gx")
    parts = combine((parts[0],) + got, x_at, 4, after=(axlo, axhi))
    got = tuple(x_turn(parts[k], k) for k in (1, 2, 3))
    arows, ayl, ayh = call(
        act_y_faces_kernel,
        [((12, 32, 896), BF16), ((32, 896), BF16), ((32, 896), BF16)],
        (arows, axlo, axhi),
        [pltpu.VMEM((12, 32, 896), F32), pltpu.VMEM((16, 896), F32), pltpu.VMEM((16, 896), F32)],
        after=(parts[0],), place=core,
    )
    aylo = shift(ayl, "gy", 1)
    ayhi = shift(ayh, "gy", -1)
    (part,) = combine((parts[0],) + got, z_at, 1, after=(aylo, ayhi))
    near, next_near, far = (z_partner(part, k) for k in (1, 2, 3))
    w_fine_back, done = call(
        backward_weights_kernel, [((2304, 128), BF16), ((8, 128), F32)],
        (fine_weight,), [pltpu.VMEM((1792, 128), F32)], after=(part,),
    )
    (part,) = combine((part, near, next_near, far), z_at, 1, after=(done,))
    (part,) = combine((part, z_partner(part, 7)), z_at, 1)
    part = placed((part,) + tuple(x_turn(part, k) for k in (1, 2, 3)), x_at)
    got = tuple(y_turn(part, k) for k in (1, 2, 3))
    grad_features, done = call(
        features_kernel,
        [((12, 24, 768), BF16), ((8, 128), F32)],
        (arows, aylo, ayhi, w_fine_back),
        [pltpu.VMEM((3, 448, 896), BF16)],
        flops=CONV, after=(part,),
    )
    part = placed((part,) + got, y_at, after=(done,))
    fine, coarse = call(
        last_kernel,
        [((27, 4096), F32), ((27, 8192), F32)],
        (part, core_partner(part)),
        [pltpu.VMEM((96, 32, 128), BF16)],
        place=core,
    )
    return jnp.transpose(grad_features, (1, 0, 2)), fine, coarse


def solution(mesh):
    in_specs = (P("gx", "gy", "gz"), P(), P(), P("gx", "gy", "gz"))
    out_specs = (P("gx", "gy", "gz"), P(), P())
    return jax.shard_map(body, mesh=mesh, in_specs=in_specs, out_specs=out_specs, check_vma=False)
```
